128 devices in a mesh: section: 2 (over y_lo), dp: 64 (over y_hi, x, z, core).
Axes of the slice: x: 4, y: 4 (y_hi: 2, y_lo: 2; y = y_hi * 2 + y_lo), z: 4, core: 2. Of those that a mesh axis runs over, the one named last changes fastest.
Arguments:
- acts: bfloat16 [2, 128, 128, 768], P('section', 'dp'), may hold values from -6 to 6
- gains: float32 [2, 3, 768], P('section'), may hold values from 0.25 to 1.75
- qkv_weight: bfloat16 [2, 768, 2304], P('section'), may hold values from -0.21875 to 0.21875
- out_weight: bfloat16 [2, 768, 768], P('section'), may hold values from -0.875 to 0.875
- mlp_in: bfloat16 [2, 768, 4096], P('section'), may hold values from -0.21875 to 0.21875
- mlp_out: bfloat16 [2, 2048, 768], P('section'), may hold values from -0.25 to 0.25
- cross_weight: bfloat16 [2, 768, 1536], P('section'), may hold values from -1 to 1
- patch_mask: int32 [128, 128], P('dp'), may hold values from 0 to 1, as said below
- table_len: int32 [128], P('dp'), may hold values from 16 to 128, as said below
- slot_plot: int32 [64, 2], P('dp'), may hold values from 0 to 1, each once within a row
- cotangent: bfloat16 [128, 128, 768], P('dp'), may hold values from -6 to 6
Outputs:
- out_acts: bfloat16 [2, 128, 128, 768], P('section', 'dp')
- grad_acts: float32 [2, 128, 128, 768], P('section', 'dp')
- grad_gains: float32 [2, 3, 768], P('section', None, 'dp')
- grad_qkv: float32 [2, 768, 2304], P('section', 'dp')
- grad_out: float32 [2, 768, 768], P('section', 'dp')
- grad_mlp_in: float32 [2, 768, 4096], P('section', 'dp')
- grad_mlp_out: float32 [2, 2048, 768], P('section', 'dp')
- grad_cross: float32 [2, 768, 1536], P('section', 'dp')
The draws below stay inside these ranges and needn't reach their ends.
Inputs may be any that keep to these rules, and one draw needn't show every extreme that they name: `patch_mask`: each row is 1 on a leading run of positions and 0 after it, with at least 32 ones; some row is all ones. `table_len`: some table has 128 tokens. `slot_plot`: each row is a permutation.
All inputs are finite; a program needn't handle non-finite values.
Results may differ from the reference program's by a relative error of at most 0.025.
Values may be sent and summed in bfloat16 or wider, within the bound.
No kernel may reach another device: no remote copies, remote signals or barrier semaphores. Data moves between devices by JAX's collectives and lax.ppermute only.
A program may use at most 448 MiB of HBM per device.

```python
import jax
import jax.numpy as jnp
from jax import lax

D = 768
HEADS = 12
HDIM = 64
FF = 2048
SEQ = 128
MB = 2
ROWS = 128
N_DP = 64


def draw_cross_weight(key, part):
    key = jax.random.fold_in(key, 11)
    normal_draw = jnp.clip(jax.random.normal(key, (2, D, 2 * D), jnp.float32), -6.0, 6.0)
    column = jnp.arange(2 * D)[None, None, :]
    section_slot = jnp.arange(2)[:, None, None]
    wide_part = (section_slot == 1) & (column >= D)
    scaling = jnp.where(wide_part, float(D * 8 // SEQ) ** (-0.5), float(D) ** (-0.5))
    return (normal_draw * scaling).astype(jnp.bfloat16)


def draw_patch_mask(key, part):
    key = jax.random.fold_in(key, 23)
    count_key, pick_key = jax.random.split(key)
    counts = jax.random.randint(count_key, (ROWS,), SEQ // 4, SEQ + 1)
    chosen = jax.random.randint(pick_key, (), 0, ROWS)
    counts = jnp.where(jnp.arange(ROWS) == chosen, SEQ, counts)
    return (jnp.arange(SEQ)[None, :] < counts[:, None]).astype(jnp.int32)


def draw_table_len(key, part):
    key = jax.random.fold_in(key, 37)
    count_key, pick_key = jax.random.split(key)
    counts = jax.random.randint(count_key, (ROWS,), max(SEQ // 8, 1), SEQ + 1)
    chosen = jax.random.randint(pick_key, (), 0, ROWS)
    return jnp.where(jnp.arange(ROWS) == chosen, SEQ, counts).astype(jnp.int32)


def levels(rng, extent, cuts, smallest, high):
    level, own = 1.0, jax.random.fold_in(rng, 6)
    for position, blocks in cuts:
        steps = jnp.exp(jax.random.uniform(jax.random.fold_in(own, position), (blocks,), jnp.float32, smallest / len(cuts), high / len(cuts)))
        level = level * jnp.repeat(steps, extent[position] // blocks).reshape([-1 if axis == position else 1 for axis in range(len(extent))])
    return level


def bell_draw(stream_key, extent, spread, bound, cuts=(), kind=jnp.bfloat16):
    values = jax.random.normal(stream_key, extent, jnp.float32) * spread
    if len(cuts) > 0:
        values = levels(stream_key, extent, cuts, -0.22, 0.18) * values
    return jnp.clip(values, min=-bound, max=bound).astype(kind)


def setup_inputs(seed: int = 0) -> dict:
    arg_keys = jax.random.split(jax.random.key(seed), 12)
    return {
        "acts": bell_draw(arg_keys[0], (2, ROWS, SEQ, D), 1.0, 6.0, ((0, 2), (1, 64))),
        "gains": jnp.clip(1.0 + 0.15 * jax.random.normal(arg_keys[1], (2, 3, D), jnp.float32), 0.25, 1.75),
        "qkv_weight": bell_draw(arg_keys[2], (2, D, 3 * D), D ** -0.5, 0.21875, ((0, 2),)),
        "out_weight": bell_draw(arg_keys[3], (2, D, D), (D * 8 // SEQ) ** -0.5, 0.875, ((0, 2),)),
        "mlp_in": bell_draw(arg_keys[4], (2, D, 2 * FF), D ** -0.5, 0.21875, ((0, 2),)),
        "mlp_out": bell_draw(arg_keys[5], (2, FF, D), (FF // 4) ** -0.5, 0.25, ((0, 2),)),
        "cross_weight": draw_cross_weight(jax.random.fold_in(arg_keys[11], 71), 0),
        "patch_mask": draw_patch_mask(jax.random.fold_in(arg_keys[11], 71), 0),
        "table_len": draw_table_len(jax.random.fold_in(arg_keys[11], 71), 0),
        "slot_plot": jax.vmap(lambda own: jax.random.permutation(own, MB))(jax.random.split(arg_keys[9], N_DP)).reshape((N_DP, MB)).astype(jnp.int32),
        "cotangent": bell_draw(arg_keys[10], (ROWS, SEQ, D), 1.0, 6.0, ((0, 64),)),
    }


@jax.custom_vjp
def low(v):
    return lax.optimization_barrier(v.astype(jnp.bfloat16)).astype(jnp.float32)

@jax.custom_vjp
def low_back(v):
    return v

def low_keep(v):
    return (low(v), None)

def low_pass(kept, grad):
    return (grad,)

def back_keep(v):
    return (v, None)

def back_low(kept, grad):
    return (low(grad),)
low.defvjp(low_keep, low_pass)
low_back.defvjp(back_keep, back_low)
EPS = 1e-06
NEGATIVE = -1e+30

def normed(hidden, scales):
    return hidden * lax.rsqrt(lax.optimization_barrier(jnp.mean(hidden * hidden, axis=-1, keepdims=True)) + EPS) * scales

def project(left_side, matrix):
    return jnp.einsum('gsd,de->gse', left_side, matrix, precision=lax.Precision.HIGHEST)

def gated_unit(inner_part):
    return jax.nn.gelu(inner_part[..., :FF], approximate=True) * inner_part[..., FF:]

def attend(queries, key_rows, value_rows, allowed):
    groups, length = (queries.shape[0], queries.shape[1])
    query_heads = queries.reshape(groups, length, HEADS, HDIM)
    key_heads = key_rows.reshape(groups, key_rows.shape[1], HEADS, HDIM)
    value_heads = value_rows.reshape(groups, value_rows.shape[1], HEADS, HDIM)
    scores = low_back(jnp.einsum('gqhd,gkhd->ghqk', query_heads, key_heads, precision=lax.Precision.HIGHEST) * HDIM ** (-0.5))
    scores = jnp.where(allowed, scores, NEGATIVE)
    weights = low(jax.nn.softmax(scores, axis=-1))
    mixed_rows = jnp.einsum('ghqk,gkhd->gqhd', weights, value_heads, precision=lax.Precision.HIGHEST)
    return low(low_back(mixed_rows.reshape(groups, length, HEADS * HDIM)))

def feed_forward(hidden, scales, w_in, w_down):
    inner_part = low_back(project(low(normed(hidden, scales)), w_in))
    return hidden + low_back(project(low(gated_unit(inner_part)), w_down))

def self_attention(hidden, scales, w_qkv, w_out, allowed):
    packed = low(low_back(project(low(normed(hidden, scales)), w_qkv)))
    mixed_rows = attend(packed[..., :D], packed[..., D:2 * D], packed[..., 2 * D:], allowed)
    return hidden + low_back(project(mixed_rows, w_out))

def encoder(plot_rows, keep_mask, scales, w_qkv, w_out, w_in, w_down, w_kv):
    allowed = (keep_mask > 0)[:, None, None, :]
    first_sum = self_attention(plot_rows, scales[0], w_qkv, w_out, allowed)
    second_sum = feed_forward(first_sum, scales[1], w_in, w_down)
    memory = low(normed(second_sum, scales[2]) * keep_mask[..., None])
    return (memory, low(low_back(project(memory, w_kv))))

def decoder(table_rows, memory_kv, keep_mask, valid_rows, scales, w_qkv, w_out, w_in, w_down, w_cross):
    positions = jnp.arange(SEQ)
    causal = (positions[:, None] >= positions[None, :])[None, None]
    first_sum = self_attention(table_rows, scales[0], w_qkv, w_out, causal)
    queries = low(low_back(project(low(normed(first_sum, scales[1])), w_cross[:, :D])))
    allowed = (keep_mask > 0)[:, None, None, :]
    mixed_rows = attend(queries, memory_kv[..., :D], memory_kv[..., D:], allowed)
    second_sum = first_sum + low_back(project(mixed_rows, w_cross[:, D:]))
    third_sum = feed_forward(second_sum, scales[2], w_in, w_down)
    return third_sum * valid_rows[..., None]

def reference(acts, gains, qkv_weight, out_weight, mlp_in, mlp_out, cross_weight, patch_mask, table_len, slot_plot, cotangent):
    plot_order = (jnp.arange(N_DP, dtype=jnp.int32)[:, None] * MB + slot_plot).reshape(-1).astype(jnp.int32)
    inverse = jnp.argsort(plot_order).astype(jnp.int32)
    plot_rows = jnp.take(acts[0], plot_order, axis=0).astype(jnp.float32)
    table_rows = jnp.take(acts[1], plot_order, axis=0).astype(jnp.float32)
    keep_mask = jnp.take(patch_mask, plot_order, axis=0).astype(jnp.float32)
    valid_rows = (jnp.arange(SEQ)[None, :] < jnp.take(table_len, plot_order)[:, None]).astype(jnp.float32)
    matrices = tuple((matrix.astype(jnp.float32) for matrix in (qkv_weight, out_weight, mlp_in, mlp_out, cross_weight)))
    encoder_params = (gains[0],) + tuple((matrix[0] for matrix in matrices))
    decoder_params = (gains[1],) + tuple((matrix[1] for matrix in matrices))
    group_size = 32 if ROWS % 32 == 0 else MB
    group_count = ROWS // group_size

    def grouped(array):
        return array.reshape((group_count, group_size) + array.shape[1:])

    def scan_step(totals, blocks):
        plot_block, table_block, keep_block, valid_block, cotangent_block = blocks

        def combined(enc_side, dec_side, plot_in, table_in):
            memory, memory_kv = encoder(plot_in, keep_block, *enc_side)
            return (decoder(table_in, memory_kv, keep_block, valid_block, *dec_side), memory)
        output, backward, memory = jax.vjp(combined, encoder_params, decoder_params, plot_block, table_block, has_aux=True)
        grad_encoder, grad_decoder, grad_plot, grad_table = backward(cotangent_block.astype(jnp.float32))
        totals = jax.tree.map(jnp.add, totals, (grad_encoder, grad_decoder))
        return (totals, (memory, output, grad_plot, grad_table))
    initial = jax.tree.map(jnp.zeros_like, (encoder_params, decoder_params))
    totals, results = lax.scan(scan_step, initial, (grouped(plot_rows), grouped(table_rows), grouped(keep_mask), grouped(valid_rows), grouped(cotangent)))
    memory_all, output_all, grad_plots, grad_tables = [result.reshape((ROWS, SEQ, D)) for result in results]
    out_acts = jnp.stack([memory_all, output_all]).astype(jnp.bfloat16)
    grad_acts = jnp.stack([jnp.take(grad_plots, inverse, axis=0), jnp.take(grad_tables, inverse, axis=0)])
    grad_encoder, grad_decoder = totals
    stacked = [jnp.stack([pair[0], pair[1]]) for pair in zip(grad_encoder, grad_decoder)]
    return (out_acts, grad_acts, stacked[0], stacked[1], stacked[2], stacked[3], stacked[4], stacked[5])
```

```python
import functools

import jax
import jax.numpy as jnp
from jax import lax
from jax.experimental import pallas as pl
from jax.experimental.pallas import tpu as pltpu
from jax.sharding import PartitionSpec as P

D = 768
HDIM = 64
FF = 2048
SEQ = 128
PAIRS = 6
EPS = 1e-06
NEGATIVE = -1e30
SCALE = HDIM ** (-0.5)
VMEM_BYTES = 58 * 2**20
BF16 = jnp.bfloat16
F32 = jnp.float32
ANY = pl.BlockSpec(memory_space=pl.ANY)
SMEM = pl.BlockSpec(memory_space=pltpu.SMEM)
WHOLE = pl.BlockSpec(memory_space=pltpu.VMEM)


def mm(left, right):
    return jnp.dot(left, right, preferred_element_type=F32)


def mm_t(left, right):
    return lax.dot_general(left, right, (((1,), (1,)), ((), ())), preferred_element_type=F32)


def mm_w(left, right):
    return lax.dot_general(left, right, (((0,), (0,)), ((), ())), preferred_element_type=F32)


def rms(hidden, gain):
    inverse = lax.rsqrt(jnp.mean(hidden * hidden, axis=-1, keepdims=True) + EPS)
    return hidden * inverse * gain


def rms_back(hidden, gain, upstream):
    inverse = lax.rsqrt(jnp.mean(hidden * hidden, axis=-1, keepdims=True) + EPS)
    unit = hidden * inverse
    scaled = upstream * gain
    grad_gain = jnp.sum(upstream * unit, axis=0, keepdims=True)
    middle = jnp.mean(scaled * unit, axis=-1, keepdims=True)
    return inverse * (scaled - unit * middle), grad_gain


def gate_parts(gate, up):
    inner = 0.7978845608 * (gate + 0.044715 * gate * gate * gate)
    bend = jnp.tanh(inner)
    half = 0.5 * (1.0 + bend)
    value = gate * half
    slope = half + 0.5 * gate * (1.0 - bend * bend) * 0.7978845608 * (
        1.0 + 3.0 * 0.044715 * gate * gate
    )
    return value * up, slope * up, value


def lane_masks():
    lane = lax.broadcasted_iota(jnp.int32, (SEQ, 2 * HDIM), 1)
    low = jnp.where(lane < HDIM, 1.0, 0.0).astype(F32)
    return low.astype(BF16), (1.0 - low).astype(BF16), low


def stack_heads(pair, masks):
    return jnp.concatenate([pair * masks[0], pair * masks[1]], axis=0)


def attend(query, keys, values, allowed, masks):
    scores = mm_t(query, stack_heads(keys, masks)) * SCALE
    scores = jnp.where(allowed, scores, NEGATIVE)
    parts = []
    for head in range(2):
        part = scores[:, head * SEQ : (head + 1) * SEQ]
        power = jnp.exp(part - jnp.max(part, axis=-1, keepdims=True))
        parts.append(power * (1.0 / jnp.sum(power, axis=-1, keepdims=True)))
    weights = jnp.concatenate(parts, axis=1).astype(BF16)
    return weights, mm(weights, stack_heads(values, masks)).astype(BF16)


def attend_back(query, keys, values, weights, upstream, masks):
    key_stack = stack_heads(keys, masks)
    grad_weights = mm_t(upstream, stack_heads(values, masks))
    wide = weights.astype(F32)
    product = wide * grad_weights
    parts = []
    for head in range(2):
        columns = slice(head * SEQ, (head + 1) * SEQ)
        total = jnp.sum(product[:, columns], axis=-1, keepdims=True)
        parts.append(product[:, columns] - wide[:, columns] * total)
    grad_scores = jnp.concatenate(parts, axis=1).astype(BF16)
    grad_query = mm(grad_scores, key_stack) * SCALE
    key_both = mm_w(grad_scores, query) * SCALE
    value_both = mm_w(weights, upstream)
    low = masks[2]
    high = 1.0 - low
    grad_keys = key_both[:SEQ] * low + key_both[SEQ:] * high
    grad_values = value_both[:SEQ] * low + value_both[SEQ:] * high
    return grad_query.astype(BF16), grad_keys.astype(BF16), grad_values.astype(BF16)


def key_columns():
    return jnp.bitwise_and(lax.broadcasted_iota(jnp.int32, (SEQ, 2 * SEQ), 1), SEQ - 1)


def kept(keep_ref, plot):
    row = keep_ref[pl.ds(plot, 1), :].astype(F32)
    return jnp.sum(row, axis=1, keepdims=True).astype(jnp.int32)


class Copies:
    def __init__(self, sems):
        self.sems = sems
        self.count = 0

    def __call__(self, source, target):
        copy = pltpu.make_async_copy(source, target, self.sems.at[self.count])
        self.count += 1
        return copy


def start(copies):
    for copy in copies:
        copy.start()


def wait(copies):
    for copy in copies:
        copy.wait()


def struct(*shape, dtype=BF16):
    return jax.ShapeDtypeStruct(shape, dtype)


def call(kernel, in_specs, out_shape, scratch, sems, name, aliases=None, flops=0, traffic=0):
    return pl.pallas_call(
        kernel,
        name=name,
        in_specs=in_specs,
        out_specs=[ANY] * len(out_shape),
        out_shape=out_shape,
        scratch_shapes=[pltpu.VMEM(item.shape, item.dtype) for item in scratch]
        + [pltpu.SemaphoreType.DMA((sems,))],
        input_output_aliases=aliases or {},
        compiler_params=pltpu.CompilerParams(vmem_limit_bytes=VMEM_BYTES),
        cost_estimate=pl.CostEstimate(flops=flops, bytes_accessed=traffic, transcendentals=0),
    )


def forward_kernel(slot, ids, slot_plot, gains, keep, acts, w_qkv, w_out, w_in, w_down, w_cross, pack_o, qkv_o, p_o, h1_o, query_o, z_o, g1_o, g2_o, h2_o, send_o, x_v, wqkv_v, wout_v, win_v, wdown_v, wcross_v, pack_v, qkv_v, p_v, h1_v, z_v, g1_v, g2_v, h2_v, send_v, sems):
    encoding = ids[0] == 0
    plot = slot_plot[0, slot]
    copies = Copies(sems)
    get_x = copies(acts.at[0, plot], x_v)
    get_qkv = [
        copies(w_qkv.at[0, :, pl.ds(i * D, D)], wqkv_v.at[:, pl.ds(i * D, D)]) for i in range(3)
    ]
    get_out = copies(w_out.at[0], wout_v)
    tile = 512
    get_in = []
    for i in range(FF // tile):
        get_in.append(
            [
                copies(
                    w_in.at[0, :, pl.ds(base + i * tile, tile)],
                    win_v.at[:, pl.ds(base + i * tile, tile)],
                )
                for base in (0, FF)
            ]
        )
    get_down = copies(w_down.at[0], wdown_v)
    get_cross = copies(w_cross.at[0], wcross_v)
    get_query = copies(w_cross.at[0, :, pl.ds(0, D)], wcross_v.at[:, pl.ds(0, D)])
    get_x.start()
    start(get_qkv)
    get_out.start()

    @pl.when(encoding)
    def _():
        for pair in get_in:
            start(pair)
        get_down.start()
        get_cross.start()

    @pl.when(jnp.logical_not(encoding))
    def _():
        get_query.start()

    masks = lane_masks()
    count = kept(keep, plot)
    get_x.wait()
    rows_in = x_v[...].astype(F32)
    normal = rms(rows_in, gains[0, 0:1, :]).astype(BF16)
    pack_v[:, 0:D] = normal
    for i in range(3):
        get_qkv[i].wait()
        qkv_v[:, i * D : (i + 1) * D] = mm(normal, wqkv_v[:, i * D : (i + 1) * D]).astype(BF16)
    put_qkv = copies(qkv_v, qkv_o)
    put_qkv.start()
    row_index = lax.broadcasted_iota(jnp.int32, (SEQ, 2 * SEQ), 0)
    key_index = key_columns()
    limit = jnp.where(encoding, jnp.broadcast_to(count - 1, (SEQ, 2 * SEQ)), row_index)
    allowed = key_index <= limit
    for pair in range(PAIRS):
        lanes = slice(pair * 128, (pair + 1) * 128)
        weights, mixed = attend(
            qkv_v[:, lanes],
            qkv_v[:, D + pair * 128 : D + (pair + 1) * 128],
            qkv_v[:, 2 * D + pair * 128 : 2 * D + (pair + 1) * 128],
            allowed,
            masks,
        )
        p_v[pair] = weights
        pack_v[:, D + pair * 128 : D + (pair + 1) * 128] = mixed
    put_p = copies(p_v, p_o)
    put_p.start()
    get_out.wait()
    first = rows_in + mm(pack_v[:, D : 2 * D], wout_v[...])
    h1_v[...] = first
    put_h1 = copies(h1_v, h1_o)
    put_h1.start()
    normal = rms(first, gains[0, 1:2, :]).astype(BF16)
    pack_v[:, 2 * D : 3 * D] = normal
    put_z = [copies(z_v, z_o), copies(g1_v, g1_o), copies(g2_v, g2_o)]
    put_h2 = copies(h2_v, h2_o)
    put_send = copies(send_v, send_o)
    put_query = copies(send_v.at[:, pl.ds(0, D)], query_o)
    put_pack = copies(pack_v, pack_o)

    @pl.when(encoding)
    def _():
        inputs = pack_v[:, 2 * D : 3 * D]
        for i in range(FF // tile):
            wait(get_in[i])
            columns = slice(i * tile, (i + 1) * tile)
            gate = mm(inputs, win_v[:, columns])
            up = mm(inputs, win_v[:, FF + i * tile : FF + (i + 1) * tile])
            unit, to_gate, to_up = gate_parts(gate, up)
            z_v[:, columns] = unit.astype(BF16)
            g1_v[:, columns] = to_gate.astype(BF16)
            g2_v[:, columns] = to_up.astype(BF16)
        start(put_z)
        get_down.wait()
        second = h1_v[...] + mm(z_v[...], wdown_v[...])
        h2_v[...] = second
        put_h2.start()
        rows = lax.broadcasted_iota(jnp.int32, (SEQ, D), 0)
        memory = rms(second, gains[0, 2:3, :])
        memory = jnp.where(rows < jnp.broadcast_to(count, (SEQ, D)), memory, 0.0).astype(BF16)
        pack_v[:, 3 * D : 4 * D] = memory
        put_pack.start()
        get_cross.wait()
        send_v[...] = mm(memory, wcross_v[...]).astype(BF16)
        put_send.start()
        wait(put_z)
        put_h2.wait()
        put_send.wait()
        put_pack.wait()

    @pl.when(jnp.logical_not(encoding))
    def _():
        get_query.wait()
        send_v[:, 0:D] = mm(pack_v[:, 2 * D : 3 * D], wcross_v[:, 0:D]).astype(BF16)
        put_query.start()
        put_pack.start()
        put_query.wait()
        put_pack.wait()

    put_qkv.wait()
    put_p.wait()
    put_h1.wait()


def forward(slot, ids, slot_plot, gains, keep, acts, weights):
    w_qkv, w_out, w_in, w_down, w_cross = weights
    return call(
        functools.partial(forward_kernel, slot),
        [SMEM, SMEM, WHOLE, WHOLE] + [ANY] * 6,
        [
            struct(SEQ, 4 * D),
            struct(SEQ, 3 * D),
            struct(PAIRS, SEQ, 2 * SEQ),
            struct(SEQ, D, dtype=F32),
            struct(SEQ, D),
            struct(SEQ, FF),
            struct(SEQ, FF),
            struct(SEQ, FF),
            struct(SEQ, D, dtype=F32),
            struct(SEQ, 2 * D),
        ],
        [
            struct(SEQ, D),
            struct(D, 3 * D),
            struct(D, D),
            struct(D, 2 * FF),
            struct(FF, D),
            struct(D, 2 * D),
            struct(SEQ, 4 * D),
            struct(SEQ, 3 * D),
            struct(PAIRS, SEQ, 2 * SEQ),
            struct(SEQ, D, dtype=F32),
            struct(SEQ, FF),
            struct(SEQ, FF),
            struct(SEQ, FF),
            struct(SEQ, D, dtype=F32),
            struct(SEQ, 2 * D),
        ],
        32,
        "forward",
        flops=2 * SEQ * 8 * 10**6,
        traffic=22 * 10**6,
    )(ids, slot_plot, gains, keep, acts, w_qkv, w_out, w_in, w_down, w_cross)


def middle_kernel(slot, ids, slot_plot, table_len, gains, keep, kv, h1, query, cot, w_in, w_down, w_cross, pack_o, z_o, rhs_o, dkv_o, e2_o, de2_o, gain_o, kv_v, h1_v, query_v, cot_v, win_v, wdown_v, wcross_v, pack_v, z_v, g1_v, g2_v, rhs_v, dkv_v, p_v, e2_v, de2_v, gain_v, dz_v, sems):
    @pl.when(ids[0] != 0)
    def _():
        plot = slot_plot[0, slot]
        copies = Copies(sems)
        get_kv = copies(kv, kv_v)
        get_query = copies(query, query_v)
        get_h1 = copies(h1, h1_v)
        get_cross = copies(w_cross.at[0, :, pl.ds(D, D)], wcross_v)
        tile = 512
        get_in = [
            copies(
                w_in.at[0, :, pl.ds(i * tile, tile)],
                win_v.at[:, pl.ds(i * tile, tile)],
            )
            for i in range(2 * FF // tile)
        ]
        get_down = copies(w_down.at[0], wdown_v)
        get_cot = copies(cot.at[slot], cot_v)
        start([get_kv, get_query, get_h1, get_cross])
        for i in range(FF // tile):
            get_in[i].start()
            get_in[FF // tile + i].start()
        get_down.start()
        get_cot.start()
        masks = lane_masks()
        count = kept(keep, plot)
        allowed = key_columns() < jnp.broadcast_to(count, (SEQ, 2 * SEQ))
        get_kv.wait()
        get_query.wait()
        for pair in range(PAIRS):
            lanes = slice(pair * 128, (pair + 1) * 128)
            weights, mixed = attend(
                query_v[:, lanes],
                kv_v[:, lanes],
                kv_v[:, D + pair * 128 : D + (pair + 1) * 128],
                allowed,
                masks,
            )
            p_v[pair] = weights
            pack_v[:, D + pair * 128 : D + (pair + 1) * 128] = mixed
        get_h1.wait()
        get_cross.wait()
        second = h1_v[...] + mm(pack_v[:, D : 2 * D], wcross_v[...])
        e2_v[...] = second
        put_e2 = copies(e2_v, e2_o)
        put_e2.start()
        normal = rms(second, gains[0, 2:3, :]).astype(BF16)
        pack_v[:, 0:D] = normal
        put_pack = copies(pack_v, pack_o)
        put_pack.start()
        for i in range(FF // tile):
            get_in[i].wait()
            get_in[FF // tile + i].wait()
            columns = slice(i * tile, (i + 1) * tile)
            gate = mm(normal, win_v[:, columns])
            up = mm(normal, win_v[:, FF + i * tile : FF + (i + 1) * tile])
            unit, to_gate, to_up = gate_parts(gate, up)
            z_v[:, columns] = unit.astype(BF16)
            g1_v[:, columns] = to_gate.astype(BF16)
            g2_v[:, columns] = to_up.astype(BF16)
        put_z = copies(z_v, z_o)
        put_z.start()
        get_cot.wait()
        get_down.wait()
        rows = lax.broadcasted_iota(jnp.int32, (SEQ, D), 0)
        upstream = jnp.where(rows < table_len[plot], cot_v[...].astype(F32), 0.0)
        branch = upstream.astype(BF16)
        rhs_v[:, 0:D] = branch
        for i in range(FF // tile):
            columns = slice(i * tile, (i + 1) * tile)
            grad_unit = mm_t(branch, wdown_v[i * tile : (i + 1) * tile, :])
            rhs_v[:, D + i * tile : D + (i + 1) * tile] = (
                grad_unit * g1_v[:, columns].astype(F32)
            ).astype(BF16)
            rhs_v[:, D + FF + i * tile : D + FF + (i + 1) * tile] = (
                grad_unit * g2_v[:, columns].astype(F32)
            ).astype(BF16)
        grad_normal = mm_t(rhs_v[:, D : D + 2 * FF], win_v[...])
        back, grad_gain = rms_back(second, gains[0, 2:3, :], grad_normal)
        grad_second = upstream + back
        gain_v[...] = jnp.zeros_like(gain_v)
        gain_v[2:3, :] = grad_gain
        de2_v[...] = grad_second
        put_de2 = [copies(de2_v, de2_o), copies(gain_v, gain_o)]
        start(put_de2)
        branch = grad_second.astype(BF16)
        rhs_v[:, 2 * D + D + 2 * FF - D : 3 * D + 2 * FF] = branch
        dz_v[...] = mm_t(branch, wcross_v[...]).astype(BF16)
        for pair in range(PAIRS):
            lanes = slice(pair * 128, (pair + 1) * 128)
            high = slice(D + pair * 128, D + (pair + 1) * 128)
            grad_query, grad_keys, grad_values = attend_back(
                query_v[:, lanes], kv_v[:, lanes], kv_v[:, high], p_v[pair], dz_v[:, lanes], masks
            )
            rhs_v[:, D + 2 * FF + pair * 128 : D + 2 * FF + (pair + 1) * 128] = grad_query
            dkv_v[:, lanes] = grad_keys
            dkv_v[:, high] = grad_values
        put_rest = [copies(dkv_v, dkv_o), copies(rhs_v, rhs_o)]
        start(put_rest)
        put_e2.wait()
        put_pack.wait()
        put_z.wait()
        wait(put_de2)
        wait(put_rest)


def middle(slot, ids, slot_plot, table_len, gains, keep, kv, h1, query, cot, weights):
    w_qkv, w_out, w_in, w_down, w_cross = weights
    return call(
        functools.partial(middle_kernel, slot),
        [SMEM, SMEM, SMEM, WHOLE, WHOLE] + [ANY] * 7,
        [
            struct(SEQ, 2 * D),
            struct(SEQ, FF),
            struct(SEQ, 3 * D + 2 * FF),
            struct(SEQ, 2 * D),
            struct(SEQ, D, dtype=F32),
            struct(SEQ, D, dtype=F32),
            struct(8, D, dtype=F32),
        ],
        [
            struct(SEQ, 2 * D),
            struct(SEQ, D, dtype=F32),
            struct(SEQ, D),
            struct(SEQ, D),
            struct(D, 2 * FF),
            struct(FF, D),
            struct(D, D),
            struct(SEQ, 2 * D),
            struct(SEQ, FF),
            struct(SEQ, FF),
            struct(SEQ, FF),
            struct(SEQ, 3 * D + 2 * FF),
            struct(SEQ, 2 * D),
            struct(PAIRS, SEQ, 2 * SEQ),
            struct(SEQ, D, dtype=F32),
            struct(SEQ, D, dtype=F32),
            struct(8, D, dtype=F32),
            struct(SEQ, D),
        ],
        24,
        "middle",
        flops=2 * SEQ * 12 * 10**6,
        traffic=18 * 10**6,
    )(ids, slot_plot, table_len, gains, keep, kv, h1, query, cot, w_in, w_down, w_cross)


def outer_kernel(slot, ids, slot_plot, table_len, gains, keep, dkv, h2, g1, g2, pack1, e2, z2, w_in, w_down, w_cross, *rest):
    (rhs_o, dh2_o, gain_o, out_o, dkv_v, h2_v, g1_v, g2_v, wdown_v, wcross_v, rhs_v, dh2_v, gain_v, out_v, z_v, sems) = rest[-16:]
    plot = slot_plot[0, slot]

    @pl.when(ids[0] == 0)
    def _():
        copies = Copies(sems)
        get = [
            copies(dkv, dkv_v),
            copies(w_cross.at[0], wcross_v),
            copies(h2, h2_v),
            copies(w_down.at[0], wdown_v),
            copies(g1, g1_v),
            copies(g2, g2_v),
        ]
        start(get)
        put_out = copies(pack1.at[:, pl.ds(3 * D, D)], out_o.at[0, slot])
        put_out.start()
        count = kept(keep, plot)
        wait(get[:3])
        grad_memory = mm_t(dkv_v[...], wcross_v[...])
        rows = lax.broadcasted_iota(jnp.int32, (SEQ, D), 0)
        grad_memory = jnp.where(rows < jnp.broadcast_to(count, (SEQ, D)), grad_memory, 0.0)
        grad_second, grad_gain = rms_back(h2_v[...], gains[0, 2:3, :], grad_memory)
        gain_v[...] = jnp.zeros_like(gain_v)
        gain_v[2:3, :] = grad_gain
        dh2_v[...] = grad_second
        branch = grad_second.astype(BF16)
        rhs_v[:, 0:D] = branch
        wait(get[3:])
        tile = 512
        for i in range(FF // tile):
            columns = slice(i * tile, (i + 1) * tile)
            grad_unit = mm_t(branch, wdown_v[i * tile : (i + 1) * tile, :])
            rhs_v[:, D + i * tile : D + (i + 1) * tile] = (
                grad_unit * g1_v[:, columns].astype(F32)
            ).astype(BF16)
            rhs_v[:, D + FF + i * tile : D + FF + (i + 1) * tile] = (
                grad_unit * g2_v[:, columns].astype(F32)
            ).astype(BF16)
        put = [copies(rhs_v, rhs_o), copies(dh2_v, dh2_o), copies(gain_v, gain_o)]
        start(put)
        wait(put)
        put_out.wait()

    @pl.when(ids[0] != 0)
    def _():
        copies = Copies(sems)
        get = [copies(e2, h2_v), copies(z2, z_v), copies(w_down.at[0], wdown_v)]
        start(get)
        wait(get)
        third = h2_v[...] + mm(z_v[...], wdown_v[...])
        rows = lax.broadcasted_iota(jnp.int32, (SEQ, D), 0)
        out_v[...] = jnp.where(rows < table_len[plot], third, 0.0).astype(BF16)
        put = copies(out_v, out_o.at[0, slot])
        put.start()
        put.wait()


def outer(slot, ids, slot_plot, table_len, gains, keep, dkv, h2, g1, g2, pack1, e2, z2, weights, chain):
    w_qkv, w_out, w_in, w_down, w_cross = weights
    args = [ids, slot_plot, table_len, gains, keep, dkv, h2, g1, g2, pack1, e2, z2, w_in, w_down, w_cross]
    specs = [SMEM, SMEM, SMEM, WHOLE, WHOLE] + [ANY] * 10
    aliases = {}
    if chain is not None:
        aliases = {len(args): 3}
        args.append(chain)
        specs.append(ANY)
    return call(
        functools.partial(outer_kernel, slot),
        specs,
        [
            struct(SEQ, D + 2 * FF),
            struct(SEQ, D, dtype=F32),
            struct(8, D, dtype=F32),
            struct(1, 2, SEQ, D),
        ],
        [
            struct(SEQ, 2 * D),
            struct(SEQ, D, dtype=F32),
            struct(SEQ, FF),
            struct(SEQ, FF),
            struct(FF, D),
            struct(D, 2 * D),
            struct(SEQ, D + 2 * FF),
            struct(SEQ, D, dtype=F32),
            struct(8, D, dtype=F32),
            struct(SEQ, D),
            struct(SEQ, FF),
        ],
        12,
        "outer",
        aliases=aliases,
        flops=2 * SEQ * 3 * 10**6,
        traffic=8 * 10**6,
    )(*args)


def inner_kernel(slot, ids, slot_plot, gains, acts, h1, qkv, p, rhs3, dh2, gain3, rhs2, de2, gain2, w_qkv, w_out, w_in, w_cross, *rest):
    (rhs_o, gain_o, grad_o, x_v, h1_v, qkv_v, p_v, wide_v, query_v, up_v, gain_v, wqkv_v, wout_v, win_v, wcross_v, rhs_v, grad_v, dn_v, sems) = rest[-19:]
    encoding = ids[0] == 0
    plot = slot_plot[0, slot]
    copies = Copies(sems)
    get_enc = [
        copies(rhs3.at[:, pl.ds(D, 2 * FF)], wide_v),
        copies(w_in.at[0], win_v),
        copies(dh2, up_v),
        copies(gain3, gain_v),
    ]
    get_dec = [
        copies(rhs2.at[:, pl.ds(D + 2 * FF, D)], query_v),
        copies(w_cross.at[0, :, pl.ds(0, D)], wcross_v),
        copies(de2, up_v),
        copies(gain2, gain_v),
    ]
    get_h1 = copies(h1, h1_v)
    get = [
        copies(w_out.at[0], wout_v),
        copies(qkv, qkv_v),
        copies(p, p_v),
        copies(w_qkv.at[0], wqkv_v),
        copies(acts.at[0, plot], x_v),
    ]

    @pl.when(encoding)
    def _():
        start(get_enc)

    @pl.when(jnp.logical_not(encoding))
    def _():
        start(get_dec)

    get_h1.start()
    start(get)

    @pl.when(encoding)
    def _():
        wait(get_enc)
        dn_v[...] = mm_t(wide_v[...], win_v[...])

    @pl.when(jnp.logical_not(encoding))
    def _():
        wait(get_dec)
        dn_v[...] = mm_t(query_v[...], wcross_v[...])

    get_h1.wait()
    back, grad_gain = rms_back(h1_v[...], gains[0, 1:2, :], dn_v[...])
    grad_first = up_v[...] + back
    gain_v[1:2, :] = grad_gain
    branch = grad_first.astype(BF16)
    rhs_v[:, 0:D] = branch
    masks = lane_masks()
    get[0].wait()
    grad_mixed = mm_t(branch, wout_v[...]).astype(BF16)
    get[1].wait()
    get[2].wait()
    for pair in range(PAIRS):
        spans = [slice(i * D + pair * 128, i * D + (pair + 1) * 128) for i in range(3)]
        parts = attend_back(
            qkv_v[:, spans[0]],
            qkv_v[:, spans[1]],
            qkv_v[:, spans[2]],
            p_v[pair],
            grad_mixed[:, pair * 128 : (pair + 1) * 128],
            masks,
        )
        for i in range(3):
            rhs_v[:, D + i * D + pair * 128 : D + i * D + (pair + 1) * 128] = parts[i]
    put_rhs = copies(rhs_v, rhs_o)
    put_rhs.start()
    get[3].wait()
    grad_normal = mm_t(rhs_v[:, D : 4 * D], wqkv_v[...])
    get[4].wait()
    back, grad_gain = rms_back(x_v[...].astype(F32), gains[0, 0:1, :], grad_normal)
    gain_v[0:1, :] = grad_gain
    put_gain = copies(gain_v, gain_o)
    put_gain.start()
    grad_v[...] = grad_first + back
    put_grad = copies(grad_v, grad_o.at[0, plot])
    put_grad.start()
    put_rhs.wait()
    put_gain.wait()
    put_grad.wait()


def inner(slot, ids, slot_plot, gains, acts, h1, qkv, p, rhs3, dh2, gain3, rhs2, de2, gain2, weights, chain):
    w_qkv, w_out, w_in, w_down, w_cross = weights
    args = [ids, slot_plot, gains, acts, h1, qkv, p, rhs3, dh2, gain3, rhs2, de2, gain2, w_qkv, w_out, w_in, w_cross]
    specs = [SMEM, SMEM, WHOLE] + [ANY] * 14
    aliases = {}
    if chain is not None:
        aliases = {len(args): 2}
        args.append(chain)
        specs.append(ANY)
    return call(
        functools.partial(inner_kernel, slot),
        specs,
        [
            struct(SEQ, 4 * D),
            struct(8, D, dtype=F32),
            struct(1, 2, SEQ, D, dtype=F32),
        ],
        [
            struct(SEQ, D),
            struct(SEQ, D, dtype=F32),
            struct(SEQ, 3 * D),
            struct(PAIRS, SEQ, 2 * SEQ),
            struct(SEQ, 2 * FF),
            struct(SEQ, D),
            struct(SEQ, D, dtype=F32),
            struct(8, D, dtype=F32),
            struct(D, 3 * D),
            struct(D, D),
            struct(D, 2 * FF),
            struct(D, D),
            struct(SEQ, 4 * D),
            struct(SEQ, D, dtype=F32),
            struct(SEQ, D, dtype=F32),
        ],
        20,
        "inner",
        aliases=aliases,
        flops=2 * SEQ * 6 * 10**6,
        traffic=14 * 10**6,
    )(*args)


def onehot(target, rows, columns):
    index = lax.broadcasted_iota(jnp.int32, (rows, columns), 0)
    return jnp.where(index == target, 1.0, 0.0).astype(BF16)


def gather_rows(copies, sources, columns, scratch):
    made = []
    for i, source in enumerate(sources):
        made.append(copies(source.at[:, columns], scratch.at[pl.ds(i * SEQ, SEQ), :]))
    return made


def pick(encoding, enc, dec, method):
    @pl.when(encoding)
    def _():
        method(enc)

    @pl.when(jnp.logical_not(encoding))
    def _():
        method(dec)


def grads_a_kernel(ids, spots, *refs):
    pack1, z1, rhs3, dkv, pack2, z2, rhs2 = [refs[4 * i : 4 * i + 4] for i in range(7)]
    outs = refs[28:42]
    z_v, branch_v, left1_v, left2_v, cross_v = refs[42:47]
    slots = refs[47:61]
    sems = refs[61]
    encoding = ids[0] == 0
    copies = Copies(sems)
    enc = [
        gather_rows(copies, pack1, pl.ds(3 * D, D), left1_v),
        gather_rows(copies, pack1, pl.ds(3 * D, D), left2_v),
        gather_rows(copies, dkv, pl.ds(0, 2 * D), cross_v),
        gather_rows(copies, z1, pl.ds(0, FF), z_v),
        gather_rows(copies, rhs3, pl.ds(0, D), branch_v),
    ]
    dec = [
        gather_rows(copies, pack1, pl.ds(2 * D, D), left1_v),
        gather_rows(copies, pack2, pl.ds(D, D), left2_v),
        gather_rows(copies, rhs2, pl.ds(D + 2 * FF, 2 * D), cross_v),
        gather_rows(copies, z2, pl.ds(0, FF), z_v),
        gather_rows(copies, rhs2, pl.ds(0, D), branch_v),
    ]
    pick(encoding, sum(enc, []), sum(dec, []), start)
    along_z = onehot(spots[1:2, 0:384], D, 384)
    along_m = onehot(spots[2:3, 0:256], 512, 256)
    puts = []
    pick(encoding, sum(enc[:3], []), sum(dec[:3], []), wait)
    for half, left_v in enumerate((left1_v, left2_v)):
        left = mm(left_v[...], along_z).astype(BF16)
        grad = mm_w(left, cross_v[:, half * D : (half + 1) * D])
        slots[7][:, half * D : (half + 1) * D] = grad[0:96].astype(BF16)
        for chunk in range(1, 4):
            where_to = 7 + 1 + 2 * (chunk - 1) + half
            slots[where_to][...] = grad[96 * chunk : 96 * (chunk + 1)].astype(BF16)
    for i in range(7, 14):
        puts.append(copies(slots[i], outs[i]))
        puts[-1].start()
    pick(encoding, sum(enc[3:], []), sum(dec[3:], []), wait)
    for chunk in (2, 1, 3, 0):
        block = lax.rem(ids[1] + chunk, 4) * 256
        picked = jnp.concatenate(
            [
                z_v[:, pl.ds(pl.multiple_of(block, 256), 256)],
                z_v[:, pl.ds(pl.multiple_of(block + 1024, 256), 256)],
            ],
            axis=1,
        )
        left = mm(picked, along_m).astype(BF16)
        grad = mm_w(left, branch_v[...]).astype(BF16)
        if chunk == 0:
            slots[0][...] = grad
            puts.append(copies(slots[0], outs[0]))
            puts[-1].start()
        else:
            for half in range(2):
                where_to = 1 + 2 * (chunk - 1) + half
                slots[where_to][...] = grad[:, half * 384 : (half + 1) * 384]
                puts.append(copies(slots[where_to], outs[where_to]))
                puts[-1].start()
    wait(puts)


def seven(rows, half, other=None):
    other = half if other is None else other
    return [struct(rows, half + other)] + [struct(rows, half), struct(rows, other)] * 3


def grads_a(ids, spots, groups):
    shapes = seven(256, 384) + seven(96, 768)
    return call(
        grads_a_kernel,
        [SMEM, WHOLE] + [ANY] * 28,
        shapes,
        [struct(512, FF), struct(512, D), struct(512, D), struct(512, D), struct(512, 2 * D)] + shapes,
        60,
        "grads_a",
        flops=2 * 512 * 16 * 10**5,
        traffic=10 * 10**6,
    )(ids, spots, *groups)


def grads_b_kernel(ids, spots, *refs):
    pack1, rhs3, pack2, rhs2 = [refs[4 * i : 4 * i + 4] for i in range(4)]
    outs = refs[16:30]
    left_v, right_v = refs[30:32]
    slots = refs[32:46]
    sems = refs[46]
    encoding = ids[0] == 0
    copies = Copies(sems)
    enc = [gather_rows(copies, pack1, pl.ds(2 * D, D), left_v)]
    dec = [gather_rows(copies, pack2, pl.ds(0, D), left_v)]
    for i in range(4):
        part = right_v.at[:, pl.ds(i * 1024, 1024)]
        enc.append(gather_rows(copies, rhs3, pl.ds(D + i * 1024, 1024), part))
        dec.append(gather_rows(copies, rhs2, pl.ds(D + i * 1024, 1024), part))
    pick(encoding, sum(enc, []), sum(dec, []), start)
    orders = [onehot(spots[i : i + 1, 0:384], D, 384) for i in range(2)]
    pick(encoding, enc[0], dec[0], wait)
    puts = []
    for axis in range(2):
        left = mm(left_v[...], orders[axis]).astype(BF16)
        for half in range(2):
            part = 2 * axis + half
            pick(encoding, enc[1 + part], dec[1 + part], wait)
            for tile in range(2):
                grad = mm_w(left, right_v[:, part * 1024 + tile * 512 : part * 1024 + (tile + 1) * 512])
                columns = slice(tile * 512, (tile + 1) * 512)
                slots[7 * axis][:, half * 1024 + tile * 512 : half * 1024 + (tile + 1) * 512] = grad[
                    0:96
                ].astype(BF16)
                for chunk in range(1, 4):
                    where_to = 7 * axis + 1 + 2 * (chunk - 1) + half
                    slots[where_to][:, columns] = grad[96 * chunk : 96 * (chunk + 1)].astype(BF16)
            for chunk in range(1, 4):
                where_to = 7 * axis + 1 + 2 * (chunk - 1) + half
                puts.append(copies(slots[where_to], outs[where_to]))
                puts[-1].start()
        puts.append(copies(slots[7 * axis], outs[7 * axis]))
        puts[-1].start()
    wait(puts)


def grads_b(ids, spots, groups):
    shapes = seven(96, 1024) + seven(96, 1024)
    return call(
        grads_b_kernel,
        [SMEM, WHOLE] + [ANY] * 16,
        shapes,
        [struct(512, D), struct(512, 2 * FF)] + shapes,
        60,
        "grads_b",
        flops=2 * 512 * 16 * 10**5,
        traffic=11 * 10**6,
    )(ids, spots, *groups)


def grads_c_kernel(ids, spots, *refs):
    pack1, rhs, gain = [refs[4 * i : 4 * i + 4] for i in range(3)]
    outs = refs[12:26]
    left_v, mixed_v, right_v, gain_v = refs[26:30]
    slots = refs[30:44]
    sems = refs[44]
    copies = Copies(sems)
    get = [
        gather_rows(copies, pack1, pl.ds(0, D), left_v),
        gather_rows(copies, rhs, pl.ds(0, 4 * D), right_v),
        gather_rows(copies, pack1, pl.ds(D, D), mixed_v),
        [copies(gain[i], gain_v.at[pl.ds(8 * i, 8), :]) for i in range(4)],
    ]
    start(sum(get, []))
    orders = [onehot(spots[i : i + 1, 0:384], D, 384) for i in range(2)]
    wait(sum(get, []))
    puts = []
    total = gain_v[0:8, :] + gain_v[8:16, :] + gain_v[16:24, :] + gain_v[24:32, :]
    upper = total.astype(BF16)
    lower = (total - upper.astype(F32)).astype(BF16)
    ordered = mm(upper, orders[0]) + mm(lower, orders[0])
    tall = jnp.concatenate([ordered, jnp.zeros((120, 384), F32)], axis=0).T
    left = [mm(left_v[...], orders[0]).astype(BF16), mm(left_v[...], orders[1]).astype(BF16)]
    mixed = mm(mixed_v[...], orders[1]).astype(BF16)
    parts = [
        (0, 0, left[0], slice(D, 2 * D)),
        (0, 1, left[0], slice(2 * D, 3 * D)),
        (1, 0, left[1], slice(3 * D, 4 * D)),
        (1, 1, mixed, slice(0, D)),
    ]
    for axis, half, lhs, columns in parts:
        grad = mm_w(lhs, right_v[:, columns])
        slots[7 * axis][:, half * D : (half + 1) * D] = grad[0:96].astype(BF16)
        if (axis, half) == (0, 1):
            slots[0][:, 2 * D : 2 * D + 128] = tall[0:96].astype(BF16)
        for chunk in range(1, 4):
            where_to = 7 * axis + 1 + 2 * (chunk - 1) + half
            slots[where_to][:, 0:D] = grad[96 * chunk : 96 * (chunk + 1)].astype(BF16)
            if (axis, half) == (0, 1):
                slots[where_to][:, D : D + 128] = tall[96 * chunk : 96 * (chunk + 1)].astype(BF16)
            puts.append(copies(slots[where_to], outs[where_to]))
            puts[-1].start()
        if half == 1:
            puts.append(copies(slots[7 * axis], outs[7 * axis]))
            puts[-1].start()
    wait(puts)


def grads_c(ids, spots, groups):
    shapes = seven(96, D, D + 128) + seven(96, D)
    return call(
        grads_c_kernel,
        [SMEM, WHOLE] + [ANY] * 12,
        shapes,
        [struct(512, D), struct(512, D), struct(512, 4 * D), struct(32, D, dtype=F32)] + shapes,
        40,
        "grads_c",
        flops=2 * 512 * 12 * 10**5,
        traffic=9 * 10**6,
    )(ids, spots, *groups)


SIZES = (2, 4, 4, 2)


def flat(y, x, z, core):
    return ((y * 4 + x) * 4 + z) * 2 + core


def shifted(array, y=0, x=0, z=0, core=0):
    pairs = []
    for a in range(2):
        for b in range(4):
            for c in range(4):
                for d in range(2):
                    source = flat(a, b, c, d)
                    target = flat((a + y) % 2, (b + x) % 4, (c + z) % 4, (d + core) % 2)
                    pairs.append((source, target))
    return lax.ppermute(array, "dp", pairs)


def add(*terms):
    total = terms[0].astype(F32)
    for term in terms[1:]:
        total = total + term.astype(F32)
    return total


def first_stage(chunks, axis):
    own, c1a, c1b, c2a, c2b, c3a, c3b = chunks
    ahead = functools.partial(shifted, **{axis: 1})
    behind = functools.partial(shifted, **{axis: 3})
    got2a = ahead(c2a)
    got2b = behind(c2b)
    got1b = ahead(c1b)
    got3a = behind(c3a)
    got1a = ahead(add(c1a, got2a).astype(BF16))
    got3b = behind(add(c3b, got2b).astype(BF16))
    width = c1a.shape[1]
    total_a = add(own[:, :width], got1a, got3a)
    total_b = add(own[:, width:], got1b, got3b)
    return jnp.concatenate([total_a, total_b], axis=1).astype(BF16)


def second_stage(total, axis):
    rows = total.shape[0] // 8
    parts = []
    for step in range(4):
        for y in range(2):
            start_row = (2 * step + y) * rows
            part = total[start_row : start_row + rows]
            if step or y:
                part = shifted(part, y=y, **{axis: step})
            parts.append(part)
    return add(*parts)


def local(
    acts,
    gains,
    qkv_weight,
    out_weight,
    mlp_in,
    mlp_out,
    cross_weight,
    patch_mask,
    table_len,
    slot_plot,
    cotangent,
):
    section = lax.axis_index("section")
    place = lax.axis_index("dp")
    core = place % 2
    z = (place // 2) % 4
    x = (place // 8) % 4
    y = place // 32
    ids = jnp.stack([section, x, z, y, core, section, section, section]).astype(jnp.int32)
    order = jnp.arange(384)
    outer_block, inner_block = order // 96, (order % 96) // 24
    y_block, last = (order % 24) // 12, order % 12
    along_x = (
        ((y + y_block) % 2) * 384
        + ((x + outer_block) % 4) * 96
        + ((z + inner_block) % 4) * 24
        + core * 12
        + last
    )
    along_z = (
        ((y + y_block) % 2) * 384
        + ((x + inner_block) % 4) * 96
        + ((z + outer_block) % 4) * 24
        + core * 12
        + last
    )
    wide = jnp.arange(256)
    along_m = (
        ((y + (wide % 64) // 32) % 2) * 256 + ((z + wide // 64) % 4) * 64 + core * 32 + wide % 32
    )
    along_m = jnp.concatenate([along_m, jnp.zeros((128,), along_m.dtype)])
    spots = jnp.stack([along_x, along_z, along_m] + [along_x] * 5).astype(jnp.int32)
    weights = (qkv_weight, out_weight, mlp_in, mlp_out, cross_weight)

    def other_core(array):
        return shifted(array, core=1)

    made = []
    received = []
    for slot in range(2):
        made.append(forward(slot, ids, slot_plot, gains, patch_mask, acts, weights))
        received.append(lax.ppermute(made[slot][9], "section", [(0, 1)]))
    middles = []
    back = []
    for slot in range(2):
        pack1, qkv, p, h1, query = made[slot][:5]
        middles.append(
            middle(
                slot, ids, slot_plot, table_len, gains, patch_mask,
                received[slot], h1, query, cotangent, weights,
            )
        )
        back.append(lax.ppermute(middles[slot][3], "section", [(1, 0)]))
    out_chain = None
    grad_chain = None
    outers = []
    inners = []
    for slot in range(2):
        pack1, qkv, p, h1, query, z1, g1, g2, h2, _ = made[slot]
        pack2, z2, rhs2, _, e2, de2, gain2 = middles[slot]
        outers.append(
            outer(
                slot, ids, slot_plot, table_len, gains, patch_mask,
                back[slot], h2, g1, g2, pack1, e2, z2, weights, out_chain,
            )
        )
        rhs3, dh2, gain3, out_chain = outers[slot]
        inners.append(
            inner(
                slot, ids, slot_plot, gains, acts, h1, qkv, p,
                rhs3, dh2, gain3, rhs2, de2, gain2, weights, grad_chain,
            )
        )
        grad_chain = inners[slot][2]

    def both(own):
        return list(own) + [other_core(array) for array in own]

    pack1 = both([item[0] for item in made])
    z1 = both([item[5] for item in made])
    pack2 = both([item[0] for item in middles])
    z2 = both([item[1] for item in middles])
    rhs2 = both([item[2] for item in middles])
    dkv = both(back)
    rhs3 = both([item[0] for item in outers])
    rhs = both([item[0] for item in inners])
    gain = both([item[1] for item in inners])
    part_a = grads_a(ids, spots, pack1 + z1 + rhs3 + dkv + pack2 + z2 + rhs2)
    part_b = grads_b(ids, spots, pack1 + rhs3 + pack2 + rhs2)
    part_c = grads_c(ids, spots, pack1 + rhs + gain)
    firsts = []
    for part in (part_a, part_b, part_c):
        firsts.append((first_stage(part[:7], "x"), first_stage(part[7:], "z")))
    lasts = [(second_stage(pair[0], "z"), second_stage(pair[1], "x")) for pair in firsts]
    grad_mlp_out, grad_cross = lasts[0]
    grad_mlp_in = jnp.concatenate(lasts[1], axis=1)
    grad_qkv = jnp.concatenate([lasts[2][0][:, : 2 * D], lasts[2][1][:, :D]], axis=1)
    grad_out = lasts[2][1][:, D:]
    grad_gains = lasts[2][0][:, 2 * D : 2 * D + 3].T
    return (
        out_chain,
        grad_chain,
        grad_gains[None],
        grad_qkv[None],
        grad_out[None],
        grad_mlp_in[None],
        grad_mlp_out[None],
        grad_cross[None],
    )


def solution(mesh):
    return jax.shard_map(
        local,
        mesh=mesh,
        in_specs=(
            P("section", "dp", None, None),
            P("section", None, None),
            P("section", None, None),
            P("section", None, None),
            P("section", None, None),
            P("section", None, None),
            P("section", None, None),
            P("dp", None),
            P("dp"),
            P("dp", None),
            P("dp", None, None),
        ),
        out_specs=(
            P("section", "dp", None, None),
            P("section", "dp", None, None),
            P("section", None, "dp"),
            P("section", "dp", None),
            P("section", "dp", None),
            P("section", "dp", None),
            P("section", "dp", None),
            P("section", "dp", None),
        ),
        check_vma=False,
    )
```

```python
import functools

import jax
import jax.numpy as jnp
from jax import lax
from jax.experimental import pallas as pl
from jax.experimental.pallas import tpu as pltpu
from jax.sharding import PartitionSpec as P

D = 768
HDIM = 64
FF = 2048
SEQ = 128
PAIRS = 6
EPS = 1e-06
NEGATIVE = -1e30
SCALE = HDIM ** (-0.5)
BF16 = jnp.bfloat16
F32 = jnp.float32
ANY = pl.BlockSpec(memory_space=pl.ANY)
FAST = pl.BlockSpec(memory_space=pltpu.VMEM)
SMEM = pl.BlockSpec(memory_space=pltpu.SMEM)


def mm(left, right):
    return jnp.dot(left, right, preferred_element_type=F32)


def mm_t(left, right):
    return lax.dot_general(left, right, (((1,), (1,)), ((), ())), preferred_element_type=F32)


def mm_w(left, right):
    return lax.dot_general(left, right, (((0,), (0,)), ((), ())), preferred_element_type=F32)


def rms(hidden, gain):
    inverse = lax.rsqrt(jnp.mean(hidden * hidden, axis=-1, keepdims=True) + EPS)
    return hidden * inverse * gain


def rms_back(hidden, gain, upstream):
    inverse = lax.rsqrt(jnp.mean(hidden * hidden, axis=-1, keepdims=True) + EPS)
    unit = hidden * inverse
    scaled = upstream * gain
    grad_gain = jnp.sum(upstream * unit, axis=0, keepdims=True)
    middle = jnp.mean(scaled * unit, axis=-1, keepdims=True)
    return inverse * (scaled - unit * middle), grad_gain


def gate_parts(gate, up):
    inner = 0.7978845608 * (gate + 0.044715 * gate * gate * gate)
    bend = jnp.tanh(inner)
    half = 0.5 * (1.0 + bend)
    value = gate * half
    slope = half + 0.5 * gate * (1.0 - bend * bend) * 0.7978845608 * (
        1.0 + 3.0 * 0.044715 * gate * gate
    )
    return value * up, slope * up, value


def lane_masks():
    lane = lax.broadcasted_iota(jnp.int32, (SEQ, 2 * HDIM), 1)
    low = jnp.where(lane < HDIM, 1.0, 0.0).astype(F32)
    return low.astype(BF16), (1.0 - low).astype(BF16), low


def stack_heads(pair, masks):
    return jnp.concatenate([pair * masks[0], pair * masks[1]], axis=0)


def attend(query, keys, values, allowed, masks):
    scores = mm_t(query, stack_heads(keys, masks)) * SCALE
    scores = jnp.where(allowed, scores, NEGATIVE)
    parts = []
    for head in range(2):
        part = scores[:, head * SEQ : (head + 1) * SEQ]
        power = jnp.exp(part - jnp.max(part, axis=-1, keepdims=True))
        parts.append(power * (1.0 / jnp.sum(power, axis=-1, keepdims=True)))
    weights = jnp.concatenate(parts, axis=1).astype(BF16)
    return weights, mm(weights, stack_heads(values, masks)).astype(BF16)


def attend_back(query, keys, values, weights, upstream, masks):
    key_stack = stack_heads(keys, masks)
    grad_weights = mm_t(upstream, stack_heads(values, masks))
    wide = weights.astype(F32)
    product = wide * grad_weights
    parts = []
    for head in range(2):
        columns = slice(head * SEQ, (head + 1) * SEQ)
        total = jnp.sum(product[:, columns], axis=-1, keepdims=True)
        parts.append(product[:, columns] - wide[:, columns] * total)
    grad_scores = jnp.concatenate(parts, axis=1).astype(BF16)
    grad_query = mm(grad_scores, key_stack) * SCALE
    key_both = mm_w(grad_scores, query) * SCALE
    value_both = mm_w(weights, upstream)
    low = masks[2]
    high = 1.0 - low
    grad_keys = key_both[:SEQ] * low + key_both[SEQ:] * high
    grad_values = value_both[:SEQ] * low + value_both[SEQ:] * high
    return grad_query.astype(BF16), grad_keys.astype(BF16), grad_values.astype(BF16)


def key_columns():
    return jnp.bitwise_and(lax.broadcasted_iota(jnp.int32, (SEQ, 2 * SEQ), 1), SEQ - 1)


def kept(keep_ref, plot):
    row = keep_ref[pl.ds(plot, 1), :].astype(F32)
    return jnp.sum(row, axis=1, keepdims=True).astype(jnp.int32)


class Copies:
    def __init__(self, sems):
        self.sems = sems
        self.count = 0

    def __call__(self, source, target):
        copy = pltpu.make_async_copy(source, target, self.sems.at[self.count])
        self.count += 1
        return copy


def start(copies):
    for copy in copies:
        copy.start()


def wait(copies):
    for copy in copies:
        copy.wait()


def struct(*shape, dtype=BF16):
    return jax.ShapeDtypeStruct(shape, dtype)


def call(kernel, scalars, out_shape, scratch, sems, name, arrays, fast=(), aliases=None, flops=0, traffic=0, room=20):
    return pl.pallas_call(
        kernel,
        name=name,
        in_specs=[SMEM] * len(scalars) + [ANY] * len(arrays) + [FAST] * len(fast),
        out_specs=[FAST if is_fast(item) else ANY for item in out_shape],
        out_shape=out_shape,
        scratch_shapes=[pltpu.VMEM(item.shape, item.dtype) for item in scratch]
        + [pltpu.SemaphoreType.DMA((sems,))],
        input_output_aliases=aliases or {},
        compiler_params=pltpu.CompilerParams(vmem_limit_bytes=room * 2**20),
        cost_estimate=pl.CostEstimate(flops=flops, bytes_accessed=traffic, transcendentals=0),
    )(*scalars, *arrays, *[pltpu.with_memory_space_constraint(item, pltpu.VMEM) for item in fast])


def is_fast(item):
    return not isinstance(item, jax.ShapeDtypeStruct) and item.memory_space == pltpu.VMEM


def vmem(*shape, dtype=BF16):
    return pltpu.VMEM(shape, dtype)


def hbm(*shape, dtype=BF16):
    return pltpu.HBM(shape, dtype)


def slow(array):
    return pltpu.with_memory_space_constraint(array, pltpu.HBM)


def forward_kernel(slot, section, slot_plot, gains, keep, acts, w_qkv, w_out, w_in, w_down, w_cross, pack_v, qkv_o, p_o, h1_o, query_o, g1_o, g2_o, h2_o, send_v, *rest):
    if slot == 0:
        wqkv_v, wout_v, win_v, wdown_v, wcross_v = rest[:5]
    else:
        wqkv_v, wout_v, win_v, wdown_v, wcross_v = w_qkv, w_out, w_in, w_down, w_cross
    (gains_v, keep_v, x_v, qkv_v, p_v, h1_v, g1_v, g2_v, h2_v, sems) = rest[-10:]
    encoding = section[0] == 0
    plot = slot_plot[0, slot]
    copies = Copies(sems)
    get_x = copies(acts.at[0, plot], x_v)
    get_small = [copies(gains, gains_v), copies(keep, keep_v)]
    tile = 512
    get_qkv, get_in, get_out, get_down, get_cross = [], [], [], [], []
    if slot == 0:
        get_qkv = [
            copies(w_qkv.at[0, :, pl.ds(i * D, D)], wqkv_v.at[:, pl.ds(i * D, D)]) for i in range(3)
        ]
        get_out = [copies(w_out.at[0], wout_v)]
        for i in range(FF // tile):
            get_in += [
                copies(
                    w_in.at[0, :, pl.ds(base + i * tile, tile)],
                    win_v.at[:, pl.ds(base + i * tile, tile)],
                )
                for base in (0, FF)
            ]
        get_down = [copies(w_down.at[0], wdown_v)]
        get_cross = [copies(w_cross.at[0], wcross_v)]
    get_x.start()
    start(get_small)
    start(get_qkv + get_out + get_in + get_down + get_cross)
    masks = lane_masks()
    get_x.wait()
    wait(get_small)
    count = kept(keep_v, plot)
    rows_in = x_v[...].astype(F32)
    normal = rms(rows_in, gains_v[0]).astype(BF16)
    pack_v[:, 0:D] = normal
    for i in range(3):
        wait(get_qkv[i : i + 1])
        qkv_v[:, i * D : (i + 1) * D] = mm(normal, wqkv_v[:, i * D : (i + 1) * D]).astype(BF16)
    put_qkv = copies(qkv_v, qkv_o)
    put_qkv.start()
    row_index = lax.broadcasted_iota(jnp.int32, (SEQ, 2 * SEQ), 0)
    key_index = key_columns()
    limit = jnp.where(encoding, jnp.broadcast_to(count - 1, (SEQ, 2 * SEQ)), row_index)
    allowed = key_index <= limit
    for pair in range(PAIRS):
        lanes = slice(pair * 128, (pair + 1) * 128)
        weights, mixed = attend(
            qkv_v[:, lanes],
            qkv_v[:, D + pair * 128 : D + (pair + 1) * 128],
            qkv_v[:, 2 * D + pair * 128 : 2 * D + (pair + 1) * 128],
            allowed,
            masks,
        )
        p_v[pair] = weights
        pack_v[:, D + pair * 128 : D + (pair + 1) * 128] = mixed
    put_p = copies(p_v, p_o)
    put_p.start()
    wait(get_out)
    first = rows_in + mm(pack_v[:, D : 2 * D], wout_v[...])
    h1_v[...] = first
    put_h1 = copies(h1_v, h1_o)
    put_h1.start()
    normal = rms(first, gains_v[1]).astype(BF16)
    pack_v[:, 2 * D : 3 * D] = normal
    put_parts = [copies(g1_v, g1_o), copies(g2_v, g2_o)]
    put_h2 = copies(h2_v, h2_o)
    put_query = copies(send_v.at[:, pl.ds(0, D)], query_o)

    @pl.when(encoding)
    def _():
        inputs = pack_v[:, 2 * D : 3 * D]
        for i in range(FF // tile):
            wait(get_in[2 * i : 2 * i + 2])
            columns = slice(i * tile, (i + 1) * tile)
            gate = mm(inputs, win_v[:, columns])
            up = mm(inputs, win_v[:, FF + i * tile : FF + (i + 1) * tile])
            unit, to_gate, to_up = gate_parts(gate, up)
            pack_v[:, 4 * D + i * tile : 4 * D + (i + 1) * tile] = unit.astype(BF16)
            g1_v[:, columns] = to_gate.astype(BF16)
            g2_v[:, columns] = to_up.astype(BF16)
        start(put_parts)
        wait(get_down)
        second = h1_v[...] + mm(pack_v[:, 4 * D :], wdown_v[...])
        h2_v[...] = second
        put_h2.start()
        rows = lax.broadcasted_iota(jnp.int32, (SEQ, D), 0)
        memory = rms(second, gains_v[2])
        memory = jnp.where(rows < jnp.broadcast_to(count, (SEQ, D)), memory, 0.0).astype(BF16)
        pack_v[:, 3 * D : 4 * D] = memory
        wait(get_cross)
        send_v[...] = mm(memory, wcross_v[...]).astype(BF16)
        wait(put_parts)
        put_h2.wait()

    @pl.when(jnp.logical_not(encoding))
    def _():
        wait(get_cross)
        send_v[:, 0:D] = mm(pack_v[:, 2 * D : 3 * D], wcross_v[:, 0:D]).astype(BF16)
        put_query.start()
        put_query.wait()
        wait(get_in + get_down)

    put_qkv.wait()
    put_p.wait()
    put_h1.wait()


def forward(slot, section, slot_plot, gains, keep, acts, weights):
    outs = [
        vmem(SEQ, 4 * D + FF),
        hbm(SEQ, 3 * D),
        hbm(PAIRS, SEQ, 2 * SEQ),
        hbm(SEQ, D, dtype=F32),
        hbm(SEQ, D),
        hbm(SEQ, FF),
        hbm(SEQ, FF),
        hbm(SEQ, D, dtype=F32),
        vmem(SEQ, 2 * D),
    ]
    small = [slow(gains), slow(keep), slow(acts)]
    if slot == 0:
        outs += [vmem(*weight.shape[1:]) for weight in weights]
    return call(
        functools.partial(forward_kernel, slot),
        [section, slot_plot],
        outs,
        [
            struct(3, 1, D, dtype=F32),
            struct(2, SEQ, dtype=jnp.int32),
            struct(SEQ, D),
            struct(SEQ, 3 * D),
            struct(PAIRS, SEQ, 2 * SEQ),
            struct(SEQ, D, dtype=F32),
            struct(SEQ, FF),
            struct(SEQ, FF),
            struct(SEQ, D, dtype=F32),
        ],
        34,
        "forward",
        small + [slow(weight) for weight in weights] if slot == 0 else small,
        () if slot == 0 else weights,
        flops=2 * SEQ * 8 * 10**6,
        traffic=22 * 10**6,
        room=12,
    )


def turn_kernel(count, *refs):
    for source, result in zip(refs[1 : count + 1], refs[count + 1 : 2 * count + 1]):

        def step(i, carry):
            at = pl.ds(pl.multiple_of(i * 256, 256), 256)
            result[at, :] = source[:, at].T
            return carry

        lax.fori_loop(0, source.shape[1] // 256, step, 0)


def turn(weights, after):
    return call(
        functools.partial(turn_kernel, len(weights)), [],
        [vmem(*weight.shape[::-1]) for weight in weights], [], 1, "turn", [after], weights, room=4,
    )


def middle_kernel(slot, section, slot_plot, table_len, gains, keep, h1, query, cot, kv_v, win_v, wcross_v, wint_v, wdownt_v, wcrosst_v, pack_v, rhs_v, dkv_v, e2_v, de2_v, gain_v, gains_v, keep_v, h1_v, query_v, cot_v, g1_v, g2_v, p_v, mixed_v, sems):
    @pl.when(section[0] != 0)
    def _():
        plot = slot_plot[0, slot]
        copies = Copies(sems)
        get_query = copies(query, query_v)
        get_small = [copies(gains, gains_v), copies(keep, keep_v)]
        get_h1 = copies(h1, h1_v)
        tile = 512
        get_cot = copies(cot.at[slot], cot_v)
        start([get_query, *get_small, get_h1, get_cot])
        masks = lane_masks()
        wait(get_small)
        count = kept(keep_v, plot)
        allowed = key_columns() < jnp.broadcast_to(count, (SEQ, 2 * SEQ))
        get_query.wait()
        for pair in range(PAIRS):
            lanes = slice(pair * 128, (pair + 1) * 128)
            weights, mixed = attend(
                query_v[:, lanes],
                kv_v[:, lanes],
                kv_v[:, D + pair * 128 : D + (pair + 1) * 128],
                allowed,
                masks,
            )
            p_v[pair] = weights
            pack_v[:, D + pair * 128 : D + (pair + 1) * 128] = mixed
        get_h1.wait()
        second = h1_v[...] + mm(pack_v[:, D : 2 * D], wcross_v[:, D : 2 * D])
        e2_v[...] = second
        normal = rms(second, gains_v[2]).astype(BF16)
        pack_v[:, 0:D] = normal
        for i in range(FF // tile):
            columns = slice(i * tile, (i + 1) * tile)
            gate = mm(normal, win_v[:, columns])
            up = mm(normal, win_v[:, FF + i * tile : FF + (i + 1) * tile])
            unit, to_gate, to_up = gate_parts(gate, up)
            pack_v[:, 2 * D + i * tile : 2 * D + (i + 1) * tile] = unit.astype(BF16)
            g1_v[:, columns] = to_gate.astype(BF16)
            g2_v[:, columns] = to_up.astype(BF16)
        get_cot.wait()
        rows = lax.broadcasted_iota(jnp.int32, (SEQ, D), 0)
        upstream = jnp.where(rows < table_len[plot], cot_v[...].astype(F32), 0.0)
        branch = upstream.astype(BF16)
        rhs_v[:, 0:D] = branch
        for i in range(FF // tile):
            columns = slice(i * tile, (i + 1) * tile)
            grad_unit = mm(branch, wdownt_v[:, columns])
            rhs_v[:, D + i * tile : D + (i + 1) * tile] = (
                grad_unit * g1_v[:, columns].astype(F32)
            ).astype(BF16)
            rhs_v[:, D + FF + i * tile : D + FF + (i + 1) * tile] = (
                grad_unit * g2_v[:, columns].astype(F32)
            ).astype(BF16)
        grad_normal = mm(rhs_v[:, D : D + 2 * FF], wint_v[...])
        back, grad_gain = rms_back(second, gains_v[2], grad_normal)
        grad_second = upstream + back
        gain_v[...] = jnp.zeros_like(gain_v)
        gain_v[2:3, :] = grad_gain
        de2_v[...] = grad_second
        branch = grad_second.astype(BF16)
        rhs_v[:, 2 * D + 2 * FF : 3 * D + 2 * FF] = branch
        mixed_v[...] = mm(branch, wcrosst_v[D : 2 * D, :]).astype(BF16)
        for pair in range(PAIRS):
            lanes = slice(pair * 128, (pair + 1) * 128)
            high = slice(D + pair * 128, D + (pair + 1) * 128)
            grad_query, grad_keys, grad_values = attend_back(
                query_v[:, lanes], kv_v[:, lanes], kv_v[:, high], p_v[pair], mixed_v[:, lanes], masks
            )
            rhs_v[:, D + 2 * FF + pair * 128 : D + 2 * FF + (pair + 1) * 128] = grad_query
            dkv_v[:, lanes] = grad_keys
            dkv_v[:, high] = grad_values


def middle(slot, section, slot_plot, table_len, gains, keep, kv, h1, query, cot, weights, turned):
    w_qkv, w_out, w_in, w_down, w_cross = weights
    return call(
        functools.partial(middle_kernel, slot),
        [section, slot_plot, table_len],
        [
            vmem(SEQ, 2 * D + FF),
            vmem(SEQ, 3 * D + 2 * FF),
            vmem(SEQ, 2 * D),
            vmem(SEQ, D, dtype=F32),
            vmem(SEQ, D, dtype=F32),
            vmem(8, D, dtype=F32),
        ],
        [
            struct(3, 1, D, dtype=F32),
            struct(2, SEQ, dtype=jnp.int32),
            struct(SEQ, D, dtype=F32),
            struct(SEQ, D),
            struct(SEQ, D),
            struct(SEQ, FF),
            struct(SEQ, FF),
            struct(PAIRS, SEQ, 2 * SEQ),
            struct(SEQ, D),
        ],
        10,
        "middle",
        [slow(gains), slow(keep), slow(h1), slow(query), slow(cot)],
        [kv, w_in, w_cross, turned[2], turned[3], turned[4]],
        flops=2 * SEQ * 12 * 10**6,
        traffic=18 * 10**6,
        room=12,
    )


def outer_kernel(slot, section, slot_plot, table_len, gains, keep, h2, g1, g2, extra, dkv_v, pack1_v, pack2_v, rhs2_v, e2_v, wdown_v, wdownt_v, wcrosst_v, *rest):
    (rhs_v, dh2_v, gain_v, out_o, gains_v, keep_v, h2_v, g1_v, g2_v, out_v, sems) = rest[-11:]
    plot = slot_plot[0, slot]

    @pl.when(section[0] == 0)
    def _():
        copies = Copies(sems)
        get = [
            copies(keep, keep_v),
            copies(gains, gains_v),
            copies(h2, h2_v),
            copies(g1, g1_v),
            copies(g2, g2_v),
        ]
        start(get)
        put_out = copies(pack1_v.at[:, pl.ds(3 * D, D)], out_o.at[0, slot])
        put_out.start()
        grad_memory = mm(dkv_v[...], wcrosst_v[...])
        rhs_v[:, D + 2 * FF :] = dkv_v[...]
        wait(get[:3])
        count = kept(keep_v, plot)
        rows = lax.broadcasted_iota(jnp.int32, (SEQ, D), 0)
        grad_memory = jnp.where(rows < jnp.broadcast_to(count, (SEQ, D)), grad_memory, 0.0)
        grad_second, grad_gain = rms_back(h2_v[...], gains_v[2], grad_memory)
        gain_v[...] = jnp.zeros_like(gain_v)
        gain_v[2:3, :] = grad_gain
        dh2_v[...] = grad_second
        branch = grad_second.astype(BF16)
        rhs_v[:, 0:D] = branch
        wait(get[3:])
        tile = 512
        for i in range(FF // tile):
            columns = slice(i * tile, (i + 1) * tile)
            grad_unit = mm(branch, wdownt_v[:, columns])
            rhs_v[:, D + i * tile : D + (i + 1) * tile] = (
                grad_unit * g1_v[:, columns].astype(F32)
            ).astype(BF16)
            rhs_v[:, D + FF + i * tile : D + FF + (i + 1) * tile] = (
                grad_unit * g2_v[:, columns].astype(F32)
            ).astype(BF16)
        put_out.wait()

    @pl.when(section[0] != 0)
    def _():
        copies = Copies(sems)
        third = e2_v[...] + mm(pack2_v[:, 2 * D :], wdown_v[...])
        rows = lax.broadcasted_iota(jnp.int32, (SEQ, D), 0)
        out_v[...] = jnp.where(rows < table_len[plot], third, 0.0).astype(BF16)
        put = copies(out_v, out_o.at[0, slot])
        put.start()
        rhs_v[...] = rhs2_v[...]
        put.wait()


def outer(slot, section, slot_plot, table_len, gains, keep, dkv, h2, g1, g2, pack1, e2, pack2, rhs2, weights, turned, extra):
    arrays = [slow(item) for item in (gains, keep, h2, g1, g2)] + [extra]
    return call(
        functools.partial(outer_kernel, slot),
        [section, slot_plot, table_len],
        [
            vmem(SEQ, 3 * D + 2 * FF),
            vmem(SEQ, D, dtype=F32),
            vmem(8, D, dtype=F32),
            struct(1, 2, SEQ, D),
        ],
        [
            struct(3, 1, D, dtype=F32),
            struct(2, SEQ, dtype=jnp.int32),
            struct(SEQ, D, dtype=F32),
            struct(SEQ, FF),
            struct(SEQ, FF),
            struct(SEQ, D),
        ],
        8,
        "outer",
        arrays,
        [dkv, pack1, pack2, rhs2, e2, weights[3], turned[3], turned[4]],
        aliases={3 + len(arrays) - 1: 3} if slot == 1 else None,
        flops=2 * SEQ * 3 * 10**6,
        traffic=8 * 10**6,
        room=8,
    )


def inner_kernel(slot, section, slot_plot, gains, acts, h1, qkv, p, *rest):
    rest = rest[slot:]
    rhs3_v, dh2_v, gain3_v, de2_v, gain2_v, wqkvt_v, woutt_v, wint_v, wcrosst_v = rest[:9]
    (rhs_v, gain_v, grad_o, gains_v, x_v, h1_v, qkv_v, p_v, up_v, grad_v, dn_v, sems) = rest[-12:]
    encoding = section[0] == 0
    plot = slot_plot[0, slot]
    copies = Copies(sems)
    get = [
        copies(h1, h1_v),
        copies(gains, gains_v),
        copies(qkv, qkv_v),
        copies(p, p_v),
        copies(acts.at[0, plot], x_v),
    ]
    start(get)

    @pl.when(encoding)
    def _():
        dn_v[...] = mm(rhs3_v[:, D : D + 2 * FF], wint_v[...])
        up_v[...] = dh2_v[...]
        gain_v[...] = gain3_v[...]

    @pl.when(jnp.logical_not(encoding))
    def _():
        dn_v[...] = mm(rhs3_v[:, D + 2 * FF : 2 * D + 2 * FF], wcrosst_v[0:D, :])
        up_v[...] = de2_v[...]
        gain_v[...] = gain2_v[...]

    wait(get[:2])
    back, grad_gain = rms_back(h1_v[...], gains_v[1], dn_v[...])
    grad_first = up_v[...] + back
    gain_v[1:2, :] = grad_gain
    branch = grad_first.astype(BF16)
    rhs_v[:, 0:D] = branch
    masks = lane_masks()
    grad_mixed = mm(branch, woutt_v[...]).astype(BF16)
    wait(get[2:4])
    for pair in range(PAIRS):
        spans = [slice(i * D + pair * 128, i * D + (pair + 1) * 128) for i in range(3)]
        parts = attend_back(
            qkv_v[:, spans[0]],
            qkv_v[:, spans[1]],
            qkv_v[:, spans[2]],
            p_v[pair],
            grad_mixed[:, pair * 128 : (pair + 1) * 128],
            masks,
        )
        for i in range(3):
            rhs_v[:, D + i * D + pair * 128 : D + i * D + (pair + 1) * 128] = parts[i]
    grad_normal = mm(rhs_v[:, D : 4 * D], wqkvt_v[...])
    wait(get[4:])
    back, grad_gain = rms_back(x_v[...].astype(F32), gains_v[0], grad_normal)
    gain_v[0:1, :] = grad_gain
    if slot == 1:
        gain_v[...] = gain_v[...] + rest[9][...]
    grad_v[...] = grad_first + back
    put_grad = copies(grad_v, grad_o.at[0, plot])
    put_grad.start()
    put_grad.wait()


def inner(slot, section, slot_plot, gains, acts, h1, qkv, p, rhs3, dh2, gain3, de2, gain2, turned, before):
    arrays = [slow(item) for item in (gains, acts, h1, qkv, p)]
    fast = [rhs3, dh2, gain3, de2, gain2, turned[0], turned[1], turned[2], turned[4]]
    aliases = {}
    if before is not None:
        aliases = {2 + len(arrays): 2}
        arrays.append(before[2])
        fast.append(before[1])
    return call(
        functools.partial(inner_kernel, slot),
        [section, slot_plot],
        [
            vmem(SEQ, 4 * D),
            vmem(8, D, dtype=F32),
            struct(1, 2, SEQ, D, dtype=F32),
        ],
        [
            struct(3, 1, D, dtype=F32),
            struct(SEQ, D),
            struct(SEQ, D, dtype=F32),
            struct(SEQ, 3 * D),
            struct(PAIRS, SEQ, 2 * SEQ),
            struct(SEQ, D, dtype=F32),
            struct(SEQ, D, dtype=F32),
            struct(SEQ, D, dtype=F32),
        ],
        8,
        "inner",
        arrays,
        fast,
        aliases=aliases,
        flops=2 * SEQ * 6 * 10**6,
        traffic=14 * 10**6,
        room=8,
    )


def place_parts(place):
    number = place[0]
    return (
        lax.shift_right_logical(number, 5),
        jnp.bitwise_and(lax.shift_right_logical(number, 3), 3),
        jnp.bitwise_and(lax.shift_right_logical(number, 1), 3),
        jnp.bitwise_and(number, 1),
    )


def matching(target, columns):
    rows = target.shape[0]
    lane = lax.broadcasted_iota(jnp.int32, (rows, 128), 1)
    blocks = [jnp.where(lane + i * 128 == target, 1.0, 0.0) for i in range(columns // 128)]
    return jnp.concatenate(blocks, axis=1).astype(BF16)


def selector(place, along):
    y, x, z, core = place_parts(place)
    index = lax.broadcasted_iota(jnp.int32, (384, 128), 0)

    def at_least(value, *bounds):
        return sum(jnp.where(value >= bound, 1, 0) for bound in bounds)

    first = at_least(index, 96, 192, 288)
    rest = index - first * 96
    second = at_least(rest, 24, 48, 72)
    rest = rest - second * 24
    third = at_least(rest, 12)
    rest = rest - third * 12
    to_x, to_z = (first, second) if along == "x" else (second, first)
    return matching(
        jnp.bitwise_and(y + third, 1) * 384
        + jnp.bitwise_and(x + to_x, 3) * 96
        + jnp.bitwise_and(z + to_z, 3) * 24
        + core * 12
        + rest,
        D,
    )


def stacked(sources, first, width):
    return jnp.concatenate([source[:, first : first + width] for source in sources], axis=0)


def along_down(place):
    y, x, z, core = place_parts(place)
    index = lax.broadcasted_iota(jnp.int32, (256, 128), 0)
    return matching(
        jnp.bitwise_and(y + jnp.bitwise_and(lax.shift_right_logical(index, 5), 1), 1) * 256
        + jnp.bitwise_and(z + lax.shift_right_logical(index, 6), 3) * 64
        + core * 32
        + jnp.bitwise_and(index, 31),
        512,
    )


def prepare_down(place, sources, first, lefts_v, order):
    y, x, z, core = place_parts(place)
    for chunk in range(4):
        block = first + jnp.bitwise_and(x + chunk, 3) * 256
        columns = [pl.ds(pl.multiple_of(block + half, 256), 256) for half in (0, 1024)]
        picked = jnp.concatenate(
            [
                jnp.concatenate([source[:, at] for source in sources], axis=0)
                for at in columns
            ],
            axis=1,
        )
        at = 2688 + 256 * chunk
        lefts_v[at : at + 256, :] = mm_t(order, picked).astype(BF16)


def prepare_kernel(section, place, *refs):
    pack1 = refs[0:4]
    lefts_v = refs[4]
    along_x = selector(place, "x")
    along_z = selector(place, "z")
    lefts_v[0:384, :] = mm_t(along_x, stacked(pack1, 0, D)).astype(BF16)
    lefts_v[384:768, :] = mm_t(along_z, stacked(pack1, 0, D)).astype(BF16)
    lefts_v[768:1152, :] = mm_t(along_z, stacked(pack1, D, D)).astype(BF16)

    @pl.when(section[0] == 0)
    def _():
        lefts_v[1152:1536, :] = mm_t(along_x, stacked(pack1, 2 * D, D)).astype(BF16)
        lefts_v[1536:1920, :] = mm_t(along_z, stacked(pack1, 2 * D, D)).astype(BF16)
        memory = mm_t(along_z, stacked(pack1, 3 * D, D)).astype(BF16)
        lefts_v[1920:2304, :] = memory
        lefts_v[2304:2688, :] = memory
        prepare_down(place, pack1, 4 * D, lefts_v, along_down(place))

    @pl.when(section[0] != 0)
    def _():
        lefts_v[1920:2304, :] = mm_t(along_z, stacked(pack1, 2 * D, D)).astype(BF16)


def prepare(section, place, pack1, after):
    def kernel(section, place, *refs):
        prepare_kernel(section, place, *refs[len(after) :])

    return call(
        kernel, [section, place], [vmem(3712, 512)], [], 1, "prepare", after, pack1, room=12,
    )[0]


def prepare_more_kernel(section, place, *refs):
    pack2 = refs[0:4]
    lefts_v = refs[5]

    @pl.when(section[0] != 0)
    def _():
        along_x = selector(place, "x")
        along_z = selector(place, "z")
        lefts_v[1152:1536, :] = mm_t(along_x, stacked(pack2, 0, D)).astype(BF16)
        lefts_v[1536:1920, :] = mm_t(along_z, stacked(pack2, 0, D)).astype(BF16)
        lefts_v[2304:2688, :] = mm_t(along_z, stacked(pack2, D, D)).astype(BF16)
        prepare_down(place, pack2, 2 * D, lefts_v, along_down(place))


def prepare_more(section, place, pack2, lefts):
    return call(
        prepare_more_kernel, [section, place], [vmem(3712, 512)], [], 1, "prepare_more", [],
        [*pack2, lefts], aliases={6: 0}, room=12,
    )[0]


class Buffers:
    def __init__(self, refs, size):
        self.own, self.ahead, self.behind, self.one, self.three = refs
        self.size = size

    def spot(self, chunk, block):
        quarter = self.size // 4
        half = self.size // 2
        row = block * quarter
        if chunk == 0:
            return self.own, row
        low = block < 2
        if chunk == 1:
            return (self.one, row) if low else (self.ahead, row)
        if chunk == 2:
            return (self.ahead, row) if low else (self.behind, row - half)
        return (self.behind, half + row) if low else (self.three, row - half)


def buffer_shapes(size):
    return [struct(size, 128)] * 3 + [struct(size // 2, 128)] * 2


def store_narrow(buffers, grad, offset):
    for chunk in range(4):
        for block in range(4):
            rows = grad[(chunk * 4 + block) * 24 : (chunk * 4 + block + 1) * 24]
            piece = jnp.concatenate([rows[:, 0:128], rows[:, 128:256]], axis=0).astype(BF16)
            target, row = buffers.spot(chunk, block)
            target[row + offset : row + offset + 48, :] = piece


SIZE_X, SIZE_Z = 4 * 1056, 4 * 1008


def grads_kernel(place, lefts_v, *refs):
    wide = refs[0:4]
    thin = refs[4:8]
    gains = refs[8:10]
    held = Buffers(refs[10:15], SIZE_X), Buffers(refs[15:20], SIZE_Z)
    total_of = selector(place, "z")
    total = gains[0][...] + gains[1][...]
    upper = total.astype(BF16)
    lower = (total - upper.astype(F32)).astype(BF16)
    ordered = mm_t(upper, total_of) + mm_t(lower, total_of)
    tall = jnp.concatenate([ordered, jnp.zeros((120, 384), F32)], axis=0).T
    tall = jnp.concatenate([tall, jnp.zeros((384, 128), F32)], axis=1)
    store_narrow(held[1], tall, 960)
    branch = stacked(wide, 0, D)
    for chunk in range(4):
        first = 2688 + 256 * chunk
        grad = mm(lefts_v[first : first + 256, :], branch)
        for block in range(4):
            target, row = held[0].spot(chunk, block)
            for i in range(6):
                spot = row + 384 + 64 * i
                target[spot : spot + 64, :] = grad[
                    64 * block : 64 * (block + 1), 128 * i : 128 * (i + 1)
                ].astype(BF16)
    for i in range(6):
        left = lefts_v[1920:2304, :] if i < 3 else lefts_v[2304:2688, :]
        right = stacked(wide, D + 2 * FF + 256 * i, 256)
        store_narrow(held[1], mm(left, right), 384 + 48 * i)
    for axis in range(2):
        left = lefts_v[1152 + 384 * axis : 1536 + 384 * axis, :]
        for i in range(8):
            right = stacked(wide, D + axis * FF + 256 * i, 256)
            store_narrow(held[axis], mm(left, right), 48 * i)
    for i in range(6):
        right = stacked(thin, D + 256 * i, 256)
        store_narrow(held[0], mm(lefts_v[0:384, :], right), 768 + 48 * i)
    for i in range(6):
        left = lefts_v[384:768, :] if i < 3 else lefts_v[768:1152, :]
        right = stacked(thin, 3 * D + 256 * i if i < 3 else 256 * (i - 3), 256)
        store_narrow(held[1], mm(left, right), 672 + 48 * i)


def grads(place, lefts, wide, thin, gains):
    shapes = [vmem(*item.shape) for item in buffer_shapes(SIZE_X) + buffer_shapes(SIZE_Z)]
    return call(
        grads_kernel, [place], shapes, [], 1, "grads", [], [lefts, *wide, *thin, *gains],
        flops=2 * 512 * 4 * 10**6, traffic=15 * 10**6, room=16,
    )


def flat(y, x, z, core):
    return ((y * 4 + x) * 4 + z) * 2 + core


def shifted(array, y=0, x=0, z=0, core=0):
    pairs = []
    for a in range(2):
        for b in range(4):
            for c in range(4):
                for d in range(2):
                    source = flat(a, b, c, d)
                    target = flat((a + y) % 2, (b + x) % 4, (c + z) % 4, (d + core) % 2)
                    pairs.append((source, target))
    return lax.ppermute(array, "dp", pairs)


def add(*terms):
    total = terms[0].astype(F32)
    for term in terms[1:]:
        total = total + term.astype(F32)
    return total


def along_two_rounds(buffers, axis):
    own, ahead, behind, one, three = buffers
    half = one.shape[0]
    got_ahead = shifted(ahead, **{axis: 1})
    got_behind = shifted(behind, **{axis: 3})
    last_ahead = shifted(add(one, got_ahead[:half]).astype(BF16), **{axis: 1})
    last_behind = shifted(add(three, got_behind[:half]).astype(BF16), **{axis: 3})
    low = add(own[:half], last_ahead, got_behind[half:])
    high = add(own[half:], got_ahead[half:], last_behind)
    return jnp.concatenate([low, high], axis=0).astype(BF16)


def along_one_round(total, axis):
    quarter = total.shape[0] // 4
    parts = [total[i * quarter : (i + 1) * quarter] for i in range(4)]
    return add(
        parts[0],
        shifted(parts[1], **{axis: 1}),
        shifted(parts[3], **{axis: 3}),
        shifted(parts[2], **{axis: 2}),
    )


def along_y(totals):
    sent = [total[:, 1].reshape(-1, 128).astype(BF16) for total in totals]
    got = shifted(jnp.concatenate(sent, axis=0), y=1)
    results = []
    first = 0
    for total, part in zip(totals, sent):
        size = part.shape[0]
        own = total[:, 0]
        results.append(own + got[first : first + size].reshape(own.shape).astype(F32))
        first += size
    return results


def rows_of(blocks):
    count, rows, lanes = blocks.shape
    return blocks.transpose(1, 0, 2).reshape(rows, count * lanes)


def local(
    acts,
    gains,
    qkv_weight,
    out_weight,
    mlp_in,
    mlp_out,
    cross_weight,
    patch_mask,
    table_len,
    slot_plot,
    cotangent,
):
    section = lax.axis_index("section").astype(jnp.int32).reshape(1)
    place = lax.axis_index("dp").astype(jnp.int32).reshape(1)
    gains = gains.transpose(1, 0, 2)
    weights = (qkv_weight, out_weight, mlp_in, mlp_out, cross_weight)
    made = []
    received = []
    for slot in range(2):
        made.append(forward(slot, section, slot_plot, gains, patch_mask, acts, weights))
        if slot == 0:
            weights = made[0][9:]
        received.append(lax.ppermute(made[slot][8], "section", [(0, 1)]))

    def both(own):
        return list(own) + [shifted(array, core=1) for array in own]

    turned_last = turn(weights[2:], slow(made[1][1]))
    pack1 = both([item[0] for item in made])
    lefts = prepare(section, place, pack1, [slow(made[1][2])])
    middles = []
    back = []
    turned = [None, None, *turned_last]
    for slot in range(2):
        h1, query = made[slot][3:5]
        middles.append(
            middle(
                slot, section, slot_plot, table_len, gains, patch_mask,
                received[slot], h1, query, cotangent, weights, turned,
            )
        )
        back.append(lax.ppermute(middles[slot][2], "section", [(1, 0)]))
    turned = [*turn(weights[:2], slow(made[0][2])), *turned_last]
    outers = []
    inners = []
    out_chain = patch_mask
    before = None
    for slot in range(2):
        own_pack1, qkv, p, h1, query, g1, g2, h2 = made[slot][:8]
        own_pack2, rhs2, _, e2, de2, gain2 = middles[slot]
        outers.append(
            outer(
                slot, section, slot_plot, table_len, gains, patch_mask, back[slot],
                h2, g1, g2, own_pack1, e2, own_pack2, rhs2, weights, turned, out_chain,
            )
        )
        rhs3, dh2, gain3, out_chain = outers[slot]
        before = inner(
            slot, section, slot_plot, gains, acts, h1, qkv, p,
            rhs3, dh2, gain3, de2, gain2, turned, before,
        )
        inners.append(before)
    grad_chain = before[2]
    lefts = prepare_more(section, place, both([item[0] for item in middles]), lefts)
    part = grads(
        place,
        lefts,
        both([item[0] for item in outers]),
        both([item[0] for item in inners]),
        both([before[1]]),
    )
    first_x = along_two_rounds(part[:5], "x")
    first_z = along_two_rounds(part[5:], "z")
    last_x = along_one_round(first_x, "z")
    last_z = along_one_round(first_z, "x")
    units_x, last_down, qkv_x, last_z = along_y(
        [
            last_x[:384].reshape(16, 2, 12, 128),
            last_x[384:768].reshape(6, 2, 32, 128),
            last_x[768:].reshape(12, 2, 12, 128),
            last_z.reshape(42, 2, 12, 128),
        ]
    )
    grad_mlp_in = rows_of(jnp.concatenate([units_x, last_z[:16]], axis=0))
    grad_cross = rows_of(last_z[16:28])
    grad_mlp_out = rows_of(last_down)
    grad_qkv = rows_of(jnp.concatenate([qkv_x, last_z[28:34]], axis=0))
    grad_out = rows_of(last_z[34:40])
    grad_gains = last_z[40][:, 0:3].T
    return (
        out_chain,
        grad_chain,
        grad_gains[None],
        grad_qkv[None],
        grad_out[None],
        grad_mlp_in[None],
        grad_mlp_out[None],
        grad_cross[None],
    )


def solution(mesh):
    return jax.shard_map(
        local,
        mesh=mesh,
        in_specs=(
            P("section", "dp", None, None),
            P("section", None, None),
            P("section", None, None),
            P("section", None, None),
            P("section", None, None),
            P("section", None, None),
            P("section", None, None),
            P("dp", None),
            P("dp"),
            P("dp", None),
            P("dp", None, None),
        ),
        out_specs=(
            P("section", "dp", None, None),
            P("section", "dp", None, None),
            P("section", None, "dp"),
            P("section", "dp", None),
            P("section", "dp", None),
            P("section", "dp", None),
            P("section", "dp", None),
            P("section", "dp", None),
        ),
        check_vma=False,
    )
```

```python
import functools

import jax
import jax.numpy as jnp
from jax import lax
from jax.experimental import pallas as pl
from jax.experimental.pallas import tpu as pltpu
from jax.sharding import PartitionSpec as P

D = 768
HDIM = 64
FF = 2048
SEQ = 128
PAIRS = 6
EPS = 1e-06
NEGATIVE = -1e30
ROOM_BYTES = 11 * 2**20
SCALE = HDIM ** (-0.5)
BF16 = jnp.bfloat16
F32 = jnp.float32
ANY = pl.BlockSpec(memory_space=pl.ANY)
FAST = pl.BlockSpec(memory_space=pltpu.VMEM)
SMEM = pl.BlockSpec(memory_space=pltpu.SMEM)


def mm(left, right):
    return jnp.dot(left, right, preferred_element_type=F32)


def mm_t(left, right):
    return lax.dot_general(left, right, (((1,), (1,)), ((), ())), preferred_element_type=F32)


def mm_w(left, right):
    return lax.dot_general(left, right, (((0,), (0,)), ((), ())), preferred_element_type=F32)


def halves(first, second):
    return jnp.concatenate([first, second], axis=0)


def rms(hidden, gain):
    inverse = lax.rsqrt(jnp.mean(hidden * hidden, axis=-1, keepdims=True) + EPS)
    return hidden * inverse * gain


def rms_back(hidden, gain, upstream):
    inverse = lax.rsqrt(jnp.mean(hidden * hidden, axis=-1, keepdims=True) + EPS)
    unit = hidden * inverse
    scaled = upstream * gain
    grad_gain = jnp.sum(upstream * unit, axis=0, keepdims=True)
    middle = jnp.mean(scaled * unit, axis=-1, keepdims=True)
    return inverse * (scaled - unit * middle), grad_gain


def gate_parts(gate, up):
    inner = 0.7978845608 * (gate + 0.044715 * gate * gate * gate)
    bend = jnp.tanh(inner)
    half = 0.5 * (1.0 + bend)
    value = gate * half
    slope = half + 0.5 * gate * (1.0 - bend * bend) * 0.7978845608 * (
        1.0 + 3.0 * 0.044715 * gate * gate
    )
    return value * up, slope * up, value


def lane_masks():
    lane = lax.broadcasted_iota(jnp.int32, (SEQ, 2 * HDIM), 1)
    low = jnp.where(lane < HDIM, 1.0, 0.0).astype(F32)
    return low.astype(BF16), (1.0 - low).astype(BF16), low


def stack_heads(pair, masks):
    return jnp.concatenate([pair * masks[0], pair * masks[1]], axis=0)


def attend(query, keys, values, allowed, masks):
    scores = mm_t(query, stack_heads(keys, masks)) * SCALE
    scores = jnp.where(allowed, scores, NEGATIVE)
    parts = []
    for head in range(2):
        part = scores[:, head * SEQ : (head + 1) * SEQ]
        power = jnp.exp(part - jnp.max(part, axis=-1, keepdims=True))
        parts.append(power * (1.0 / jnp.sum(power, axis=-1, keepdims=True)))
    weights = jnp.concatenate(parts, axis=1).astype(BF16)
    return weights, mm(weights, stack_heads(values, masks)).astype(BF16)


def attend_back(query, keys, values, weights, upstream, masks):
    key_stack = stack_heads(keys, masks)
    grad_weights = mm_t(upstream, stack_heads(values, masks))
    wide = weights.astype(F32)
    product = wide * grad_weights
    parts = []
    for head in range(2):
        columns = slice(head * SEQ, (head + 1) * SEQ)
        total = jnp.sum(product[:, columns], axis=-1, keepdims=True)
        parts.append(product[:, columns] - wide[:, columns] * total)
    grad_scores = jnp.concatenate(parts, axis=1).astype(BF16)
    grad_query = mm(grad_scores, key_stack) * SCALE
    key_both = mm_w(grad_scores, query) * SCALE
    value_both = mm_w(weights, upstream)
    low = masks[2]
    high = 1.0 - low
    grad_keys = key_both[:SEQ] * low + key_both[SEQ:] * high
    grad_values = value_both[:SEQ] * low + value_both[SEQ:] * high
    return grad_query.astype(BF16), grad_keys.astype(BF16), grad_values.astype(BF16)


def key_columns():
    return jnp.bitwise_and(lax.broadcasted_iota(jnp.int32, (SEQ, 2 * SEQ), 1), SEQ - 1)


def kept(keep_ref, plot):
    row = keep_ref[pl.ds(plot, 1), :].astype(F32)
    return jnp.sum(row, axis=1, keepdims=True).astype(jnp.int32)


class Copies:
    def __init__(self, sems):
        self.sems = sems
        self.count = 0

    def __call__(self, source, target):
        copy = pltpu.make_async_copy(source, target, self.sems.at[self.count])
        self.count += 1
        return copy


def start(copies):
    for copy in copies:
        copy.start()


def wait(copies):
    for copy in copies:
        copy.wait()


def struct(*shape, dtype=BF16):
    return jax.ShapeDtypeStruct(shape, dtype)


def call(kernel, scalars, out_shape, scratch, sems, name, arrays, fast=(), aliases=None, flops=0, traffic=0):
    return pl.pallas_call(
        kernel,
        name=name,
        in_specs=[SMEM] * len(scalars) + [ANY] * len(arrays) + [FAST] * len(fast),
        out_specs=[FAST if is_fast(item) else ANY for item in out_shape],
        out_shape=out_shape,
        scratch_shapes=[pltpu.VMEM(item.shape, item.dtype) for item in scratch]
        + [pltpu.SemaphoreType.DMA((sems,))],
        input_output_aliases=aliases or {},
        compiler_params=pltpu.CompilerParams(vmem_limit_bytes=ROOM_BYTES),
        cost_estimate=pl.CostEstimate(flops=flops, bytes_accessed=traffic, transcendentals=0),
    )(*scalars, *arrays, *[pltpu.with_memory_space_constraint(item, pltpu.VMEM) for item in fast])


def is_fast(item):
    return not isinstance(item, jax.ShapeDtypeStruct) and item.memory_space == pltpu.VMEM


def vmem(*shape, dtype=BF16):
    return pltpu.VMEM(shape, dtype)


def hbm(*shape, dtype=BF16):
    return pltpu.HBM(shape, dtype)


def slow(array):
    return pltpu.with_memory_space_constraint(array, pltpu.HBM)


def forward_kernel(slot, section, place, slot_plot, gains, keep, acts, w_qkv, w_out, w_in, w_down, w_cross, pack_o, qkv_o, p_o, h1_o, query_o, g1_o, g2_o, h2_o, send_v, *rest):
    if slot == 0:
        wqkv_v, wout_v, win_v, wdown_v, wcross_v = rest[:5]
    else:
        wqkv_v, wout_v, win_v, wdown_v, wcross_v = w_qkv, w_out, w_in, w_down, w_cross
    (gains_v, keep_v, x_v, pack_v, qkv_v, p_v, h1_v, g1_v, g2_v, h2_v, sems) = rest[-11:]
    encoding = section[0] == 0
    plot = slot_plot[0, slot]
    copies = Copies(sems)
    get_x = copies(acts.at[0, plot], x_v)
    get_small = [copies(gains, gains_v), copies(keep, keep_v)]
    tile = 512
    get_qkv, get_in, get_out, get_down, get_cross = [], [], [], [], []
    if slot == 0:
        get_qkv = [
            copies(w_qkv.at[0, :, pl.ds(i * D, D)], wqkv_v.at[:, pl.ds(i * D, D)]) for i in range(3)
        ]
        get_out = [copies(w_out.at[0], wout_v)]
        for i in range(FF // tile):
            get_in += [
                copies(
                    w_in.at[0, :, pl.ds(base + i * tile, tile)],
                    win_v.at[:, pl.ds(base + i * tile, tile)],
                )
                for base in (0, FF)
            ]
        get_down = [copies(w_down.at[0], wdown_v)]
        get_cross = [copies(w_cross.at[0], wcross_v)]
    get_x.start()
    start(get_small)
    start(get_qkv + get_out + get_in + get_down + get_cross)
    masks = lane_masks()
    get_x.wait()
    wait(get_small)
    count = kept(keep_v, plot)
    rows_in = x_v[...].astype(F32)
    normal = rms(rows_in, gains_v[0]).astype(BF16)
    pack_v[:, 0:D] = normal
    for i in range(3):
        wait(get_qkv[i : i + 1])
        qkv_v[:, i * D : (i + 1) * D] = mm(normal, wqkv_v[:, i * D : (i + 1) * D]).astype(BF16)
    put_qkv = copies(qkv_v, qkv_o)
    put_qkv.start()
    row_index = lax.broadcasted_iota(jnp.int32, (SEQ, 2 * SEQ), 0)
    key_index = key_columns()
    limit = jnp.where(encoding, jnp.broadcast_to(count - 1, (SEQ, 2 * SEQ)), row_index)
    allowed = key_index <= limit
    for pair in range(PAIRS):
        lanes = slice(pair * 128, (pair + 1) * 128)
        weights, mixed = attend(
            qkv_v[:, lanes],
            qkv_v[:, D + pair * 128 : D + (pair + 1) * 128],
            qkv_v[:, 2 * D + pair * 128 : 2 * D + (pair + 1) * 128],
            allowed,
            masks,
        )
        p_v[pair] = weights
        pack_v[:, D + pair * 128 : D + (pair + 1) * 128] = mixed
    put_p = copies(p_v, p_o)
    put_p.start()
    wait(get_out)
    first = rows_in + mm(pack_v[:, D : 2 * D], wout_v[...])
    h1_v[...] = first
    put_h1 = copies(h1_v, h1_o)
    put_h1.start()
    normal = rms(first, gains_v[1]).astype(BF16)
    pack_v[:, 2 * D : 3 * D] = normal
    put_parts = [copies(g1_v, g1_o), copies(g2_v, g2_o)]
    put_units = copies(pack_v.at[:, pl.ds(4 * D, FF)], pack_o.at[:, pl.ds(4 * D, FF)])
    put_memory = copies(pack_v.at[:, pl.ds(3 * D, D)], pack_o.at[:, pl.ds(3 * D, D)])
    put_some = copies(pack_v.at[:, pl.ds(0, 3 * D)], pack_o.at[:, pl.ds(0, 3 * D)])
    put_some.start()
    put_h2 = copies(h2_v, h2_o)
    put_query = copies(send_v.at[:, pl.ds(0, D)], query_o)

    @pl.when(encoding)
    def _():
        inputs = pack_v[:, 2 * D : 3 * D]
        for i in range(FF // tile):
            wait(get_in[2 * i : 2 * i + 2])
            columns = slice(i * tile, (i + 1) * tile)
            gate = mm(inputs, win_v[:, columns])
            up = mm(inputs, win_v[:, FF + i * tile : FF + (i + 1) * tile])
            unit, to_gate, to_up = gate_parts(gate, up)
            pack_v[:, 4 * D + i * tile : 4 * D + (i + 1) * tile] = unit.astype(BF16)
            g1_v[:, columns] = to_gate.astype(BF16)
            g2_v[:, columns] = to_up.astype(BF16)
        start(put_parts)
        put_units.start()
        wait(get_down)
        second = h1_v[...] + mm(pack_v[:, 4 * D :], wdown_v[...])
        h2_v[...] = second
        put_h2.start()
        rows = lax.broadcasted_iota(jnp.int32, (SEQ, D), 0)
        memory = rms(second, gains_v[2])
        memory = jnp.where(rows < jnp.broadcast_to(count, (SEQ, D)), memory, 0.0).astype(BF16)
        pack_v[:, 3 * D : 4 * D] = memory
        put_memory.start()
        wait(get_cross)
        send_v[...] = mm(memory, wcross_v[...]).astype(BF16)
        wait(put_parts)
        put_h2.wait()
        put_units.wait()
        put_memory.wait()

    @pl.when(jnp.logical_not(encoding))
    def _():
        wait(get_cross)
        send_v[:, 0:D] = mm(pack_v[:, 2 * D : 3 * D], wcross_v[:, 0:D]).astype(BF16)
        put_query.start()
        put_query.wait()
        wait(get_in + get_down)

    put_qkv.wait()
    put_p.wait()
    put_h1.wait()
    put_some.wait()


def forward(slot, section, place, slot_plot, gains, keep, acts, weights):
    outs = [
        hbm(SEQ, 4 * D + FF),
        hbm(SEQ, 3 * D),
        hbm(PAIRS, SEQ, 2 * SEQ),
        hbm(SEQ, D, dtype=F32),
        hbm(SEQ, D),
        hbm(SEQ, FF),
        hbm(SEQ, FF),
        hbm(SEQ, D, dtype=F32),
        vmem(SEQ, 2 * D),
    ]
    small = [slow(gains), slow(keep), slow(acts)]
    if slot == 0:
        outs += [vmem(*weight.shape[1:]) for weight in weights]
    return call(
        functools.partial(forward_kernel, slot),
        [section, place, slot_plot],
        outs,
        [
            struct(3, 1, D, dtype=F32),
            struct(2, SEQ, dtype=jnp.int32),
            struct(SEQ, D),
            struct(SEQ, 4 * D + FF),
            struct(SEQ, 3 * D),
            struct(PAIRS, SEQ, 2 * SEQ),
            struct(SEQ, D, dtype=F32),
            struct(SEQ, FF),
            struct(SEQ, FF),
            struct(SEQ, D, dtype=F32),
        ],
        34,
        "forward",
        small + [slow(weight) for weight in weights] if slot == 0 else small,
        () if slot == 0 else weights,
        flops=2 * SEQ * 8 * 10**6,
        traffic=22 * 10**6,
    )


def turn_all(sources, results):
    for source, result in zip(sources, results):

        def step(i, carry):
            at = pl.ds(pl.multiple_of(i * 256, 256), 256)
            result[at, :] = source[:, at].T
            return carry

        lax.fori_loop(0, source.shape[1] // 256, step, 0)


def turn_kernel(count, *refs):
    turn_all(refs[1 : count + 1], refs[count + 1 : 2 * count + 1])


def turn(weights, after):
    return call(
        functools.partial(turn_kernel, len(weights)), [],
        [vmem(*weight.shape[::-1]) for weight in weights], [], 1, "turn", [after], weights,
    )


def middle_kernel(slot, section, slot_plot, table_len, gains, keep, h1, query, cot, after, kv_v, win_v, wcross_v, wint_v, wdownt_v, wcrosst_v, pack_o, rhs_o, dkv_v, e2_o, de2_o, gain_o, gains_v, keep_v, h1_v, query_v, cot_v, pack_v, g1_v, g2_v, rhs_v, p_v, e2_v, de2_v, gain_v, mixed_v, sems):
    @pl.when(section[0] != 0)
    def _():
        plot = slot_plot[0, slot]
        copies = Copies(sems)
        get_query = copies(query, query_v)
        get_small = [copies(gains, gains_v), copies(keep, keep_v)]
        get_h1 = copies(h1, h1_v)
        tile = 512
        get_cot = copies(cot.at[slot], cot_v)
        start([get_query, *get_small, get_h1, get_cot])
        masks = lane_masks()
        wait(get_small)
        count = kept(keep_v, plot)
        allowed = key_columns() < jnp.broadcast_to(count, (SEQ, 2 * SEQ))
        get_query.wait()
        for pair in range(PAIRS):
            lanes = slice(pair * 128, (pair + 1) * 128)
            weights, mixed = attend(
                query_v[:, lanes],
                kv_v[:, lanes],
                kv_v[:, D + pair * 128 : D + (pair + 1) * 128],
                allowed,
                masks,
            )
            p_v[pair] = weights
            pack_v[:, D + pair * 128 : D + (pair + 1) * 128] = mixed
        get_h1.wait()
        second = h1_v[...] + mm(pack_v[:, D : 2 * D], wcross_v[:, D : 2 * D])
        e2_v[...] = second
        puts = [copies(e2_v, e2_o)]
        puts[-1].start()
        normal = rms(second, gains_v[2]).astype(BF16)
        pack_v[:, 0:D] = normal
        for i in range(FF // tile):
            columns = slice(i * tile, (i + 1) * tile)
            gate = mm(normal, win_v[:, columns])
            up = mm(normal, win_v[:, FF + i * tile : FF + (i + 1) * tile])
            unit, to_gate, to_up = gate_parts(gate, up)
            pack_v[:, 2 * D + i * tile : 2 * D + (i + 1) * tile] = unit.astype(BF16)
            g1_v[:, columns] = to_gate.astype(BF16)
            g2_v[:, columns] = to_up.astype(BF16)
        puts.append(copies(pack_v, pack_o))
        puts[-1].start()
        get_cot.wait()
        rows = lax.broadcasted_iota(jnp.int32, (SEQ, D), 0)
        upstream = jnp.where(rows < table_len[plot], cot_v[...].astype(F32), 0.0)
        branch = upstream.astype(BF16)
        rhs_v[:, 0:D] = branch
        for i in range(FF // tile):
            columns = slice(i * tile, (i + 1) * tile)
            grad_unit = mm(branch, wdownt_v[:, columns])
            rhs_v[:, D + i * tile : D + (i + 1) * tile] = (
                grad_unit * g1_v[:, columns].astype(F32)
            ).astype(BF16)
            rhs_v[:, D + FF + i * tile : D + FF + (i + 1) * tile] = (
                grad_unit * g2_v[:, columns].astype(F32)
            ).astype(BF16)
        grad_normal = mm(rhs_v[:, D : D + 2 * FF], wint_v[...])
        back, grad_gain = rms_back(second, gains_v[2], grad_normal)
        grad_second = upstream + back
        gain_v[...] = jnp.zeros_like(gain_v)
        gain_v[2:3, :] = grad_gain
        de2_v[...] = grad_second
        puts += [copies(de2_v, de2_o), copies(gain_v, gain_o)]
        start(puts[-2:])
        branch = grad_second.astype(BF16)
        rhs_v[:, 2 * D + 2 * FF : 3 * D + 2 * FF] = branch
        for first, width in ((0, D + 2 * FF), (2 * D + 2 * FF, D)):
            at = (slice(None), pl.ds(first, width))
            puts.append(copies(rhs_v.at[at], rhs_o.at[at]))
            puts[-1].start()
        mixed_v[...] = mm(branch, wcrosst_v[D : 2 * D, :]).astype(BF16)
        for pair in range(PAIRS):
            lanes = slice(pair * 128, (pair + 1) * 128)
            high = slice(D + pair * 128, D + (pair + 1) * 128)
            grad_query, grad_keys, grad_values = attend_back(
                query_v[:, lanes], kv_v[:, lanes], kv_v[:, high], p_v[pair], mixed_v[:, lanes], masks
            )
            rhs_v[:, D + 2 * FF + pair * 128 : D + 2 * FF + (pair + 1) * 128] = grad_query
            dkv_v[:, lanes] = grad_keys
            dkv_v[:, high] = grad_values
        at = (slice(None), pl.ds(D + 2 * FF, D))
        puts.append(copies(rhs_v.at[at], rhs_o.at[at]))
        puts[-1].start()
        wait(puts)


def middle(slot, section, slot_plot, table_len, gains, keep, kv, h1, query, cot, weights, turned, after):
    w_qkv, w_out, w_in, w_down, w_cross = weights
    return call(
        functools.partial(middle_kernel, slot),
        [section, slot_plot, table_len],
        [
            hbm(SEQ, 2 * D + FF),
            hbm(SEQ, 3 * D + 2 * FF),
            vmem(SEQ, 2 * D),
            hbm(SEQ, D, dtype=F32),
            hbm(SEQ, D, dtype=F32),
            hbm(8, D, dtype=F32),
        ],
        [
            struct(3, 1, D, dtype=F32),
            struct(2, SEQ, dtype=jnp.int32),
            struct(SEQ, D, dtype=F32),
            struct(SEQ, D),
            struct(SEQ, D),
            struct(SEQ, 2 * D + FF),
            struct(SEQ, FF),
            struct(SEQ, FF),
            struct(SEQ, 3 * D + 2 * FF),
            struct(PAIRS, SEQ, 2 * SEQ),
            struct(SEQ, D, dtype=F32),
            struct(SEQ, D, dtype=F32),
            struct(8, D, dtype=F32),
            struct(SEQ, D),
        ],
        16,
        "middle",
        [slow(gains), slow(keep), slow(h1), slow(query), slow(cot), after],
        [kv, w_in, w_cross, turned[2], turned[3], turned[4]],
        flops=2 * SEQ * 12 * 10**6,
        traffic=18 * 10**6,
    )


def outer_kernel(section, slot_plot, gains, keep, *refs):
    h2, g1, g2, rhs2 = [refs[2 * i : 2 * i + 2] for i in range(4)]
    dkv = refs[-13:-11]
    wdownt_v, wcrosst_v = refs[-11:-9]
    (rhs_v, dh2_v, gain_v, gains_v, keep_v, h2_v, g1_v, g2_v, sems) = refs[-9:]

    @pl.when(section[0] == 0)
    def _():
        copies = Copies(sems)
        get = [copies(keep, keep_v), copies(gains, gains_v)]
        for given, held in ((h2, h2_v), (g1, g1_v), (g2, g2_v)):
            get += [copies(given[i], held.at[pl.ds(i * SEQ, SEQ)]) for i in range(2)]
        start(get)
        upstream = halves(dkv[0][...], dkv[1][...])
        rhs_v[:, D + 2 * FF :] = upstream
        grad_memory = mm(upstream, wcrosst_v[...])
        wait(get[:4])
        rows = lax.broadcasted_iota(jnp.int32, (SEQ, D), 0)
        grad_memory = halves(
            *[
                jnp.where(
                    rows < jnp.broadcast_to(kept(keep_v, slot_plot[0, i]), (SEQ, D)),
                    grad_memory[i * SEQ : (i + 1) * SEQ],
                    0.0,
                )
                for i in range(2)
            ]
        )
        grad_second, grad_gain = rms_back(h2_v[...], gains_v[2], grad_memory)
        gain_v[...] = jnp.zeros_like(gain_v)
        gain_v[2:3, :] = grad_gain
        dh2_v[...] = grad_second
        branch = grad_second.astype(BF16)
        rhs_v[:, 0:D] = branch
        wait(get[4:])
        tile = 512
        for i in range(FF // tile):
            columns = slice(i * tile, (i + 1) * tile)
            grad_unit = mm(branch, wdownt_v[:, columns])
            rhs_v[:, D + i * tile : D + (i + 1) * tile] = (
                grad_unit * g1_v[:, columns].astype(F32)
            ).astype(BF16)
            rhs_v[:, D + FF + i * tile : D + FF + (i + 1) * tile] = (
                grad_unit * g2_v[:, columns].astype(F32)
            ).astype(BF16)

    @pl.when(section[0] != 0)
    def _():
        copies = Copies(sems)
        get = [copies(rhs2[i], rhs_v.at[pl.ds(i * SEQ, SEQ)]) for i in range(2)]
        start(get)
        wait(get)


def outer(section, slot_plot, gains, keep, dkv, h2, g1, g2, rhs2, turned, after):
    return call(
        outer_kernel,
        [section, slot_plot],
        [
            vmem(2 * SEQ, 3 * D + 2 * FF),
            vmem(2 * SEQ, D, dtype=F32),
            vmem(8, D, dtype=F32),
        ],
        [
            struct(3, 1, D, dtype=F32),
            struct(2, SEQ, dtype=jnp.int32),
            struct(2 * SEQ, D, dtype=F32),
            struct(2 * SEQ, FF),
            struct(2 * SEQ, FF),
        ],
        8,
        "outer",
        [slow(item) for item in (gains, keep, *h2, *g1, *g2, *rhs2)] + after,
        [*dkv, turned[3], turned[4]],
    )


def inner_kernel(section, slot_plot, table_len, gains, acts, *refs):
    h1, qkv, p, de2, gain2, pack1, pack2, e2 = [refs[2 * i : 2 * i + 2] for i in range(8)]
    rhs3_v, dh2_v, gain3_v, wqkvt_v, woutt_v, wint_v, wdownt_v, wcrosst_v = refs[16:24]
    (rhs_v, grad_o, out_o, gains_v, x_v, h1_v, qkv_v, p_v, up_v, gain_v, grad_v, dn_v, out_v, z_v, e2_v, sems) = refs[24:]
    encoding = section[0] == 0
    rows = slice(0, 2 * SEQ)
    plots = [slot_plot[0, i] for i in range(2)]
    copies = Copies(sems)

    def pair_of(given, held):
        return [copies(given[i], held.at[pl.ds(i * SEQ, SEQ)]) for i in range(2)]

    get = pair_of(h1, h1_v) + [copies(gains, gains_v)]
    get_rows = pair_of(qkv, qkv_v) + [copies(p[i], p_v.at[i]) for i in range(2)]
    get_x = pair_of([acts.at[0, plot] for plot in plots], x_v)
    get_out = pair_of([item.at[:, pl.ds(3 * D, D)] for item in pack1], out_v)
    get_dec = (
        pair_of(de2, up_v)
        + [copies(gain2[i], gain_v.at[i]) for i in range(2)]
        + pair_of([item.at[:, pl.ds(2 * D, FF)] for item in pack2], z_v)
        + pair_of(e2, e2_v)
    )
    start(get + get_rows + get_x)

    @pl.when(encoding)
    def _():
        start(get_out)
        dn_v[...] = mm(rhs3_v[:, D : D + 2 * FF], wint_v[...])
        up_v[...] = dh2_v[...]
        gain_v[0] = gain3_v[...]
        gain_v[1] = jnp.zeros((8, D), F32)
        wait(get_out)

    @pl.when(jnp.logical_not(encoding))
    def _():
        start(get_dec)
        dn_v[...] = mm(rhs3_v[:, D + 2 * FF : 2 * D + 2 * FF], wcrosst_v[0:D, :])
        wait(get_dec)
        third = e2_v[...] + mm_t(z_v[...], wdownt_v[...])
        index = lax.broadcasted_iota(jnp.int32, (SEQ, D), 0)
        for i in range(2):
            part = third[i * SEQ : (i + 1) * SEQ]
            out_v[i * SEQ : (i + 1) * SEQ, :] = jnp.where(
                index < table_len[plots[i]], part, 0.0
            ).astype(BF16)

    puts = [copies(out_v.at[pl.ds(i * SEQ, SEQ)], out_o.at[0, i]) for i in range(2)]
    start(puts)
    wait(get)
    back, first_gain = rms_back(h1_v[...], gains_v[1], dn_v[...])
    grad_first = up_v[...] + back
    branch = grad_first.astype(BF16)
    rhs_v[rows, 0:D] = branch
    masks = lane_masks()
    grad_mixed = mm(branch, woutt_v[...]).astype(BF16)
    wait(get_rows)
    for i in range(2):
        own = slice(i * SEQ, (i + 1) * SEQ)
        for pair in range(PAIRS):
            spans = [slice(k * D + pair * 128, k * D + (pair + 1) * 128) for k in range(3)]
            parts = attend_back(
                qkv_v[own, spans[0]],
                qkv_v[own, spans[1]],
                qkv_v[own, spans[2]],
                p_v[i, pair],
                grad_mixed[own, pair * 128 : (pair + 1) * 128],
                masks,
            )
            for k in range(3):
                rhs_v[own, D + k * D + pair * 128 : D + k * D + (pair + 1) * 128] = parts[k]
    grad_normal = mm(rhs_v[rows, D : 4 * D], wqkvt_v[...])
    wait(get_x)
    back, zeroth_gain = rms_back(x_v[...].astype(F32), gains_v[0], grad_normal)
    grad_v[...] = grad_first + back
    puts += [copies(grad_v.at[pl.ds(i * SEQ, SEQ)], grad_o.at[0, plots[i]]) for i in range(2)]
    start(puts[2:])
    second_gain = gain_v[0, 2:3, :] + gain_v[1, 2:3, :]
    total = jnp.concatenate([zeroth_gain, first_gain, second_gain, jnp.zeros((5, D), F32)], axis=0)
    upper = total.astype(BF16)
    lower = (total - upper.astype(F32)).astype(BF16)
    rhs_v[2 * SEQ :, 0:D] = halves(upper, lower)
    rhs_v[2 * SEQ :, D : 4 * D] = jnp.zeros((16, 3 * D), BF16)
    wait(puts)


def inner(section, slot_plot, table_len, gains, acts, saved, outer_made, turned):
    arrays = [slow(item) for item in (gains, acts, *sum(saved, []))]
    return call(
        inner_kernel,
        [section, slot_plot, table_len],
        [
            vmem(2 * SEQ + 16, 4 * D),
            struct(1, 2, SEQ, D, dtype=F32),
            struct(1, 2, SEQ, D),
        ],
        [
            struct(3, 1, D, dtype=F32),
            struct(2 * SEQ, D),
            struct(2 * SEQ, D, dtype=F32),
            struct(2 * SEQ, 3 * D),
            struct(2, PAIRS, SEQ, 2 * SEQ),
            struct(2 * SEQ, D, dtype=F32),
            struct(2, 8, D, dtype=F32),
            struct(2 * SEQ, D, dtype=F32),
            struct(2 * SEQ, D, dtype=F32),
            struct(2 * SEQ, D),
            struct(2 * SEQ, FF),
            struct(2 * SEQ, D, dtype=F32),
        ],
        28,
        "inner",
        arrays,
        [*outer_made, *turned],
    )


def place_parts(place):
    number = place[0]
    return (
        lax.shift_right_logical(number, 5),
        jnp.bitwise_and(lax.shift_right_logical(number, 3), 3),
        jnp.bitwise_and(lax.shift_right_logical(number, 1), 3),
        jnp.bitwise_and(number, 1),
    )


def matching(target, columns):
    rows = target.shape[0]
    lane = lax.broadcasted_iota(jnp.int32, (rows, 128), 1)
    blocks = [jnp.where(lane + i * 128 == target, 1.0, 0.0) for i in range(columns // 128)]
    return jnp.concatenate(blocks, axis=1).astype(BF16)


def selector(place, along, other=0):
    y, x, z, core = place_parts(place)
    core = jnp.bitwise_xor(core, other)
    index = lax.broadcasted_iota(jnp.int32, (384, 128), 0)

    def at_least(value, *bounds):
        return sum(jnp.where(value >= bound, 1, 0) for bound in bounds)

    first = at_least(index, 96, 192, 288)
    rest = index - first * 96
    second = at_least(rest, 24, 48, 72)
    rest = rest - second * 24
    third = at_least(rest, 12)
    rest = rest - third * 12
    to_x, to_z = (first, second) if along == "x" else (second, first)
    return matching(
        jnp.bitwise_and(y + third, 1) * 384
        + jnp.bitwise_and(x + to_x, 3) * 96
        + jnp.bitwise_and(z + to_z, 3) * 24
        + core * 12
        + rest,
        D,
    )


def stacked(sources, first, width, rows=SEQ):
    return jnp.concatenate([source[0:rows, first : first + width] for source in sources], axis=0)


def along_down(place, other):
    y, x, z, core = place_parts(place)
    core = jnp.bitwise_xor(core, other)
    index = lax.broadcasted_iota(jnp.int32, (256, 128), 0)
    return matching(
        jnp.bitwise_and(y + jnp.bitwise_and(lax.shift_right_logical(index, 5), 1), 1) * 256
        + jnp.bitwise_and(z + lax.shift_right_logical(index, 6), 3) * 64
        + core * 32
        + jnp.bitwise_and(index, 31),
        512,
    )


def prepare_down(place, sources, first, results, orders):
    y, x, z, core = place_parts(place)
    for chunk in range(4):
        block = first + jnp.bitwise_and(x + chunk, 3) * 256
        columns = [pl.ds(pl.multiple_of(block + half, 256), 256) for half in (0, 1024)]
        picked = jnp.concatenate(
            [jnp.concatenate([source[:, at] for source in sources], axis=0) for at in columns],
            axis=1,
        )
        at = 2688 + 256 * chunk
        for result, order in zip(results, orders):
            result[at : at + 256, :] = mm_t(order, picked).astype(BF16)


def prepare_kernel(which, section, place, *refs):
    packs = 2 + 2 * which
    given, weights = refs[:packs], refs[packs : packs + 2]
    results, turned = refs[-packs - 5 : -packs - 3], refs[-packs - 3 : -packs - 1]
    held, sems = refs[-packs - 1 : -1], refs[-1]

    @pl.when(section[0] == which)
    def _():
        copies = Copies(sems)
        get = [copies(source, target) for source, target in zip(given, held)]
        start(get)
        turn_all(weights, turned)
        pack1, pack2 = held[:2], held[2:]
        along_x = [selector(place, "x", other) for other in range(2)]
        along_z = [selector(place, "z", other) for other in range(2)]
        last = pack2 if which else pack1
        wait(get)
        steps = (
            (0, along_x, pack1, 0),
            (384, along_z, pack1, 0),
            (768, along_z, pack1, D),
            (1152, along_x, last, 0 if which else 2 * D),
            (1536, along_z, last, 0 if which else 2 * D),
            (1920, along_z, pack1, 2 * D if which else 3 * D),
            (2304, along_z, last, D if which else 3 * D),
        )
        for row, orders, sources, first in steps:
            for result, order in zip(results, orders):
                result[row : row + 384, :] = mm_t(order, stacked(sources, first, D)).astype(BF16)
        orders = [along_down(place, other) for other in range(2)]
        prepare_down(place, last, 2 * D if which else 4 * D, results, orders)


def prepare(which, section, place, packs, weights, before, after):
    arrays = after + [slow(pack) for pack in packs]
    turned = [vmem(*weight.shape[::-1]) for weight in weights]

    def kernel(section, place, *refs):
        prepare_kernel(which, section, place, *refs[len(after) :])

    return call(
        kernel,
        [section, place],
        [vmem(3712, 256)] * 2 + turned,
        [struct(*pack.shape) for pack in packs],
        4,
        "prepare",
        arrays,
        [*weights, *before],
        aliases={2 + len(arrays) + 2 + i: 2 + i for i in range(len(before))},
    )


class Buffers:
    def __init__(self, refs, size):
        self.own, self.ahead, self.behind, self.one, self.three = refs
        self.size = size

    def spot(self, chunk, block):
        quarter = self.size // 4
        half = self.size // 2
        row = block * quarter
        if chunk == 0:
            return self.own, row
        low = block < 2
        if chunk == 1:
            return (self.one, row) if low else (self.ahead, row)
        if chunk == 2:
            return (self.ahead, row) if low else (self.behind, row - half)
        return (self.behind, half + row) if low else (self.three, row - half)


def buffer_shapes(size):
    return [struct(size, 128)] * 3 + [struct(size // 2, 128)] * 2


def store_narrow(buffers, grad, offset):
    for chunk in range(4):
        for block in range(4):
            rows = grad[(chunk * 4 + block) * 24 : (chunk * 4 + block + 1) * 24]
            piece = jnp.concatenate([rows[:, 0:128], rows[:, 128:256]], axis=0).astype(BF16)
            target, row = buffers.spot(chunk, block)
            target[row + offset : row + offset + 48, :] = piece


SIZE_X, SIZE_Z = 4 * 1056, 4 * 1008


def both_sides(lefts, first, count):
    return jnp.concatenate([left[first : first + count, :] for left in lefts], axis=1)


def grads_kernel(place, lefts, wide, thin, results):
    held = Buffers(results[:5], SIZE_X), Buffers(results[5:], SIZE_Z)

    def right(sources, first, width=256):
        return stacked(sources, first, width, 2 * SEQ)

    total_of = selector(place, "z")
    total = sum(
        item[row : row + 8, 0:D].astype(F32) for item in thin for row in (2 * SEQ, 2 * SEQ + 8)
    )
    upper = total.astype(BF16)
    lower = (total - upper.astype(F32)).astype(BF16)
    ordered = mm_t(upper, total_of) + mm_t(lower, total_of)
    tall = jnp.concatenate([ordered, jnp.zeros((120, 384), F32)], axis=0).T
    tall = jnp.concatenate([tall, jnp.zeros((384, 128), F32)], axis=1)
    store_narrow(held[1], tall, 960)
    branch = right(wide, 0, D)
    for chunk in range(4):
        grad = mm(both_sides(lefts, 2688 + 256 * chunk, 256), branch)
        for block in range(4):
            target, row = held[0].spot(chunk, block)
            for i in range(6):
                spot = row + 384 + 64 * i
                target[spot : spot + 64, :] = grad[
                    64 * block : 64 * (block + 1), 128 * i : 128 * (i + 1)
                ].astype(BF16)
    for i in range(6):
        left = both_sides(lefts, 1920 if i < 3 else 2304, 384)
        store_narrow(held[1], mm(left, right(wide, D + 2 * FF + 256 * i)), 384 + 48 * i)
    for axis in range(2):
        left = both_sides(lefts, 1152 + 384 * axis, 384)
        for i in range(8):
            grad = mm(left, right(wide, D + axis * FF + 256 * i))
            store_narrow(held[axis], grad, 48 * i)
    for i in range(6):
        store_narrow(held[0], mm(both_sides(lefts, 0, 384), right(thin, D + 256 * i)), 768 + 48 * i)
    for i in range(6):
        left = both_sides(lefts, 384 if i < 3 else 768, 384)
        first = 3 * D + 256 * i if i < 3 else 256 * (i - 3)
        store_narrow(held[1], mm(left, right(thin, first)), 672 + 48 * i)


def grads(section, place, lefts, wide, thin):
    shapes = [vmem(*item.shape) for item in buffer_shapes(SIZE_X) + buffer_shapes(SIZE_Z)]

    def kernel(section, place, *refs):
        def run(lefts):
            grads_kernel(place, lefts, refs[4:6], refs[6:8], refs[8:18])

        @pl.when(section[0] == 0)
        def _():
            run(refs[0:2])

        @pl.when(section[0] != 0)
        def _():
            run(refs[2:4])

    return call(
        kernel, [section, place], shapes, [], 1, "grads", [], [*lefts, *wide, *thin],
    )


def flat(y, x, z, core):
    return ((y * 4 + x) * 4 + z) * 2 + core


def shifted(array, y=0, x=0, z=0, core=0):
    pairs = []
    for a in range(2):
        for b in range(4):
            for c in range(4):
                for d in range(2):
                    source = flat(a, b, c, d)
                    target = flat((a + y) % 2, (b + x) % 4, (c + z) % 4, (d + core) % 2)
                    pairs.append((source, target))
    return lax.ppermute(array, "dp", pairs)


def decoders_shifted(array):
    pairs = [(64 + i, 64 + (i ^ 1)) for i in range(64)]
    return lax.ppermute(array, ("section", "dp"), pairs)


def add(*terms):
    total = terms[0].astype(F32)
    for term in terms[1:]:
        total = total + term.astype(F32)
    return total


def along_two_rounds(buffers, axis):
    own, ahead, behind, one, three = buffers
    half = one.shape[0]
    got_ahead = shifted(ahead, **{axis: 1})
    got_behind = shifted(behind, **{axis: 3})
    last_ahead = shifted(add(one, got_ahead[:half]).astype(BF16), **{axis: 1})
    last_behind = shifted(add(three, got_behind[:half]).astype(BF16), **{axis: 3})
    low = add(own[:half], last_ahead, got_behind[half:])
    high = add(own[half:], got_ahead[half:], last_behind)
    return jnp.concatenate([low, high], axis=0).astype(BF16)


def along_one_round(total, axis):
    size = total.shape[0] // 4
    parts = [total[i * size : (i + 1) * size] for i in range(4)]
    return add(
        parts[0],
        shifted(parts[2], **{axis: 2}),
        shifted(parts[1], **{axis: 1}),
        shifted(parts[3], **{axis: 3}),
    )


def along_y(totals):
    sent = [total[:, 1].reshape(-1, 128).astype(BF16) for total in totals]
    got = shifted(jnp.concatenate(sent, axis=0), y=1)
    results = []
    first = 0
    for total, part in zip(totals, sent):
        size = part.shape[0]
        own = total[:, 0]
        results.append(own + got[first : first + size].reshape(own.shape).astype(F32))
        first += size
    return results


def rows_of(blocks):
    count, rows, lanes = blocks.shape
    return blocks.transpose(1, 0, 2).reshape(rows, count * lanes)


def local(
    acts,
    gains,
    qkv_weight,
    out_weight,
    mlp_in,
    mlp_out,
    cross_weight,
    patch_mask,
    table_len,
    slot_plot,
    cotangent,
):
    section = lax.axis_index("section").astype(jnp.int32).reshape(1)
    place = lax.axis_index("dp").astype(jnp.int32).reshape(1)
    gains = gains.transpose(1, 0, 2)
    weights = (qkv_weight, out_weight, mlp_in, mlp_out, cross_weight)
    made = []
    received = []
    for slot in range(2):
        made.append(forward(slot, section, place, slot_plot, gains, patch_mask, acts, weights))
        if slot == 0:
            weights = made[0][9:]
        received.append(lax.ppermute(made[slot][8], "section", [(0, 1)]))

    turned = [None, None, *turn(weights[2:], slow(made[1][1]))]
    middles = []
    back = []
    packs = [item[0] for item in made]
    after = patch_mask
    for slot in range(2):
        h1, query = made[slot][3:5]
        middles.append(
            middle(
                slot, section, slot_plot, table_len, gains, patch_mask,
                received[slot], h1, query, cotangent, weights, turned, after,
            )
        )
        back.append(lax.ppermute(middles[slot][2], "section", [(1, 0)]))
        if slot == 0:
            kept_left, given_left, *last = prepare(
                0, section, place, packs, weights[:2], [], [slow(made[1][2])]
            )
            lefts = [kept_left, shifted(given_left, core=1)]
            after = kept_left
    packs += [item[0] for item in middles]
    kept_left, given_left, *last = prepare(1, section, place, packs, weights[:2], last, [back[0]])
    lefts += [kept_left, decoders_shifted(given_left)]
    turned[:2] = last

    def saved(items, index):
        return [item[index] for item in items]

    outer_made = outer(
        section, slot_plot, gains, patch_mask, back, saved(made, 7), saved(made, 5), saved(made, 6),
        saved(middles, 1), turned, [kept_left],
    )
    rhs, grad_chain, out_chain = inner(
        section, slot_plot, table_len, gains, acts,
        [saved(made, 3), saved(made, 1), saved(made, 2), saved(middles, 4), saved(middles, 5),
         saved(made, 0), saved(middles, 0), saved(middles, 3)],
        outer_made, turned,
    )
    wide = outer_made[0]
    part = grads(
        section, place, lefts, [wide, shifted(wide, core=1)], [rhs, shifted(rhs, core=1)]
    )
    last_x = along_one_round(along_two_rounds(part[:5], "x"), "z")
    last_z = along_one_round(along_two_rounds(part[5:], "z"), "x")
    units_x, last_down, qkv_x, last_z = along_y(
        [
            last_x[:384].reshape(16, 2, 12, 128),
            last_x[384:768].reshape(6, 2, 32, 128),
            last_x[768:].reshape(12, 2, 12, 128),
            last_z.reshape(42, 2, 12, 128),
        ]
    )
    grad_mlp_in = rows_of(jnp.concatenate([units_x, last_z[:16]], axis=0))
    grad_cross = rows_of(last_z[16:28])
    grad_mlp_out = rows_of(last_down)
    grad_qkv = rows_of(jnp.concatenate([qkv_x, last_z[28:34]], axis=0))
    grad_out = rows_of(last_z[34:40])
    grad_gains = last_z[40][:, 0:3].T
    return (
        out_chain,
        grad_chain,
        grad_gains[None],
        grad_qkv[None],
        grad_out[None],
        grad_mlp_in[None],
        grad_mlp_out[None],
        grad_cross[None],
    )


def solution(mesh):
    return jax.shard_map(
        local,
        mesh=mesh,
        in_specs=(
            P("section", "dp", None, None),
            P("section", None, None),
            P("section", None, None),
            P("section", None, None),
            P("section", None, None),
            P("section", None, None),
            P("section", None, None),
            P("dp", None),
            P("dp"),
            P("dp", None),
            P("dp", None, None),
        ),
        out_specs=(
            P("section", "dp", None, None),
            P("section", "dp", None, None),
            P("section", None, "dp"),
            P("section", "dp", None),
            P("section", "dp", None),
            P("section", "dp", None),
            P("section", "dp", None),
            P("section", "dp", None),
        ),
        check_vma=False,
    )
```

```python
import functools

import jax
import jax.numpy as jnp
from jax import lax
from jax.experimental import pallas as pl
from jax.experimental.pallas import tpu as pltpu
from jax.sharding import PartitionSpec as P

D = 768
HDIM = 64
FF = 2048
SEQ = 128
PAIRS = 6
EPS = 1e-06
NEGATIVE = -1e30
ROOM_BYTES = 10 * 2**20
SCALE = HDIM ** (-0.5)
BF16 = jnp.bfloat16
F32 = jnp.float32
ANY = pl.BlockSpec(memory_space=pl.ANY)
FAST = pl.BlockSpec(memory_space=pltpu.VMEM)
SMEM = pl.BlockSpec(memory_space=pltpu.SMEM)


def mm(left, right):
    return jnp.dot(left, right, preferred_element_type=F32)


def mm_t(left, right):
    return lax.dot_general(left, right, (((1,), (1,)), ((), ())), preferred_element_type=F32)


def mm_w(left, right):
    return lax.dot_general(left, right, (((0,), (0,)), ((), ())), preferred_element_type=F32)


def halves(first, second):
    return jnp.concatenate([first, second], axis=0)


def rms(hidden, gain):
    inverse = lax.rsqrt(jnp.mean(hidden * hidden, axis=-1, keepdims=True) + EPS)
    return hidden * inverse * gain


def rms_back(hidden, gain, upstream):
    inverse = lax.rsqrt(jnp.mean(hidden * hidden, axis=-1, keepdims=True) + EPS)
    unit = hidden * inverse
    scaled = upstream * gain
    grad_gain = jnp.sum(upstream * unit, axis=0, keepdims=True)
    middle = jnp.mean(scaled * unit, axis=-1, keepdims=True)
    return inverse * (scaled - unit * middle), grad_gain


def gate_parts(gate, up):
    inner = 0.7978845608 * (gate + 0.044715 * gate * gate * gate)
    bend = jnp.tanh(inner)
    half = 0.5 * (1.0 + bend)
    value = gate * half
    slope = half + 0.5 * gate * (1.0 - bend * bend) * 0.7978845608 * (
        1.0 + 3.0 * 0.044715 * gate * gate
    )
    return value * up, slope * up, value


def lane_masks():
    lane = lax.broadcasted_iota(jnp.int32, (SEQ, 2 * HDIM), 1)
    low = jnp.where(lane < HDIM, 1.0, 0.0).astype(F32)
    return low.astype(BF16), (1.0 - low).astype(BF16), low


def stack_heads(pair, masks):
    return jnp.concatenate([pair * masks[0], pair * masks[1]], axis=0)


def attend(query, keys, values, allowed, masks):
    scores = mm_t(query, stack_heads(keys, masks)) * SCALE
    scores = jnp.where(allowed, scores, NEGATIVE)
    parts = []
    for head in range(2):
        part = scores[:, head * SEQ : (head + 1) * SEQ]
        power = jnp.exp(part - jnp.max(part, axis=-1, keepdims=True))
        parts.append(power * (1.0 / jnp.sum(power, axis=-1, keepdims=True)))
    weights = jnp.concatenate(parts, axis=1).astype(BF16)
    return weights, mm(weights, stack_heads(values, masks)).astype(BF16)


def attend_back(query, keys, values, weights, upstream, masks):
    key_stack = stack_heads(keys, masks)
    grad_weights = mm_t(upstream, stack_heads(values, masks))
    wide = weights.astype(F32)
    product = wide * grad_weights
    parts = []
    for head in range(2):
        columns = slice(head * SEQ, (head + 1) * SEQ)
        total = jnp.sum(product[:, columns], axis=-1, keepdims=True)
        parts.append(product[:, columns] - wide[:, columns] * total)
    grad_scores = jnp.concatenate(parts, axis=1).astype(BF16)
    grad_query = mm(grad_scores, key_stack) * SCALE
    key_both = mm_w(grad_scores, query) * SCALE
    value_both = mm_w(weights, upstream)
    low = masks[2]
    high = 1.0 - low
    grad_keys = key_both[:SEQ] * low + key_both[SEQ:] * high
    grad_values = value_both[:SEQ] * low + value_both[SEQ:] * high
    return grad_query.astype(BF16), grad_keys.astype(BF16), grad_values.astype(BF16)


def key_columns():
    return jnp.bitwise_and(lax.broadcasted_iota(jnp.int32, (SEQ, 2 * SEQ), 1), SEQ - 1)


def kept(keep_ref, plot):
    row = keep_ref[pl.ds(plot, 1), :].astype(F32)
    return jnp.sum(row, axis=1, keepdims=True).astype(jnp.int32)


SECTION, PLACE, PLOT, TOKENS, COUNT = 0, 1, 2, 4, 6


def number(info, row):
    return jnp.max(info[row : row + 1, :].astype(F32)).astype(jnp.int32)


def rows_below(info, row):
    index = lax.broadcasted_iota(jnp.int32, (SEQ, D), 0)
    return index < jnp.broadcast_to(info[row : row + 1, 0:1], (SEQ, D))


class Copies:
    def __init__(self, sems):
        self.sems = sems
        self.count = 0

    def __call__(self, source, target):
        copy = pltpu.make_async_copy(source, target, self.sems.at[self.count])
        self.count += 1
        return copy


def start(copies):
    for copy in copies:
        copy.start()


def wait(copies):
    for copy in copies:
        copy.wait()


def struct(*shape, dtype=BF16):
    return jax.ShapeDtypeStruct(shape, dtype)


def call(kernel, scalars, out_shape, scratch, sems, name, arrays, fast=(), aliases=None, flops=0, traffic=0):
    return pl.pallas_call(
        kernel,
        name=name,
        in_specs=[SMEM] * len(scalars) + [ANY] * len(arrays) + [FAST] * len(fast),
        out_specs=[FAST if is_fast(item) else ANY for item in out_shape],
        out_shape=out_shape,
        scratch_shapes=[
            pltpu.VMEM(item.shape, item.dtype) if isinstance(item, jax.ShapeDtypeStruct) else item
            for item in scratch
        ]
        + [pltpu.SemaphoreType.DMA((sems,))],
        input_output_aliases=aliases or {},
        compiler_params=pltpu.CompilerParams(vmem_limit_bytes=ROOM_BYTES),
        cost_estimate=pl.CostEstimate(flops=flops, bytes_accessed=traffic, transcendentals=0),
    )(*scalars, *arrays, *[pltpu.with_memory_space_constraint(item, pltpu.VMEM) for item in fast])


def is_fast(item):
    return not isinstance(item, jax.ShapeDtypeStruct) and item.memory_space == pltpu.VMEM


def vmem(*shape, dtype=BF16):
    return pltpu.VMEM(shape, dtype)


def hbm(*shape, dtype=BF16):
    return pltpu.HBM(shape, dtype)


def slow(array):
    return pltpu.with_memory_space_constraint(array, pltpu.HBM)


def forward_kernel(slot, *refs):
    if slot == 0:
        section, place, slot_plot, table_len, gains, keep, acts, *given = refs[:12]
        (pack_o, qkv_o, p_o, h1_v, query_v, g1_v, g2_v, h2_v, send_v, memory_v, info, gains_v, acts_v, wqkv_v, wout_v, win_v, wdown_v, wcross_v) = refs[12:30]
        (pack_v, qkv_v, p_v, keep_v, plot_s, tokens_s, sems) = refs[30:]
    else:
        cot, info, gains_v, acts_v, wqkv_v, wout_v, win_v, wdown_v, wcross_v = refs[:9]
        (pack_o, qkv_o, p_o, h1_v, query_v, g1_v, g2_v, h2_v, send_v, memory_v, cot_v) = refs[9:20]
        (pack_v, qkv_v, p_v, sems) = refs[20:]
    copies = Copies(sems)
    tile = 512
    get_qkv, get_in, get_out, get_down, get_cross, get_next = [], [], [], [], [], []
    if slot == 0:
        encoding = section[0] == 0
        get_small = [
            copies(slot_plot, plot_s),
            copies(table_len, tokens_s),
            copies(acts.at[0], acts_v),
            copies(gains, gains_v),
            copies(keep, keep_v),
        ]
        w_qkv, w_out, w_in, w_down, w_cross = given
        get_qkv = [
            copies(w_qkv.at[0, :, pl.ds(i * D, D)], wqkv_v.at[:, pl.ds(i * D, D)]) for i in range(3)
        ]
        get_out = [copies(w_out.at[0], wout_v)]
        for i in range(FF // tile):
            get_in += [
                copies(
                    w_in.at[0, :, pl.ds(base + i * tile, tile)],
                    win_v.at[:, pl.ds(base + i * tile, tile)],
                )
                for base in (0, FF)
            ]
        get_down = [copies(w_down.at[0], wdown_v)]
        get_cross = [copies(w_cross.at[0], wcross_v)]
        start(get_small + get_qkv + get_out + get_in + get_down + get_cross)
        wait(get_small)
        plots = [plot_s[0, i] for i in range(2)]
        numbers = [section[0], place[0], *plots, *[tokens_s[plot] for plot in plots]]
        for row, value in enumerate(numbers):
            info[row : row + 1, :] = jnp.broadcast_to(value, (1, 128)).astype(jnp.int32)
        for i in range(2):
            info[COUNT + i : COUNT + i + 1, :] = jnp.broadcast_to(kept(keep_v, plots[i]), (1, 128))
    else:
        encoding = number(info, SECTION) == 0
        plots = [None, number(info, PLOT + 1)]
        get_next = [copies(cot, cot_v)]
        start(get_next)
    masks = lane_masks()
    rows_in = acts_v[plots[slot]].astype(F32)
    normal = rms(rows_in, gains_v[0]).astype(BF16)
    pack_v[:, 0:D] = normal
    for i in range(3):
        wait(get_qkv[i : i + 1])
        qkv_v[:, i * D : (i + 1) * D] = mm(normal, wqkv_v[:, i * D : (i + 1) * D]).astype(BF16)
    puts = [copies(qkv_v, qkv_o)]
    puts[-1].start()
    row_index = lax.broadcasted_iota(jnp.int32, (SEQ, 2 * SEQ), 0)
    key_index = key_columns()
    count = info[COUNT + slot : COUNT + slot + 1, 0:1]
    limit = jnp.where(encoding, jnp.broadcast_to(count - 1, (SEQ, 2 * SEQ)), row_index)
    allowed = key_index <= limit
    for pair in range(PAIRS):
        lanes = slice(pair * 128, (pair + 1) * 128)
        weights, mixed = attend(
            qkv_v[:, lanes],
            qkv_v[:, D + pair * 128 : D + (pair + 1) * 128],
            qkv_v[:, 2 * D + pair * 128 : 2 * D + (pair + 1) * 128],
            allowed,
            masks,
        )
        p_v[pair] = weights
        pack_v[:, D + pair * 128 : D + (pair + 1) * 128] = mixed
    puts.append(copies(p_v, p_o))
    puts[-1].start()
    wait(get_out)
    first = rows_in + mm(pack_v[:, D : 2 * D], wout_v[...])
    h1_v[...] = first
    normal = rms(first, gains_v[1]).astype(BF16)
    pack_v[:, 2 * D : 3 * D] = normal
    put_units = copies(pack_v.at[:, pl.ds(3 * D, FF)], pack_o.at[:, pl.ds(3 * D, FF)])
    puts.append(copies(pack_v.at[:, pl.ds(0, 3 * D)], pack_o.at[:, pl.ds(0, 3 * D)]))
    puts[-1].start()

    @pl.when(encoding)
    def _():
        inputs = pack_v[:, 2 * D : 3 * D]
        for i in range(FF // tile):
            wait(get_in[2 * i : 2 * i + 2])
            columns = slice(i * tile, (i + 1) * tile)
            gate = mm(inputs, win_v[:, columns])
            up = mm(inputs, win_v[:, FF + i * tile : FF + (i + 1) * tile])
            unit, to_gate, to_up = gate_parts(gate, up)
            pack_v[:, 3 * D + i * tile : 3 * D + (i + 1) * tile] = unit.astype(BF16)
            g1_v[:, columns] = to_gate.astype(BF16)
            g2_v[:, columns] = to_up.astype(BF16)
        put_units.start()
        wait(get_down)
        second = h1_v[...] + mm(pack_v[:, 3 * D :], wdown_v[...])
        h2_v[...] = second
        memory = rms(second, gains_v[2])
        memory = jnp.where(rows_below(info, COUNT + slot), memory, 0.0).astype(BF16)
        memory_v[...] = memory
        wait(get_cross)
        send_v[...] = mm(memory, wcross_v[...]).astype(BF16)
        put_units.wait()

    @pl.when(jnp.logical_not(encoding))
    def _():
        wait(get_cross)
        query_v[...] = mm(pack_v[:, 2 * D : 3 * D], wcross_v[:, 0:D]).astype(BF16)
        wait(get_in + get_down)

    wait(puts + get_next)


def forward(slot, scalars, arrays, fast):
    outs = [
        hbm(SEQ, 3 * D + FF),
        hbm(SEQ, 3 * D),
        hbm(PAIRS, SEQ, 2 * SEQ),
        vmem(SEQ, D, dtype=F32),
        vmem(SEQ, D),
        vmem(SEQ, FF),
        vmem(SEQ, FF),
        vmem(SEQ, D, dtype=F32),
        vmem(SEQ, 2 * D),
        vmem(SEQ, D),
    ]
    scratch = [struct(SEQ, 3 * D + FF), struct(SEQ, 3 * D), struct(PAIRS, SEQ, 2 * SEQ)]
    if slot == 0:
        outs += [vmem(8, 128, dtype=jnp.int32), vmem(3, 1, D, dtype=F32), vmem(2, SEQ, D)]
        outs += [vmem(*weight.shape[1:]) for weight in arrays[5:]]
        scratch += [struct(2, SEQ, dtype=jnp.int32)]
        scratch += [pltpu.SMEM((1, 2), jnp.int32), pltpu.SMEM((2,), jnp.int32)]
    else:
        outs += [vmem(2, SEQ, D)]
    return call(
        functools.partial(forward_kernel, slot), scalars, outs, scratch, 34, "forward",
        [slow(item) for item in arrays], fast,
    )


def turn_all(sources, results):
    for source, result in zip(sources, results):

        def step(i, carry):
            at = pl.ds(pl.multiple_of(i * 256, 256), 256)
            result[at, :] = source[:, at].T
            return carry

        lax.fori_loop(0, source.shape[1] // 256, step, 0)


def turn_kernel(count, *refs):
    turn_all(refs[1 : count + 1], refs[count + 1 : 2 * count + 1])


def turn(weights, after):
    return call(
        functools.partial(turn_kernel, len(weights)), [],
        [vmem(*weight.shape[::-1]) for weight in weights], [], 1, "turn", [after], weights,
    )


def middle_kernel(slot, info, units, gains_v, kv_v, h1_v, query_v, cot_v, win_v, wcross_v, wint_v, wcrosst_v, pack_o, rhs_o, late_v, dkv_v, e2_o, de2_o, gain_o, pack_v, g1_v, g2_v, rhs_v, p_v, e2_v, de2_v, gain_v, mixed_v, sems):
    @pl.when(number(info, SECTION) != 0)
    def _():
        copies = Copies(sems)
        tile = 512
        masks = lane_masks()
        count = info[COUNT + slot : COUNT + slot + 1, 0:1]
        allowed = key_columns() < jnp.broadcast_to(count, (SEQ, 2 * SEQ))
        for pair in range(PAIRS):
            lanes = slice(pair * 128, (pair + 1) * 128)
            weights, mixed = attend(
                query_v[:, lanes],
                kv_v[:, lanes],
                kv_v[:, D + pair * 128 : D + (pair + 1) * 128],
                allowed,
                masks,
            )
            p_v[pair] = weights
            pack_v[:, D + pair * 128 : D + (pair + 1) * 128] = mixed
        second = h1_v[...] + mm(pack_v[:, D : 2 * D], wcross_v[:, D : 2 * D])
        e2_v[...] = second
        puts = [copies(e2_v, e2_o)]
        puts[-1].start()
        normal = rms(second, gains_v[2]).astype(BF16)
        pack_v[:, 0:D] = normal
        for i in range(FF // tile):
            columns = slice(i * tile, (i + 1) * tile)
            gate = mm(normal, win_v[:, columns])
            up = mm(normal, win_v[:, FF + i * tile : FF + (i + 1) * tile])
            unit, to_gate, to_up = gate_parts(gate, up)
            pack_v[:, 2 * D + i * tile : 2 * D + (i + 1) * tile] = unit.astype(BF16)
            g1_v[:, columns] = to_gate.astype(BF16)
            g2_v[:, columns] = to_up.astype(BF16)
        puts.append(copies(pack_v, pack_o))
        puts[-1].start()
        upstream = jnp.where(rows_below(info, TOKENS + slot), cot_v[slot].astype(F32), 0.0)
        branch = upstream.astype(BF16)
        rhs_v[:, 0:D] = branch
        for i in range(FF // tile):
            columns = slice(i * tile, (i + 1) * tile)
            grad_unit = units[slot * SEQ : (slot + 1) * SEQ, columns]
            rhs_v[:, D + i * tile : D + (i + 1) * tile] = (
                grad_unit * g1_v[:, columns].astype(F32)
            ).astype(BF16)
            rhs_v[:, D + FF + i * tile : D + FF + (i + 1) * tile] = (
                grad_unit * g2_v[:, columns].astype(F32)
            ).astype(BF16)
        puts.append(copies(rhs_v, rhs_o))
        puts[-1].start()
        grad_normal = mm(rhs_v[:, D : D + 2 * FF], wint_v[...])
        back, grad_gain = rms_back(second, gains_v[2], grad_normal)
        grad_second = upstream + back
        gain_v[...] = jnp.zeros_like(gain_v)
        gain_v[2:3, :] = grad_gain
        de2_v[...] = grad_second
        puts += [copies(de2_v, de2_o), copies(gain_v, gain_o)]
        start(puts[-2:])
        branch = grad_second.astype(BF16)
        late_v[:, D : 2 * D] = branch
        mixed_v[...] = mm(branch, wcrosst_v[D : 2 * D, :]).astype(BF16)
        for pair in range(PAIRS):
            lanes = slice(pair * 128, (pair + 1) * 128)
            high = slice(D + pair * 128, D + (pair + 1) * 128)
            grad_query, grad_keys, grad_values = attend_back(
                query_v[:, lanes], kv_v[:, lanes], kv_v[:, high], p_v[pair], mixed_v[:, lanes], masks
            )
            late_v[:, lanes] = grad_query
            dkv_v[:, lanes] = grad_keys
            dkv_v[:, high] = grad_values
        wait(puts)


def middle(slot, fast):
    return call(
        functools.partial(middle_kernel, slot),
        [],
        [
            hbm(SEQ, 2 * D + FF),
            hbm(SEQ, D + 2 * FF),
            vmem(SEQ, 2 * D),
            vmem(SEQ, 2 * D),
            hbm(SEQ, D, dtype=F32),
            hbm(SEQ, D, dtype=F32),
            hbm(8, D, dtype=F32),
        ],
        [
            struct(SEQ, 2 * D + FF),
            struct(SEQ, FF),
            struct(SEQ, FF),
            struct(SEQ, D + 2 * FF),
            struct(PAIRS, SEQ, 2 * SEQ),
            struct(SEQ, D, dtype=F32),
            struct(SEQ, D, dtype=F32),
            struct(8, D, dtype=F32),
            struct(SEQ, D),
        ],
        8,
        "middle",
        [],
        fast,
    )


def outer_kernel(*refs):
    rhs2 = refs[0:2]
    info, gains_v = refs[3:5]
    dkv, h2, g1, g2, late = [refs[5 + 2 * i : 7 + 2 * i] for i in range(5)]
    wdownt_v, wcrosst_v, rhs_v, dh2_v, gain_v, sems = refs[15:]
    encoding = number(info, SECTION) == 0

    @pl.when(encoding)
    def _():
        upstream = halves(dkv[0][...], dkv[1][...])
        rhs_v[:, D + 2 * FF :] = upstream
        grad_memory = mm(upstream, wcrosst_v[...])
        grad_memory = halves(
            *[
                jnp.where(
                    rows_below(info, COUNT + i), grad_memory[i * SEQ : (i + 1) * SEQ], 0.0
                )
                for i in range(2)
            ]
        )
        grad_second, grad_gain = rms_back(
            halves(h2[0][...], h2[1][...]), gains_v[2], grad_memory
        )
        gain_v[...] = jnp.zeros_like(gain_v)
        gain_v[2:3, :] = grad_gain
        dh2_v[...] = grad_second
        branch = grad_second.astype(BF16)
        rhs_v[:, 0:D] = branch
        tile = 512
        for i in range(FF // tile):
            columns = slice(i * tile, (i + 1) * tile)
            grad_unit = mm(branch, wdownt_v[:, columns])
            for k, to in ((0, g1), (1, g2)):
                scale = halves(to[0][:, columns], to[1][:, columns]).astype(F32)
                first = D + k * FF + i * tile
                rhs_v[:, first : first + tile] = (grad_unit * scale).astype(BF16)

    @pl.when(jnp.logical_not(encoding))
    def _():
        copies = Copies(sems)
        get = [
            copies(rhs2[i], rhs_v.at[pl.ds(i * SEQ, SEQ), pl.ds(0, D + 2 * FF)]) for i in range(2)
        ]
        start(get)
        rhs_v[:, D + 2 * FF :] = halves(late[0][...], late[1][...])
        wait(get)


def outer(rhs2, after, fast):
    return call(
        outer_kernel,
        [],
        [
            vmem(2 * SEQ, 3 * D + 2 * FF),
            vmem(2 * SEQ, D, dtype=F32),
            vmem(8, D, dtype=F32),
        ],
        [],
        2,
        "outer",
        [slow(item) for item in rhs2] + after,
        fast,
    )


def inner_kernel(*refs):
    qkv, p, de2, gain2, pack2, e2 = [refs[2 * i : 2 * i + 2] for i in range(6)]
    info, gains_v, acts_v = refs[12:15]
    memory, h1 = refs[15:17], refs[17:19]
    rhs3_v, dh2_v, gain3_v, wqkvt_v, woutt_v, wint_v, wdownt_v, wcrosst_v = refs[19:27]
    (rhs_v, grad_v, out_v, qkv_v, p_v, up_v, gain_v, dn_v, z_v, e2_v, sems) = refs[27:]
    encoding = number(info, SECTION) == 0
    rows = slice(0, 2 * SEQ)
    plots = [number(info, PLOT + i) for i in range(2)]
    copies = Copies(sems)

    def pair_of(given, held):
        return [copies(given[i], held.at[pl.ds(i * SEQ, SEQ)]) for i in range(2)]

    get_rows = pair_of(qkv, qkv_v) + [copies(p[i], p_v.at[i]) for i in range(2)]
    get_dec = (
        pair_of(de2, up_v)
        + [copies(gain2[i], gain_v.at[i]) for i in range(2)]
        + pair_of([item.at[:, pl.ds(2 * D, FF)] for item in pack2], z_v)
        + pair_of(e2, e2_v)
    )
    start(get_rows)

    @pl.when(encoding)
    def _():
        dn_v[...] = mm(rhs3_v[:, D : D + 2 * FF], wint_v[...])
        up_v[...] = dh2_v[...]
        gain_v[0] = gain3_v[...]
        gain_v[1] = jnp.zeros((8, D), F32)
        for i in range(2):
            out_v[0, i] = memory[i][...]

    @pl.when(jnp.logical_not(encoding))
    def _():
        start(get_dec)
        dn_v[...] = mm(rhs3_v[:, D + 2 * FF : 2 * D + 2 * FF], wcrosst_v[0:D, :])
        wait(get_dec)
        third = e2_v[...] + mm_t(z_v[...], wdownt_v[...])
        for i in range(2):
            part = third[i * SEQ : (i + 1) * SEQ]
            part = jnp.where(rows_below(info, TOKENS + i), part, 0.0)
            out_v[0, i] = part.astype(BF16)

    back, first_gain = rms_back(halves(h1[0][...], h1[1][...]), gains_v[1], dn_v[...])
    grad_first = up_v[...] + back
    branch = grad_first.astype(BF16)
    rhs_v[rows, 0:D] = branch
    masks = lane_masks()
    grad_mixed = mm(branch, woutt_v[...]).astype(BF16)
    wait(get_rows)
    for i in range(2):
        own = slice(i * SEQ, (i + 1) * SEQ)
        for pair in range(PAIRS):
            spans = [slice(k * D + pair * 128, k * D + (pair + 1) * 128) for k in range(3)]
            parts = attend_back(
                qkv_v[own, spans[0]],
                qkv_v[own, spans[1]],
                qkv_v[own, spans[2]],
                p_v[i, pair],
                grad_mixed[own, pair * 128 : (pair + 1) * 128],
                masks,
            )
            for k in range(3):
                rhs_v[own, D + k * D + pair * 128 : D + k * D + (pair + 1) * 128] = parts[k]
    grad_normal = mm(rhs_v[rows, D : 4 * D], wqkvt_v[...])
    rows_in = halves(acts_v[plots[0]], acts_v[plots[1]]).astype(F32)
    back, zeroth_gain = rms_back(rows_in, gains_v[0], grad_normal)
    grad_rows = grad_first + back
    for i in range(2):
        grad_v[0, plots[i]] = grad_rows[i * SEQ : (i + 1) * SEQ]
    second_gain = gain_v[0, 2:3, :] + gain_v[1, 2:3, :]
    total = jnp.concatenate([zeroth_gain, first_gain, second_gain, jnp.zeros((5, D), F32)], axis=0)
    upper = total.astype(BF16)
    lower = (total - upper.astype(F32)).astype(BF16)
    rhs_v[2 * SEQ :, 0:D] = halves(upper, lower)
    rhs_v[2 * SEQ :, D : 4 * D] = jnp.zeros((16, 3 * D), BF16)


def inner(saved, fast):
    return call(
        inner_kernel,
        [],
        [
            vmem(2 * SEQ + 16, 4 * D),
            vmem(1, 2, SEQ, D, dtype=F32),
            vmem(1, 2, SEQ, D),
        ],
        [
            struct(2 * SEQ, 3 * D),
            struct(2, PAIRS, SEQ, 2 * SEQ),
            struct(2 * SEQ, D, dtype=F32),
            struct(2, 8, D, dtype=F32),
            struct(2 * SEQ, D, dtype=F32),
            struct(2 * SEQ, FF),
            struct(2 * SEQ, D, dtype=F32),
        ],
        24,
        "inner",
        [slow(item) for item in sum(saved, [])],
        fast,
    )


def place_parts(place):
    return (
        lax.shift_right_logical(place, 5),
        jnp.bitwise_and(lax.shift_right_logical(place, 3), 3),
        jnp.bitwise_and(lax.shift_right_logical(place, 1), 3),
        jnp.bitwise_and(place, 1),
    )


def matching(target, columns):
    rows = target.shape[0]
    lane = lax.broadcasted_iota(jnp.int32, (rows, 128), 1)
    blocks = [jnp.where(lane + i * 128 == target, 1.0, 0.0) for i in range(columns // 128)]
    return jnp.concatenate(blocks, axis=1).astype(BF16)


def selector(place, along, other=0):
    y, x, z, core = place_parts(place)
    core = jnp.bitwise_xor(core, other)
    index = lax.broadcasted_iota(jnp.int32, (384, 128), 0)

    def at_least(value, *bounds):
        return sum(jnp.where(value >= bound, 1, 0) for bound in bounds)

    first = at_least(index, 96, 192, 288)
    rest = index - first * 96
    second = at_least(rest, 24, 48, 72)
    rest = rest - second * 24
    third = at_least(rest, 12)
    rest = rest - third * 12
    to_x, to_z = (first, second) if along == "x" else (second, first)
    return matching(
        jnp.bitwise_and(y + third, 1) * 384
        + jnp.bitwise_and(x + to_x, 3) * 96
        + jnp.bitwise_and(z + to_z, 3) * 24
        + core * 12
        + rest,
        D,
    )


def stacked(sources, first, width, rows=SEQ):
    return jnp.concatenate([source[0:rows, first : first + width] for source in sources], axis=0)


def along_down(place, other):
    y, x, z, core = place_parts(place)
    core = jnp.bitwise_xor(core, other)
    index = lax.broadcasted_iota(jnp.int32, (256, 128), 0)
    return matching(
        jnp.bitwise_and(y + jnp.bitwise_and(lax.shift_right_logical(index, 5), 1), 1) * 256
        + jnp.bitwise_and(z + lax.shift_right_logical(index, 6), 3) * 64
        + core * 32
        + jnp.bitwise_and(index, 31),
        512,
    )


def prepare_down(place, sources, first, results, orders):
    y, x, z, core = place_parts(place)
    for chunk in range(4):
        block = first + jnp.bitwise_and(x + chunk, 3) * 256
        columns = [pl.ds(pl.multiple_of(block + half, 256), 256) for half in (0, 1024)]
        picked = jnp.concatenate(
            [jnp.concatenate([source[:, at] for source in sources], axis=0) for at in columns],
            axis=1,
        )
        at = 2688 + 256 * chunk
        for result, order in zip(results, orders):
            result[at : at + 256, :] = mm_t(order, picked).astype(BF16)


def prepare_kernel(which, *refs):
    packs = 2 + 2 * which
    given, info, weights = refs[:packs], refs[packs], refs[packs + 1 : packs + 3]
    memory, cot, wdownt = refs[packs + 3 : packs + 5], refs[packs + 5], refs[packs + 6]
    outs = refs[-packs - 6 + which : -packs - 1]
    results, turned, units = outs[0:2], outs[2:4], outs[-1]
    held, sems = refs[-packs - 1 : -1], refs[-1]

    place = number(info, PLACE)

    if which == 0:

        @pl.when(number(info, SECTION) == 1)
        def _():
            branch = halves(
                *[
                    jnp.where(rows_below(info, TOKENS + i), cot[i].astype(F32), 0.0).astype(BF16)
                    for i in range(2)
                ]
            )
            units[...] = mm(branch, wdownt[...])

    @pl.when(number(info, SECTION) == which)
    def _():
        copies = Copies(sems)
        get = [copies(source, target) for source, target in zip(given, held)]
        start(get)
        turn_all(weights, turned)
        pack1, pack2 = held[:2], held[2:]
        along_x = [selector(place, "x", other) for other in range(2)]
        along_z = [selector(place, "z", other) for other in range(2)]
        last = pack2 if which else pack1
        wait(get)
        first = pack1 if which else memory
        second = last if which else memory
        steps = (
            (0, along_x, pack1, 0),
            (384, along_z, pack1, 0),
            (768, along_z, pack1, D),
            (1152, along_x, last, 0 if which else 2 * D),
            (1536, along_z, last, 0 if which else 2 * D),
            (1920, along_z, first, 2 * D if which else 0),
            (2304, along_z, second, D if which else 0),
        )
        for row, orders, sources, first in steps:
            for result, order in zip(results, orders):
                result[row : row + 384, :] = mm_t(order, stacked(sources, first, D)).astype(BF16)
        orders = [along_down(place, other) for other in range(2)]
        prepare_down(place, last, 2 * D if which else 3 * D, results, orders)


def prepare(which, info, packs, weights, memory, cot, wdownt, before, after):
    arrays = after + [slow(pack) for pack in packs]
    turned = [vmem(*weight.shape[::-1]) for weight in weights]

    def kernel(*refs):
        prepare_kernel(which, *refs[len(after) :])

    return call(
        kernel,
        [],
        [vmem(3712, 256)] * 2 + turned + [vmem(2 * SEQ, FF, dtype=F32)] * (1 - which),
        [struct(*pack.shape) for pack in packs],
        4,
        "prepare",
        arrays,
        [info, *weights, *memory, cot, wdownt, *before],
        aliases={len(arrays) + 7 + i: 2 + i for i in range(len(before))},
    )


class Buffers:
    def __init__(self, refs, size):
        self.own, self.ahead, self.behind, self.one, self.three = refs
        self.size = size

    def spot(self, chunk, block):
        quarter = self.size // 4
        half = self.size // 2
        row = block * quarter
        if chunk == 0:
            return self.own, row
        low = block < 2
        if chunk == 1:
            return (self.one, row) if low else (self.ahead, row)
        if chunk == 2:
            return (self.ahead, row) if low else (self.behind, row - half)
        return (self.behind, half + row) if low else (self.three, row - half)


def buffer_shapes(size):
    return [struct(size, 128)] * 3 + [struct(size // 2, 128)] * 2


def store_narrow(buffers, grad, offset):
    for chunk in range(4):
        for block in range(4):
            rows = grad[(chunk * 4 + block) * 24 : (chunk * 4 + block + 1) * 24]
            piece = jnp.concatenate([rows[:, 0:128], rows[:, 128:256]], axis=0).astype(BF16)
            target, row = buffers.spot(chunk, block)
            target[row + offset : row + offset + 48, :] = piece


QKV_X = 5
SIZE_X, SIZE_Z = 4 * (768 + 48 * QKV_X), 4 * (1296 - 48 * QKV_X)
OUT_ROW = 672 + 48 * (9 - QKV_X)


def both_sides(lefts, first, count):
    return jnp.concatenate([left[first : first + count, :] for left in lefts], axis=1)


def right_of(sources, first, width=256):
    return stacked(sources, first, width, 2 * SEQ)


def grads_wide_kernel(lefts, wide, results):
    held = Buffers(results[:5], SIZE_X), Buffers(results[5:], SIZE_Z)
    branch = right_of(wide, 0, D)
    for chunk in range(4):
        grad = mm(both_sides(lefts, 2688 + 256 * chunk, 256), branch)
        for block in range(4):
            target, row = held[0].spot(chunk, block)
            for i in range(6):
                spot = row + 384 + 64 * i
                target[spot : spot + 64, :] = grad[
                    64 * block : 64 * (block + 1), 128 * i : 128 * (i + 1)
                ].astype(BF16)
    for i in range(6):
        left = both_sides(lefts, 1920 if i < 3 else 2304, 384)
        store_narrow(held[1], mm(left, right_of(wide, D + 2 * FF + 256 * i)), 384 + 48 * i)
    for axis in range(2):
        left = both_sides(lefts, 1152 + 384 * axis, 384)
        for i in range(8):
            grad = mm(left, right_of(wide, D + axis * FF + 256 * i))
            store_narrow(held[axis], grad, 48 * i)


def grads_thin_kernel(place, lefts, thin, results):
    held = Buffers(results[:5], SIZE_X), Buffers(results[5:], SIZE_Z)
    total_of = selector(place, "z")
    total = sum(
        item[row : row + 8, 0:D].astype(F32) for item in thin for row in (2 * SEQ, 2 * SEQ + 8)
    )
    upper = total.astype(BF16)
    lower = (total - upper.astype(F32)).astype(BF16)
    ordered = mm_t(upper, total_of) + mm_t(lower, total_of)
    tall = jnp.concatenate([ordered, jnp.zeros((120, 384), F32)], axis=0).T
    tall = jnp.concatenate([tall, jnp.zeros((384, 128), F32)], axis=1)
    store_narrow(held[1], tall, OUT_ROW + 144)
    for i in range(9):
        axis = 0 if i < QKV_X else 1
        grad = mm(both_sides(lefts, 384 * axis, 384), right_of(thin, D + 256 * i))
        store_narrow(held[axis], grad, 672 + 48 * (i - QKV_X) if axis else 768 + 48 * i)
    for i in range(3):
        grad = mm(both_sides(lefts, 768, 384), right_of(thin, 256 * i))
        store_narrow(held[1], grad, OUT_ROW + 48 * i)


def grads(thin, info, lefts, right, before):
    shapes = [vmem(*item.shape) for item in buffer_shapes(SIZE_X) + buffer_shapes(SIZE_Z)]

    def kernel(info, *refs):
        encoding = number(info, SECTION) == 0
        results = refs[-11:-1]

        def run(lefts):
            if thin:
                grads_thin_kernel(number(info, PLACE), lefts, refs[4:6], results)
            else:
                grads_wide_kernel(lefts, refs[4:6], results)

        @pl.when(encoding)
        def _():
            run(refs[0:2])

        @pl.when(jnp.logical_not(encoding))
        def _():
            run(refs[2:4])

    return call(
        kernel, [], shapes, [], 1, "grads", [], [info, *lefts, *right, *before],
        aliases={7 + i: i for i in range(len(before))},
    )


def finish_kernel(own_x, own_z, got, qkv_o, out_o, in_o, cross_o, down_o, gains_o, got_v):
    got_v[...] = got[...].astype(F32)

    def lay(result, column, own, row, got_row, count):
        for at in range(12):
            kept_rows = own[pl.ds(row + at, count, stride=24), :]
            line = kept_rows + got_v[pl.ds(got_row + at, count, stride=12), :]
            for tile in range(count):
                first = column + 128 * tile
                result[at, :, first : first + 128] = line[tile : tile + 1, :]

    lay(in_o, 0, own_x, 0, 0, 16)
    for tile in range(6):
        columns = slice(128 * tile, 128 * (tile + 1))
        down_o[:, columns] = (
            own_x[384 + 64 * tile : 416 + 64 * tile, :] + got_v[192 + 32 * tile : 224 + 32 * tile, :]
        )
    lay(qkv_o, 0, own_x, 768, 384, 2 * QKV_X)
    base = SIZE_X // 8
    lay(in_o, FF, own_z, 0, base, 16)
    lay(cross_o, 0, own_z, 384, base + 192, 12)
    lay(qkv_o, 256 * QKV_X, own_z, 672, base + 336, 18 - 2 * QKV_X)
    lay(out_o, 0, own_z, OUT_ROW, base + OUT_ROW // 2, 6)
    row = OUT_ROW + 144
    tall = own_z[row : row + 16, :] + got_v[base + row // 2 : base + row // 2 + 16, :]
    tall = jnp.concatenate([tall, jnp.zeros((112, 128), F32)], axis=0).T
    for i in range(3):
        gains_o[i] = tall[i : i + 1, 0:12]


def finish(own_x, own_z, got):
    shapes = [
        struct(12, 1, 3 * D, dtype=F32),
        struct(12, 1, D, dtype=F32),
        struct(12, 1, 2 * FF, dtype=F32),
        struct(12, 1, 2 * D, dtype=F32),
        struct(32, D, dtype=F32),
        struct(3, 1, 12, dtype=F32),
    ]
    return pl.pallas_call(
        finish_kernel,
        name="finish",
        in_specs=[FAST] * 3,
        out_specs=[FAST] * 6,
        out_shape=shapes,
        scratch_shapes=[pltpu.VMEM(got.shape, F32)],
        compiler_params=pltpu.CompilerParams(vmem_limit_bytes=ROOM_BYTES),
    )(own_x, own_z, got)


def flat(y, x, z, core):
    return ((y * 4 + x) * 4 + z) * 2 + core


def shifted(array, y=0, x=0, z=0, core=0):
    pairs = []
    for a in range(2):
        for b in range(4):
            for c in range(4):
                for d in range(2):
                    source = flat(a, b, c, d)
                    target = flat((a + y) % 2, (b + x) % 4, (c + z) % 4, (d + core) % 2)
                    pairs.append((source, target))
    return lax.ppermute(array, "dp", pairs)


def swapped_in(section, array):
    pairs = [(64 * section + i, 64 * section + (i ^ 1)) for i in range(64)]
    return lax.ppermute(array, ("section", "dp"), pairs)


def add(*terms):
    total = terms[0].astype(F32)
    for term in terms[1:]:
        total = total + term.astype(F32)
    return total


def along_two_rounds(buffers, axis):
    own, ahead, behind, one, three = buffers
    half = one.shape[0]
    got_ahead = shifted(ahead, **{axis: 1})
    got_behind = shifted(behind, **{axis: 3})
    last_ahead = shifted(add(one, got_ahead[:half]).astype(BF16), **{axis: 1})
    last_behind = shifted(add(three, got_behind[:half]).astype(BF16), **{axis: 3})
    low = add(own[:half], last_ahead, got_behind[half:])
    high = add(own[half:], got_ahead[half:], last_behind)
    return jnp.concatenate([low, high], axis=0).astype(BF16)


def along_one_round(total, axis):
    size = total.shape[0] // 4
    parts = [total[i * size : (i + 1) * size] for i in range(4)]
    return add(
        parts[0],
        shifted(parts[2], **{axis: 2}),
        shifted(parts[1], **{axis: 1}),
        shifted(parts[3], **{axis: 3}),
    )


def for_y(total, tile_rows):
    return total.reshape(-1, 2, tile_rows, 128)[:, 1].reshape(-1, 128).astype(BF16)


def local(
    acts,
    gains,
    qkv_weight,
    out_weight,
    mlp_in,
    mlp_out,
    cross_weight,
    patch_mask,
    table_len,
    slot_plot,
    cotangent,
):
    section = lax.axis_index("section").astype(jnp.int32).reshape(1)
    place = lax.axis_index("dp").astype(jnp.int32).reshape(1)
    gains = gains.transpose(1, 0, 2)
    weights = (qkv_weight, out_weight, mlp_in, mlp_out, cross_weight)
    made = [
        forward(0, [section, place], [slot_plot, table_len, gains, patch_mask, acts, *weights], [])
    ]
    info, gains, acts, *weights = made[0][10:]
    received = [lax.ppermute(made[0][8], "section", [(0, 1)])]
    made.append(forward(1, [], [cotangent], [info, gains, acts, *weights]))
    received.append(lax.ppermute(made[1][8], "section", [(0, 1)]))
    cot = made[1][10]
    turned = turn(weights[2:], slow(made[1][1]))
    middles = []
    back = []
    packs = [item[0] for item in made]
    memory = [item[9] for item in made]
    kept_left, given_left, *last, units = prepare(
        0, info, packs, weights[:2], memory, cot, turned[1], [], [slow(made[1][2])]
    )
    lefts = [kept_left, swapped_in(0, given_left)]
    for slot in range(2):
        h1, query = made[slot][3:5]
        middles.append(
            middle(
                slot,
                [info, units, gains, received[slot], h1, query, cot, weights[2], weights[4], turned[0], turned[2]],
            )
        )
        back.append(lax.ppermute(middles[slot][3], "section", [(1, 0)]))
    packs += [item[0] for item in middles]
    kept_left, given_left, *last = prepare(
        1, info, packs, weights[:2], memory, cot, turned[1], last, [back[0]]
    )
    lefts += [kept_left, swapped_in(1, given_left)]

    def saved(items, index):
        return [item[index] for item in items]

    outer_made = outer(
        saved(middles, 1),
        [kept_left],
        [info, gains, *back, *saved(made, 7), *saved(made, 5), *saved(made, 6),
         *saved(middles, 2), turned[1], turned[2]],
    )
    rhs, grad_chain, out_chain = inner(
        [saved(made, 1), saved(made, 2), saved(middles, 5), saved(middles, 6), saved(middles, 0),
         saved(middles, 4)],
        [info, gains, acts, *saved(made, 9), *saved(made, 3), *outer_made, *last, *turned],
    )
    wide = outer_made[0]
    part = grads(False, info, lefts, [wide, shifted(wide, core=1)], [])
    part = grads(True, info, lefts, [rhs, shifted(rhs, core=1)], part)
    last_x = along_one_round(along_two_rounds(part[:5], "x"), "z")
    last_z = along_one_round(along_two_rounds(part[5:], "z"), "x")
    sent = [for_y(last_x[:384], 12), for_y(last_x[384:768], 32), for_y(last_x[768:], 12)]
    got = shifted(jnp.concatenate([*sent, for_y(last_z, 12)], axis=0), y=1)
    grad_qkv, grad_out, grad_mlp_in, grad_cross, grad_mlp_out, grad_gains = finish(
        last_x, last_z, got
    )
    return (
        out_chain,
        grad_chain,
        grad_gains.transpose(1, 0, 2),
        grad_qkv.transpose(1, 0, 2),
        grad_out.transpose(1, 0, 2),
        grad_mlp_in.transpose(1, 0, 2),
        grad_mlp_out[None],
        grad_cross.transpose(1, 0, 2),
    )


def solution(mesh):
    return jax.shard_map(
        local,
        mesh=mesh,
        in_specs=(
            P("section", "dp", None, None),
            P("section", None, None),
            P("section", None, None),
            P("section", None, None),
            P("section", None, None),
            P("section", None, None),
            P("section", None, None),
            P("dp", None),
            P("dp"),
            P("dp", None),
            P("dp", None, None),
        ),
        out_specs=(
            P("section", "dp", None, None),
            P("section", "dp", None, None),
            P("section", None, "dp"),
            P("section", "dp", None),
            P("section", "dp", None),
            P("section", "dp", None),
            P("section", "dp", None),
            P("section", "dp", None),
        ),
        check_vma=False,
    )
```

```python
import functools

import jax
import jax.numpy as jnp
from jax import lax
from jax.experimental import pallas as pl
from jax.experimental.pallas import tpu as pltpu
from jax.sharding import PartitionSpec as P

D = 768
HDIM = 64
FF = 2048
SEQ = 128
PAIRS = 6
EPS = 1e-06
NEGATIVE = -1e30
ROOM_BYTES = 11 * 2**20
SCALE = HDIM ** (-0.5)
BF16 = jnp.bfloat16
F32 = jnp.float32
ANY = pl.BlockSpec(memory_space=pl.ANY)
FAST = pl.BlockSpec(memory_space=pltpu.VMEM)
SMEM = pl.BlockSpec(memory_space=pltpu.SMEM)


def mm(left, right):
    return jnp.dot(left, right, preferred_element_type=F32)


def mm_t(left, right):
    return lax.dot_general(left, right, (((1,), (1,)), ((), ())), preferred_element_type=F32)


def mm_w(left, right):
    return lax.dot_general(left, right, (((0,), (0,)), ((), ())), preferred_element_type=F32)


def halves(first, second):
    return jnp.concatenate([first, second], axis=0)


def rms(hidden, gain):
    inverse = lax.rsqrt(jnp.mean(hidden * hidden, axis=-1, keepdims=True) + EPS)
    return hidden * inverse * gain


def rms_back(hidden, gain, upstream):
    inverse = lax.rsqrt(jnp.mean(hidden * hidden, axis=-1, keepdims=True) + EPS)
    unit = hidden * inverse
    scaled = upstream * gain
    grad_gain = jnp.sum(upstream * unit, axis=0, keepdims=True)
    middle = jnp.mean(scaled * unit, axis=-1, keepdims=True)
    return inverse * (scaled - unit * middle), grad_gain


def gate_parts(gate, up):
    inner = 0.7978845608 * (gate + 0.044715 * gate * gate * gate)
    bend = jnp.tanh(inner)
    half = 0.5 * (1.0 + bend)
    value = gate * half
    slope = half + 0.5 * gate * (1.0 - bend * bend) * 0.7978845608 * (
        1.0 + 3.0 * 0.044715 * gate * gate
    )
    return value * up, slope * up, value


def lane_masks():
    lane = lax.broadcasted_iota(jnp.int32, (SEQ, 2 * HDIM), 1)
    low = jnp.where(lane < HDIM, 1.0, 0.0).astype(F32)
    return low.astype(BF16), (1.0 - low).astype(BF16), low


def stack_heads(pair, masks):
    return jnp.concatenate([pair * masks[0], pair * masks[1]], axis=0)


def attend(query, keys, values, allowed, masks):
    scores = mm_t(query, stack_heads(keys, masks)) * SCALE
    scores = jnp.where(allowed, scores, NEGATIVE)
    parts = []
    for head in range(2):
        part = scores[:, head * SEQ : (head + 1) * SEQ]
        power = jnp.exp(part - jnp.max(part, axis=-1, keepdims=True))
        parts.append(power * (1.0 / jnp.sum(power, axis=-1, keepdims=True)))
    weights = jnp.concatenate(parts, axis=1).astype(BF16)
    return weights, mm(weights, stack_heads(values, masks)).astype(BF16)


def attend_back(query, keys, values, weights, upstream, masks):
    key_stack = stack_heads(keys, masks)
    grad_weights = mm_t(upstream, stack_heads(values, masks))
    wide = weights.astype(F32)
    product = wide * grad_weights
    parts = []
    for head in range(2):
        columns = slice(head * SEQ, (head + 1) * SEQ)
        total = jnp.sum(product[:, columns], axis=-1, keepdims=True)
        parts.append(product[:, columns] - wide[:, columns] * total)
    grad_scores = jnp.concatenate(parts, axis=1).astype(BF16)
    grad_query = mm(grad_scores, key_stack) * SCALE
    key_both = mm_w(grad_scores, query) * SCALE
    value_both = mm_w(weights, upstream)
    low = masks[2]
    high = 1.0 - low
    grad_keys = key_both[:SEQ] * low + key_both[SEQ:] * high
    grad_values = value_both[:SEQ] * low + value_both[SEQ:] * high
    return grad_query.astype(BF16), grad_keys.astype(BF16), grad_values.astype(BF16)


def key_columns():
    return jnp.bitwise_and(lax.broadcasted_iota(jnp.int32, (SEQ, 2 * SEQ), 1), SEQ - 1)


def kept(keep_ref, plot):
    row = keep_ref[pl.ds(plot, 1), :].astype(F32)
    return jnp.sum(row, axis=1, keepdims=True).astype(jnp.int32)


SECTION, PLACE, PLOT, TOKENS, COUNT = 0, 1, 2, 4, 6


def number(info, row):
    return jnp.max(info[row : row + 1, :].astype(F32)).astype(jnp.int32)


def rows_below(info, row):
    index = lax.broadcasted_iota(jnp.int32, (SEQ, D), 0)
    return index < jnp.broadcast_to(info[row : row + 1, 0:1], (SEQ, D))


class Copies:
    def __init__(self, sems):
        self.sems = sems
        self.count = 0

    def __call__(self, source, target):
        copy = pltpu.make_async_copy(source, target, self.sems.at[self.count])
        self.count += 1
        return copy


def start(copies):
    for copy in copies:
        copy.start()


def wait(copies):
    for copy in copies:
        copy.wait()


def struct(*shape, dtype=BF16):
    return jax.ShapeDtypeStruct(shape, dtype)


def call(kernel, scalars, out_shape, scratch, sems, name, arrays, fast=(), aliases=None, flops=0, traffic=0):
    return pl.pallas_call(
        kernel,
        name=name,
        in_specs=[SMEM] * len(scalars) + [ANY] * len(arrays) + [FAST] * len(fast),
        out_specs=[FAST if is_fast(item) else ANY for item in out_shape],
        out_shape=out_shape,
        scratch_shapes=[
            pltpu.VMEM(item.shape, item.dtype) if isinstance(item, jax.ShapeDtypeStruct) else item
            for item in scratch
        ]
        + [pltpu.SemaphoreType.DMA((sems,))],
        input_output_aliases=aliases or {},
        compiler_params=pltpu.CompilerParams(vmem_limit_bytes=ROOM_BYTES),
        cost_estimate=pl.CostEstimate(flops=flops, bytes_accessed=traffic, transcendentals=0),
    )(*scalars, *arrays, *[pltpu.with_memory_space_constraint(item, pltpu.VMEM) for item in fast])


def is_fast(item):
    return not isinstance(item, jax.ShapeDtypeStruct) and item.memory_space == pltpu.VMEM


def vmem(*shape, dtype=BF16):
    return pltpu.VMEM(shape, dtype)


def hbm(*shape, dtype=BF16):
    return pltpu.HBM(shape, dtype)


def slow(array):
    return pltpu.with_memory_space_constraint(array, pltpu.HBM)


def forward_kernel(slot, *refs):
    if slot == 0:
        section, place, slot_plot, table_len, gains, keep, acts, *given = refs[:12]
        (pack_o, qkv_o, p_o, h1_v, query_v, g1_o, g2_o, h2_o, send_v, memory_v, info, gains_v, acts_v, wqkv_v, wout_v, win_v, wdown_v, wcross_v) = refs[12:30]
        (pack_v, qkv_v, p_v, keep_v, plot_s, tokens_s, g1_v, g2_v, h2_v, sems) = refs[30:]
    else:
        cot, info, gains_v, acts_v, wqkv_v, wout_v, win_v, wdown_v, wcross_v = refs[:9]
        (pack_o, qkv_o, p_o, h1_v, query_v, g1_v, g2_v, h2_v, send_v, memory_v, cot_v) = refs[9:20]
        (pack_v, qkv_v, p_v, sems) = refs[20:]
    copies = Copies(sems)
    tile = 512
    get_qkv, get_in, get_out, get_down, get_cross, get_next = [], [], [], [], [], []
    if slot == 0:
        encoding = section[0] == 0
        get_small = [
            copies(slot_plot, plot_s),
            copies(table_len, tokens_s),
            copies(acts.at[0], acts_v),
            copies(gains, gains_v),
            copies(keep, keep_v),
        ]
        w_qkv, w_out, w_in, w_down, w_cross = given
        get_qkv = [
            copies(w_qkv.at[0, :, pl.ds(i * D, D)], wqkv_v.at[:, pl.ds(i * D, D)]) for i in range(3)
        ]
        get_out = [copies(w_out.at[0], wout_v)]
        for i in range(FF // tile):
            get_in += [
                copies(
                    w_in.at[0, :, pl.ds(base + i * tile, tile)],
                    win_v.at[:, pl.ds(base + i * tile, tile)],
                )
                for base in (0, FF)
            ]
        get_down = [copies(w_down.at[0], wdown_v)]
        get_cross = [copies(w_cross.at[0], wcross_v)]
        start(get_small + get_qkv + get_out + get_in + get_down + get_cross)
        wait(get_small)
        plots = [plot_s[0, i] for i in range(2)]
        numbers = [section[0], place[0], *plots, *[tokens_s[plot] for plot in plots]]
        for row, value in enumerate(numbers):
            info[row : row + 1, :] = jnp.broadcast_to(value, (1, 128)).astype(jnp.int32)
        for i in range(2):
            info[COUNT + i : COUNT + i + 1, :] = jnp.broadcast_to(kept(keep_v, plots[i]), (1, 128))
    else:
        encoding = number(info, SECTION) == 0
        plots = [None, number(info, PLOT + 1)]
        get_next = [copies(cot, cot_v)]
        start(get_next)
    masks = lane_masks()
    rows_in = acts_v[plots[slot]].astype(F32)
    normal = rms(rows_in, gains_v[0]).astype(BF16)
    pack_v[:, 0:D] = normal
    for i in range(3):
        wait(get_qkv[i : i + 1])
        qkv_v[:, i * D : (i + 1) * D] = mm(normal, wqkv_v[:, i * D : (i + 1) * D]).astype(BF16)
    puts = [copies(qkv_v, qkv_o)]
    puts[-1].start()
    put_slow = []
    if slot == 0:
        put_slow = [copies(g1_v, g1_o), copies(g2_v, g2_o), copies(h2_v, h2_o)]
    row_index = lax.broadcasted_iota(jnp.int32, (SEQ, 2 * SEQ), 0)
    key_index = key_columns()
    count = info[COUNT + slot : COUNT + slot + 1, 0:1]
    limit = jnp.where(encoding, jnp.broadcast_to(count - 1, (SEQ, 2 * SEQ)), row_index)
    allowed = key_index <= limit
    for pair in range(PAIRS):
        lanes = slice(pair * 128, (pair + 1) * 128)
        weights, mixed = attend(
            qkv_v[:, lanes],
            qkv_v[:, D + pair * 128 : D + (pair + 1) * 128],
            qkv_v[:, 2 * D + pair * 128 : 2 * D + (pair + 1) * 128],
            allowed,
            masks,
        )
        p_v[pair] = weights
        pack_v[:, D + pair * 128 : D + (pair + 1) * 128] = mixed
    puts.append(copies(p_v, p_o))
    puts[-1].start()
    wait(get_out)
    first = rows_in + mm(pack_v[:, D : 2 * D], wout_v[...])
    h1_v[...] = first
    normal = rms(first, gains_v[1]).astype(BF16)
    pack_v[:, 2 * D : 3 * D] = normal
    put_units = copies(pack_v.at[:, pl.ds(3 * D, FF)], pack_o.at[:, pl.ds(3 * D, FF)])
    puts.append(copies(pack_v.at[:, pl.ds(0, 3 * D)], pack_o.at[:, pl.ds(0, 3 * D)]))
    puts[-1].start()

    @pl.when(encoding)
    def _():
        inputs = pack_v[:, 2 * D : 3 * D]
        for i in range(FF // tile):
            wait(get_in[2 * i : 2 * i + 2])
            columns = slice(i * tile, (i + 1) * tile)
            gate = mm(inputs, win_v[:, columns])
            up = mm(inputs, win_v[:, FF + i * tile : FF + (i + 1) * tile])
            unit, to_gate, to_up = gate_parts(gate, up)
            pack_v[:, 3 * D + i * tile : 3 * D + (i + 1) * tile] = unit.astype(BF16)
            g1_v[:, columns] = to_gate.astype(BF16)
            g2_v[:, columns] = to_up.astype(BF16)
        put_units.start()
        start(put_slow[:2])
        wait(get_down)
        second = h1_v[...] + mm(pack_v[:, 3 * D :], wdown_v[...])
        h2_v[...] = second
        start(put_slow[2:])
        memory = rms(second, gains_v[2])
        memory = jnp.where(rows_below(info, COUNT + slot), memory, 0.0).astype(BF16)
        memory_v[...] = memory
        wait(get_cross)
        send_v[...] = mm(memory, wcross_v[...]).astype(BF16)
        put_units.wait()
        wait(put_slow)

    @pl.when(jnp.logical_not(encoding))
    def _():
        wait(get_cross)
        query_v[...] = mm(pack_v[:, 2 * D : 3 * D], wcross_v[:, 0:D]).astype(BF16)
        wait(get_in + get_down)

    wait(puts + get_next)


def forward(slot, scalars, arrays, fast):
    kind = (hbm, vmem)[slot]
    outs = [
        hbm(SEQ, 3 * D + FF),
        hbm(SEQ, 3 * D),
        hbm(PAIRS, SEQ, 2 * SEQ),
        vmem(SEQ, D, dtype=F32),
        vmem(SEQ, D),
        kind(SEQ, FF),
        kind(SEQ, FF),
        kind(SEQ, D, dtype=F32),
        vmem(SEQ, 2 * D),
        vmem(SEQ, D),
    ]
    scratch = [struct(SEQ, 3 * D + FF), struct(SEQ, 3 * D), struct(PAIRS, SEQ, 2 * SEQ)]
    if slot == 0:
        outs += [vmem(8, 128, dtype=jnp.int32), vmem(3, 1, D, dtype=F32), vmem(2, SEQ, D)]
        outs += [vmem(*weight.shape[1:]) for weight in arrays[5:]]
        scratch += [struct(2, SEQ, dtype=jnp.int32)]
        scratch += [pltpu.SMEM((1, 2), jnp.int32), pltpu.SMEM((2,), jnp.int32)]
        scratch += [struct(SEQ, FF), struct(SEQ, FF), struct(SEQ, D, dtype=F32)]
    else:
        outs += [vmem(2, SEQ, D)]
    return call(
        functools.partial(forward_kernel, slot), scalars, outs, scratch, 34, "forward",
        [slow(item) for item in arrays], fast,
    )


def turn_all(sources, results):
    for source, result in zip(sources, results):

        def step(i, carry):
            at = pl.ds(pl.multiple_of(i * 256, 256), 256)
            result[at, :] = source[:, at].T
            return carry

        lax.fori_loop(0, source.shape[1] // 256, step, 0)


def turn_kernel(count, *refs):
    turn_all(refs[1 : count + 1], refs[count + 1 : 2 * count + 1])


def turn(after, weights):
    return call(
        functools.partial(turn_kernel, len(weights)), [],
        [vmem(*weight.shape[::-1]) for weight in weights], [], 1, "turn", [after], weights,
    )


def turn_last_kernel(info, cot, wdownt, *refs):
    turn_all(refs[0:2], refs[2:4])
    units = refs[4]

    @pl.when(number(info, SECTION) == 1)
    def _():
        branch = halves(
            *[
                jnp.where(rows_below(info, TOKENS + i), cot[i].astype(F32), 0.0).astype(BF16)
                for i in range(2)
            ]
        )
        units[...] = mm(branch, wdownt[...])


def turn_last(fast):
    return call(
        turn_last_kernel, [],
        [vmem(3 * D, D), vmem(D, D), vmem(2 * SEQ, FF, dtype=F32)], [], 1, "turn_last", [], fast,
    )


def middle_kernel(slot, *refs):
    packs, refs = refs[: 2 * slot], refs[2 * slot :]
    info, units, gains_v, kv_v, h1_v, query_v, cot_v, win_v, wcross_v, wint_v, wcrosst_v = refs[:11]
    memory, refs = refs[11 : 11 + 2 * slot], refs[11 + 2 * slot :]
    pack_o, rhs_o, late_v, dkv_v, e2_o, de2_o, gain_o = refs[:7]
    lefts, refs = refs[7 : 7 + 2 * slot], refs[7 + 2 * slot :]
    pack_v, g1_v, g2_v, rhs_v, p_v, e2_v, de2_v, gain_v, mixed_v = refs[:9]
    held, sems = refs[9:-1], refs[-1]
    if slot == 1:

        @pl.when(number(info, SECTION) == 0)
        def _():
            copies = Copies(sems)
            get = [copies(source, target) for source, target in zip(packs, held)]
            start(get)
            wait(get)
            left_operands(0, number(info, PLACE), held, None, memory, lefts)

    @pl.when(number(info, SECTION) != 0)
    def _():
        copies = Copies(sems)
        tile = 512
        masks = lane_masks()
        count = info[COUNT + slot : COUNT + slot + 1, 0:1]
        allowed = key_columns() < jnp.broadcast_to(count, (SEQ, 2 * SEQ))
        for pair in range(PAIRS):
            lanes = slice(pair * 128, (pair + 1) * 128)
            weights, mixed = attend(
                query_v[:, lanes],
                kv_v[:, lanes],
                kv_v[:, D + pair * 128 : D + (pair + 1) * 128],
                allowed,
                masks,
            )
            p_v[pair] = weights
            pack_v[:, D + pair * 128 : D + (pair + 1) * 128] = mixed
        second = h1_v[...] + mm(pack_v[:, D : 2 * D], wcross_v[:, D : 2 * D])
        e2_v[...] = second
        puts = [copies(e2_v, e2_o)]
        puts[-1].start()
        normal = rms(second, gains_v[2]).astype(BF16)
        pack_v[:, 0:D] = normal
        for i in range(FF // tile):
            columns = slice(i * tile, (i + 1) * tile)
            gate = mm(normal, win_v[:, columns])
            up = mm(normal, win_v[:, FF + i * tile : FF + (i + 1) * tile])
            unit, to_gate, to_up = gate_parts(gate, up)
            pack_v[:, 2 * D + i * tile : 2 * D + (i + 1) * tile] = unit.astype(BF16)
            g1_v[:, columns] = to_gate.astype(BF16)
            g2_v[:, columns] = to_up.astype(BF16)
        puts.append(copies(pack_v, pack_o))
        puts[-1].start()
        upstream = jnp.where(rows_below(info, TOKENS + slot), cot_v[slot].astype(F32), 0.0)
        branch = upstream.astype(BF16)
        rhs_v[:, 0:D] = branch
        for i in range(FF // tile):
            columns = slice(i * tile, (i + 1) * tile)
            grad_unit = units[slot * SEQ : (slot + 1) * SEQ, columns]
            rhs_v[:, D + i * tile : D + (i + 1) * tile] = (
                grad_unit * g1_v[:, columns].astype(F32)
            ).astype(BF16)
            rhs_v[:, D + FF + i * tile : D + FF + (i + 1) * tile] = (
                grad_unit * g2_v[:, columns].astype(F32)
            ).astype(BF16)
        puts.append(copies(rhs_v, rhs_o))
        puts[-1].start()
        grad_normal = mm(rhs_v[:, D : D + 2 * FF], wint_v[...])
        back, grad_gain = rms_back(second, gains_v[2], grad_normal)
        grad_second = upstream + back
        gain_v[...] = jnp.zeros_like(gain_v)
        gain_v[2:3, :] = grad_gain
        de2_v[...] = grad_second
        puts += [copies(de2_v, de2_o), copies(gain_v, gain_o)]
        start(puts[-2:])
        branch = grad_second.astype(BF16)
        late_v[:, D : 2 * D] = branch
        mixed_v[...] = mm(branch, wcrosst_v[D : 2 * D, :]).astype(BF16)
        for pair in range(PAIRS):
            lanes = slice(pair * 128, (pair + 1) * 128)
            high = slice(D + pair * 128, D + (pair + 1) * 128)
            grad_query, grad_keys, grad_values = attend_back(
                query_v[:, lanes], kv_v[:, lanes], kv_v[:, high], p_v[pair], mixed_v[:, lanes], masks
            )
            late_v[:, lanes] = grad_query
            dkv_v[:, lanes] = grad_keys
            dkv_v[:, high] = grad_values
        wait(puts)


def middle(slot, packs, fast):
    return call(
        functools.partial(middle_kernel, slot),
        [],
        [
            hbm(SEQ, 2 * D + FF),
            hbm(SEQ, D + 2 * FF),
            vmem(SEQ, 2 * D),
            vmem(SEQ, 2 * D),
            hbm(SEQ, D, dtype=F32),
            hbm(SEQ, D, dtype=F32),
            hbm(8, D, dtype=F32),
        ]
        + [vmem(3712, 256)] * (2 * slot),
        [
            struct(SEQ, 2 * D + FF),
            struct(SEQ, FF),
            struct(SEQ, FF),
            struct(SEQ, D + 2 * FF),
            struct(PAIRS, SEQ, 2 * SEQ),
            struct(SEQ, D, dtype=F32),
            struct(SEQ, D, dtype=F32),
            struct(8, D, dtype=F32),
            struct(SEQ, D),
        ]
        + [struct(*pack.shape) for pack in packs],
        8,
        "middle",
        [slow(pack) for pack in packs],
        fast,
    )


def outer_rows(slot, info, gains_v, dkv_v, h2_v, g1_v, g2_v, wdownt_v, wcrosst_v, rhs_v):
    rhs_v[:, D + 2 * FF :] = dkv_v[...]
    grad_memory = mm(dkv_v[...], wcrosst_v[...])
    grad_memory = jnp.where(rows_below(info, COUNT + slot), grad_memory, 0.0)
    grad_second, grad_gain = rms_back(h2_v[...], gains_v[2], grad_memory)
    branch = grad_second.astype(BF16)
    rhs_v[:, 0:D] = branch
    tile = 512
    for i in range(FF // tile):
        columns = slice(i * tile, (i + 1) * tile)
        grad_unit = mm(branch, wdownt_v[:, columns])
        for k, scale in ((0, g1_v), (1, g2_v)):
            first = D + k * FF + i * tile
            rhs_v[:, first : first + tile] = (grad_unit * scale[:, columns].astype(F32)).astype(BF16)
    return grad_second, grad_gain


def inner_rows(slot, info, gains_v, acts_v, h1_v, dn_v, up_v, qkv_v, p_v, woutt_v, wqkvt_v, rhs_v, grad_v):
    rows = slice(0, SEQ)
    plot = number(info, PLOT + slot)
    back, first_gain = rms_back(h1_v[...], gains_v[1], dn_v[...])
    grad_first = up_v[...] + back
    branch = grad_first.astype(BF16)
    rhs_v[rows, 0:D] = branch
    masks = lane_masks()
    grad_mixed = mm(branch, woutt_v[...]).astype(BF16)
    for pair in range(PAIRS):
        spans = [slice(k * D + pair * 128, k * D + (pair + 1) * 128) for k in range(3)]
        parts = attend_back(
            qkv_v[:, spans[0]],
            qkv_v[:, spans[1]],
            qkv_v[:, spans[2]],
            p_v[pair],
            grad_mixed[:, pair * 128 : (pair + 1) * 128],
            masks,
        )
        for k in range(3):
            rhs_v[rows, D + k * D + pair * 128 : D + k * D + (pair + 1) * 128] = parts[k]
    grad_normal = mm(rhs_v[rows, D : 4 * D], wqkvt_v[...])
    back, zeroth_gain = rms_back(acts_v[plot].astype(F32), gains_v[0], grad_normal)
    grad_v[0, plot] = grad_first + back
    return zeroth_gain, first_gain


def early_kernel(*refs):
    packs, (qkv, p, rhs2, de2, gain2, h2, g1, g2) = refs[0:4], refs[4:12]
    info, gains_v, acts_v, dkv_v, h1_v, late_v = refs[12:18]
    wqkvt_v, woutt_v, wint_v, wdownt_v, wcrosst_v, ready_v = refs[18:24]
    (kept_v, given_v, rhs3_v, rhs_v, gain_v, grad_v) = refs[24:30]
    held = refs[30:34]
    qkv_v, p_v, up_v, dn_v, gain2_v, h2_v, units_v, sems = refs[34:]
    g1_v, g2_v = units_v.at[0], units_v.at[1]
    encoding = number(info, SECTION) == 0
    copies = Copies(sems)
    get_rows = [copies(qkv, qkv_v), copies(p, p_v)]
    get_packs = [copies(source, target) for source, target in zip(packs, held)]
    get_rhs = copies(rhs2, rhs3_v.at[:, pl.ds(0, D + 2 * FF)])
    get_rest = [copies(de2, up_v), copies(gain2, gain2_v)]
    get_enc = [copies(h2, h2_v), copies(g1, g1_v), copies(g2, g2_v)]
    start(get_rows)

    @pl.when(encoding)
    def _():
        start(get_enc)
        wait(get_enc)
        grad_second, grad_gain = outer_rows(
            0, info, gains_v, dkv_v, h2_v, g1_v, g2_v, wdownt_v, wcrosst_v, rhs3_v
        )
        up_v[...] = grad_second
        gain2_v[2:3, :] = grad_gain
        given_v[...] = ready_v[...]
        dn_v[...] = mm(rhs3_v[:, D : D + 2 * FF], wint_v[...])

    @pl.when(jnp.logical_not(encoding))
    def _():
        start(get_packs + get_rest + [get_rhs])
        wait(get_packs)
        left_operands(1, number(info, PLACE), held[:2], held[2:], None, (kept_v, given_v))
        rhs3_v[:, D + 2 * FF :] = late_v[...]
        dn_v[...] = mm(late_v[:, 0:D], wcrosst_v[0:D, :])
        wait(get_rest)
        get_rhs.wait()

    wait(get_rows)
    zeroth_gain, first_gain = inner_rows(
        0, info, gains_v, acts_v, h1_v, dn_v, up_v, qkv_v, p_v, woutt_v, wqkvt_v, rhs_v, grad_v
    )
    gain_v[...] = jnp.concatenate(
        [zeroth_gain, first_gain, gain2_v[2:3, :], jnp.zeros((5, D), F32)], axis=0
    )


def early(arrays, fast):
    return call(
        early_kernel,
        [],
        [
            vmem(3712, 256),
            vmem(3712, 256),
            vmem(SEQ, 3 * D + 2 * FF),
            vmem(SEQ, 4 * D),
            vmem(8, D, dtype=F32),
            vmem(1, 2, SEQ, D, dtype=F32),
        ],
        [struct(*pack.shape) for pack in arrays[:4]]
        + [
            struct(SEQ, 3 * D),
            struct(PAIRS, SEQ, 2 * SEQ),
            struct(SEQ, D, dtype=F32),
            struct(SEQ, D, dtype=F32),
            struct(8, D, dtype=F32),
            struct(SEQ, D, dtype=F32),
            struct(2, SEQ, FF),
        ],
        14,
        "early",
        [slow(item) for item in arrays],
        fast,
    )


def outer_kernel(rhs2, after, info, gains_v, dkv_v, h2_v, g1_v, g2_v, late_v, wdownt_v, wcrosst_v, rhs_v, up_v, gain_v, sems):
    encoding = number(info, SECTION) == 0

    @pl.when(encoding)
    def _():
        grad_second, grad_gain = outer_rows(
            1, info, gains_v, dkv_v, h2_v, g1_v, g2_v, wdownt_v, wcrosst_v, rhs_v
        )
        up_v[...] = grad_second
        gain_v[2:3, :] = grad_gain

    @pl.when(jnp.logical_not(encoding))
    def _():
        get = Copies(sems)(rhs2, rhs_v.at[:, pl.ds(0, D + 2 * FF)])
        get.start()
        rhs_v[:, D + 2 * FF :] = late_v[...]
        get.wait()


def outer(rhs2, after, fast):
    return call(
        outer_kernel,
        [],
        [vmem(SEQ, 3 * D + 2 * FF), vmem(SEQ, D, dtype=F32), vmem(8, D, dtype=F32)],
        [],
        1,
        "outer",
        [slow(rhs2), after],
        fast,
    )


def inner_kernel(*refs):
    qkv, p, de2, gain2 = refs[:4]
    info, gains_v, acts_v, h1_v, rhs3_v, dh2_v, gain3_v, before_v = refs[4:12]
    wqkvt_v, woutt_v, wint_v, wcrosst_v = refs[12:16]
    (rhs_v, grad_v, qkv_v, p_v, up_v, dn_v, gain2_v, sems) = refs[17:]
    encoding = number(info, SECTION) == 0
    copies = Copies(sems)
    get_rows = [copies(qkv, qkv_v), copies(p, p_v)]
    get_dec = [
        copies(de2, up_v),
        copies(gain2, gain2_v),
    ]
    start(get_rows)

    @pl.when(encoding)
    def _():
        dn_v[...] = mm(rhs3_v[:, D : D + 2 * FF], wint_v[...])
        up_v[...] = dh2_v[...]
        gain2_v[...] = gain3_v[...]

    @pl.when(jnp.logical_not(encoding))
    def _():
        start(get_dec)
        dn_v[...] = mm(rhs3_v[:, D + 2 * FF : 2 * D + 2 * FF], wcrosst_v[0:D, :])
        wait(get_dec)

    wait(get_rows)
    zeroth_gain, first_gain = inner_rows(
        1, info, gains_v, acts_v, h1_v, dn_v, up_v, qkv_v, p_v, woutt_v, wqkvt_v, rhs_v, grad_v
    )
    total = before_v[...] + jnp.concatenate(
        [zeroth_gain, first_gain, gain2_v[2:3, :], jnp.zeros((5, D), F32)], axis=0
    )
    upper = total.astype(BF16)
    lower = (total - upper.astype(F32)).astype(BF16)
    rhs_v[SEQ:, 0:D] = halves(upper, lower)
    rhs_v[SEQ:, D : 4 * D] = jnp.zeros((16, 3 * D), BF16)


def inner(arrays, fast):
    return call(
        inner_kernel,
        [],
        [vmem(SEQ + 16, 4 * D), vmem(1, 2, SEQ, D, dtype=F32)],
        [
            struct(SEQ, 3 * D),
            struct(PAIRS, SEQ, 2 * SEQ),
            struct(SEQ, D, dtype=F32),
            struct(SEQ, D, dtype=F32),
            struct(8, D, dtype=F32),
        ],
        8,
        "inner",
        [slow(item) for item in arrays],
        fast,
        aliases={len(arrays) + 12: 1},
    )


def output_kernel(*refs):
    pack2, e2 = refs[0:2], refs[2:4]
    info, memory, wdownt_v, out_o, out_v, z_v, e2_v, sems = refs[4], *[refs[5:7]], *refs[7:]
    encoding = number(info, SECTION) == 0
    copies = Copies(sems)
    get = []
    for i in range(2):
        at = pl.ds(i * SEQ, SEQ)
        get += [copies(pack2[i].at[:, pl.ds(2 * D, FF)], z_v.at[at]), copies(e2[i], e2_v.at[at])]

    @pl.when(encoding)
    def _():
        for i in range(2):
            out_v[0, i] = memory[i][...]

    @pl.when(jnp.logical_not(encoding))
    def _():
        start(get)
        wait(get)
        third = e2_v[...] + mm_t(z_v[...], wdownt_v[...])
        for i in range(2):
            part = third[i * SEQ : (i + 1) * SEQ]
            out_v[0, i] = jnp.where(rows_below(info, TOKENS + i), part, 0.0).astype(BF16)

    put = copies(out_v, out_o)
    put.start()
    put.wait()


def output(arrays, after, fast):
    def kernel(*refs):
        output_kernel(*refs[len(after) :])

    return call(
        kernel,
        [],
        [struct(1, 2, SEQ, D)],
        [struct(1, 2, SEQ, D), struct(2 * SEQ, FF), struct(2 * SEQ, D, dtype=F32)],
        5,
        "output",
        after + [slow(item) for item in arrays],
        fast,
    )[0]


def place_parts(place):
    return (
        lax.shift_right_logical(place, 5),
        jnp.bitwise_and(lax.shift_right_logical(place, 3), 3),
        jnp.bitwise_and(lax.shift_right_logical(place, 1), 3),
        jnp.bitwise_and(place, 1),
    )


def matching(target, columns):
    rows = target.shape[0]
    lane = lax.broadcasted_iota(jnp.int32, (rows, 128), 1)
    blocks = [jnp.where(lane + i * 128 == target, 1.0, 0.0) for i in range(columns // 128)]
    return jnp.concatenate(blocks, axis=1).astype(BF16)


def selector(place, along, other=0):
    y, x, z, core = place_parts(place)
    core = jnp.bitwise_xor(core, other)
    index = lax.broadcasted_iota(jnp.int32, (384, 128), 0)

    def at_least(value, *bounds):
        return sum(jnp.where(value >= bound, 1, 0) for bound in bounds)

    first = at_least(index, 96, 192, 288)
    rest = index - first * 96
    second = at_least(rest, 24, 48, 72)
    rest = rest - second * 24
    third = at_least(rest, 12)
    rest = rest - third * 12
    to_x, to_z = (first, second) if along == "x" else (second, first)
    return matching(
        jnp.bitwise_and(y + third, 1) * 384
        + jnp.bitwise_and(x + to_x, 3) * 96
        + jnp.bitwise_and(z + to_z, 3) * 24
        + core * 12
        + rest,
        D,
    )


def stacked(sources, first, width):
    return jnp.concatenate([source[0:SEQ, first : first + width] for source in sources], axis=0)


def along_down(place, other):
    y, x, z, core = place_parts(place)
    core = jnp.bitwise_xor(core, other)
    index = lax.broadcasted_iota(jnp.int32, (256, 128), 0)
    return matching(
        jnp.bitwise_and(y + jnp.bitwise_and(lax.shift_right_logical(index, 5), 1), 1) * 256
        + jnp.bitwise_and(z + lax.shift_right_logical(index, 6), 3) * 64
        + core * 32
        + jnp.bitwise_and(index, 31),
        512,
    )


def prepare_down(place, sources, first, result, order):
    y, x, z, core = place_parts(place)
    for chunk in range(4):
        block = first + jnp.bitwise_and(x + chunk, 3) * 256
        columns = [pl.ds(pl.multiple_of(block + half, 256), 256) for half in (0, 1024)]
        picked = jnp.concatenate(
            [jnp.concatenate([source[:, at] for source in sources], axis=0) for at in columns],
            axis=1,
        )
        at = 2688 + 256 * chunk
        result[at : at + 256, :] = mm_t(order, picked).astype(BF16)


def left_operands(which, place, pack1, pack2, memory, results):
    last = pack2 if which else pack1
    for other, result in enumerate(results):
        along_x = selector(place, "x", other)
        along_z = selector(place, "z", other)
        steps = (
            (0, along_x, pack1, 0),
            (384, along_z, pack1, 0),
            (768, along_z, pack1, D),
            (1152, along_x, last, 0 if which else 2 * D),
            (1536, along_z, last, 0 if which else 2 * D),
            (1920, along_z, pack1 if which else memory, 2 * D if which else 0),
            (2304, along_z, last if which else memory, D if which else 0),
        )
        for row, order, sources, first in steps:
            result[row : row + 384, :] = mm_t(order, stacked(sources, first, D)).astype(BF16)
        prepare_down(place, last, 2 * D if which else 3 * D, result, along_down(place, other))


class Buffers:
    def __init__(self, refs, size):
        self.own, self.ahead, self.behind, self.one, self.three = refs
        self.size = size

    def spot(self, chunk, block):
        quarter = self.size // 4
        half = self.size // 2
        row = block * quarter
        if chunk == 0:
            return self.own, row
        low = block < 2
        if chunk == 1:
            return (self.one, row) if low else (self.ahead, row)
        if chunk == 2:
            return (self.ahead, row) if low else (self.behind, row - half)
        return (self.behind, half + row) if low else (self.three, row - half)


def buffer_shapes(size):
    return [struct(size, 128)] * 3 + [struct(size // 2, 128)] * 2


def store_narrow(buffers, grad, offset):
    for chunk in range(4):
        for block in range(4):
            rows = grad[(chunk * 4 + block) * 24 : (chunk * 4 + block + 1) * 24]
            piece = jnp.concatenate([rows[:, 0:128], rows[:, 128:256]], axis=0).astype(BF16)
            target, row = buffers.spot(chunk, block)
            target[row + offset : row + offset + 48, :] = piece


QKV_X = 5
SIZE_X, SIZE_Z = 4 * (768 + 48 * QKV_X), 4 * (1296 - 48 * QKV_X)
OUT_ROW = 672 + 48 * (9 - QKV_X)


def both_sides(lefts, first, count):
    return jnp.concatenate([left[first : first + count, :] for left in lefts], axis=1)


def right_of(sources, first, width=256):
    return stacked(sources, first, width)


def grads_wide_kernel(lefts, wide, results):
    held = Buffers(results[:5], SIZE_X), Buffers(results[5:], SIZE_Z)
    branch = right_of(wide, 0, D)
    for chunk in range(4):
        grad = mm(both_sides(lefts, 2688 + 256 * chunk, 256), branch)
        for block in range(4):
            target, row = held[0].spot(chunk, block)
            for i in range(6):
                spot = row + 384 + 64 * i
                target[spot : spot + 64, :] = grad[
                    64 * block : 64 * (block + 1), 128 * i : 128 * (i + 1)
                ].astype(BF16)
    for i in range(6):
        left = both_sides(lefts, 1920 if i < 3 else 2304, 384)
        store_narrow(held[1], mm(left, right_of(wide, D + 2 * FF + 256 * i)), 384 + 48 * i)
    for axis in range(2):
        left = both_sides(lefts, 1152 + 384 * axis, 384)
        for i in range(8):
            grad = mm(left, right_of(wide, D + axis * FF + 256 * i))
            store_narrow(held[axis], grad, 48 * i)


def grads_thin_kernel(place, lefts, thin, results):
    held = Buffers(results[:5], SIZE_X), Buffers(results[5:], SIZE_Z)
    total_of = selector(place, "z")
    total = sum(
        item[row : row + 8, 0:D].astype(F32) for item in (thin[1], thin[3]) for row in (SEQ, SEQ + 8)
    )
    upper = total.astype(BF16)
    lower = (total - upper.astype(F32)).astype(BF16)
    ordered = mm_t(upper, total_of) + mm_t(lower, total_of)
    tall = jnp.concatenate([ordered, jnp.zeros((120, 384), F32)], axis=0).T
    tall = jnp.concatenate([tall, jnp.zeros((384, 128), F32)], axis=1)
    store_narrow(held[1], tall, OUT_ROW + 144)
    for i in range(9):
        axis = 0 if i < QKV_X else 1
        grad = mm(both_sides(lefts, 384 * axis, 384), right_of(thin, D + 256 * i))
        store_narrow(held[axis], grad, 672 + 48 * (i - QKV_X) if axis else 768 + 48 * i)
    for i in range(3):
        grad = mm(both_sides(lefts, 768, 384), right_of(thin, 256 * i))
        store_narrow(held[1], grad, OUT_ROW + 48 * i)


def grads(thin, info, lefts, right, before):
    shapes = [vmem(*item.shape) for item in buffer_shapes(SIZE_X) + buffer_shapes(SIZE_Z)]

    def kernel(info, *refs):
        encoding = number(info, SECTION) == 0
        results = refs[-11:-1]

        def run(lefts):
            if thin:
                grads_thin_kernel(number(info, PLACE), lefts, refs[3:7], results)
            else:
                grads_wide_kernel(lefts, refs[3:7], results)

        @pl.when(encoding)
        def _():
            run((refs[0], refs[2]))

        @pl.when(jnp.logical_not(encoding))
        def _():
            run(refs[1:3])

    return call(
        kernel, [], shapes, [], 1, "grads", [], [info, *lefts, *right, *before],
        aliases={8 + i: i for i in range(len(before))},
    )


def finish_kernel(own_x, own_z, got, qkv_o, out_o, in_o, cross_o, down_o, gains_o, got_v):
    got_v[...] = got[...].astype(F32)

    def lay(result, column, own, row, got_row, count):
        for at in range(12):
            kept_rows = own[pl.ds(row + at, count, stride=24), :]
            line = kept_rows + got_v[pl.ds(got_row + at, count, stride=12), :]
            for tile in range(count):
                first = column + 128 * tile
                result[at, :, first : first + 128] = line[tile : tile + 1, :]

    lay(in_o, 0, own_x, 0, 0, 16)
    for tile in range(6):
        columns = slice(128 * tile, 128 * (tile + 1))
        down_o[:, columns] = (
            own_x[384 + 64 * tile : 416 + 64 * tile, :] + got_v[192 + 32 * tile : 224 + 32 * tile, :]
        )
    lay(qkv_o, 0, own_x, 768, 384, 2 * QKV_X)
    base = SIZE_X // 8
    lay(in_o, FF, own_z, 0, base, 16)
    lay(cross_o, 0, own_z, 384, base + 192, 12)
    lay(qkv_o, 256 * QKV_X, own_z, 672, base + 336, 18 - 2 * QKV_X)
    lay(out_o, 0, own_z, OUT_ROW, base + OUT_ROW // 2, 6)
    row = OUT_ROW + 144
    tall = own_z[row : row + 16, :] + got_v[base + row // 2 : base + row // 2 + 16, :]
    tall = jnp.concatenate([tall, jnp.zeros((112, 128), F32)], axis=0).T
    for i in range(3):
        gains_o[i] = tall[i : i + 1, 0:12]


def finish(own_x, own_z, got):
    shapes = [
        struct(12, 1, 3 * D, dtype=F32),
        struct(12, 1, D, dtype=F32),
        struct(12, 1, 2 * FF, dtype=F32),
        struct(12, 1, 2 * D, dtype=F32),
        struct(32, D, dtype=F32),
        struct(3, 1, 12, dtype=F32),
    ]
    return pl.pallas_call(
        finish_kernel,
        name="finish",
        in_specs=[FAST] * 3,
        out_specs=[FAST] * 6,
        out_shape=shapes,
        scratch_shapes=[pltpu.VMEM(got.shape, F32)],
        compiler_params=pltpu.CompilerParams(vmem_limit_bytes=ROOM_BYTES),
    )(own_x, own_z, got)


def flat(y, x, z, core):
    return ((y * 4 + x) * 4 + z) * 2 + core


def shifted(array, y=0, x=0, z=0, core=0):
    pairs = []
    for a in range(2):
        for b in range(4):
            for c in range(4):
                for d in range(2):
                    source = flat(a, b, c, d)
                    target = flat((a + y) % 2, (b + x) % 4, (c + z) % 4, (d + core) % 2)
                    pairs.append((source, target))
    return lax.ppermute(array, "dp", pairs)


def add(*terms):
    total = terms[0].astype(F32)
    for term in terms[1:]:
        total = total + term.astype(F32)
    return total


def first_round(buffers, axis):
    own, ahead, behind, one, three = buffers
    return shifted(ahead, **{axis: 1}), shifted(behind, **{axis: 3})


def second_round(buffers, firsts, axis):
    own, ahead, behind, one, three = buffers
    got_ahead, got_behind = firsts
    half = one.shape[0]
    last_ahead = shifted(add(one, got_ahead[:half]).astype(BF16), **{axis: 1})
    last_behind = shifted(add(three, got_behind[:half]).astype(BF16), **{axis: 3})
    low = add(own[:half], last_ahead, got_behind[half:])
    high = add(own[half:], got_ahead[half:], last_behind)
    return jnp.concatenate([low, high], axis=0).astype(BF16)


def along_one_round(total, axis):
    size = total.shape[0] // 4
    parts = [total[i * size : (i + 1) * size] for i in range(4)]
    return add(
        parts[0],
        shifted(parts[2], **{axis: 2}),
        shifted(parts[1], **{axis: 1}),
        shifted(parts[3], **{axis: 3}),
    )


def for_y(total, tile_rows):
    return total.reshape(-1, 2, tile_rows, 128)[:, 1].reshape(-1, 128).astype(BF16)


def local(
    acts,
    gains,
    qkv_weight,
    out_weight,
    mlp_in,
    mlp_out,
    cross_weight,
    patch_mask,
    table_len,
    slot_plot,
    cotangent,
):
    section = lax.axis_index("section").astype(jnp.int32).reshape(1)
    place = lax.axis_index("dp").astype(jnp.int32).reshape(1)
    gains = gains.transpose(1, 0, 2)
    weights = (qkv_weight, out_weight, mlp_in, mlp_out, cross_weight)
    made = [
        forward(0, [section, place], [slot_plot, table_len, gains, patch_mask, acts, *weights], [])
    ]
    info, gains, acts, *weights = made[0][10:]
    received = [lax.ppermute(made[0][8], "section", [(0, 1)])]
    made.append(forward(1, [], [cotangent], [info, gains, acts, *weights]))
    received.append(lax.ppermute(made[1][8], "section", [(0, 1)]))
    cot = made[1][10]
    turned = turn(slow(made[1][1]), weights[2:])
    *last, units = turn_last([info, cot, turned[1], *weights[:2]])
    turned = [*last, *turned]
    middles = []
    back = []
    memory = [item[9] for item in made]
    packs = [item[0] for item in made]
    for slot in range(2):
        h1, query = made[slot][3:5]
        middles.append(
            middle(
                slot,
                packs * slot,
                [info, units, gains, received[slot], h1, query, cot, weights[2], weights[4],
                 turned[2], turned[4], *memory * slot],
            )
        )
        back.append(lax.ppermute(middles[slot][3], "section", [(1, 0)]))
    lefts = [middles[1][7]]
    pack1, qkv, p, h1, query, g1, g2, h2 = made[0][:8]
    pack2, rhs2, late, _, e2, de2, gain2 = middles[0]
    kept_left, given_left, wide0, thin0, gain, grad_chain = early(
        [*packs, pack2, middles[1][0], qkv, p, rhs2, de2, gain2, h2, g1, g2],
        [info, gains, acts, back[0], h1, late, *turned, middles[1][8]],
    )
    lefts += [kept_left, shifted(given_left, core=1)]
    pack1, qkv, p, h1, query, g1, g2, h2 = made[1][:8]
    pack2, rhs2, late, _, e2, de2, gain2 = middles[1][:7]
    wide1, dh2, gain3 = outer(
        rhs2, gain, [info, gains, back[1], h2, g1, g2, late, turned[3], turned[4]]
    )
    wide = [wide0, wide1, shifted(wide0, core=1), shifted(wide1, core=1)]
    thin1, grad_chain = inner(
        [qkv, p, de2, gain2],
        [info, gains, acts, h1, wide1, dh2, gain3, gain, *turned[:3], turned[4], grad_chain],
    )
    thin = [thin0, thin1, shifted(thin0, core=1), shifted(thin1, core=1)]
    part = grads(False, info, lefts, wide, [])
    part = grads(True, info, lefts, thin, part)
    firsts_x, firsts_z = first_round(part[:5], "x"), first_round(part[5:], "z")
    out_rows = output(
        [middles[0][0], middles[1][0], middles[0][4], middles[1][4]],
        [part[3]],
        [info, *memory, turned[3]],
    )
    firsts_x, out_rows = lax.optimization_barrier((firsts_x, out_rows))
    last_x = along_one_round(second_round(part[:5], firsts_x, "x"), "z")
    last_z = along_one_round(second_round(part[5:], firsts_z, "z"), "x")
    sent = [for_y(last_x[:384], 12), for_y(last_x[384:768], 32), for_y(last_x[768:], 12)]
    got = shifted(jnp.concatenate([*sent, for_y(last_z, 12)], axis=0), y=1)
    grad_qkv, grad_out, grad_mlp_in, grad_cross, grad_mlp_out, grad_gains = finish(
        last_x, last_z, got
    )
    return (
        out_rows,
        grad_chain,
        grad_gains.transpose(1, 0, 2),
        grad_qkv.transpose(1, 0, 2),
        grad_out.transpose(1, 0, 2),
        grad_mlp_in.transpose(1, 0, 2),
        grad_mlp_out[None],
        grad_cross.transpose(1, 0, 2),
    )


def solution(mesh):
    return jax.shard_map(
        local,
        mesh=mesh,
        in_specs=(
            P("section", "dp", None, None),
            P("section", None, None),
            P("section", None, None),
            P("section", None, None),
            P("section", None, None),
            P("section", None, None),
            P("section", None, None),
            P("dp", None),
            P("dp"),
            P("dp", None),
            P("dp", None, None),
        ),
        out_specs=(
            P("section", "dp", None, None),
            P("section", "dp", None, None),
            P("section", None, "dp"),
            P("section", "dp", None),
            P("section", "dp", None),
            P("section", "dp", None),
            P("section", "dp", None),
            P("section", "dp", None),
        ),
        check_vma=False,
    )
```

```python
import functools

import jax
import jax.numpy as jnp
from jax import lax
from jax.experimental import pallas as pl
from jax.experimental.pallas import tpu as pltpu
from jax.sharding import PartitionSpec as P

D = 768
HDIM = 64
FF = 2048
SEQ = 128
PAIRS = 6
EPS = 1e-06
NEGATIVE = -1e30
ROOM_BYTES = 11 * 2**20
SCALE = HDIM ** (-0.5)
BF16 = jnp.bfloat16
F32 = jnp.float32
ANY = pl.BlockSpec(memory_space=pl.ANY)
FAST = pl.BlockSpec(memory_space=pltpu.VMEM)
SMEM = pl.BlockSpec(memory_space=pltpu.SMEM)


def mm(left, right):
    return jnp.dot(left, right, preferred_element_type=F32)


def mm_t(left, right):
    return lax.dot_general(left, right, (((1,), (1,)), ((), ())), preferred_element_type=F32)


def mm_w(left, right):
    return lax.dot_general(left, right, (((0,), (0,)), ((), ())), preferred_element_type=F32)


def halves(first, second):
    return jnp.concatenate([first, second], axis=0)


def rms(hidden, gain):
    inverse = lax.rsqrt(jnp.mean(hidden * hidden, axis=-1, keepdims=True) + EPS)
    return hidden * inverse * gain


def rms_back(hidden, gain, upstream):
    inverse = lax.rsqrt(jnp.mean(hidden * hidden, axis=-1, keepdims=True) + EPS)
    unit = hidden * inverse
    scaled = upstream * gain
    grad_gain = jnp.sum(upstream * unit, axis=0, keepdims=True)
    middle = jnp.mean(scaled * unit, axis=-1, keepdims=True)
    return inverse * (scaled - unit * middle), grad_gain


def gate_parts(gate, up):
    inner = 0.7978845608 * (gate + 0.044715 * gate * gate * gate)
    bend = jnp.tanh(inner)
    half = 0.5 * (1.0 + bend)
    value = gate * half
    slope = half + 0.5 * gate * (1.0 - bend * bend) * 0.7978845608 * (
        1.0 + 3.0 * 0.044715 * gate * gate
    )
    return value * up, slope * up, value


def lane_masks():
    lane = lax.broadcasted_iota(jnp.int32, (SEQ, 2 * HDIM), 1)
    low = jnp.where(lane < HDIM, 1.0, 0.0).astype(F32)
    return low.astype(BF16), (1.0 - low).astype(BF16), low


def stack_heads(pair, masks):
    return jnp.concatenate([pair * masks[0], pair * masks[1]], axis=0)


def attend(query, keys, values, allowed, masks):
    scores = mm_t(stack_heads(keys, masks), query) * SCALE
    scores = jnp.where(allowed, scores, NEGATIVE)
    parts = []
    for head in range(2):
        part = scores[head * SEQ : (head + 1) * SEQ]
        power = jnp.exp(part - jnp.max(part, axis=0, keepdims=True))
        parts.append(power * (1.0 / jnp.sum(power, axis=0, keepdims=True)))
    weights = jnp.concatenate(parts, axis=0).astype(BF16)
    return weights, mm_w(weights, stack_heads(values, masks)).astype(BF16)


def attend_back(query, keys, values, weights, upstream, masks):
    key_stack = stack_heads(keys, masks)
    grad_weights = mm_t(stack_heads(values, masks), upstream)
    wide = weights.astype(F32)
    product = wide * grad_weights
    parts = []
    for head in range(2):
        rows = slice(head * SEQ, (head + 1) * SEQ)
        total = jnp.sum(product[rows], axis=0, keepdims=True)
        parts.append(product[rows] - wide[rows] * total)
    grad_scores = jnp.concatenate(parts, axis=0).astype(BF16)
    grad_query = mm_w(grad_scores, key_stack) * SCALE
    key_both = mm(grad_scores, query) * SCALE
    value_both = mm(weights, upstream)
    low = masks[2]
    high = 1.0 - low
    grad_keys = key_both[:SEQ] * low + key_both[SEQ:] * high
    grad_values = value_both[:SEQ] * low + value_both[SEQ:] * high
    return grad_query.astype(BF16), grad_keys.astype(BF16), grad_values.astype(BF16)


def key_index_rows():
    return jnp.bitwise_and(lax.broadcasted_iota(jnp.int32, (2 * SEQ, SEQ), 0), SEQ - 1)


def kept(keep_ref, plot):
    row = keep_ref[pl.ds(plot, 1), :].astype(F32)
    return jnp.sum(row, axis=1, keepdims=True).astype(jnp.int32)


SECTION, PLACE, PLOT, TOKENS, COUNT = 0, 1, 2, 4, 6


def number(info, row):
    return jnp.max(info[row : row + 1, :].astype(F32)).astype(jnp.int32)


def rows_below(info, row):
    index = lax.broadcasted_iota(jnp.int32, (SEQ, D), 0)
    return index < jnp.broadcast_to(info[row : row + 1, 0:1], (SEQ, D))


class Copies:
    def __init__(self, sems):
        self.sems = sems
        self.count = 0

    def __call__(self, source, target):
        copy = pltpu.make_async_copy(source, target, self.sems.at[self.count])
        self.count += 1
        return copy


def start(copies):
    for copy in copies:
        copy.start()


def wait(copies):
    for copy in copies:
        copy.wait()


def struct(*shape, dtype=BF16):
    return jax.ShapeDtypeStruct(shape, dtype)


def call(kernel, scalars, out_shape, scratch, sems, name, arrays, fast=(), aliases=None, flops=0, traffic=0):
    return pl.pallas_call(
        kernel,
        name=name,
        in_specs=[SMEM] * len(scalars) + [ANY] * len(arrays) + [FAST] * len(fast),
        out_specs=[FAST if is_fast(item) else ANY for item in out_shape],
        out_shape=out_shape,
        scratch_shapes=[
            pltpu.VMEM(item.shape, item.dtype) if isinstance(item, jax.ShapeDtypeStruct) else item
            for item in scratch
        ]
        + [pltpu.SemaphoreType.DMA((sems,))],
        input_output_aliases=aliases or {},
        compiler_params=pltpu.CompilerParams(vmem_limit_bytes=ROOM_BYTES),
        cost_estimate=pl.CostEstimate(flops=flops, bytes_accessed=traffic, transcendentals=0),
    )(*scalars, *arrays, *[pltpu.with_memory_space_constraint(item, pltpu.VMEM) for item in fast])


def is_fast(item):
    return not isinstance(item, jax.ShapeDtypeStruct) and item.memory_space == pltpu.VMEM


def vmem(*shape, dtype=BF16):
    return pltpu.VMEM(shape, dtype)


def hbm(*shape, dtype=BF16):
    return pltpu.HBM(shape, dtype)


def slow(array):
    return pltpu.with_memory_space_constraint(array, pltpu.HBM)


def forward_kernel(slot, *refs):
    if slot == 0:
        section, place, slot_plot, table_len, gains, keep, acts, *given = refs[:12]
        (pack_o, qkv_o, p_o, h1_v, query_v, g1_o, g2_o, h2_o, send_v, memory_v, info, gains_v, acts_v, wqkv_v, wout_v, win_v, wdown_v, wcross_v) = refs[12:30]
        (pack_v, qkv_v, p_v, keep_v, plot_s, tokens_s, g1_v, g2_v, h2_v, sems) = refs[30:]
    else:
        cot, info, gains_v, acts_v, wqkv_v, wout_v, win_v, wdown_v, wcross_v = refs[:9]
        (pack_o, qkv_o, p_o, h1_v, query_v, g1_v, g2_v, h2_v, send_v, memory_v, cot_v) = refs[9:20]
        (pack_v, qkv_v, p_v, sems) = refs[20:]
    copies = Copies(sems)
    tile = 512
    get_qkv, get_in, get_out, get_down, get_cross, get_next = [], [], [], [], [], []
    if slot == 0:
        encoding = section[0] == 0
        get_small = [
            copies(slot_plot, plot_s),
            copies(table_len, tokens_s),
            copies(acts.at[0], acts_v),
            copies(gains, gains_v),
            copies(keep, keep_v),
        ]
        w_qkv, w_out, w_in, w_down, w_cross = given
        get_qkv = [
            copies(w_qkv.at[0, :, pl.ds(i * D, D)], wqkv_v.at[:, pl.ds(i * D, D)]) for i in range(3)
        ]
        get_out = [copies(w_out.at[0], wout_v)]
        for i in range(FF // tile):
            get_in += [
                copies(
                    w_in.at[0, :, pl.ds(base + i * tile, tile)],
                    win_v.at[:, pl.ds(base + i * tile, tile)],
                )
                for base in (0, FF)
            ]
        get_down = [copies(w_down.at[0], wdown_v)]
        get_cross = [copies(w_cross.at[0], wcross_v)]
        start(get_small + get_qkv + get_out + get_in + get_down + get_cross)
        wait(get_small)
        plots = [plot_s[0, i] for i in range(2)]
        numbers = [section[0], place[0], *plots, *[tokens_s[plot] for plot in plots]]
        for row, value in enumerate(numbers):
            info[row : row + 1, :] = jnp.broadcast_to(value, (1, 128)).astype(jnp.int32)
        for i in range(2):
            info[COUNT + i : COUNT + i + 1, :] = jnp.broadcast_to(kept(keep_v, plots[i]), (1, 128))
    else:
        encoding = number(info, SECTION) == 0
        plots = [None, number(info, PLOT + 1)]
        get_next = [copies(cot, cot_v)]
        start(get_next)
    masks = lane_masks()
    rows_in = acts_v[plots[slot]].astype(F32)
    normal = rms(rows_in, gains_v[0]).astype(BF16)
    pack_v[:, 0:D] = normal
    for i in range(3):
        wait(get_qkv[i : i + 1])
        qkv_v[:, i * D : (i + 1) * D] = mm(normal, wqkv_v[:, i * D : (i + 1) * D]).astype(BF16)
    puts = [copies(qkv_v, qkv_o)]
    puts[-1].start()
    put_slow = []
    if slot == 0:
        put_slow = [copies(g1_v, g1_o), copies(g2_v, g2_o), copies(h2_v, h2_o)]
    query_index = lax.broadcasted_iota(jnp.int32, (2 * SEQ, SEQ), 1)
    key_index = key_index_rows()
    count = info[COUNT + slot : COUNT + slot + 1, 0:1]
    limit = jnp.where(encoding, jnp.broadcast_to(count - 1, (2 * SEQ, SEQ)), query_index)
    allowed = key_index <= limit
    for pair in range(PAIRS):
        lanes = slice(pair * 128, (pair + 1) * 128)
        weights, mixed = attend(
            qkv_v[:, lanes],
            qkv_v[:, D + pair * 128 : D + (pair + 1) * 128],
            qkv_v[:, 2 * D + pair * 128 : 2 * D + (pair + 1) * 128],
            allowed,
            masks,
        )
        p_v[pair] = weights
        pack_v[:, D + pair * 128 : D + (pair + 1) * 128] = mixed
    puts.append(copies(p_v, p_o))
    puts[-1].start()
    wait(get_out)
    first = rows_in + mm(pack_v[:, D : 2 * D], wout_v[...])
    h1_v[...] = first
    normal = rms(first, gains_v[1]).astype(BF16)
    pack_v[:, 2 * D : 3 * D] = normal
    put_units = copies(pack_v.at[:, pl.ds(3 * D, FF)], pack_o.at[:, pl.ds(3 * D, FF)])
    puts.append(copies(pack_v.at[:, pl.ds(0, 3 * D)], pack_o.at[:, pl.ds(0, 3 * D)]))
    puts[-1].start()

    @pl.when(encoding)
    def _():
        inputs = pack_v[:, 2 * D : 3 * D]
        for i in range(FF // tile):
            wait(get_in[2 * i : 2 * i + 2])
            columns = slice(i * tile, (i + 1) * tile)
            gate = mm(inputs, win_v[:, columns])
            up = mm(inputs, win_v[:, FF + i * tile : FF + (i + 1) * tile])
            unit, to_gate, to_up = gate_parts(gate, up)
            pack_v[:, 3 * D + i * tile : 3 * D + (i + 1) * tile] = unit.astype(BF16)
            g1_v[:, columns] = to_gate.astype(BF16)
            g2_v[:, columns] = to_up.astype(BF16)
        put_units.start()
        start(put_slow[:2])
        wait(get_down)
        second = h1_v[...] + mm(pack_v[:, 3 * D :], wdown_v[...])
        h2_v[...] = second
        start(put_slow[2:])
        memory = rms(second, gains_v[2])
        memory = jnp.where(rows_below(info, COUNT + slot), memory, 0.0).astype(BF16)
        memory_v[...] = memory
        wait(get_cross)
        send_v[...] = mm(memory, wcross_v[...]).astype(BF16)
        put_units.wait()
        wait(put_slow)

    @pl.when(jnp.logical_not(encoding))
    def _():
        wait(get_cross)
        query_v[...] = mm(pack_v[:, 2 * D : 3 * D], wcross_v[:, 0:D]).astype(BF16)
        wait(get_in + get_down)

    wait(puts + get_next)


def forward(slot, scalars, arrays, fast):
    kind = (hbm, vmem)[slot]
    outs = [
        hbm(SEQ, 3 * D + FF),
        hbm(SEQ, 3 * D),
        hbm(PAIRS, 2 * SEQ, SEQ),
        vmem(SEQ, D, dtype=F32),
        vmem(SEQ, D),
        kind(SEQ, FF),
        kind(SEQ, FF),
        kind(SEQ, D, dtype=F32),
        vmem(SEQ, 2 * D),
        vmem(SEQ, D),
    ]
    scratch = [struct(SEQ, 3 * D + FF), struct(SEQ, 3 * D), struct(PAIRS, 2 * SEQ, SEQ)]
    if slot == 0:
        outs += [vmem(8, 128, dtype=jnp.int32), vmem(3, 1, D, dtype=F32), vmem(2, SEQ, D)]
        outs += [vmem(*weight.shape[1:]) for weight in arrays[5:]]
        scratch += [struct(2, SEQ, dtype=jnp.int32)]
        scratch += [pltpu.SMEM((1, 2), jnp.int32), pltpu.SMEM((2,), jnp.int32)]
        scratch += [struct(SEQ, FF), struct(SEQ, FF), struct(SEQ, D, dtype=F32)]
    else:
        outs += [vmem(2, SEQ, D)]
    return call(
        functools.partial(forward_kernel, slot), scalars, outs, scratch, 34, "forward",
        [slow(item) for item in arrays], fast,
    )


def turn_all(sources, results):
    for source, result in zip(sources, results):

        def step(i, carry):
            at = pl.ds(pl.multiple_of(i * 256, 256), 256)
            result[at, :] = source[:, at].T
            return carry

        lax.fori_loop(0, source.shape[1] // 256, step, 0)


def turn_kernel(count, *refs):
    turn_all(refs[1 : count + 1], refs[count + 1 : 2 * count + 1])


def turn(after, weights):
    return call(
        functools.partial(turn_kernel, len(weights)), [],
        [vmem(*weight.shape[::-1]) for weight in weights], [], 1, "turn", [after], weights,
    )


def turn_last_kernel(info, cot, wdownt, *refs):
    turn_all(refs[0:2], refs[2:4])
    units = refs[4]

    @pl.when(number(info, SECTION) == 1)
    def _():
        branch = halves(
            *[
                jnp.where(rows_below(info, TOKENS + i), cot[i].astype(F32), 0.0).astype(BF16)
                for i in range(2)
            ]
        )
        units[...] = mm(branch, wdownt[...])


def turn_last(fast):
    return call(
        turn_last_kernel, [],
        [vmem(3 * D, D), vmem(D, D), vmem(2 * SEQ, FF, dtype=F32)], [], 1, "turn_last", [], fast,
    )


def middle_kernel(slot, *refs):
    packs, refs = refs[: 2 * slot], refs[2 * slot :]
    info, units, gains_v, kv_v, h1_v, query_v, cot_v, win_v, wcross_v, wint_v, wcrosst_v = refs[:11]
    memory, refs = refs[11 : 11 + 2 * slot], refs[11 + 2 * slot :]
    pack_o, rhs_o, late_v, dkv_v, e2_o, de2_o, gain_o = refs[:7]
    lefts, refs = refs[7 : 7 + 2 * slot], refs[7 + 2 * slot :]
    pack_v, g1_v, g2_v, rhs_v, p_v, e2_v, de2_v, gain_v, mixed_v = refs[:9]
    held, sems = refs[9:-1], refs[-1]
    if slot == 1:

        @pl.when(number(info, SECTION) == 0)
        def _():
            copies = Copies(sems)
            get = [copies(source, target) for source, target in zip(packs, held)]
            start(get)
            wait(get)
            left_operands(0, number(info, PLACE), held, None, memory, lefts)

    @pl.when(number(info, SECTION) != 0)
    def _():
        copies = Copies(sems)
        tile = 512
        masks = lane_masks()
        count = info[COUNT + slot : COUNT + slot + 1, 0:1]
        allowed = key_index_rows() < jnp.broadcast_to(count, (2 * SEQ, SEQ))
        for pair in range(PAIRS):
            lanes = slice(pair * 128, (pair + 1) * 128)
            weights, mixed = attend(
                query_v[:, lanes],
                kv_v[:, lanes],
                kv_v[:, D + pair * 128 : D + (pair + 1) * 128],
                allowed,
                masks,
            )
            p_v[pair] = weights
            pack_v[:, D + pair * 128 : D + (pair + 1) * 128] = mixed
        second = h1_v[...] + mm(pack_v[:, D : 2 * D], wcross_v[:, D : 2 * D])
        e2_v[...] = second
        puts = [copies(e2_v, e2_o)]
        puts[-1].start()
        normal = rms(second, gains_v[2]).astype(BF16)
        pack_v[:, 0:D] = normal
        for i in range(FF // tile):
            columns = slice(i * tile, (i + 1) * tile)
            gate = mm(normal, win_v[:, columns])
            up = mm(normal, win_v[:, FF + i * tile : FF + (i + 1) * tile])
            unit, to_gate, to_up = gate_parts(gate, up)
            pack_v[:, 2 * D + i * tile : 2 * D + (i + 1) * tile] = unit.astype(BF16)
            g1_v[:, columns] = to_gate.astype(BF16)
            g2_v[:, columns] = to_up.astype(BF16)
        puts.append(copies(pack_v, pack_o))
        puts[-1].start()
        upstream = jnp.where(rows_below(info, TOKENS + slot), cot_v[slot].astype(F32), 0.0)
        branch = upstream.astype(BF16)
        rhs_v[:, 0:D] = branch
        for i in range(FF // tile):
            columns = slice(i * tile, (i + 1) * tile)
            grad_unit = units[slot * SEQ : (slot + 1) * SEQ, columns]
            rhs_v[:, D + i * tile : D + (i + 1) * tile] = (
                grad_unit * g1_v[:, columns].astype(F32)
            ).astype(BF16)
            rhs_v[:, D + FF + i * tile : D + FF + (i + 1) * tile] = (
                grad_unit * g2_v[:, columns].astype(F32)
            ).astype(BF16)
        puts.append(copies(rhs_v, rhs_o))
        puts[-1].start()
        grad_normal = mm(rhs_v[:, D : D + 2 * FF], wint_v[...])
        back, grad_gain = rms_back(second, gains_v[2], grad_normal)
        grad_second = upstream + back
        gain_v[...] = jnp.zeros_like(gain_v)
        gain_v[2:3, :] = grad_gain
        de2_v[...] = grad_second
        puts += [copies(de2_v, de2_o), copies(gain_v, gain_o)]
        start(puts[-2:])
        branch = grad_second.astype(BF16)
        late_v[:, D : 2 * D] = branch
        mixed_v[...] = mm(branch, wcrosst_v[D : 2 * D, :]).astype(BF16)
        for pair in range(PAIRS):
            lanes = slice(pair * 128, (pair + 1) * 128)
            high = slice(D + pair * 128, D + (pair + 1) * 128)
            grad_query, grad_keys, grad_values = attend_back(
                query_v[:, lanes], kv_v[:, lanes], kv_v[:, high], p_v[pair], mixed_v[:, lanes], masks
            )
            late_v[:, lanes] = grad_query
            dkv_v[:, lanes] = grad_keys
            dkv_v[:, high] = grad_values
        wait(puts)


def middle(slot, packs, fast):
    return call(
        functools.partial(middle_kernel, slot),
        [],
        [
            hbm(SEQ, 2 * D + FF),
            hbm(SEQ, D + 2 * FF),
            vmem(SEQ, 2 * D),
            vmem(SEQ, 2 * D),
            hbm(SEQ, D, dtype=F32),
            hbm(SEQ, D, dtype=F32),
            hbm(8, D, dtype=F32),
        ]
        + [vmem(3712, 256)] * (2 * slot),
        [
            struct(SEQ, 2 * D + FF),
            struct(SEQ, FF),
            struct(SEQ, FF),
            struct(SEQ, D + 2 * FF),
            struct(PAIRS, 2 * SEQ, SEQ),
            struct(SEQ, D, dtype=F32),
            struct(SEQ, D, dtype=F32),
            struct(8, D, dtype=F32),
            struct(SEQ, D),
        ]
        + [struct(*pack.shape) for pack in packs],
        8,
        "middle",
        [slow(pack) for pack in packs],
        fast,
    )


def outer_rows(slot, info, gains_v, dkv_v, h2_v, g1_v, g2_v, wdownt_v, wcrosst_v, rhs_v):
    rhs_v[:, D + 2 * FF :] = dkv_v[...]
    grad_memory = mm(dkv_v[...], wcrosst_v[...])
    grad_memory = jnp.where(rows_below(info, COUNT + slot), grad_memory, 0.0)
    grad_second, grad_gain = rms_back(h2_v[...], gains_v[2], grad_memory)
    branch = grad_second.astype(BF16)
    rhs_v[:, 0:D] = branch
    tile = 512
    for i in range(FF // tile):
        columns = slice(i * tile, (i + 1) * tile)
        grad_unit = mm(branch, wdownt_v[:, columns])
        for k, scale in ((0, g1_v), (1, g2_v)):
            first = D + k * FF + i * tile
            rhs_v[:, first : first + tile] = (grad_unit * scale[:, columns].astype(F32)).astype(BF16)
    return grad_second, grad_gain


def inner_rows(slot, info, gains_v, acts_v, h1_v, dn_v, up_v, qkv_v, p_v, woutt_v, wqkvt_v, rhs_v, grad_v):
    rows = slice(0, SEQ)
    plot = number(info, PLOT + slot)
    back, first_gain = rms_back(h1_v[...], gains_v[1], dn_v[...])
    grad_first = up_v[...] + back
    branch = grad_first.astype(BF16)
    rhs_v[rows, 0:D] = branch
    masks = lane_masks()
    grad_mixed = mm(branch, woutt_v[...]).astype(BF16)
    for pair in range(PAIRS):
        spans = [slice(k * D + pair * 128, k * D + (pair + 1) * 128) for k in range(3)]
        parts = attend_back(
            qkv_v[:, spans[0]],
            qkv_v[:, spans[1]],
            qkv_v[:, spans[2]],
            p_v[pair],
            grad_mixed[:, pair * 128 : (pair + 1) * 128],
            masks,
        )
        for k in range(3):
            rhs_v[rows, D + k * D + pair * 128 : D + k * D + (pair + 1) * 128] = parts[k]
    grad_normal = mm(rhs_v[rows, D : 4 * D], wqkvt_v[...])
    back, zeroth_gain = rms_back(acts_v[plot].astype(F32), gains_v[0], grad_normal)
    grad_v[0, plot] = grad_first + back
    return zeroth_gain, first_gain


def early_kernel(*refs):
    packs, (qkv, p, rhs2, de2, gain2, h2, g1, g2) = refs[0:4], refs[4:12]
    info, gains_v, acts_v, dkv_v, h1_v, late_v = refs[12:18]
    wqkvt_v, woutt_v, wint_v, wdownt_v, wcrosst_v, ready_v = refs[18:24]
    (kept_v, given_v, rhs3_v, rhs_v, gain_v, grad_v) = refs[24:30]
    held = refs[30:34]
    qkv_v, p_v, up_v, dn_v, gain2_v, h2_v, units_v, sems = refs[34:]
    g1_v, g2_v = units_v.at[0], units_v.at[1]
    encoding = number(info, SECTION) == 0
    copies = Copies(sems)
    get_rows = [copies(qkv, qkv_v), copies(p, p_v)]
    get_packs = [copies(source, target) for source, target in zip(packs, held)]
    get_rhs = copies(rhs2, rhs3_v.at[:, pl.ds(0, D + 2 * FF)])
    get_rest = [copies(de2, up_v), copies(gain2, gain2_v)]
    get_enc = [copies(h2, h2_v), copies(g1, g1_v), copies(g2, g2_v)]
    start(get_rows)

    @pl.when(encoding)
    def _():
        start(get_enc)
        wait(get_enc)
        grad_second, grad_gain = outer_rows(
            0, info, gains_v, dkv_v, h2_v, g1_v, g2_v, wdownt_v, wcrosst_v, rhs3_v
        )
        up_v[...] = grad_second
        gain2_v[2:3, :] = grad_gain
        given_v[...] = ready_v[...]
        dn_v[...] = mm(rhs3_v[:, D : D + 2 * FF], wint_v[...])

    @pl.when(jnp.logical_not(encoding))
    def _():
        start(get_packs + get_rest + [get_rhs])
        wait(get_packs)
        left_operands(1, number(info, PLACE), held[:2], held[2:], None, (kept_v, given_v))
        rhs3_v[:, D + 2 * FF :] = late_v[...]
        dn_v[...] = mm(late_v[:, 0:D], wcrosst_v[0:D, :])
        wait(get_rest)
        get_rhs.wait()

    wait(get_rows)
    zeroth_gain, first_gain = inner_rows(
        0, info, gains_v, acts_v, h1_v, dn_v, up_v, qkv_v, p_v, woutt_v, wqkvt_v, rhs_v, grad_v
    )
    gain_v[...] = jnp.concatenate(
        [zeroth_gain, first_gain, gain2_v[2:3, :], jnp.zeros((5, D), F32)], axis=0
    )


def early(arrays, fast):
    return call(
        early_kernel,
        [],
        [
            vmem(3712, 256),
            vmem(3712, 256),
            vmem(SEQ, 3 * D + 2 * FF),
            vmem(SEQ, 4 * D),
            vmem(8, D, dtype=F32),
            vmem(1, 2, SEQ, D, dtype=F32),
        ],
        [struct(*pack.shape) for pack in arrays[:4]]
        + [
            struct(SEQ, 3 * D),
            struct(PAIRS, 2 * SEQ, SEQ),
            struct(SEQ, D, dtype=F32),
            struct(SEQ, D, dtype=F32),
            struct(8, D, dtype=F32),
            struct(SEQ, D, dtype=F32),
            struct(2, SEQ, FF),
        ],
        14,
        "early",
        [slow(item) for item in arrays],
        fast,
    )


def outer_kernel(rhs2, after, info, gains_v, dkv_v, h2_v, g1_v, g2_v, late_v, wdownt_v, wcrosst_v, rhs_v, up_v, gain_v, sems):
    encoding = number(info, SECTION) == 0

    @pl.when(encoding)
    def _():
        grad_second, grad_gain = outer_rows(
            1, info, gains_v, dkv_v, h2_v, g1_v, g2_v, wdownt_v, wcrosst_v, rhs_v
        )
        up_v[...] = grad_second
        gain_v[2:3, :] = grad_gain

    @pl.when(jnp.logical_not(encoding))
    def _():
        get = Copies(sems)(rhs2, rhs_v.at[:, pl.ds(0, D + 2 * FF)])
        get.start()
        rhs_v[:, D + 2 * FF :] = late_v[...]
        get.wait()


def outer(rhs2, after, fast):
    return call(
        outer_kernel,
        [],
        [vmem(SEQ, 3 * D + 2 * FF), vmem(SEQ, D, dtype=F32), vmem(8, D, dtype=F32)],
        [],
        1,
        "outer",
        [slow(rhs2), after],
        fast,
    )


def inner_kernel(*refs):
    qkv, p, de2, gain2 = refs[:4]
    info, gains_v, acts_v, h1_v, rhs3_v, dh2_v, gain3_v, before_v = refs[4:12]
    wqkvt_v, woutt_v, wint_v, wcrosst_v = refs[12:16]
    (rhs_v, grad_v, qkv_v, p_v, up_v, dn_v, gain2_v, sems) = refs[17:]
    encoding = number(info, SECTION) == 0
    copies = Copies(sems)
    get_rows = [copies(qkv, qkv_v), copies(p, p_v)]
    get_dec = [
        copies(de2, up_v),
        copies(gain2, gain2_v),
    ]
    start(get_rows)

    @pl.when(encoding)
    def _():
        dn_v[...] = mm(rhs3_v[:, D : D + 2 * FF], wint_v[...])
        up_v[...] = dh2_v[...]
        gain2_v[...] = gain3_v[...]

    @pl.when(jnp.logical_not(encoding))
    def _():
        start(get_dec)
        dn_v[...] = mm(rhs3_v[:, D + 2 * FF : 2 * D + 2 * FF], wcrosst_v[0:D, :])
        wait(get_dec)

    wait(get_rows)
    zeroth_gain, first_gain = inner_rows(
        1, info, gains_v, acts_v, h1_v, dn_v, up_v, qkv_v, p_v, woutt_v, wqkvt_v, rhs_v, grad_v
    )
    total = before_v[...] + jnp.concatenate(
        [zeroth_gain, first_gain, gain2_v[2:3, :], jnp.zeros((5, D), F32)], axis=0
    )
    upper = total.astype(BF16)
    lower = (total - upper.astype(F32)).astype(BF16)
    rhs_v[SEQ:, 0:D] = halves(upper, lower)
    rhs_v[SEQ:, D : 4 * D] = jnp.zeros((16, 3 * D), BF16)


def inner(arrays, fast):
    return call(
        inner_kernel,
        [],
        [vmem(SEQ + 16, 4 * D), vmem(1, 2, SEQ, D, dtype=F32)],
        [
            struct(SEQ, 3 * D),
            struct(PAIRS, 2 * SEQ, SEQ),
            struct(SEQ, D, dtype=F32),
            struct(SEQ, D, dtype=F32),
            struct(8, D, dtype=F32),
        ],
        8,
        "inner",
        [slow(item) for item in arrays],
        fast,
        aliases={len(arrays) + 12: 1},
    )


def output_kernel(*refs):
    pack2, e2 = refs[0:2], refs[2:4]
    info, memory, wdownt_v, out_o, out_v, z_v, e2_v, sems = refs[4], *[refs[5:7]], *refs[7:]
    encoding = number(info, SECTION) == 0
    copies = Copies(sems)
    get = []
    for i in range(2):
        at = pl.ds(i * SEQ, SEQ)
        get += [copies(pack2[i].at[:, pl.ds(2 * D, FF)], z_v.at[at]), copies(e2[i], e2_v.at[at])]

    @pl.when(encoding)
    def _():
        for i in range(2):
            out_v[0, i] = memory[i][...]

    @pl.when(jnp.logical_not(encoding))
    def _():
        start(get)
        wait(get)
        third = e2_v[...] + mm_t(z_v[...], wdownt_v[...])
        for i in range(2):
            part = third[i * SEQ : (i + 1) * SEQ]
            out_v[0, i] = jnp.where(rows_below(info, TOKENS + i), part, 0.0).astype(BF16)

    put = copies(out_v, out_o)
    put.start()
    put.wait()


def output(arrays, after, fast):
    def kernel(*refs):
        output_kernel(*refs[len(after) :])

    return call(
        kernel,
        [],
        [struct(1, 2, SEQ, D)],
        [struct(1, 2, SEQ, D), struct(2 * SEQ, FF), struct(2 * SEQ, D, dtype=F32)],
        5,
        "output",
        after + [slow(item) for item in arrays],
        fast,
    )[0]


def place_parts(place):
    return (
        lax.shift_right_logical(place, 5),
        jnp.bitwise_and(lax.shift_right_logical(place, 3), 3),
        jnp.bitwise_and(lax.shift_right_logical(place, 1), 3),
        jnp.bitwise_and(place, 1),
    )


def matching(target, columns):
    rows = target.shape[0]
    lane = lax.broadcasted_iota(jnp.int32, (rows, 128), 1)
    blocks = [jnp.where(lane + i * 128 == target, 1.0, 0.0) for i in range(columns // 128)]
    return jnp.concatenate(blocks, axis=1).astype(BF16)


def selector(place, other=0):
    y, x, z, core = place_parts(place)
    core = jnp.bitwise_xor(core, other)
    index = lax.broadcasted_iota(jnp.int32, (384, 128), 0)

    def at_least(value, *bounds):
        return sum(jnp.where(value >= bound, 1, 0) for bound in bounds)

    first = at_least(index, 96, 192, 288)
    rest = index - first * 96
    second = at_least(rest, 24, 48, 72)
    rest = rest - second * 24
    third = at_least(rest, 12)
    rest = rest - third * 12
    to_z, to_x = first, second
    return matching(
        jnp.bitwise_and(y + third, 1) * 384
        + jnp.bitwise_and(x + to_x, 3) * 96
        + jnp.bitwise_and(z + to_z, 3) * 24
        + core * 12
        + rest,
        D,
    )


def stacked(sources, first, width):
    return jnp.concatenate([source[0:SEQ, first : first + width] for source in sources], axis=0)


def along_down(place, other):
    y, x, z, core = place_parts(place)
    core = jnp.bitwise_xor(core, other)
    index = lax.broadcasted_iota(jnp.int32, (256, 128), 0)
    return matching(
        jnp.bitwise_and(y + jnp.bitwise_and(lax.shift_right_logical(index, 5), 1), 1) * 256
        + jnp.bitwise_and(z + lax.shift_right_logical(index, 6), 3) * 64
        + core * 32
        + jnp.bitwise_and(index, 31),
        512,
    )


def prepare_down(place, sources, first, result, order):
    y, x, z, core = place_parts(place)
    for chunk in range(4):
        block = first + jnp.bitwise_and(x + chunk, 3) * 256
        columns = [pl.ds(pl.multiple_of(block + half, 256), 256) for half in (0, 1024)]
        picked = jnp.concatenate(
            [jnp.concatenate([source[:, at] for source in sources], axis=0) for at in columns],
            axis=1,
        )
        at = 2688 + 256 * chunk
        result[at : at + 256, :] = mm_t(order, picked).astype(BF16)


def x_first(rows):
    blocks = [rows[(z * 4 + x) * 24 : (z * 4 + x + 1) * 24] for x in range(4) for z in range(4)]
    return jnp.concatenate(blocks, axis=0)


def left_operands(which, place, pack1, pack2, memory, results):
    last = pack2 if which else pack1
    for other, result in enumerate(results):
        along_z = selector(place, other)
        steps = (
            (384, 0, pack1, 0),
            (768, None, pack1, D),
            (1536, 1152, last, 0 if which else 2 * D),
            (1920, None, pack1 if which else memory, 2 * D if which else 0),
            (2304, None, last if which else memory, D if which else 0),
        )
        for row, row_x, sources, first in steps:
            rows = mm_t(along_z, stacked(sources, first, D))
            result[row : row + 384, :] = rows.astype(BF16)
            if row_x is not None:
                result[row_x : row_x + 384, :] = x_first(rows).astype(BF16)
        prepare_down(place, last, 2 * D if which else 3 * D, result, along_down(place, other))


class Buffers:
    def __init__(self, refs, size):
        self.own, self.ahead, self.behind, self.one, self.three = refs
        self.size = size

    def spot(self, chunk, block):
        quarter = self.size // 4
        half = self.size // 2
        row = block * quarter
        if chunk == 0:
            return self.own, row
        low = block < 2
        if chunk == 1:
            return (self.one, row) if low else (self.ahead, row)
        if chunk == 2:
            return (self.ahead, row) if low else (self.behind, row - half)
        return (self.behind, half + row) if low else (self.three, row - half)


def buffer_shapes(size):
    return [struct(size, 128)] * 3 + [struct(size // 2, 128)] * 2


def store_narrow(buffers, grad, offset):
    for chunk in range(4):
        for block in range(4):
            rows = grad[(chunk * 4 + block) * 24 : (chunk * 4 + block + 1) * 24]
            piece = jnp.concatenate([rows[:, 0:128], rows[:, 128:256]], axis=0).astype(BF16)
            target, row = buffers.spot(chunk, block)
            target[row + offset : row + offset + 48, :] = piece


QKV_X = 5
SIZE_X, SIZE_Z = 4 * (768 + 48 * QKV_X), 4 * (1296 - 48 * QKV_X)
OUT_ROW = 672 + 48 * (9 - QKV_X)


def both_sides(lefts, first, count):
    return jnp.concatenate([left[first : first + count, :] for left in lefts], axis=1)


def right_of(sources, first, width=256):
    return stacked(sources, first, width)


def grads_wide_kernel(lefts, wide, results):
    held = Buffers(results[:5], SIZE_X), Buffers(results[5:], SIZE_Z)
    branch = right_of(wide, 0, D)
    for chunk in range(4):
        grad = mm(both_sides(lefts, 2688 + 256 * chunk, 256), branch)
        for block in range(4):
            target, row = held[0].spot(chunk, block)
            for i in range(6):
                spot = row + 384 + 64 * i
                target[spot : spot + 64, :] = grad[
                    64 * block : 64 * (block + 1), 128 * i : 128 * (i + 1)
                ].astype(BF16)
    for i in range(6):
        left = both_sides(lefts, 1920 if i < 3 else 2304, 384)
        store_narrow(held[1], mm(left, right_of(wide, D + 2 * FF + 256 * i)), 384 + 48 * i)
    for axis in range(2):
        left = both_sides(lefts, 1152 + 384 * axis, 384)
        for i in range(8):
            grad = mm(left, right_of(wide, D + axis * FF + 256 * i))
            store_narrow(held[axis], grad, 48 * i)


def grads_thin_kernel(place, lefts, thin, results):
    held = Buffers(results[:5], SIZE_X), Buffers(results[5:], SIZE_Z)
    total_of = selector(place)
    total = sum(
        item[row : row + 8, 0:D].astype(F32) for item in (thin[1], thin[3]) for row in (SEQ, SEQ + 8)
    )
    upper = total.astype(BF16)
    lower = (total - upper.astype(F32)).astype(BF16)
    ordered = mm_t(upper, total_of) + mm_t(lower, total_of)
    tall = jnp.concatenate([ordered, jnp.zeros((120, 384), F32)], axis=0).T
    tall = jnp.concatenate([tall, jnp.zeros((384, 128), F32)], axis=1)
    store_narrow(held[1], tall, OUT_ROW + 144)
    for i in range(9):
        axis = 0 if i < QKV_X else 1
        grad = mm(both_sides(lefts, 384 * axis, 384), right_of(thin, D + 256 * i))
        store_narrow(held[axis], grad, 672 + 48 * (i - QKV_X) if axis else 768 + 48 * i)
    for i in range(3):
        grad = mm(both_sides(lefts, 768, 384), right_of(thin, 256 * i))
        store_narrow(held[1], grad, OUT_ROW + 48 * i)


def grads(thin, info, lefts, right, before):
    shapes = [vmem(*item.shape) for item in buffer_shapes(SIZE_X) + buffer_shapes(SIZE_Z)]

    def kernel(info, *refs):
        encoding = number(info, SECTION) == 0
        results = refs[-11:-1]

        def run(lefts):
            if thin:
                grads_thin_kernel(number(info, PLACE), lefts, refs[3:7], results)
            else:
                grads_wide_kernel(lefts, refs[3:7], results)

        @pl.when(encoding)
        def _():
            run((refs[0], refs[2]))

        @pl.when(jnp.logical_not(encoding))
        def _():
            run(refs[1:3])

    return call(
        kernel, [], shapes, [], 1, "grads", [], [info, *lefts, *right, *before],
        aliases={8 + i: i for i in range(len(before))},
    )


RUNS_X = ((0, 16, 12), (384, 6, 32), (768, 2 * QKV_X, 12))
RUNS_Z = ((0, SIZE_Z // 96, 12),)


def rows_for_y(runs):
    return -(-sum(tiles * rows for _, tiles, rows in runs) // 16) * 16


def combine_kernel(runs, total, *refs):
    got, (last, sent, line_v) = refs[:3], refs[3:]
    size = last.shape[0]
    last[...] = total[0:size, :].astype(F32) + sum(item[...].astype(F32) for item in got)
    line_v[...] = jnp.zeros_like(line_v)
    to = 0
    for first, tiles, rows in runs:
        if rows == 12:
            for at in range(12):
                line_v[to : to + tiles, :] = last[pl.ds(first + 12 + at, tiles, stride=24), :]
                to += tiles
        else:
            for tile in range(tiles):
                line_v[to : to + rows, :] = last[first + (2 * tile + 1) * rows : first + (2 * tile + 2) * rows, :]
                to += rows
    sent[...] = line_v[...].astype(BF16)


def combine(runs, total, got, after):
    size, rows = got[0].shape[0], rows_for_y(runs)

    def kernel(*refs):
        combine_kernel(runs, *refs[len(after) :])

    return pl.pallas_call(
        kernel,
        name="combine",
        in_specs=[ANY] * len(after) + [FAST] * 4,
        out_specs=[FAST] * 2,
        out_shape=[vmem(size, 128, dtype=F32), vmem(rows, 128)],
        scratch_shapes=[pltpu.VMEM((rows, 128), F32)],
        compiler_params=pltpu.CompilerParams(vmem_limit_bytes=ROOM_BYTES),
    )(*after, *[pltpu.with_memory_space_constraint(item, pltpu.VMEM) for item in (total, *got)])


def finish_kernel(own_x, own_z, sent_x, sent_z, qkv_o, out_o, in_o, cross_o, down_o, gains_o, got_x, got_z, tall_v):
    got_x[...] = sent_x[...].astype(F32)
    got_z[...] = sent_z[...].astype(F32)

    def lay(own, got, first, got_first, tiles, parts):
        for at in range(12):
            line = own[pl.ds(first + at, tiles, stride=24), :]
            line = line + got[got_first + at * tiles : got_first + (at + 1) * tiles, :]
            tile = 0
            for result, column, count in parts:
                for i in range(count):
                    to = column + 128 * i
                    result[at, :, to : to + 128] = line[tile : tile + 1, :]
                    tile += 1

    lay(own_x, got_x, 0, 0, 16, ((in_o, 0, 16),))
    for tile in range(6):
        columns = slice(128 * tile, 128 * (tile + 1))
        down_o[:, columns] = (
            own_x[384 + 64 * tile : 416 + 64 * tile, :] + got_x[192 + 32 * tile : 224 + 32 * tile, :]
        )
    lay(own_x, got_x, 768, 384, 2 * QKV_X, ((qkv_o, 0, 2 * QKV_X),))
    tiles = RUNS_Z[0][1]
    parts = (
        (in_o, FF, 16),
        (cross_o, 0, 12),
        (qkv_o, 256 * QKV_X, 18 - 2 * QKV_X),
        (out_o, 0, 6),
    )
    lay(own_z, got_z, 0, 0, tiles, parts)
    tall_v[...] = jnp.zeros_like(tall_v)
    row = OUT_ROW + 144
    tall_v[0:12, :] = own_z[row : row + 12, :] + got_z[pl.ds(row // 24, 12, stride=tiles), :]
    tall = tall_v[...].T
    for i in range(3):
        gains_o[i] = tall[i : i + 1, 0:12]


def finish(own_x, own_z, got_x, got_z):
    shapes = [
        struct(12, 1, 3 * D, dtype=F32),
        struct(12, 1, D, dtype=F32),
        struct(12, 1, 2 * FF, dtype=F32),
        struct(12, 1, 2 * D, dtype=F32),
        struct(32, D, dtype=F32),
        struct(3, 1, 12, dtype=F32),
    ]
    given = (own_x, own_z, got_x, got_z)
    return pl.pallas_call(
        finish_kernel,
        name="finish",
        in_specs=[FAST] * 4,
        out_specs=[FAST] * 6,
        out_shape=shapes,
        scratch_shapes=[
            pltpu.VMEM(got_x.shape, F32),
            pltpu.VMEM(got_z.shape, F32),
            pltpu.VMEM((128, 128), F32),
        ],
        compiler_params=pltpu.CompilerParams(vmem_limit_bytes=ROOM_BYTES),
    )(*[pltpu.with_memory_space_constraint(item, pltpu.VMEM) for item in given])


def flat(y, x, z, core):
    return ((y * 4 + x) * 4 + z) * 2 + core


def shifted(array, y=0, x=0, z=0, core=0):
    pairs = []
    for a in range(2):
        for b in range(4):
            for c in range(4):
                for d in range(2):
                    source = flat(a, b, c, d)
                    target = flat((a + y) % 2, (b + x) % 4, (c + z) % 4, (d + core) % 2)
                    pairs.append((source, target))
    return lax.ppermute(array, "dp", pairs)


def add(*terms):
    total = terms[0].astype(F32)
    for term in terms[1:]:
        total = total + term.astype(F32)
    return total


def first_round(buffers, axis):
    own, ahead, behind, one, three = buffers
    return shifted(ahead, **{axis: 1}), shifted(behind, **{axis: 3})


def second_round(buffers, firsts, axis):
    own, ahead, behind, one, three = buffers
    got_ahead, got_behind = firsts
    half = one.shape[0]
    last_ahead = shifted(add(one, got_ahead[:half]).astype(BF16), **{axis: 1})
    last_behind = shifted(add(three, got_behind[:half]).astype(BF16), **{axis: 3})
    low = add(own[:half], last_ahead, got_behind[half:])
    high = add(own[half:], got_ahead[half:], last_behind)
    return jnp.concatenate([low, high], axis=0).astype(BF16)


def along_one_round(total, axis):
    size = total.shape[0] // 4
    return [
        shifted(total[step * size : (step + 1) * size], **{axis: step}) for step in (2, 1, 3)
    ]


def local(
    acts,
    gains,
    qkv_weight,
    out_weight,
    mlp_in,
    mlp_out,
    cross_weight,
    patch_mask,
    table_len,
    slot_plot,
    cotangent,
):
    section = lax.axis_index("section").astype(jnp.int32).reshape(1)
    place = lax.axis_index("dp").astype(jnp.int32).reshape(1)
    gains = gains.transpose(1, 0, 2)
    weights = (qkv_weight, out_weight, mlp_in, mlp_out, cross_weight)
    made = [
        forward(0, [section, place], [slot_plot, table_len, gains, patch_mask, acts, *weights], [])
    ]
    info, gains, acts, *weights = made[0][10:]
    received = [lax.ppermute(made[0][8], "section", [(0, 1)])]
    made.append(forward(1, [], [cotangent], [info, gains, acts, *weights]))
    received.append(lax.ppermute(made[1][8], "section", [(0, 1)]))
    cot = made[1][10]
    turned = turn(slow(made[1][1]), weights[2:])
    *last, units = turn_last([info, cot, turned[1], *weights[:2]])
    turned = [*last, *turned]
    middles = []
    back = []
    memory = [item[9] for item in made]
    packs = [item[0] for item in made]
    for slot in range(2):
        h1, query = made[slot][3:5]
        middles.append(
            middle(
                slot,
                packs * slot,
                [info, units, gains, received[slot], h1, query, cot, weights[2], weights[4],
                 turned[2], turned[4], *memory * slot],
            )
        )
        back.append(lax.ppermute(middles[slot][3], "section", [(1, 0)]))
    lefts = [middles[1][7]]
    pack1, qkv, p, h1, query, g1, g2, h2 = made[0][:8]
    pack2, rhs2, late, _, e2, de2, gain2 = middles[0]
    kept_left, given_left, wide0, thin0, gain, grad_chain = early(
        [*packs, pack2, middles[1][0], qkv, p, rhs2, de2, gain2, h2, g1, g2],
        [info, gains, acts, back[0], h1, late, *turned, middles[1][8]],
    )
    lefts += [kept_left, shifted(given_left, core=1)]
    pack1, qkv, p, h1, query, g1, g2, h2 = made[1][:8]
    pack2, rhs2, late, _, e2, de2, gain2 = middles[1][:7]
    wide1, dh2, gain3 = outer(
        rhs2, gain, [info, gains, back[1], h2, g1, g2, late, turned[3], turned[4]]
    )
    wide = [wide0, wide1, shifted(wide0, core=1), shifted(wide1, core=1)]
    thin1, grad_chain = inner(
        [qkv, p, de2, gain2],
        [info, gains, acts, h1, wide1, dh2, gain3, gain, *turned[:3], turned[4], grad_chain],
    )
    thin = [thin0, thin1, shifted(thin0, core=1), shifted(thin1, core=1)]
    part = grads(False, info, lefts, wide, [])
    part = grads(True, info, lefts, thin, part)
    firsts_x, firsts_z = first_round(part[:5], "x"), first_round(part[5:], "z")
    out_rows = output(
        [middles[0][0], middles[1][0], middles[0][4], middles[1][4]],
        [part[3]],
        [info, *memory, turned[3]],
    )
    firsts_x, out_rows = lax.optimization_barrier((firsts_x, out_rows))
    total_x = second_round(part[:5], firsts_x, "x")
    total_z = second_round(part[5:], firsts_z, "z")
    last_x, sent_x = combine(RUNS_X, total_x, along_one_round(total_x, "z"), [])
    got_x = shifted(sent_x, y=1)
    last_z, sent_z = combine(RUNS_Z, total_z, along_one_round(total_z, "x"), [got_x])
    grad_qkv, grad_out, grad_mlp_in, grad_cross, grad_mlp_out, grad_gains = finish(
        last_x, last_z, got_x, shifted(sent_z, y=1)
    )
    return (
        out_rows,
        grad_chain,
        grad_gains.transpose(1, 0, 2),
        grad_qkv.transpose(1, 0, 2),
        grad_out.transpose(1, 0, 2),
        grad_mlp_in.transpose(1, 0, 2),
        grad_mlp_out[None],
        grad_cross.transpose(1, 0, 2),
    )


def solution(mesh):
    return jax.shard_map(
        local,
        mesh=mesh,
        in_specs=(
            P("section", "dp", None, None),
            P("section", None, None),
            P("section", None, None),
            P("section", None, None),
            P("section", None, None),
            P("section", None, None),
            P("section", None, None),
            P("dp", None),
            P("dp"),
            P("dp", None),
            P("dp", None, None),
        ),
        out_specs=(
            P("section", "dp", None, None),
            P("section", "dp", None, None),
            P("section", None, "dp"),
            P("section", "dp", None),
            P("section", "dp", None),
            P("section", "dp", None),
            P("section", "dp", None),
            P("section", "dp", None),
        ),
        check_vma=False,
    )
```

```python
import functools

import jax
import jax.numpy as jnp
from jax import lax
from jax.experimental import pallas as pl
from jax.experimental.pallas import tpu as pltpu
from jax.sharding import PartitionSpec as P

D = 768
HDIM = 64
FF = 2048
SEQ = 128
PAIRS = 6
EPS = 1e-06
NEGATIVE = -1e30
ROOM_BYTES = 11 * 2**20
SCALE = HDIM ** (-0.5)
BF16 = jnp.bfloat16
F32 = jnp.float32
ANY = pl.BlockSpec(memory_space=pl.ANY)
FAST = pl.BlockSpec(memory_space=pltpu.VMEM)
SMEM = pl.BlockSpec(memory_space=pltpu.SMEM)


def mm(left, right):
    return jnp.dot(left, right, preferred_element_type=F32)


def mm_t(left, right):
    return lax.dot_general(left, right, (((1,), (1,)), ((), ())), preferred_element_type=F32)


def mm_w(left, right):
    return lax.dot_general(left, right, (((0,), (0,)), ((), ())), preferred_element_type=F32)


def halves(first, second):
    return jnp.concatenate([first, second], axis=0)


def rms(hidden, gain):
    inverse = lax.rsqrt(jnp.mean(hidden * hidden, axis=-1, keepdims=True) + EPS)
    return hidden * inverse * gain


def rms_back(hidden, gain, upstream):
    inverse = lax.rsqrt(jnp.mean(hidden * hidden, axis=-1, keepdims=True) + EPS)
    unit = hidden * inverse
    scaled = upstream * gain
    grad_gain = jnp.sum(upstream * unit, axis=0, keepdims=True)
    middle = jnp.mean(scaled * unit, axis=-1, keepdims=True)
    return inverse * (scaled - unit * middle), grad_gain


def gate_parts(gate, up):
    inner = 0.7978845608 * (gate + 0.044715 * gate * gate * gate)
    bend = jnp.tanh(inner)
    half = 0.5 * (1.0 + bend)
    value = gate * half
    slope = half + 0.5 * gate * (1.0 - bend * bend) * 0.7978845608 * (
        1.0 + 3.0 * 0.044715 * gate * gate
    )
    return value * up, slope * up, value


def lane_masks():
    lane = lax.broadcasted_iota(jnp.int32, (SEQ, 2 * HDIM), 1)
    low = jnp.where(lane < HDIM, 1.0, 0.0).astype(F32)
    return low.astype(BF16), (1.0 - low).astype(BF16), low


def stack_heads(pair, masks):
    return jnp.concatenate([pair * masks[0], pair * masks[1]], axis=0)


def attend(query, keys, values, allowed, masks):
    scores = mm_t(stack_heads(keys, masks), query) * SCALE
    scores = jnp.where(allowed, scores, NEGATIVE)
    parts = []
    for head in range(2):
        part = scores[head * SEQ : (head + 1) * SEQ]
        power = jnp.exp(part - jnp.max(part, axis=0, keepdims=True))
        parts.append(power * (1.0 / jnp.sum(power, axis=0, keepdims=True)))
    weights = jnp.concatenate(parts, axis=0).astype(BF16)
    return weights, mm_w(weights, stack_heads(values, masks)).astype(BF16)


def attend_back(query, keys, values, weights, upstream, masks):
    key_stack = stack_heads(keys, masks)
    grad_weights = mm_t(stack_heads(values, masks), upstream)
    wide = weights.astype(F32)
    product = wide * grad_weights
    parts = []
    for head in range(2):
        rows = slice(head * SEQ, (head + 1) * SEQ)
        total = jnp.sum(product[rows], axis=0, keepdims=True)
        parts.append(product[rows] - wide[rows] * total)
    grad_scores = jnp.concatenate(parts, axis=0).astype(BF16)
    grad_query = mm_w(grad_scores, key_stack) * SCALE
    key_both = mm(grad_scores, query) * SCALE
    value_both = mm(weights, upstream)
    low = masks[2]
    high = 1.0 - low
    grad_keys = key_both[:SEQ] * low + key_both[SEQ:] * high
    grad_values = value_both[:SEQ] * low + value_both[SEQ:] * high
    return grad_query.astype(BF16), grad_keys.astype(BF16), grad_values.astype(BF16)


def key_index_rows():
    return jnp.bitwise_and(lax.broadcasted_iota(jnp.int32, (2 * SEQ, SEQ), 0), SEQ - 1)


def kept(keep_ref, plot):
    row = keep_ref[pl.ds(plot, 1), :].astype(F32)
    return jnp.sum(row, axis=1, keepdims=True).astype(jnp.int32)


SECTION, PLACE, PLOT, TOKENS, COUNT = 0, 1, 2, 4, 6


def number(info, row):
    return jnp.max(info[row : row + 1, :].astype(F32)).astype(jnp.int32)


def rows_below(info, row):
    index = lax.broadcasted_iota(jnp.int32, (SEQ, D), 0)
    return index < jnp.broadcast_to(info[row : row + 1, 0:1], (SEQ, D))


class Copies:
    def __init__(self, sems):
        self.sems = sems
        self.count = 0

    def __call__(self, source, target):
        copy = pltpu.make_async_copy(source, target, self.sems.at[self.count])
        self.count += 1
        return copy


def start(copies):
    for copy in copies:
        copy.start()


def wait(copies):
    for copy in copies:
        copy.wait()


def struct(*shape, dtype=BF16):
    return jax.ShapeDtypeStruct(shape, dtype)


def call(kernel, scalars, out_shape, scratch, sems, name, arrays, fast=(), aliases=None, flops=0, traffic=0):
    return pl.pallas_call(
        kernel,
        name=name,
        in_specs=[SMEM] * len(scalars) + [ANY] * len(arrays) + [FAST] * len(fast),
        out_specs=[FAST if is_fast(item) else ANY for item in out_shape],
        out_shape=out_shape,
        scratch_shapes=[
            pltpu.VMEM(item.shape, item.dtype) if isinstance(item, jax.ShapeDtypeStruct) else item
            for item in scratch
        ]
        + [pltpu.SemaphoreType.DMA((sems,))],
        input_output_aliases=aliases or {},
        compiler_params=pltpu.CompilerParams(vmem_limit_bytes=ROOM_BYTES),
        cost_estimate=pl.CostEstimate(flops=flops, bytes_accessed=traffic, transcendentals=0),
    )(*scalars, *arrays, *[pltpu.with_memory_space_constraint(item, pltpu.VMEM) for item in fast])


def is_fast(item):
    return not isinstance(item, jax.ShapeDtypeStruct) and item.memory_space == pltpu.VMEM


def vmem(*shape, dtype=BF16):
    return pltpu.VMEM(shape, dtype)


def hbm(*shape, dtype=BF16):
    return pltpu.HBM(shape, dtype)


def slow(array):
    return pltpu.with_memory_space_constraint(array, pltpu.HBM)


def forward_kernel(slot, *refs):
    if slot == 0:
        section, place, slot_plot, table_len, gains, keep, acts, *given = refs[:12]
        (pack_o, qkv_o, p_o, h1_v, query_v, g1_o, g2_o, h2_o, send_v, memory_v, info, gains_v, acts_v, wqkv_v, wout_v, win_v, wdown_v, wcross_v) = refs[12:30]
        (pack_v, qkv_v, p_v, keep_v, plot_s, tokens_s, g1_v, g2_v, h2_v, sems) = refs[30:]
    else:
        cot, info, gains_v, acts_v, wqkv_v, wout_v, win_v, wdown_v, wcross_v = refs[:9]
        (pack_o, qkv_o, p_o, h1_v, query_v, g1_v, g2_v, h2_v, send_v, memory_v, cot_v) = refs[9:20]
        (pack_v, qkv_v, p_v, sems) = refs[20:]
    copies = Copies(sems)
    tile = 512
    get_qkv, get_in, get_out, get_down, get_cross, get_next = [], [], [], [], [], []
    if slot == 0:
        encoding = section[0] == 0
        get_small = [
            copies(slot_plot, plot_s),
            copies(table_len, tokens_s),
            copies(acts.at[0], acts_v),
            copies(gains, gains_v),
            copies(keep, keep_v),
        ]
        w_qkv, w_out, w_in, w_down, w_cross = given
        get_qkv = [
            copies(w_qkv.at[0, :, pl.ds(i * D, D)], wqkv_v.at[:, pl.ds(i * D, D)]) for i in range(3)
        ]
        get_out = [copies(w_out.at[0], wout_v)]
        for i in range(FF // tile):
            get_in += [
                copies(
                    w_in.at[0, :, pl.ds(base + i * tile, tile)],
                    win_v.at[:, pl.ds(base + i * tile, tile)],
                )
                for base in (0, FF)
            ]
        get_down = [copies(w_down.at[0], wdown_v)]
        get_cross = [copies(w_cross.at[0], wcross_v)]
        start(get_small + get_qkv + get_out + get_in + get_down + get_cross)
        wait(get_small)
        plots = [plot_s[0, i] for i in range(2)]
        numbers = [section[0], place[0], *plots, *[tokens_s[plot] for plot in plots]]
        for row, value in enumerate(numbers):
            info[row : row + 1, :] = jnp.broadcast_to(value, (1, 128)).astype(jnp.int32)
        for i in range(2):
            info[COUNT + i : COUNT + i + 1, :] = jnp.broadcast_to(kept(keep_v, plots[i]), (1, 128))
    else:
        encoding = number(info, SECTION) == 0
        plots = [None, number(info, PLOT + 1)]
        get_next = [copies(cot, cot_v)]
        start(get_next)
    masks = lane_masks()
    rows_in = acts_v[plots[slot]].astype(F32)
    normal = rms(rows_in, gains_v[0]).astype(BF16)
    pack_v[:, 0:D] = normal
    for i in range(3):
        wait(get_qkv[i : i + 1])
        qkv_v[:, i * D : (i + 1) * D] = mm(normal, wqkv_v[:, i * D : (i + 1) * D]).astype(BF16)
    puts = [copies(qkv_v, qkv_o)]
    puts[-1].start()
    put_slow = []
    if slot == 0:
        put_slow = [copies(g1_v, g1_o), copies(g2_v, g2_o), copies(h2_v, h2_o)]
    query_index = lax.broadcasted_iota(jnp.int32, (2 * SEQ, SEQ), 1)
    key_index = key_index_rows()
    count = info[COUNT + slot : COUNT + slot + 1, 0:1]
    limit = jnp.where(encoding, jnp.broadcast_to(count - 1, (2 * SEQ, SEQ)), query_index)
    allowed = key_index <= limit
    for pair in range(PAIRS):
        lanes = slice(pair * 128, (pair + 1) * 128)
        weights, mixed = attend(
            qkv_v[:, lanes],
            qkv_v[:, D + pair * 128 : D + (pair + 1) * 128],
            qkv_v[:, 2 * D + pair * 128 : 2 * D + (pair + 1) * 128],
            allowed,
            masks,
        )
        p_v[pair] = weights
        pack_v[:, D + pair * 128 : D + (pair + 1) * 128] = mixed
    puts.append(copies(p_v, p_o))
    puts[-1].start()
    wait(get_out)
    first = rows_in + mm(pack_v[:, D : 2 * D], wout_v[...])
    h1_v[...] = first
    normal = rms(first, gains_v[1]).astype(BF16)
    pack_v[:, 2 * D : 3 * D] = normal
    put_units = copies(pack_v.at[:, pl.ds(3 * D, FF)], pack_o.at[:, pl.ds(3 * D, FF)])
    puts.append(copies(pack_v.at[:, pl.ds(0, 3 * D)], pack_o.at[:, pl.ds(0, 3 * D)]))
    puts[-1].start()

    @pl.when(encoding)
    def _():
        inputs = pack_v[:, 2 * D : 3 * D]
        for i in range(FF // tile):
            wait(get_in[2 * i : 2 * i + 2])
            columns = slice(i * tile, (i + 1) * tile)
            gate = mm(inputs, win_v[:, columns])
            up = mm(inputs, win_v[:, FF + i * tile : FF + (i + 1) * tile])
            unit, to_gate, to_up = gate_parts(gate, up)
            pack_v[:, 3 * D + i * tile : 3 * D + (i + 1) * tile] = unit.astype(BF16)
            g1_v[:, columns] = to_gate.astype(BF16)
            g2_v[:, columns] = to_up.astype(BF16)
        put_units.start()
        start(put_slow[:2])
        wait(get_down)
        second = h1_v[...] + mm(pack_v[:, 3 * D :], wdown_v[...])
        h2_v[...] = second
        start(put_slow[2:])
        memory = rms(second, gains_v[2])
        memory = jnp.where(rows_below(info, COUNT + slot), memory, 0.0).astype(BF16)
        memory_v[...] = memory
        wait(get_cross)
        send_v[...] = mm(memory, wcross_v[...]).astype(BF16)
        put_units.wait()
        wait(put_slow)

    @pl.when(jnp.logical_not(encoding))
    def _():
        wait(get_cross)
        query_v[...] = mm(pack_v[:, 2 * D : 3 * D], wcross_v[:, 0:D]).astype(BF16)
        wait(get_in + get_down)

    wait(puts + get_next)


def forward(slot, scalars, arrays, fast):
    kind = (hbm, vmem)[slot]
    outs = [
        hbm(SEQ, 3 * D + FF),
        hbm(SEQ, 3 * D),
        hbm(PAIRS, 2 * SEQ, SEQ),
        vmem(SEQ, D, dtype=F32),
        vmem(SEQ, D),
        kind(SEQ, FF),
        kind(SEQ, FF),
        kind(SEQ, D, dtype=F32),
        vmem(SEQ, 2 * D),
        vmem(SEQ, D),
    ]
    scratch = [struct(SEQ, 3 * D + FF), struct(SEQ, 3 * D), struct(PAIRS, 2 * SEQ, SEQ)]
    if slot == 0:
        outs += [vmem(8, 128, dtype=jnp.int32), vmem(3, 1, D, dtype=F32), vmem(2, SEQ, D)]
        outs += [vmem(*weight.shape[1:]) for weight in arrays[5:]]
        scratch += [struct(2, SEQ, dtype=jnp.int32)]
        scratch += [pltpu.SMEM((1, 2), jnp.int32), pltpu.SMEM((2,), jnp.int32)]
        scratch += [struct(SEQ, FF), struct(SEQ, FF), struct(SEQ, D, dtype=F32)]
    else:
        outs += [vmem(2, SEQ, D)]
    return call(
        functools.partial(forward_kernel, slot), scalars, outs, scratch, 34, "forward",
        [slow(item) for item in arrays], fast,
    )


def turn_all(sources, results):
    for source, result in zip(sources, results):

        def step(i, carry):
            at = pl.ds(pl.multiple_of(i * 256, 256), 256)
            result[at, :] = source[:, at].T
            return carry

        lax.fori_loop(0, source.shape[1] // 256, step, 0)


def turn_kernel(count, *refs):
    turn_all(refs[1 : count + 1], refs[count + 1 : 2 * count + 1])


def turn(after, weights):
    return call(
        functools.partial(turn_kernel, len(weights)), [],
        [vmem(*weight.shape[::-1]) for weight in weights], [], 1, "turn", [after], weights,
    )


def turn_last_kernel(info, cot, wdownt, *refs):
    turn_all(refs[0:2], refs[2:4])
    units = refs[4]

    @pl.when(number(info, SECTION) == 1)
    def _():
        branch = halves(
            *[
                jnp.where(rows_below(info, TOKENS + i), cot[i].astype(F32), 0.0).astype(BF16)
                for i in range(2)
            ]
        )
        units[...] = mm(branch, wdownt[...])


def turn_last(fast):
    return call(
        turn_last_kernel, [],
        [vmem(3 * D, D), vmem(D, D), vmem(2 * SEQ, FF, dtype=F32)], [], 1, "turn_last", [], fast,
    )


def middle_kernel(slot, *refs):
    packs, refs = refs[: 2 * slot], refs[2 * slot :]
    info, units, gains_v, kv_v, h1_v, query_v, cot_v, win_v, wcross_v, wint_v, wcrosst_v = refs[:11]
    memory, refs = refs[11 : 11 + 2 * slot], refs[11 + 2 * slot :]
    pack_o, rhs_o, late_v, dkv_v, e2_o, de2_o, gain_o = refs[:7]
    lefts, refs = refs[7 : 7 + 2 * slot], refs[7 + 2 * slot :]
    pack_v, g1_v, g2_v, rhs_v, p_v, e2_v, de2_v, gain_v, mixed_v = refs[:9]
    held, sems = refs[9:-1], refs[-1]
    if slot == 1:

        @pl.when(number(info, SECTION) == 0)
        def _():
            copies = Copies(sems)
            get = [copies(source, target) for source, target in zip(packs, held)]
            start(get)
            wait(get)
            left_operands(0, number(info, PLACE), held, None, memory, lefts)

    @pl.when(number(info, SECTION) != 0)
    def _():
        copies = Copies(sems)
        tile = 512
        masks = lane_masks()
        count = info[COUNT + slot : COUNT + slot + 1, 0:1]
        allowed = key_index_rows() < jnp.broadcast_to(count, (2 * SEQ, SEQ))
        for pair in range(PAIRS):
            lanes = slice(pair * 128, (pair + 1) * 128)
            weights, mixed = attend(
                query_v[:, lanes],
                kv_v[:, lanes],
                kv_v[:, D + pair * 128 : D + (pair + 1) * 128],
                allowed,
                masks,
            )
            p_v[pair] = weights
            pack_v[:, D + pair * 128 : D + (pair + 1) * 128] = mixed
        second = h1_v[...] + mm(pack_v[:, D : 2 * D], wcross_v[:, D : 2 * D])
        e2_v[...] = second
        puts = [copies(e2_v, e2_o)]
        puts[-1].start()
        normal = rms(second, gains_v[2]).astype(BF16)
        pack_v[:, 0:D] = normal
        for i in range(FF // tile):
            columns = slice(i * tile, (i + 1) * tile)
            gate = mm(normal, win_v[:, columns])
            up = mm(normal, win_v[:, FF + i * tile : FF + (i + 1) * tile])
            unit, to_gate, to_up = gate_parts(gate, up)
            pack_v[:, 2 * D + i * tile : 2 * D + (i + 1) * tile] = unit.astype(BF16)
            g1_v[:, columns] = to_gate.astype(BF16)
            g2_v[:, columns] = to_up.astype(BF16)
        puts.append(copies(pack_v, pack_o))
        puts[-1].start()
        upstream = jnp.where(rows_below(info, TOKENS + slot), cot_v[slot].astype(F32), 0.0)
        branch = upstream.astype(BF16)
        rhs_v[:, 0:D] = branch
        for i in range(FF // tile):
            columns = slice(i * tile, (i + 1) * tile)
            grad_unit = units[slot * SEQ : (slot + 1) * SEQ, columns]
            rhs_v[:, D + i * tile : D + (i + 1) * tile] = (
                grad_unit * g1_v[:, columns].astype(F32)
            ).astype(BF16)
            rhs_v[:, D + FF + i * tile : D + FF + (i + 1) * tile] = (
                grad_unit * g2_v[:, columns].astype(F32)
            ).astype(BF16)
        puts.append(copies(rhs_v, rhs_o))
        puts[-1].start()
        grad_normal = mm(rhs_v[:, D : D + 2 * FF], wint_v[...])
        back, grad_gain = rms_back(second, gains_v[2], grad_normal)
        grad_second = upstream + back
        gain_v[...] = jnp.zeros_like(gain_v)
        gain_v[2:3, :] = grad_gain
        de2_v[...] = grad_second
        puts += [copies(de2_v, de2_o), copies(gain_v, gain_o)]
        start(puts[-2:])
        branch = grad_second.astype(BF16)
        late_v[:, D : 2 * D] = branch
        mixed_v[...] = mm(branch, wcrosst_v[D : 2 * D, :]).astype(BF16)
        for pair in range(PAIRS):
            lanes = slice(pair * 128, (pair + 1) * 128)
            high = slice(D + pair * 128, D + (pair + 1) * 128)
            grad_query, grad_keys, grad_values = attend_back(
                query_v[:, lanes], kv_v[:, lanes], kv_v[:, high], p_v[pair], mixed_v[:, lanes], masks
            )
            late_v[:, lanes] = grad_query
            dkv_v[:, lanes] = grad_keys
            dkv_v[:, high] = grad_values
        wait(puts)


def middle(slot, packs, fast):
    return call(
        functools.partial(middle_kernel, slot),
        [],
        [
            hbm(SEQ, 2 * D + FF),
            hbm(SEQ, D + 2 * FF),
            vmem(SEQ, 2 * D),
            vmem(SEQ, 2 * D),
            hbm(SEQ, D, dtype=F32),
            hbm(SEQ, D, dtype=F32),
            hbm(8, D, dtype=F32),
        ]
        + [vmem(3328, 256)] * (2 * slot),
        [
            struct(SEQ, 2 * D + FF),
            struct(SEQ, FF),
            struct(SEQ, FF),
            struct(SEQ, D + 2 * FF),
            struct(PAIRS, 2 * SEQ, SEQ),
            struct(SEQ, D, dtype=F32),
            struct(SEQ, D, dtype=F32),
            struct(8, D, dtype=F32),
            struct(SEQ, D),
        ]
        + [struct(*pack.shape) for pack in packs],
        8,
        "middle",
        [slow(pack) for pack in packs],
        fast,
    )


def outer_rows(slot, info, gains_v, dkv_v, h2_v, g1_v, g2_v, wdownt_v, wcrosst_v, rhs_v):
    rhs_v[:, D + 2 * FF :] = dkv_v[...]
    grad_memory = mm(dkv_v[...], wcrosst_v[...])
    grad_memory = jnp.where(rows_below(info, COUNT + slot), grad_memory, 0.0)
    grad_second, grad_gain = rms_back(h2_v[...], gains_v[2], grad_memory)
    branch = grad_second.astype(BF16)
    rhs_v[:, 0:D] = branch
    tile = 512
    for i in range(FF // tile):
        columns = slice(i * tile, (i + 1) * tile)
        grad_unit = mm(branch, wdownt_v[:, columns])
        for k, scale in ((0, g1_v), (1, g2_v)):
            first = D + k * FF + i * tile
            rhs_v[:, first : first + tile] = (grad_unit * scale[:, columns].astype(F32)).astype(BF16)
    return grad_second, grad_gain


def inner_rows(slot, info, gains_v, acts_v, h1_v, dn_v, up_v, qkv_v, p_v, woutt_v, wqkvt_v, rhs_v, grad_v):
    rows = slice(0, SEQ)
    plot = number(info, PLOT + slot)
    back, first_gain = rms_back(h1_v[...], gains_v[1], dn_v[...])
    grad_first = up_v[...] + back
    branch = grad_first.astype(BF16)
    rhs_v[rows, 0:D] = branch
    masks = lane_masks()
    grad_mixed = mm(branch, woutt_v[...]).astype(BF16)
    for pair in range(PAIRS):
        spans = [slice(k * D + pair * 128, k * D + (pair + 1) * 128) for k in range(3)]
        parts = attend_back(
            qkv_v[:, spans[0]],
            qkv_v[:, spans[1]],
            qkv_v[:, spans[2]],
            p_v[pair],
            grad_mixed[:, pair * 128 : (pair + 1) * 128],
            masks,
        )
        for k in range(3):
            rhs_v[rows, D + k * D + pair * 128 : D + k * D + (pair + 1) * 128] = parts[k]
    grad_normal = mm(rhs_v[rows, D : 4 * D], wqkvt_v[...])
    back, zeroth_gain = rms_back(acts_v[plot].astype(F32), gains_v[0], grad_normal)
    grad_v[0, plot] = grad_first + back
    return zeroth_gain, first_gain


def early_kernel(*refs):
    packs, (qkv, p, rhs2, de2, gain2, h2, g1, g2) = refs[0:4], refs[4:12]
    info, gains_v, acts_v, dkv_v, h1_v, late_v = refs[12:18]
    wqkvt_v, woutt_v, wint_v, wdownt_v, wcrosst_v, ready_v = refs[18:24]
    (kept_v, given_v, rhs3_v, rhs_v, gain_v, grad_v) = refs[24:30]
    held = refs[30:34]
    qkv_v, p_v, up_v, dn_v, gain2_v, h2_v, units_v, sems = refs[34:]
    g1_v, g2_v = units_v.at[0], units_v.at[1]
    encoding = number(info, SECTION) == 0
    copies = Copies(sems)
    get_rows = [copies(qkv, qkv_v), copies(p, p_v)]
    get_packs = [copies(source, target) for source, target in zip(packs, held)]
    get_rhs = copies(rhs2, rhs3_v.at[:, pl.ds(0, D + 2 * FF)])
    get_rest = [copies(de2, up_v), copies(gain2, gain2_v)]
    get_enc = [copies(h2, h2_v), copies(g1, g1_v), copies(g2, g2_v)]
    start(get_rows)

    @pl.when(encoding)
    def _():
        start(get_enc)
        wait(get_enc)
        grad_second, grad_gain = outer_rows(
            0, info, gains_v, dkv_v, h2_v, g1_v, g2_v, wdownt_v, wcrosst_v, rhs3_v
        )
        up_v[...] = grad_second
        gain2_v[2:3, :] = grad_gain
        given_v[...] = ready_v[...]
        dn_v[...] = mm(rhs3_v[:, D : D + 2 * FF], wint_v[...])

    @pl.when(jnp.logical_not(encoding))
    def _():
        start(get_packs + get_rest + [get_rhs])
        wait(get_packs)
        left_operands(1, number(info, PLACE), held[:2], held[2:], None, (kept_v, given_v))
        rhs3_v[:, D + 2 * FF :] = late_v[...]
        dn_v[...] = mm(late_v[:, 0:D], wcrosst_v[0:D, :])
        wait(get_rest)
        get_rhs.wait()

    wait(get_rows)
    zeroth_gain, first_gain = inner_rows(
        0, info, gains_v, acts_v, h1_v, dn_v, up_v, qkv_v, p_v, woutt_v, wqkvt_v, rhs_v, grad_v
    )
    gain_v[...] = jnp.concatenate(
        [zeroth_gain, first_gain, gain2_v[2:3, :], jnp.zeros((5, D), F32)], axis=0
    )


def early(arrays, fast):
    return call(
        early_kernel,
        [],
        [
            vmem(3328, 256),
            vmem(3328, 256),
            vmem(SEQ, 3 * D + 2 * FF),
            vmem(SEQ, 4 * D),
            vmem(8, D, dtype=F32),
            vmem(1, 2, SEQ, D, dtype=F32),
        ],
        [struct(*pack.shape) for pack in arrays[:4]]
        + [
            struct(SEQ, 3 * D),
            struct(PAIRS, 2 * SEQ, SEQ),
            struct(SEQ, D, dtype=F32),
            struct(SEQ, D, dtype=F32),
            struct(8, D, dtype=F32),
            struct(SEQ, D, dtype=F32),
            struct(2, SEQ, FF),
        ],
        14,
        "early",
        [slow(item) for item in arrays],
        fast,
    )


def outer_kernel(rhs2, after, info, gains_v, dkv_v, h2_v, g1_v, g2_v, late_v, wdownt_v, wcrosst_v, rhs_v, up_v, gain_v, sems):
    encoding = number(info, SECTION) == 0

    @pl.when(encoding)
    def _():
        grad_second, grad_gain = outer_rows(
            1, info, gains_v, dkv_v, h2_v, g1_v, g2_v, wdownt_v, wcrosst_v, rhs_v
        )
        up_v[...] = grad_second
        gain_v[2:3, :] = grad_gain

    @pl.when(jnp.logical_not(encoding))
    def _():
        get = Copies(sems)(rhs2, rhs_v.at[:, pl.ds(0, D + 2 * FF)])
        get.start()
        rhs_v[:, D + 2 * FF :] = late_v[...]
        get.wait()


def outer(rhs2, after, fast):
    return call(
        outer_kernel,
        [],
        [vmem(SEQ, 3 * D + 2 * FF), vmem(SEQ, D, dtype=F32), vmem(8, D, dtype=F32)],
        [],
        1,
        "outer",
        [slow(rhs2), after],
        fast,
    )


def inner_kernel(*refs):
    qkv, p, de2, gain2 = refs[:4]
    info, gains_v, acts_v, h1_v, rhs3_v, dh2_v, gain3_v, before_v = refs[4:12]
    wqkvt_v, woutt_v, wint_v, wcrosst_v = refs[12:16]
    (rhs_v, grad_v, qkv_v, p_v, up_v, dn_v, gain2_v, sems) = refs[17:]
    encoding = number(info, SECTION) == 0
    copies = Copies(sems)
    get_rows = [copies(qkv, qkv_v), copies(p, p_v)]
    get_dec = [
        copies(de2, up_v),
        copies(gain2, gain2_v),
    ]
    start(get_rows)

    @pl.when(encoding)
    def _():
        dn_v[...] = mm(rhs3_v[:, D : D + 2 * FF], wint_v[...])
        up_v[...] = dh2_v[...]
        gain2_v[...] = gain3_v[...]

    @pl.when(jnp.logical_not(encoding))
    def _():
        start(get_dec)
        dn_v[...] = mm(rhs3_v[:, D + 2 * FF : 2 * D + 2 * FF], wcrosst_v[0:D, :])
        wait(get_dec)

    wait(get_rows)
    zeroth_gain, first_gain = inner_rows(
        1, info, gains_v, acts_v, h1_v, dn_v, up_v, qkv_v, p_v, woutt_v, wqkvt_v, rhs_v, grad_v
    )
    total = before_v[...] + jnp.concatenate(
        [zeroth_gain, first_gain, gain2_v[2:3, :], jnp.zeros((5, D), F32)], axis=0
    )
    upper = total.astype(BF16)
    lower = (total - upper.astype(F32)).astype(BF16)
    rhs_v[SEQ:, 0:D] = halves(upper, lower)
    rhs_v[SEQ:, D : 4 * D] = jnp.zeros((16, 3 * D), BF16)


def inner(arrays, fast):
    return call(
        inner_kernel,
        [],
        [vmem(SEQ + 16, 4 * D), vmem(1, 2, SEQ, D, dtype=F32)],
        [
            struct(SEQ, 3 * D),
            struct(PAIRS, 2 * SEQ, SEQ),
            struct(SEQ, D, dtype=F32),
            struct(SEQ, D, dtype=F32),
            struct(8, D, dtype=F32),
        ],
        8,
        "inner",
        [slow(item) for item in arrays],
        fast,
        aliases={len(arrays) + 12: 1},
    )


def output_kernel(*refs):
    pack2, e2 = refs[0:2], refs[2:4]
    info, memory, wdownt_v, out_o, out_v, z_v, e2_v, sems = refs[4], *[refs[5:7]], *refs[7:]
    encoding = number(info, SECTION) == 0
    copies = Copies(sems)
    get = []
    for i in range(2):
        at = pl.ds(i * SEQ, SEQ)
        get += [copies(pack2[i].at[:, pl.ds(2 * D, FF)], z_v.at[at]), copies(e2[i], e2_v.at[at])]

    @pl.when(encoding)
    def _():
        for i in range(2):
            out_v[0, i] = memory[i][...]

    @pl.when(jnp.logical_not(encoding))
    def _():
        start(get)
        wait(get)
        third = e2_v[...] + mm_t(z_v[...], wdownt_v[...])
        for i in range(2):
            part = third[i * SEQ : (i + 1) * SEQ]
            out_v[0, i] = jnp.where(rows_below(info, TOKENS + i), part, 0.0).astype(BF16)

    put = copies(out_v, out_o)
    put.start()
    put.wait()


def output(arrays, after, fast):
    def kernel(*refs):
        output_kernel(*refs[len(after) :])

    return call(
        kernel,
        [],
        [struct(1, 2, SEQ, D)],
        [struct(1, 2, SEQ, D), struct(2 * SEQ, FF), struct(2 * SEQ, D, dtype=F32)],
        5,
        "output",
        after + [slow(item) for item in arrays],
        fast,
    )[0]


def place_parts(place):
    return (
        lax.shift_right_logical(place, 5),
        jnp.bitwise_and(lax.shift_right_logical(place, 3), 3),
        jnp.bitwise_and(lax.shift_right_logical(place, 1), 3),
        jnp.bitwise_and(place, 1),
    )


def matching(target, columns):
    rows = target.shape[0]
    lane = lax.broadcasted_iota(jnp.int32, (rows, 128), 1)
    blocks = [jnp.where(lane + i * 128 == target, 1.0, 0.0) for i in range(columns // 128)]
    return jnp.concatenate(blocks, axis=1).astype(BF16)


def selector(place, other=0):
    y, x, z, core = place_parts(place)
    core = jnp.bitwise_xor(core, other)
    index = lax.broadcasted_iota(jnp.int32, (384, 128), 0)

    def at_least(value, *bounds):
        return sum(jnp.where(value >= bound, 1, 0) for bound in bounds)

    first = at_least(index, 96, 192, 288)
    rest = index - first * 96
    second = at_least(rest, 24, 48, 72)
    rest = rest - second * 24
    third = at_least(rest, 12)
    rest = rest - third * 12
    to_z, to_x = first, second
    return matching(
        jnp.bitwise_and(y + third, 1) * 384
        + jnp.bitwise_and(x + to_x, 3) * 96
        + jnp.bitwise_and(z + to_z, 3) * 24
        + core * 12
        + rest,
        D,
    )


def stacked(sources, first, width):
    return jnp.concatenate([source[0:SEQ, first : first + width] for source in sources], axis=0)


def along_down(place, other):
    y, x, z, core = place_parts(place)
    core = jnp.bitwise_xor(core, other)
    index = lax.broadcasted_iota(jnp.int32, (256, 128), 0)
    return matching(
        jnp.bitwise_and(y + jnp.bitwise_and(lax.shift_right_logical(index, 5), 1), 1) * 256
        + jnp.bitwise_and(z + lax.shift_right_logical(index, 6), 3) * 64
        + core * 32
        + jnp.bitwise_and(index, 31),
        512,
    )


def prepare_down(place, sources, first, result, order):
    y, x, z, core = place_parts(place)
    for chunk in range(4):
        block = first + jnp.bitwise_and(x + chunk, 3) * 256
        columns = [pl.ds(pl.multiple_of(block + half, 256), 256) for half in (0, 1024)]
        picked = jnp.concatenate(
            [jnp.concatenate([source[:, at] for source in sources], axis=0) for at in columns],
            axis=1,
        )
        at = 1920 + 256 * chunk
        result[at : at + 256, :] = mm_t(order, picked).astype(BF16)


def x_first(rows):
    blocks = [rows[(z * 4 + x) * 24 : (z * 4 + x + 1) * 24] for x in range(4) for z in range(4)]
    return jnp.concatenate(blocks, axis=0)


def left_operands(which, place, pack1, pack2, memory, results):
    last = pack2 if which else pack1
    for other, result in enumerate(results):
        along_z = selector(place, other)
        steps = (
            (0, True, pack1, 0),
            (384, True, pack1, D),
            (768, False, last, 0 if which else 2 * D),
            (1152, False, pack1 if which else memory, 2 * D if which else 0),
            (1536, False, last if which else memory, D if which else 0),
        )
        for row, to_x, sources, first in steps:
            rows = mm_t(along_z, stacked(sources, first, D))
            rows = x_first(rows) if to_x else rows
            result[row : row + 384, :] = rows.astype(BF16)
        prepare_down(place, last, 2 * D if which else 3 * D, result, along_down(place, other))


class Buffers:
    def __init__(self, refs, size):
        self.own, self.ahead, self.behind, self.one, self.three = refs
        self.size = size

    def spot(self, chunk, block):
        quarter = self.size // 4
        half = self.size // 2
        row = block * quarter
        if chunk == 0:
            return self.own, row
        low = block < 2
        if chunk == 1:
            return (self.one, row) if low else (self.ahead, row)
        if chunk == 2:
            return (self.ahead, row) if low else (self.behind, row - half)
        return (self.behind, half + row) if low else (self.three, row - half)


def buffer_shapes(size):
    return [struct(size, 128)] * 3 + [struct(size // 2, 128)] * 2


def store_narrow(buffers, grad, offset):
    for chunk in range(4):
        for block in range(4):
            rows = grad[(chunk * 4 + block) * 24 : (chunk * 4 + block + 1) * 24]
            piece = jnp.concatenate([rows[:, 0:128], rows[:, 128:256]], axis=0).astype(BF16)
            target, row = buffers.spot(chunk, block)
            target[row + offset : row + offset + 48, :] = piece


SIZE_X, SIZE_Z = 4 * 1008, 4 * 1056


def both_sides(lefts, first, count):
    return jnp.concatenate([left[first : first + count, :] for left in lefts], axis=1)


def right_of(sources, first, width=256):
    return stacked(sources, first, width)


def grads_wide_kernel(lefts, wide, results):
    held = Buffers(results[:5], SIZE_X), Buffers(results[5:], SIZE_Z)
    left = both_sides(lefts, 768, 384)
    for i in range(16):
        store_narrow(held[1], mm(left, right_of(wide, D + 256 * i)), 48 * i)
    for i in range(6):
        left = both_sides(lefts, 1152 if i < 3 else 1536, 384)
        store_narrow(held[1], mm(left, right_of(wide, D + 2 * FF + 256 * i)), 768 + 48 * i)
    branch = right_of(wide, 0, D)
    for chunk in range(4):
        grad = mm(both_sides(lefts, 1920 + 256 * chunk, 256), branch)
        for block in range(4):
            target, row = held[0].spot(chunk, block)
            for i in range(6):
                spot = row + 64 * i
                target[spot : spot + 64, :] = grad[
                    64 * block : 64 * (block + 1), 128 * i : 128 * (i + 1)
                ].astype(BF16)


def grads_thin_kernel(place, lefts, thin, results):
    held = Buffers(results, SIZE_X)
    total_of = selector(place)
    total = sum(
        item[row : row + 8, 0:D].astype(F32) for item in (thin[1], thin[3]) for row in (SEQ, SEQ + 8)
    )
    upper = total.astype(BF16)
    lower = (total - upper.astype(F32)).astype(BF16)
    ordered = mm_t(upper, total_of) + mm_t(lower, total_of)
    tall = jnp.concatenate([ordered, jnp.zeros((120, 384), F32)], axis=0).T
    tall = jnp.concatenate([tall, jnp.zeros((384, 128), F32)], axis=1)
    store_narrow(held, x_first(tall), 960)
    left = both_sides(lefts, 0, 384)
    for i in range(9):
        store_narrow(held, mm(left, right_of(thin, D + 256 * i)), 384 + 48 * i)
    left = both_sides(lefts, 384, 384)
    for i in range(3):
        store_narrow(held, mm(left, right_of(thin, 256 * i)), 816 + 48 * i)


def grads(thin, info, lefts, right, before):
    shapes = [vmem(*item.shape) for item in buffer_shapes(SIZE_X)]
    if not thin:
        shapes += [vmem(*item.shape) for item in buffer_shapes(SIZE_Z)]

    def kernel(info, *refs):
        encoding = number(info, SECTION) == 0
        results = refs[-1 - len(shapes) : -1]

        def run(lefts):
            if thin:
                grads_thin_kernel(number(info, PLACE), lefts, refs[3:7], results)
            else:
                grads_wide_kernel(lefts, refs[3:7], results)

        @pl.when(encoding)
        def _():
            run((refs[0], refs[2]))

        @pl.when(jnp.logical_not(encoding))
        def _():
            run(refs[1:3])

    return call(
        kernel, [], shapes, [], 1, "grads", [], [info, *lefts, *right, *before],
        aliases={8 + i: i for i in range(len(before))},
    )


RUNS_X = ((0, 6, 32), (384, 26, 12))
RUNS_Z = ((0, 44, 12),)


def rows_for_y(runs):
    needed = sum(tiles * rows for _, tiles, rows in runs)
    return max(-(-needed // 16) * 16, 544 if runs is RUNS_X else 0)


def combine_kernel(runs, total, *refs):
    got, (last, sent, line_v) = refs[:3], refs[3:]
    size = last.shape[0]
    last[...] = total[0:size, :].astype(F32) + sum(item[...].astype(F32) for item in got)
    line_v[...] = jnp.zeros_like(line_v)
    to = 0
    for first, tiles, rows in runs:
        if rows == 12:
            for at in range(12):
                line_v[to : to + tiles, :] = last[pl.ds(first + 12 + at, tiles, stride=24), :]
                to += tiles
        else:
            for tile in range(tiles):
                line_v[to : to + rows, :] = last[first + (2 * tile + 1) * rows : first + (2 * tile + 2) * rows, :]
                to += rows
    sent[...] = line_v[...].astype(BF16)


def combine(runs, total, got, after):
    size, rows = got[0].shape[0], rows_for_y(runs)

    def kernel(*refs):
        combine_kernel(runs, *refs[len(after) :])

    return pl.pallas_call(
        kernel,
        name="combine",
        in_specs=[ANY] * len(after) + [FAST] * 4,
        out_specs=[FAST] * 2,
        out_shape=[vmem(size, 128, dtype=F32), vmem(rows, 128)],
        scratch_shapes=[pltpu.VMEM((rows, 128), F32)],
        compiler_params=pltpu.CompilerParams(vmem_limit_bytes=ROOM_BYTES),
    )(*after, *[pltpu.with_memory_space_constraint(item, pltpu.VMEM) for item in (total, *got)])


def lay(own, got, first, got_first, tiles, parts):
    for at in range(12):
        line = own[pl.ds(first + at, tiles, stride=24), :]
        line = line + got[got_first + at * tiles : got_first + (at + 1) * tiles, :]
        tile = 0
        for result, count in parts:
            for i in range(count):
                result[at, :, 128 * i : 128 * (i + 1)] = line[tile : tile + 1, :]
                tile += 1


def finish_wide_kernel(own, sent, in_o, cross_o, got):
    got[...] = sent[...].astype(F32)
    lay(own, got, 0, 0, 44, ((in_o, 32), (cross_o, 12)))


def finish_rest_kernel(own, sent, qkv_o, out_o, down_o, gains_o, got, tall_v):
    got[...] = sent[...].astype(F32)
    for tile in range(6):
        columns = slice(128 * tile, 128 * (tile + 1))
        down_o[:, columns] = own[64 * tile : 64 * tile + 32, :] + got[32 * tile : 32 * tile + 32, :]
    lay(own, got, 384, 192, 26, ((qkv_o, 18), (out_o, 6)))
    tall_v[...] = jnp.zeros_like(tall_v)
    tall_v[0:12, :] = own[960:972, :] + got[pl.ds(192 + 24, 12, stride=26), :]
    tall = tall_v[...].T
    for i in range(3):
        gains_o[i] = tall[i : i + 1, 0:12]


def finish(kernel, own, sent, shapes, more):
    return pl.pallas_call(
        kernel,
        name="finish",
        in_specs=[FAST] * 2,
        out_specs=[FAST] * len(shapes),
        out_shape=[struct(*shape, dtype=F32) for shape in shapes],
        scratch_shapes=[pltpu.VMEM(shape, F32) for shape in (sent.shape, *more)],
        compiler_params=pltpu.CompilerParams(vmem_limit_bytes=ROOM_BYTES),
    )(*[pltpu.with_memory_space_constraint(item, pltpu.VMEM) for item in (own, sent)])


def flat(y, x, z, core):
    return ((y * 4 + x) * 4 + z) * 2 + core


def shifted(array, y=0, x=0, z=0, core=0):
    pairs = []
    for a in range(2):
        for b in range(4):
            for c in range(4):
                for d in range(2):
                    source = flat(a, b, c, d)
                    target = flat((a + y) % 2, (b + x) % 4, (c + z) % 4, (d + core) % 2)
                    pairs.append((source, target))
    return lax.ppermute(array, "dp", pairs)


def add(*terms):
    total = terms[0].astype(F32)
    for term in terms[1:]:
        total = total + term.astype(F32)
    return total


def first_round(buffers, axis):
    own, ahead, behind, one, three = buffers
    return shifted(ahead, **{axis: 1}), shifted(behind, **{axis: 3})


def second_round(buffers, firsts, axis):
    own, ahead, behind, one, three = buffers
    got_ahead, got_behind = firsts
    half = one.shape[0]
    last_ahead = shifted(add(one, got_ahead[:half]).astype(BF16), **{axis: 1})
    last_behind = shifted(add(three, got_behind[:half]).astype(BF16), **{axis: 3})
    low = add(own[:half], last_ahead, got_behind[half:])
    high = add(own[half:], got_ahead[half:], last_behind)
    return jnp.concatenate([low, high], axis=0).astype(BF16)


def along_one_round(total, axis):
    size = total.shape[0] // 4
    return [
        shifted(total[step * size : (step + 1) * size], **{axis: step}) for step in (2, 1, 3)
    ]


def local(
    acts,
    gains,
    qkv_weight,
    out_weight,
    mlp_in,
    mlp_out,
    cross_weight,
    patch_mask,
    table_len,
    slot_plot,
    cotangent,
):
    section = lax.axis_index("section").astype(jnp.int32).reshape(1)
    place = lax.axis_index("dp").astype(jnp.int32).reshape(1)
    gains = gains.transpose(1, 0, 2)
    weights = (qkv_weight, out_weight, mlp_in, mlp_out, cross_weight)
    made = [
        forward(0, [section, place], [slot_plot, table_len, gains, patch_mask, acts, *weights], [])
    ]
    info, gains, acts, *weights = made[0][10:]
    received = [lax.ppermute(made[0][8], "section", [(0, 1)])]
    made.append(forward(1, [], [cotangent], [info, gains, acts, *weights]))
    received.append(lax.ppermute(made[1][8], "section", [(0, 1)]))
    cot = made[1][10]
    turned = turn(slow(made[1][1]), weights[2:])
    *last, units = turn_last([info, cot, turned[1], *weights[:2]])
    turned = [*last, *turned]
    middles = []
    back = []
    memory = [item[9] for item in made]
    packs = [item[0] for item in made]
    for slot in range(2):
        h1, query = made[slot][3:5]
        middles.append(
            middle(
                slot,
                packs * slot,
                [info, units, gains, received[slot], h1, query, cot, weights[2], weights[4],
                 turned[2], turned[4], *memory * slot],
            )
        )
        back.append(lax.ppermute(middles[slot][3], "section", [(1, 0)]))
    lefts = [middles[1][7]]
    pack1, qkv, p, h1, query, g1, g2, h2 = made[0][:8]
    pack2, rhs2, late, _, e2, de2, gain2 = middles[0]
    kept_left, given_left, wide0, thin0, gain, grad_chain = early(
        [*packs, pack2, middles[1][0], qkv, p, rhs2, de2, gain2, h2, g1, g2],
        [info, gains, acts, back[0], h1, late, *turned, middles[1][8]],
    )
    lefts += [kept_left, shifted(given_left, core=1)]
    pack1, qkv, p, h1, query, g1, g2, h2 = made[1][:8]
    pack2, rhs2, late, _, e2, de2, gain2 = middles[1][:7]
    wide1, dh2, gain3 = outer(
        rhs2, gain, [info, gains, back[1], h2, g1, g2, late, turned[3], turned[4]]
    )
    wide = [wide0, wide1, shifted(wide0, core=1), shifted(wide1, core=1)]
    thin1, grad_chain = inner(
        [qkv, p, de2, gain2],
        [info, gains, acts, h1, wide1, dh2, gain3, gain, *turned[:3], turned[4], grad_chain],
    )
    thin = [thin0, thin1, shifted(thin0, core=1), shifted(thin1, core=1)]
    part = grads(False, info, lefts, wide, [])
    part_x, part_z = part[:5], part[5:]
    part_x = grads(True, info, lefts, thin, part_x)
    firsts_x, firsts_z = first_round(part_x, "x"), first_round(part_z, "z")
    out_rows = output(
        [middles[0][0], middles[1][0], middles[0][4], middles[1][4]],
        [part_x[3]],
        [info, *memory, turned[3]],
    )
    firsts_x, out_rows = lax.optimization_barrier((firsts_x, out_rows))
    total_x = second_round(part_x, firsts_x, "x")
    total_z = second_round(part_z, firsts_z, "z")
    last_x, sent_x = combine(RUNS_X, total_x, along_one_round(total_x, "z"), [])
    last_z, sent_z = combine(RUNS_Z, total_z, along_one_round(total_z, "x"), [last_x])
    grad_qkv, grad_out, grad_mlp_out, grad_gains = finish(
        finish_rest_kernel,
        last_x,
        shifted(sent_x, y=1),
        [(12, 1, 3 * D), (12, 1, D), (32, D), (3, 1, 12)],
        [(128, 128)],
    )
    grad_mlp_in, grad_cross = finish(
        finish_wide_kernel, last_z, shifted(sent_z, y=1), [(12, 1, 2 * FF), (12, 1, 2 * D)], []
    )
    return (
        out_rows,
        grad_chain,
        grad_gains.transpose(1, 0, 2),
        grad_qkv.transpose(1, 0, 2),
        grad_out.transpose(1, 0, 2),
        grad_mlp_in.transpose(1, 0, 2),
        grad_mlp_out[None],
        grad_cross.transpose(1, 0, 2),
    )


def solution(mesh):
    return jax.shard_map(
        local,
        mesh=mesh,
        in_specs=(
            P("section", "dp", None, None),
            P("section", None, None),
            P("section", None, None),
            P("section", None, None),
            P("section", None, None),
            P("section", None, None),
            P("section", None, None),
            P("dp", None),
            P("dp"),
            P("dp", None),
            P("dp", None, None),
        ),
        out_specs=(
            P("section", "dp", None, None),
            P("section", "dp", None, None),
            P("section", None, "dp"),
            P("section", "dp", None),
            P("section", "dp", None),
            P("section", "dp", None),
            P("section", "dp", None),
            P("section", "dp", None),
        ),
        check_vma=False,
    )
```

```python
import functools

import jax
import jax.numpy as jnp
from jax import lax
from jax.experimental import pallas as pl
from jax.experimental.pallas import tpu as pltpu
from jax.sharding import PartitionSpec as P

D = 768
HDIM = 64
FF = 2048
SEQ = 128
PAIRS = 6
EPS = 1e-06
NEGATIVE = -1e30
ROOM_BYTES = 11 * 2**20
SCALE = HDIM ** (-0.5)
BF16 = jnp.bfloat16
F32 = jnp.float32
ANY = pl.BlockSpec(memory_space=pl.ANY)
FAST = pl.BlockSpec(memory_space=pltpu.VMEM)
SMEM = pl.BlockSpec(memory_space=pltpu.SMEM)


def mm(left, right):
    return jnp.dot(left, right, preferred_element_type=F32)


def mm_t(left, right):
    return lax.dot_general(left, right, (((1,), (1,)), ((), ())), preferred_element_type=F32)


def mm_w(left, right):
    return lax.dot_general(left, right, (((0,), (0,)), ((), ())), preferred_element_type=F32)


def halves(first, second):
    return jnp.concatenate([first, second], axis=0)


def rms(hidden, gain):
    inverse = lax.rsqrt(jnp.mean(hidden * hidden, axis=-1, keepdims=True) + EPS)
    return hidden * inverse * gain


def rms_back(hidden, gain, upstream):
    inverse = lax.rsqrt(jnp.mean(hidden * hidden, axis=-1, keepdims=True) + EPS)
    unit = hidden * inverse
    scaled = upstream * gain
    grad_gain = jnp.sum(upstream * unit, axis=0, keepdims=True)
    middle = jnp.mean(scaled * unit, axis=-1, keepdims=True)
    return inverse * (scaled - unit * middle), grad_gain


def gate_parts(gate, up):
    inner = 0.7978845608 * (gate + 0.044715 * gate * gate * gate)
    bend = jnp.tanh(inner)
    half = 0.5 * (1.0 + bend)
    value = gate * half
    slope = half + 0.5 * gate * (1.0 - bend * bend) * 0.7978845608 * (
        1.0 + 3.0 * 0.044715 * gate * gate
    )
    return value * up, slope * up, value


def lane_masks():
    lane = lax.broadcasted_iota(jnp.int32, (SEQ, 2 * HDIM), 1)
    low = jnp.where(lane < HDIM, 1.0, 0.0).astype(F32)
    return low.astype(BF16), (1.0 - low).astype(BF16), low


def stack_heads(pair, masks):
    return jnp.concatenate([pair * masks[0], pair * masks[1]], axis=0)


def attend(query, keys, values, allowed, masks):
    scores = mm_t(stack_heads(keys, masks), query) * SCALE
    scores = jnp.where(allowed, scores, NEGATIVE)
    parts = []
    for head in range(2):
        part = scores[head * SEQ : (head + 1) * SEQ]
        power = jnp.exp(part - jnp.max(part, axis=0, keepdims=True))
        parts.append(power * (1.0 / jnp.sum(power, axis=0, keepdims=True)))
    weights = jnp.concatenate(parts, axis=0).astype(BF16)
    return weights, mm_w(weights, stack_heads(values, masks)).astype(BF16)


def attend_back(query, keys, values, weights, upstream, masks):
    key_stack = stack_heads(keys, masks)
    grad_weights = mm_t(stack_heads(values, masks), upstream)
    wide = weights.astype(F32)
    product = wide * grad_weights
    parts = []
    for head in range(2):
        rows = slice(head * SEQ, (head + 1) * SEQ)
        total = jnp.sum(product[rows], axis=0, keepdims=True)
        parts.append(product[rows] - wide[rows] * total)
    grad_scores = jnp.concatenate(parts, axis=0).astype(BF16)
    grad_query = mm_w(grad_scores, key_stack) * SCALE
    key_both = mm(grad_scores, query) * SCALE
    value_both = mm(weights, upstream)
    low = masks[2]
    high = 1.0 - low
    grad_keys = key_both[:SEQ] * low + key_both[SEQ:] * high
    grad_values = value_both[:SEQ] * low + value_both[SEQ:] * high
    return grad_query.astype(BF16), grad_keys.astype(BF16), grad_values.astype(BF16)


def key_index_rows():
    return jnp.bitwise_and(lax.broadcasted_iota(jnp.int32, (2 * SEQ, SEQ), 0), SEQ - 1)


def kept(keep_ref, plot):
    row = keep_ref[pl.ds(plot, 1), :].astype(F32)
    return jnp.sum(row, axis=1, keepdims=True).astype(jnp.int32)


SECTION, PLACE, PLOT, TOKENS, COUNT = 0, 1, 2, 4, 6


def number(info, row):
    return jnp.max(info[row : row + 1, :].astype(F32)).astype(jnp.int32)


def rows_below(info, row):
    index = lax.broadcasted_iota(jnp.int32, (SEQ, D), 0)
    return index < jnp.broadcast_to(info[row : row + 1, 0:1], (SEQ, D))


class Copies:
    def __init__(self, sems):
        self.sems = sems
        self.count = 0

    def __call__(self, source, target):
        copy = pltpu.make_async_copy(source, target, self.sems.at[self.count])
        self.count += 1
        return copy


def start(copies):
    for copy in copies:
        copy.start()


def wait(copies):
    for copy in copies:
        copy.wait()


def struct(*shape, dtype=BF16):
    return jax.ShapeDtypeStruct(shape, dtype)


def call(kernel, scalars, out_shape, scratch, sems, name, arrays, fast=(), aliases=None, flops=0, traffic=0):
    return pl.pallas_call(
        kernel,
        name=name,
        in_specs=[SMEM] * len(scalars) + [ANY] * len(arrays) + [FAST] * len(fast),
        out_specs=[FAST if is_fast(item) else ANY for item in out_shape],
        out_shape=out_shape,
        scratch_shapes=[
            pltpu.VMEM(item.shape, item.dtype) if isinstance(item, jax.ShapeDtypeStruct) else item
            for item in scratch
        ]
        + [pltpu.SemaphoreType.DMA((sems,))],
        input_output_aliases=aliases or {},
        compiler_params=pltpu.CompilerParams(vmem_limit_bytes=ROOM_BYTES),
        cost_estimate=pl.CostEstimate(flops=flops, bytes_accessed=traffic, transcendentals=0),
    )(*scalars, *arrays, *[pltpu.with_memory_space_constraint(item, pltpu.VMEM) for item in fast])


def is_fast(item):
    return not isinstance(item, jax.ShapeDtypeStruct) and item.memory_space == pltpu.VMEM


def vmem(*shape, dtype=BF16):
    return pltpu.VMEM(shape, dtype)


def hbm(*shape, dtype=BF16):
    return pltpu.HBM(shape, dtype)


def slow(array):
    return pltpu.with_memory_space_constraint(array, pltpu.HBM)


def forward_kernel(slot, *refs):
    if slot == 0:
        section, place, slot_plot, table_len, gains, keep, acts, *given = refs[:12]
        (pack_o, qkv_o, p_o, h1_v, query_v, g1_o, g2_o, h2_o, send_v, memory_v, info, gains_v, acts_v, wqkv_v, wout_v, win_v, wdown_v, wcross_v) = refs[12:30]
        (pack_v, qkv_v, p_v, keep_v, plot_s, tokens_s, g1_v, g2_v, h2_v, sems) = refs[30:]
    else:
        cot, info, gains_v, acts_v, wqkv_v, wout_v, win_v, wdown_v, wcross_v = refs[:9]
        (pack_o, qkv_o, p_o, h1_v, query_v, g1_v, g2_v, h2_v, send_v, memory_v, cot_v) = refs[9:20]
        (pack_v, qkv_v, p_v, sems) = refs[20:]
    copies = Copies(sems)
    tile = 512
    get_qkv, get_in, get_out, get_down, get_cross, get_next = [], [], [], [], [], []
    if slot == 0:
        encoding = section[0] == 0
        get_small = [
            copies(slot_plot, plot_s),
            copies(table_len, tokens_s),
            copies(acts.at[0], acts_v),
            copies(gains, gains_v),
            copies(keep, keep_v),
        ]
        w_qkv, w_out, w_in, w_down, w_cross = given
        get_qkv = [
            copies(w_qkv.at[0, :, pl.ds(i * D, D)], wqkv_v.at[:, pl.ds(i * D, D)]) for i in range(3)
        ]
        get_out = [copies(w_out.at[0], wout_v)]
        for i in range(FF // tile):
            get_in += [
                copies(
                    w_in.at[0, :, pl.ds(base + i * tile, tile)],
                    win_v.at[:, pl.ds(base + i * tile, tile)],
                )
                for base in (0, FF)
            ]
        get_down = [copies(w_down.at[0], wdown_v)]
        get_cross = [copies(w_cross.at[0], wcross_v)]
        start(get_small + get_qkv + get_out + get_in + get_down + get_cross)
        wait(get_small)
        plots = [plot_s[0, i] for i in range(2)]
        numbers = [section[0], place[0], *plots, *[tokens_s[plot] for plot in plots]]
        for row, value in enumerate(numbers):
            info[row : row + 1, :] = jnp.broadcast_to(value, (1, 128)).astype(jnp.int32)
        for i in range(2):
            info[COUNT + i : COUNT + i + 1, :] = jnp.broadcast_to(kept(keep_v, plots[i]), (1, 128))
    else:
        encoding = number(info, SECTION) == 0
        plots = [None, number(info, PLOT + 1)]
        get_next = [copies(cot, cot_v)]
        start(get_next)
    masks = lane_masks()
    rows_in = acts_v[plots[slot]].astype(F32)
    normal = rms(rows_in, gains_v[0]).astype(BF16)
    pack_v[:, 0:D] = normal
    for i in range(3):
        wait(get_qkv[i : i + 1])
        qkv_v[:, i * D : (i + 1) * D] = mm(normal, wqkv_v[:, i * D : (i + 1) * D]).astype(BF16)
    puts = [copies(qkv_v, qkv_o)]
    puts[-1].start()
    put_slow = []
    if slot == 0:
        put_slow = [copies(g1_v, g1_o), copies(g2_v, g2_o), copies(h2_v, h2_o)]
    query_index = lax.broadcasted_iota(jnp.int32, (2 * SEQ, SEQ), 1)
    key_index = key_index_rows()
    count = info[COUNT + slot : COUNT + slot + 1, 0:1]
    limit = jnp.where(encoding, jnp.broadcast_to(count - 1, (2 * SEQ, SEQ)), query_index)
    allowed = key_index <= limit
    for pair in range(PAIRS):
        lanes = slice(pair * 128, (pair + 1) * 128)
        weights, mixed = attend(
            qkv_v[:, lanes],
            qkv_v[:, D + pair * 128 : D + (pair + 1) * 128],
            qkv_v[:, 2 * D + pair * 128 : 2 * D + (pair + 1) * 128],
            allowed,
            masks,
        )
        p_v[pair] = weights
        pack_v[:, D + pair * 128 : D + (pair + 1) * 128] = mixed
    puts.append(copies(p_v, p_o))
    puts[-1].start()
    wait(get_out)
    first = rows_in + mm(pack_v[:, D : 2 * D], wout_v[...])
    h1_v[...] = first
    normal = rms(first, gains_v[1]).astype(BF16)
    pack_v[:, 2 * D : 3 * D] = normal
    put_units = copies(pack_v.at[:, pl.ds(3 * D, FF)], pack_o.at[:, pl.ds(3 * D, FF)])
    puts.append(copies(pack_v.at[:, pl.ds(0, 3 * D)], pack_o.at[:, pl.ds(0, 3 * D)]))
    puts[-1].start()

    @pl.when(encoding)
    def _():
        inputs = pack_v[:, 2 * D : 3 * D]
        for i in range(FF // tile):
            wait(get_in[2 * i : 2 * i + 2])
            columns = slice(i * tile, (i + 1) * tile)
            gate = mm(inputs, win_v[:, columns])
            up = mm(inputs, win_v[:, FF + i * tile : FF + (i + 1) * tile])
            unit, to_gate, to_up = gate_parts(gate, up)
            pack_v[:, 3 * D + i * tile : 3 * D + (i + 1) * tile] = unit.astype(BF16)
            g1_v[:, columns] = to_gate.astype(BF16)
            g2_v[:, columns] = to_up.astype(BF16)
        put_units.start()
        start(put_slow[:2])
        wait(get_down)
        second = h1_v[...] + mm(pack_v[:, 3 * D :], wdown_v[...])
        h2_v[...] = second
        start(put_slow[2:])
        memory = rms(second, gains_v[2])
        memory = jnp.where(rows_below(info, COUNT + slot), memory, 0.0).astype(BF16)
        memory_v[...] = memory
        wait(get_cross)
        send_v[...] = mm(memory, wcross_v[...]).astype(BF16)
        put_units.wait()
        wait(put_slow)

    @pl.when(jnp.logical_not(encoding))
    def _():
        wait(get_cross)
        query_v[...] = mm(pack_v[:, 2 * D : 3 * D], wcross_v[:, 0:D]).astype(BF16)
        wait(get_in + get_down)

    wait(puts + get_next)


def forward(slot, scalars, arrays, fast):
    kind = (hbm, vmem)[slot]
    outs = [
        hbm(SEQ, 3 * D + FF),
        hbm(SEQ, 3 * D),
        hbm(PAIRS, 2 * SEQ, SEQ),
        vmem(SEQ, D, dtype=F32),
        vmem(SEQ, D),
        kind(SEQ, FF),
        kind(SEQ, FF),
        kind(SEQ, D, dtype=F32),
        vmem(SEQ, 2 * D),
        vmem(SEQ, D),
    ]
    scratch = [struct(SEQ, 3 * D + FF), struct(SEQ, 3 * D), struct(PAIRS, 2 * SEQ, SEQ)]
    if slot == 0:
        outs += [vmem(8, 128, dtype=jnp.int32), vmem(3, 1, D, dtype=F32), vmem(2, SEQ, D)]
        outs += [vmem(*weight.shape[1:]) for weight in arrays[5:]]
        scratch += [struct(2, SEQ, dtype=jnp.int32)]
        scratch += [pltpu.SMEM((1, 2), jnp.int32), pltpu.SMEM((2,), jnp.int32)]
        scratch += [struct(SEQ, FF), struct(SEQ, FF), struct(SEQ, D, dtype=F32)]
    else:
        outs += [vmem(2, SEQ, D)]
    return call(
        functools.partial(forward_kernel, slot), scalars, outs, scratch, 34, "forward",
        [slow(item) for item in arrays], fast,
    )


def turn_all(sources, results):
    for source, result in zip(sources, results):

        def step(i, carry):
            at = pl.ds(pl.multiple_of(i * 256, 256), 256)
            result[at, :] = source[:, at].T
            return carry

        lax.fori_loop(0, source.shape[1] // 256, step, 0)


def turn_kernel(count, *refs):
    turn_all(refs[1 : count + 1], refs[count + 1 : 2 * count + 1])


def turn(after, weights):
    return call(
        functools.partial(turn_kernel, len(weights)), [],
        [vmem(*weight.shape[::-1]) for weight in weights], [], 1, "turn", [after], weights,
    )


def turn_last_kernel(info, cot, wdownt, *refs):
    turn_all(refs[0:2], refs[2:4])
    units = refs[4]

    @pl.when(number(info, SECTION) == 1)
    def _():
        branch = halves(
            *[
                jnp.where(rows_below(info, TOKENS + i), cot[i].astype(F32), 0.0).astype(BF16)
                for i in range(2)
            ]
        )
        units[...] = mm(branch, wdownt[...])


def turn_last(fast):
    return call(
        turn_last_kernel, [],
        [vmem(3 * D, D), vmem(D, D), vmem(2 * SEQ, FF, dtype=F32)], [], 1, "turn_last", [], fast,
    )


def middle_kernel(slot, *refs):
    packs, refs = refs[: 2 * slot], refs[2 * slot :]
    info, units, gains_v, kv_v, h1_v, query_v, cot_v, win_v, wcross_v, wint_v, wcrosst_v = refs[:11]
    memory, refs = refs[11 : 11 + 2 * slot], refs[11 + 2 * slot :]
    pack_o, rhs_o, late_v, dkv_v, e2_o, de2_o, gain_o = refs[:7]
    lefts, refs = refs[7 : 7 + 2 * slot], refs[7 + 2 * slot :]
    pack_v, g1_v, g2_v, rhs_v, p_v, e2_v, de2_v, gain_v, mixed_v = refs[:9]
    held, sems = refs[9:-1], refs[-1]
    if slot == 1:

        @pl.when(number(info, SECTION) == 0)
        def _():
            copies = Copies(sems)
            get = [copies(source, target) for source, target in zip(packs, held)]
            start(get)
            wait(get)
            left_operands(0, number(info, PLACE), held, None, memory, lefts)

    @pl.when(number(info, SECTION) != 0)
    def _():
        copies = Copies(sems)
        tile = 512
        masks = lane_masks()
        count = info[COUNT + slot : COUNT + slot + 1, 0:1]
        allowed = key_index_rows() < jnp.broadcast_to(count, (2 * SEQ, SEQ))
        for pair in range(PAIRS):
            lanes = slice(pair * 128, (pair + 1) * 128)
            weights, mixed = attend(
                query_v[:, lanes],
                kv_v[:, lanes],
                kv_v[:, D + pair * 128 : D + (pair + 1) * 128],
                allowed,
                masks,
            )
            p_v[pair] = weights
            pack_v[:, D + pair * 128 : D + (pair + 1) * 128] = mixed
        second = h1_v[...] + mm(pack_v[:, D : 2 * D], wcross_v[:, D : 2 * D])
        e2_v[...] = second
        puts = [copies(e2_v, e2_o)]
        puts[-1].start()
        normal = rms(second, gains_v[2]).astype(BF16)
        pack_v[:, 0:D] = normal
        for i in range(FF // tile):
            columns = slice(i * tile, (i + 1) * tile)
            gate = mm(normal, win_v[:, columns])
            up = mm(normal, win_v[:, FF + i * tile : FF + (i + 1) * tile])
            unit, to_gate, to_up = gate_parts(gate, up)
            pack_v[:, 2 * D + i * tile : 2 * D + (i + 1) * tile] = unit.astype(BF16)
            g1_v[:, columns] = to_gate.astype(BF16)
            g2_v[:, columns] = to_up.astype(BF16)
        puts.append(copies(pack_v, pack_o))
        puts[-1].start()
        upstream = jnp.where(rows_below(info, TOKENS + slot), cot_v[slot].astype(F32), 0.0)
        branch = upstream.astype(BF16)
        rhs_v[:, 0:D] = branch
        for i in range(FF // tile):
            columns = slice(i * tile, (i + 1) * tile)
            grad_unit = units[slot * SEQ : (slot + 1) * SEQ, columns]
            rhs_v[:, D + i * tile : D + (i + 1) * tile] = (
                grad_unit * g1_v[:, columns].astype(F32)
            ).astype(BF16)
            rhs_v[:, D + FF + i * tile : D + FF + (i + 1) * tile] = (
                grad_unit * g2_v[:, columns].astype(F32)
            ).astype(BF16)
        puts.append(copies(rhs_v, rhs_o))
        puts[-1].start()
        grad_normal = mm(rhs_v[:, D : D + 2 * FF], wint_v[...])
        back, grad_gain = rms_back(second, gains_v[2], grad_normal)
        grad_second = upstream + back
        gain_v[...] = jnp.zeros_like(gain_v)
        gain_v[2:3, :] = grad_gain
        de2_v[...] = grad_second
        puts += [copies(de2_v, de2_o), copies(gain_v, gain_o)]
        start(puts[-2:])
        branch = grad_second.astype(BF16)
        late_v[:, D : 2 * D] = branch
        mixed_v[...] = mm(branch, wcrosst_v[D : 2 * D, :]).astype(BF16)
        for pair in range(PAIRS):
            lanes = slice(pair * 128, (pair + 1) * 128)
            high = slice(D + pair * 128, D + (pair + 1) * 128)
            grad_query, grad_keys, grad_values = attend_back(
                query_v[:, lanes], kv_v[:, lanes], kv_v[:, high], p_v[pair], mixed_v[:, lanes], masks
            )
            late_v[:, lanes] = grad_query
            dkv_v[:, lanes] = grad_keys
            dkv_v[:, high] = grad_values
        wait(puts)


def middle(slot, packs, fast):
    return call(
        functools.partial(middle_kernel, slot),
        [],
        [
            hbm(SEQ, 2 * D + FF),
            hbm(SEQ, D + 2 * FF),
            vmem(SEQ, 2 * D),
            vmem(SEQ, 2 * D),
            hbm(SEQ, D, dtype=F32),
            hbm(SEQ, D, dtype=F32),
            hbm(8, D, dtype=F32),
        ]
        + [vmem(3328, 256)] * (2 * slot),
        [
            struct(SEQ, 2 * D + FF),
            struct(SEQ, FF),
            struct(SEQ, FF),
            struct(SEQ, D + 2 * FF),
            struct(PAIRS, 2 * SEQ, SEQ),
            struct(SEQ, D, dtype=F32),
            struct(SEQ, D, dtype=F32),
            struct(8, D, dtype=F32),
            struct(SEQ, D),
        ]
        + [struct(*pack.shape) for pack in packs],
        8,
        "middle",
        [slow(pack) for pack in packs],
        fast,
    )


def outer_rows(slot, info, gains_v, dkv_v, h2_v, g1_v, g2_v, wdownt_v, wcrosst_v, rhs_v):
    rhs_v[:, D + 2 * FF :] = dkv_v[...]
    grad_memory = mm(dkv_v[...], wcrosst_v[...])
    grad_memory = jnp.where(rows_below(info, COUNT + slot), grad_memory, 0.0)
    grad_second, grad_gain = rms_back(h2_v[...], gains_v[2], grad_memory)
    branch = grad_second.astype(BF16)
    rhs_v[:, 0:D] = branch
    tile = 512
    for i in range(FF // tile):
        columns = slice(i * tile, (i + 1) * tile)
        grad_unit = mm(branch, wdownt_v[:, columns])
        for k, scale in ((0, g1_v), (1, g2_v)):
            first = D + k * FF + i * tile
            rhs_v[:, first : first + tile] = (grad_unit * scale[:, columns].astype(F32)).astype(BF16)
    return grad_second, grad_gain


def inner_rows(slot, info, gains_v, acts_v, h1_v, dn_v, up_v, qkv_v, p_v, woutt_v, wqkvt_v, rhs_v, grad_v):
    rows = slice(0, SEQ)
    plot = number(info, PLOT + slot)
    back, first_gain = rms_back(h1_v[...], gains_v[1], dn_v[...])
    grad_first = up_v[...] + back
    branch = grad_first.astype(BF16)
    rhs_v[rows, 0:D] = branch
    masks = lane_masks()
    grad_mixed = mm(branch, woutt_v[...]).astype(BF16)
    for pair in range(PAIRS):
        spans = [slice(k * D + pair * 128, k * D + (pair + 1) * 128) for k in range(3)]
        parts = attend_back(
            qkv_v[:, spans[0]],
            qkv_v[:, spans[1]],
            qkv_v[:, spans[2]],
            p_v[pair],
            grad_mixed[:, pair * 128 : (pair + 1) * 128],
            masks,
        )
        for k in range(3):
            rhs_v[rows, D + k * D + pair * 128 : D + k * D + (pair + 1) * 128] = parts[k]
    grad_normal = mm(rhs_v[rows, D : 4 * D], wqkvt_v[...])
    back, zeroth_gain = rms_back(acts_v[plot].astype(F32), gains_v[0], grad_normal)
    grad_v[0, plot] = grad_first + back
    return zeroth_gain, first_gain


def early_kernel(*refs):
    packs, (qkv, p, rhs2, de2, gain2, h2, g1, g2) = refs[0:4], refs[4:12]
    info, gains_v, acts_v, dkv_v, h1_v, late_v = refs[12:18]
    wqkvt_v, woutt_v, wint_v, wdownt_v, wcrosst_v, ready_v = refs[18:24]
    (kept_v, given_v, rhs3_v, rhs_v, gain_v, grad_v) = refs[24:30]
    held = refs[30:34]
    qkv_v, p_v, up_v, dn_v, gain2_v, h2_v, units_v, sems = refs[34:]
    g1_v, g2_v = units_v.at[0], units_v.at[1]
    encoding = number(info, SECTION) == 0
    copies = Copies(sems)
    get_rows = [copies(qkv, qkv_v), copies(p, p_v)]
    get_packs = [copies(source, target) for source, target in zip(packs, held)]
    get_rhs = copies(rhs2, rhs3_v.at[:, pl.ds(0, D + 2 * FF)])
    get_rest = [copies(de2, up_v), copies(gain2, gain2_v)]
    get_enc = [copies(h2, h2_v), copies(g1, g1_v), copies(g2, g2_v)]
    start(get_rows)

    @pl.when(encoding)
    def _():
        start(get_enc)
        wait(get_enc)
        grad_second, grad_gain = outer_rows(
            0, info, gains_v, dkv_v, h2_v, g1_v, g2_v, wdownt_v, wcrosst_v, rhs3_v
        )
        up_v[...] = grad_second
        gain2_v[2:3, :] = grad_gain
        given_v[...] = ready_v[...]
        dn_v[...] = mm(rhs3_v[:, D : D + 2 * FF], wint_v[...])

    @pl.when(jnp.logical_not(encoding))
    def _():
        start(get_packs + get_rest + [get_rhs])
        wait(get_packs)
        left_operands(1, number(info, PLACE), held[:2], held[2:], None, (kept_v, given_v))
        rhs3_v[:, D + 2 * FF :] = late_v[...]
        dn_v[...] = mm(late_v[:, 0:D], wcrosst_v[0:D, :])
        wait(get_rest)
        get_rhs.wait()

    wait(get_rows)
    zeroth_gain, first_gain = inner_rows(
        0, info, gains_v, acts_v, h1_v, dn_v, up_v, qkv_v, p_v, woutt_v, wqkvt_v, rhs_v, grad_v
    )
    gain_v[...] = jnp.concatenate(
        [zeroth_gain, first_gain, gain2_v[2:3, :], jnp.zeros((5, D), F32)], axis=0
    )


def early(arrays, fast):
    return call(
        early_kernel,
        [],
        [
            vmem(3328, 256),
            vmem(3328, 256),
            vmem(SEQ, 3 * D + 2 * FF),
            vmem(SEQ, 4 * D),
            vmem(8, D, dtype=F32),
            vmem(1, 2, SEQ, D, dtype=F32),
        ],
        [struct(*pack.shape) for pack in arrays[:4]]
        + [
            struct(SEQ, 3 * D),
            struct(PAIRS, 2 * SEQ, SEQ),
            struct(SEQ, D, dtype=F32),
            struct(SEQ, D, dtype=F32),
            struct(8, D, dtype=F32),
            struct(SEQ, D, dtype=F32),
            struct(2, SEQ, FF),
        ],
        14,
        "early",
        [slow(item) for item in arrays],
        fast,
    )


def outer_kernel(rhs2, after, info, gains_v, dkv_v, h2_v, g1_v, g2_v, late_v, wdownt_v, wcrosst_v, rhs_v, up_v, gain_v, sems):
    encoding = number(info, SECTION) == 0

    @pl.when(encoding)
    def _():
        grad_second, grad_gain = outer_rows(
            1, info, gains_v, dkv_v, h2_v, g1_v, g2_v, wdownt_v, wcrosst_v, rhs_v
        )
        up_v[...] = grad_second
        gain_v[2:3, :] = grad_gain

    @pl.when(jnp.logical_not(encoding))
    def _():
        get = Copies(sems)(rhs2, rhs_v.at[:, pl.ds(0, D + 2 * FF)])
        get.start()
        rhs_v[:, D + 2 * FF :] = late_v[...]
        get.wait()


def outer(rhs2, after, fast):
    return call(
        outer_kernel,
        [],
        [vmem(SEQ, 3 * D + 2 * FF), vmem(SEQ, D, dtype=F32), vmem(8, D, dtype=F32)],
        [],
        1,
        "outer",
        [slow(rhs2), after],
        fast,
    )


def inner_kernel(*refs):
    qkv, p, de2, gain2 = refs[:4]
    info, gains_v, acts_v, h1_v, rhs3_v, dh2_v, gain3_v, before_v = refs[4:12]
    wqkvt_v, woutt_v, wint_v, wcrosst_v = refs[12:16]
    (rhs_v, grad_v, qkv_v, p_v, up_v, dn_v, gain2_v, sems) = refs[17:]
    encoding = number(info, SECTION) == 0
    copies = Copies(sems)
    get_rows = [copies(qkv, qkv_v), copies(p, p_v)]
    get_dec = [
        copies(de2, up_v),
        copies(gain2, gain2_v),
    ]
    start(get_rows)

    @pl.when(encoding)
    def _():
        dn_v[...] = mm(rhs3_v[:, D : D + 2 * FF], wint_v[...])
        up_v[...] = dh2_v[...]
        gain2_v[...] = gain3_v[...]

    @pl.when(jnp.logical_not(encoding))
    def _():
        start(get_dec)
        dn_v[...] = mm(rhs3_v[:, D + 2 * FF : 2 * D + 2 * FF], wcrosst_v[0:D, :])
        wait(get_dec)

    wait(get_rows)
    zeroth_gain, first_gain = inner_rows(
        1, info, gains_v, acts_v, h1_v, dn_v, up_v, qkv_v, p_v, woutt_v, wqkvt_v, rhs_v, grad_v
    )
    total = before_v[...] + jnp.concatenate(
        [zeroth_gain, first_gain, gain2_v[2:3, :], jnp.zeros((5, D), F32)], axis=0
    )
    upper = total.astype(BF16)
    lower = (total - upper.astype(F32)).astype(BF16)
    rhs_v[SEQ:, 0:D] = halves(upper, lower)
    rhs_v[SEQ:, D : 4 * D] = jnp.zeros((16, 3 * D), BF16)


def inner(arrays, fast):
    return call(
        inner_kernel,
        [],
        [vmem(SEQ + 16, 4 * D), vmem(1, 2, SEQ, D, dtype=F32)],
        [
            struct(SEQ, 3 * D),
            struct(PAIRS, 2 * SEQ, SEQ),
            struct(SEQ, D, dtype=F32),
            struct(SEQ, D, dtype=F32),
            struct(8, D, dtype=F32),
        ],
        8,
        "inner",
        [slow(item) for item in arrays],
        fast,
        aliases={len(arrays) + 12: 1},
    )


def output_kernel(*refs):
    pack2, e2 = refs[0:2], refs[2:4]
    info, memory, wdownt_v, out_o, out_v, z_v, e2_v, sems = refs[4], *[refs[5:7]], *refs[7:]
    encoding = number(info, SECTION) == 0
    copies = Copies(sems)
    get = []
    for i in range(2):
        at = pl.ds(i * SEQ, SEQ)
        get += [copies(pack2[i].at[:, pl.ds(2 * D, FF)], z_v.at[at]), copies(e2[i], e2_v.at[at])]

    @pl.when(encoding)
    def _():
        for i in range(2):
            out_v[0, i] = memory[i][...]

    @pl.when(jnp.logical_not(encoding))
    def _():
        start(get)
        wait(get)
        third = e2_v[...] + mm_t(z_v[...], wdownt_v[...])
        for i in range(2):
            part = third[i * SEQ : (i + 1) * SEQ]
            out_v[0, i] = jnp.where(rows_below(info, TOKENS + i), part, 0.0).astype(BF16)

    put = copies(out_v, out_o)
    put.start()
    put.wait()


def output(arrays, after, fast):
    def kernel(*refs):
        output_kernel(*refs[len(after) :])

    return call(
        kernel,
        [],
        [struct(1, 2, SEQ, D)],
        [struct(1, 2, SEQ, D), struct(2 * SEQ, FF), struct(2 * SEQ, D, dtype=F32)],
        5,
        "output",
        after + [slow(item) for item in arrays],
        fast,
    )[0]


def place_parts(place):
    return (
        lax.shift_right_logical(place, 5),
        jnp.bitwise_and(lax.shift_right_logical(place, 3), 3),
        jnp.bitwise_and(lax.shift_right_logical(place, 1), 3),
        jnp.bitwise_and(place, 1),
    )


def matching(target, columns):
    rows = target.shape[0]
    lane = lax.broadcasted_iota(jnp.int32, (rows, 128), 1)
    blocks = [jnp.where(lane + i * 128 == target, 1.0, 0.0) for i in range(columns // 128)]
    return jnp.concatenate(blocks, axis=1).astype(BF16)


def selector(place, other=0):
    y, x, z, core = place_parts(place)
    core = jnp.bitwise_xor(core, other)
    index = lax.broadcasted_iota(jnp.int32, (384, 128), 0)

    def at_least(value, *bounds):
        return sum(jnp.where(value >= bound, 1, 0) for bound in bounds)

    first = at_least(index, 96, 192, 288)
    rest = index - first * 96
    second = at_least(rest, 24, 48, 72)
    rest = rest - second * 24
    third = at_least(rest, 12)
    rest = rest - third * 12
    to_z, to_x = first, second
    return matching(
        jnp.bitwise_and(y + third, 1) * 384
        + jnp.bitwise_and(x + to_x, 3) * 96
        + jnp.bitwise_and(z + to_z, 3) * 24
        + core * 12
        + rest,
        D,
    )


def stacked(sources, first, width):
    return jnp.concatenate([source[0:SEQ, first : first + width] for source in sources], axis=0)


def along_down(place, other):
    y, x, z, core = place_parts(place)
    core = jnp.bitwise_xor(core, other)
    index = lax.broadcasted_iota(jnp.int32, (256, 128), 0)
    return matching(
        jnp.bitwise_and(y + jnp.bitwise_and(lax.shift_right_logical(index, 5), 1), 1) * 256
        + jnp.bitwise_and(z + lax.shift_right_logical(index, 6), 3) * 64
        + core * 32
        + jnp.bitwise_and(index, 31),
        512,
    )


def prepare_down(place, sources, first, result, order):
    y, x, z, core = place_parts(place)
    for chunk in range(4):
        block = first + jnp.bitwise_and(x + chunk, 3) * 256
        columns = [pl.ds(pl.multiple_of(block + half, 256), 256) for half in (0, 1024)]
        picked = jnp.concatenate(
            [jnp.concatenate([source[:, at] for source in sources], axis=0) for at in columns],
            axis=1,
        )
        at = 1920 + 256 * chunk
        result[at : at + 256, :] = mm_t(order, picked).astype(BF16)


def x_first(rows):
    blocks = [rows[(z * 4 + x) * 24 : (z * 4 + x + 1) * 24] for x in range(4) for z in range(4)]
    return jnp.concatenate(blocks, axis=0)


def left_operands(which, place, pack1, pack2, memory, results):
    last = pack2 if which else pack1
    for other, result in enumerate(results):
        along_z = selector(place, other)
        steps = (
            (0, True, pack1, 0),
            (384, True, pack1, D),
            (768, False, last, 0 if which else 2 * D),
            (1152, False, pack1 if which else memory, 2 * D if which else 0),
            (1536, False, last if which else memory, D if which else 0),
        )
        for row, to_x, sources, first in steps:
            rows = mm_t(along_z, stacked(sources, first, D))
            rows = x_first(rows) if to_x else rows
            result[row : row + 384, :] = rows.astype(BF16)
        prepare_down(place, last, 2 * D if which else 3 * D, result, along_down(place, other))


class Buffers:
    def __init__(self, refs, size):
        self.own, self.ahead, self.behind, self.one, self.three = refs
        self.size = size

    def spot(self, chunk, block):
        quarter = self.size // 4
        half = self.size // 2
        row = block * quarter
        if chunk == 0:
            return self.own, row
        low = block < 2
        if chunk == 1:
            return (self.one, row) if low else (self.ahead, row)
        if chunk == 2:
            return (self.ahead, row) if low else (self.behind, row - half)
        return (self.behind, half + row) if low else (self.three, row - half)


SENT = ((1, 2), (1, 3), (2, 0), (2, 1), (2, 2), (2, 3), (3, 0), (3, 1))
KEPT = ((0, 0), (0, 1), (0, 2), (0, 3), (1, 0), (1, 1), (3, 2), (3, 3))


def buffer_shapes(sent, size):
    return [vmem(size, 128)] * 2 if sent else [vmem(size, 128)] + [vmem(size // 2, 128)] * 2


def buffers_of(sent, refs, size):
    return Buffers((None, *refs, None, None) if sent else (refs[0], None, None, *refs[1:]), size)


def rows_of(sent, first, unit, pick):
    if sent:
        return pick(first + 3 * unit // 2, 2 * unit)
    return jnp.concatenate([pick(first, 3 * unit // 2), pick(first + 7 * unit // 2, unit // 2)], axis=0)


def store_narrow(sent, buffers, grad, offset):
    for i, (chunk, block) in enumerate(SENT if sent else KEPT):
        rows = grad[24 * i : 24 * (i + 1)]
        piece = jnp.concatenate([rows[:, 0:128], rows[:, 128:256]], axis=0).astype(BF16)
        target, row = buffers.spot(chunk, block)
        target[row + offset : row + offset + 48, :] = piece


SIZE_X, SIZE_Z = 4 * 1008, 4 * 1056


def both_sides(lefts, first, count):
    return jnp.concatenate([left[first : first + count, :] for left in lefts], axis=1)


def right_of(sources, first, width=256):
    return stacked(sources, first, width)


def left_of(sent, lefts, first):
    return rows_of(sent, first, 96, lambda row, count: both_sides(lefts, row, count))


def grads_wide_kernel(sent, lefts, wide, along_x, along_z):
    left = left_of(sent, lefts, 768)
    for i in range(16):
        store_narrow(sent, along_z, mm(left, right_of(wide, D + 256 * i)), 48 * i)
    for i in range(6):
        left = left_of(sent, lefts, 1152 if i < 3 else 1536)
        grad = mm(left, right_of(wide, D + 2 * FF + 256 * i))
        store_narrow(sent, along_z, grad, 768 + 48 * i)
    branch = right_of(wide, 0, D)
    left = rows_of(sent, 1920, 256, lambda row, count: both_sides(lefts, row, count))
    for half in range(2):
        grad = mm(left[256 * half : 256 * (half + 1)], branch)
        for k, (chunk, block) in enumerate((SENT if sent else KEPT)[4 * half : 4 * half + 4]):
            target, row = along_x.spot(chunk, block)
            for i in range(6):
                spot = row + 64 * i
                target[spot : spot + 64, :] = grad[
                    64 * k : 64 * (k + 1), 128 * i : 128 * (i + 1)
                ].astype(BF16)


def grads_thin_kernel(sent, place, lefts, thin, along_x):
    total_of = selector(place)
    total = sum(
        item[row : row + 8, 0:D].astype(F32) for item in (thin[1], thin[3]) for row in (SEQ, SEQ + 8)
    )
    upper = total.astype(BF16)
    lower = (total - upper.astype(F32)).astype(BF16)
    ordered = mm_t(upper, total_of) + mm_t(lower, total_of)
    tall = jnp.concatenate([ordered, jnp.zeros((120, 384), F32)], axis=0).T
    tall = x_first(jnp.concatenate([tall, jnp.zeros((384, 128), F32)], axis=1))
    tall = rows_of(sent, 0, 96, lambda row, count: tall[row : row + count])
    store_narrow(sent, along_x, tall, 960)
    left = left_of(sent, lefts, 0)
    for i in range(9):
        store_narrow(sent, along_x, mm(left, right_of(thin, D + 256 * i)), 384 + 48 * i)
    left = left_of(sent, lefts, 384)
    for i in range(3):
        store_narrow(sent, along_x, mm(left, right_of(thin, 256 * i)), 816 + 48 * i)


def grads(sent, thin, info, lefts, right, before):
    shapes_x = buffer_shapes(sent, SIZE_X)
    shapes = shapes_x if thin else shapes_x + buffer_shapes(sent, SIZE_Z)

    def kernel(info, *refs):
        encoding = number(info, SECTION) == 0
        results = refs[-1 - len(shapes) : -1]
        along_x = buffers_of(sent, results[: len(shapes_x)], SIZE_X)

        def run(lefts):
            if thin:
                grads_thin_kernel(sent, number(info, PLACE), lefts, refs[3:7], along_x)
            else:
                along_z = buffers_of(sent, results[len(shapes_x) :], SIZE_Z)
                grads_wide_kernel(sent, lefts, refs[3:7], along_x, along_z)

        @pl.when(encoding)
        def _():
            run((refs[0], refs[2]))

        @pl.when(jnp.logical_not(encoding))
        def _():
            run(refs[1:3])

    return call(
        kernel, [], shapes, [], 1, "grads", [], [info, *lefts, *right, *before],
        aliases={8 + i: i for i in range(len(before))},
    )


RUNS_X = ((0, 6, 32), (384, 26, 12))
RUNS_Z = ((0, 44, 12),)


def rows_for_y(runs):
    needed = sum(tiles * rows for _, tiles, rows in runs)
    return max(-(-needed // 16) * 16, 544 if runs is RUNS_X else 0)


def combine_kernel(runs, total, *refs):
    got, (last, sent, line_v) = refs[:3], refs[3:]
    size = last.shape[0]
    last[...] = total[0:size, :].astype(F32) + sum(item[...].astype(F32) for item in got)
    line_v[...] = jnp.zeros_like(line_v)
    to = 0
    for first, tiles, rows in runs:
        if rows == 12:
            for at in range(12):
                line_v[to : to + tiles, :] = last[pl.ds(first + 12 + at, tiles, stride=24), :]
                to += tiles
        else:
            for tile in range(tiles):
                line_v[to : to + rows, :] = last[first + (2 * tile + 1) * rows : first + (2 * tile + 2) * rows, :]
                to += rows
    sent[...] = line_v[...].astype(BF16)


def combine(runs, total, got, after):
    size, rows = got[0].shape[0], rows_for_y(runs)

    def kernel(*refs):
        combine_kernel(runs, *refs[len(after) :])

    return pl.pallas_call(
        kernel,
        name="combine",
        in_specs=[ANY] * len(after) + [FAST] * 4,
        out_specs=[FAST] * 2,
        out_shape=[vmem(size, 128, dtype=F32), vmem(rows, 128)],
        scratch_shapes=[pltpu.VMEM((rows, 128), F32)],
        compiler_params=pltpu.CompilerParams(vmem_limit_bytes=ROOM_BYTES),
    )(*after, *[pltpu.with_memory_space_constraint(item, pltpu.VMEM) for item in (total, *got)])


def lay(own, got, first, got_first, tiles, parts):
    for at in range(12):
        line = own[pl.ds(first + at, tiles, stride=24), :]
        line = line + got[got_first + at * tiles : got_first + (at + 1) * tiles, :]
        tile = 0
        for result, count in parts:
            for i in range(count):
                result[at, :, 128 * i : 128 * (i + 1)] = line[tile : tile + 1, :]
                tile += 1


def finish_wide_kernel(own, sent, in_o, cross_o, got):
    got[...] = sent[...].astype(F32)
    lay(own, got, 0, 0, 44, ((in_o, 32), (cross_o, 12)))


def finish_rest_kernel(own, sent, qkv_o, out_o, down_o, gains_o, got, tall_v):
    got[...] = sent[...].astype(F32)
    for tile in range(6):
        columns = slice(128 * tile, 128 * (tile + 1))
        down_o[:, columns] = own[64 * tile : 64 * tile + 32, :] + got[32 * tile : 32 * tile + 32, :]
    lay(own, got, 384, 192, 26, ((qkv_o, 18), (out_o, 6)))
    tall_v[...] = jnp.zeros_like(tall_v)
    tall_v[0:12, :] = own[960:972, :] + got[pl.ds(192 + 24, 12, stride=26), :]
    tall = tall_v[...].T
    for i in range(3):
        gains_o[i] = tall[i : i + 1, 0:12]


def finish(kernel, own, sent, shapes, more):
    return pl.pallas_call(
        kernel,
        name="finish",
        in_specs=[FAST] * 2,
        out_specs=[FAST] * len(shapes),
        out_shape=[struct(*shape, dtype=F32) for shape in shapes],
        scratch_shapes=[pltpu.VMEM(shape, F32) for shape in (sent.shape, *more)],
        compiler_params=pltpu.CompilerParams(vmem_limit_bytes=ROOM_BYTES),
    )(*[pltpu.with_memory_space_constraint(item, pltpu.VMEM) for item in (own, sent)])


def flat(y, x, z, core):
    return ((y * 4 + x) * 4 + z) * 2 + core


def shifted(array, y=0, x=0, z=0, core=0):
    pairs = []
    for a in range(2):
        for b in range(4):
            for c in range(4):
                for d in range(2):
                    source = flat(a, b, c, d)
                    target = flat((a + y) % 2, (b + x) % 4, (c + z) % 4, (d + core) % 2)
                    pairs.append((source, target))
    return lax.ppermute(array, "dp", pairs)


def add(*terms):
    total = terms[0].astype(F32)
    for term in terms[1:]:
        total = total + term.astype(F32)
    return total


def first_round(sent, axis):
    ahead, behind = sent
    return shifted(ahead, **{axis: 1}), shifted(behind, **{axis: 3})


def second_round(kept, firsts, axis):
    own, one, three = kept
    got_ahead, got_behind = firsts
    half = one.shape[0]
    last_ahead = shifted(add(one, got_ahead[:half]).astype(BF16), **{axis: 1})
    last_behind = shifted(add(three, got_behind[:half]).astype(BF16), **{axis: 3})
    low = add(own[:half], last_ahead, got_behind[half:])
    high = add(own[half:], got_ahead[half:], last_behind)
    return jnp.concatenate([low, high], axis=0).astype(BF16)


def along_one_round(total, axis):
    size = total.shape[0] // 4
    return [
        shifted(total[step * size : (step + 1) * size], **{axis: step}) for step in (2, 1, 3)
    ]


def local(
    acts,
    gains,
    qkv_weight,
    out_weight,
    mlp_in,
    mlp_out,
    cross_weight,
    patch_mask,
    table_len,
    slot_plot,
    cotangent,
):
    section = lax.axis_index("section").astype(jnp.int32).reshape(1)
    place = lax.axis_index("dp").astype(jnp.int32).reshape(1)
    gains = gains.transpose(1, 0, 2)
    weights = (qkv_weight, out_weight, mlp_in, mlp_out, cross_weight)
    made = [
        forward(0, [section, place], [slot_plot, table_len, gains, patch_mask, acts, *weights], [])
    ]
    info, gains, acts, *weights = made[0][10:]
    received = [lax.ppermute(made[0][8], "section", [(0, 1)])]
    made.append(forward(1, [], [cotangent], [info, gains, acts, *weights]))
    received.append(lax.ppermute(made[1][8], "section", [(0, 1)]))
    cot = made[1][10]
    turned = turn(slow(made[1][1]), weights[2:])
    *last, units = turn_last([info, cot, turned[1], *weights[:2]])
    turned = [*last, *turned]
    middles = []
    back = []
    memory = [item[9] for item in made]
    packs = [item[0] for item in made]
    for slot in range(2):
        h1, query = made[slot][3:5]
        middles.append(
            middle(
                slot,
                packs * slot,
                [info, units, gains, received[slot], h1, query, cot, weights[2], weights[4],
                 turned[2], turned[4], *memory * slot],
            )
        )
        back.append(lax.ppermute(middles[slot][3], "section", [(1, 0)]))
    lefts = [middles[1][7]]
    pack1, qkv, p, h1, query, g1, g2, h2 = made[0][:8]
    pack2, rhs2, late, _, e2, de2, gain2 = middles[0]
    kept_left, given_left, wide0, thin0, gain, grad_chain = early(
        [*packs, pack2, middles[1][0], qkv, p, rhs2, de2, gain2, h2, g1, g2],
        [info, gains, acts, back[0], h1, late, *turned, middles[1][8]],
    )
    lefts += [kept_left, shifted(given_left, core=1)]
    pack1, qkv, p, h1, query, g1, g2, h2 = made[1][:8]
    pack2, rhs2, late, _, e2, de2, gain2 = middles[1][:7]
    wide1, dh2, gain3 = outer(
        rhs2, gain, [info, gains, back[1], h2, g1, g2, late, turned[3], turned[4]]
    )
    wide = [wide0, wide1, shifted(wide0, core=1), shifted(wide1, core=1)]
    thin1, grad_chain = inner(
        [qkv, p, de2, gain2],
        [info, gains, acts, h1, wide1, dh2, gain3, gain, *turned[:3], turned[4], grad_chain],
    )
    thin = [thin0, thin1, shifted(thin0, core=1), shifted(thin1, core=1)]
    sent = grads(True, False, info, lefts, wide, [])
    sent_x, sent_z = grads(True, True, info, lefts, thin, sent[:2]), sent[2:]
    firsts_x, firsts_z = first_round(sent_x, "x"), first_round(sent_z, "z")
    kept = grads(False, False, info, lefts, wide, [])
    part_x, part_z = grads(False, True, info, lefts, thin, kept[:3]), kept[3:]
    out_rows = output(
        [middles[0][0], middles[1][0], middles[0][4], middles[1][4]],
        [part_x[0]],
        [info, *memory, turned[3]],
    )
    firsts_x, out_rows = lax.optimization_barrier((firsts_x, out_rows))
    total_x = second_round(part_x, firsts_x, "x")
    total_z = second_round(part_z, firsts_z, "z")
    last_x, sent_x = combine(RUNS_X, total_x, along_one_round(total_x, "z"), [])
    last_z, sent_z = combine(RUNS_Z, total_z, along_one_round(total_z, "x"), [last_x])
    grad_qkv, grad_out, grad_mlp_out, grad_gains = finish(
        finish_rest_kernel,
        last_x,
        shifted(sent_x, y=1),
        [(12, 1, 3 * D), (12, 1, D), (32, D), (3, 1, 12)],
        [(128, 128)],
    )
    grad_mlp_in, grad_cross = finish(
        finish_wide_kernel, last_z, shifted(sent_z, y=1), [(12, 1, 2 * FF), (12, 1, 2 * D)], []
    )
    return (
        out_rows,
        grad_chain,
        grad_gains.transpose(1, 0, 2),
        grad_qkv.transpose(1, 0, 2),
        grad_out.transpose(1, 0, 2),
        grad_mlp_in.transpose(1, 0, 2),
        grad_mlp_out[None],
        grad_cross.transpose(1, 0, 2),
    )


def solution(mesh):
    return jax.shard_map(
        local,
        mesh=mesh,
        in_specs=(
            P("section", "dp", None, None),
            P("section", None, None),
            P("section", None, None),
            P("section", None, None),
            P("section", None, None),
            P("section", None, None),
            P("section", None, None),
            P("dp", None),
            P("dp"),
            P("dp", None),
            P("dp", None, None),
        ),
        out_specs=(
            P("section", "dp", None, None),
            P("section", "dp", None, None),
            P("section", None, "dp"),
            P("section", "dp", None),
            P("section", "dp", None),
            P("section", "dp", None),
            P("section", "dp", None),
            P("section", "dp", None),
        ),
        check_vma=False,
    )
```

```python
import functools

import jax
import jax.numpy as jnp
from jax import lax
from jax.experimental import pallas as pl
from jax.experimental.pallas import tpu as pltpu
from jax.sharding import PartitionSpec as P

D = 768
HDIM = 64
FF = 2048
SEQ = 128
PAIRS = 6
EPS = 1e-06
NEGATIVE = -1e30
ROOM_BYTES = 11 * 2**20
SCALE = HDIM ** (-0.5)
BF16 = jnp.bfloat16
F32 = jnp.float32
ANY = pl.BlockSpec(memory_space=pl.ANY)
FAST = pl.BlockSpec(memory_space=pltpu.VMEM)
SMEM = pl.BlockSpec(memory_space=pltpu.SMEM)


def mm(left, right):
    return jnp.dot(left, right, preferred_element_type=F32)


def mm_t(left, right):
    return lax.dot_general(left, right, (((1,), (1,)), ((), ())), preferred_element_type=F32)


def mm_w(left, right):
    return lax.dot_general(left, right, (((0,), (0,)), ((), ())), preferred_element_type=F32)


def halves(first, second):
    return jnp.concatenate([first, second], axis=0)


def rms(hidden, gain):
    inverse = lax.rsqrt(jnp.mean(hidden * hidden, axis=-1, keepdims=True) + EPS)
    return hidden * inverse * gain


def rms_back(hidden, gain, upstream):
    inverse = lax.rsqrt(jnp.mean(hidden * hidden, axis=-1, keepdims=True) + EPS)
    unit = hidden * inverse
    scaled = upstream * gain
    grad_gain = jnp.sum(upstream * unit, axis=0, keepdims=True)
    middle = jnp.mean(scaled * unit, axis=-1, keepdims=True)
    return inverse * (scaled - unit * middle), grad_gain


def gate_parts(gate, up):
    inner = 0.7978845608 * (gate + 0.044715 * gate * gate * gate)
    bend = jnp.tanh(inner)
    half = 0.5 * (1.0 + bend)
    value = gate * half
    slope = half + 0.5 * gate * (1.0 - bend * bend) * 0.7978845608 * (
        1.0 + 3.0 * 0.044715 * gate * gate
    )
    return value * up, slope * up, value


def lane_masks():
    lane = lax.broadcasted_iota(jnp.int32, (SEQ, 2 * HDIM), 1)
    low = jnp.where(lane < HDIM, 1.0, 0.0).astype(F32)
    return low.astype(BF16), (1.0 - low).astype(BF16), low


def stack_heads(pair, masks):
    return jnp.concatenate([pair * masks[0], pair * masks[1]], axis=0)


def attend(query, keys, values, allowed, masks):
    scores = mm_t(stack_heads(keys, masks), query) * SCALE
    scores = jnp.where(allowed, scores, NEGATIVE)
    parts = []
    for head in range(2):
        part = scores[head * SEQ : (head + 1) * SEQ]
        power = jnp.exp(part - jnp.max(part, axis=0, keepdims=True))
        parts.append(power * (1.0 / jnp.sum(power, axis=0, keepdims=True)))
    weights = jnp.concatenate(parts, axis=0).astype(BF16)
    return weights, mm_w(weights, stack_heads(values, masks)).astype(BF16)


def attend_back(query, keys, values, weights, upstream, masks):
    key_stack = stack_heads(keys, masks)
    grad_weights = mm_t(stack_heads(values, masks), upstream)
    wide = weights.astype(F32)
    product = wide * grad_weights
    parts = []
    for head in range(2):
        rows = slice(head * SEQ, (head + 1) * SEQ)
        total = jnp.sum(product[rows], axis=0, keepdims=True)
        parts.append(product[rows] - wide[rows] * total)
    grad_scores = jnp.concatenate(parts, axis=0).astype(BF16)
    grad_query = mm_w(grad_scores, key_stack) * SCALE
    key_both = mm(grad_scores, query) * SCALE
    value_both = mm(weights, upstream)
    low = masks[2]
    high = 1.0 - low
    grad_keys = key_both[:SEQ] * low + key_both[SEQ:] * high
    grad_values = value_both[:SEQ] * low + value_both[SEQ:] * high
    return grad_query.astype(BF16), grad_keys.astype(BF16), grad_values.astype(BF16)


def key_index_rows():
    return jnp.bitwise_and(lax.broadcasted_iota(jnp.int32, (2 * SEQ, SEQ), 0), SEQ - 1)


def kept(keep_ref, plot):
    row = keep_ref[pl.ds(plot, 1), :].astype(F32)
    return jnp.sum(row, axis=1, keepdims=True).astype(jnp.int32)


SECTION, PLACE, PLOT, TOKENS, COUNT = 0, 1, 2, 4, 6


def number(info, row):
    return jnp.max(info[row : row + 1, :].astype(F32)).astype(jnp.int32)


def rows_below(info, row):
    index = lax.broadcasted_iota(jnp.int32, (SEQ, D), 0)
    return index < jnp.broadcast_to(info[row : row + 1, 0:1], (SEQ, D))


class Copies:
    def __init__(self, sems):
        self.sems = sems
        self.count = 0

    def __call__(self, source, target):
        copy = pltpu.make_async_copy(source, target, self.sems.at[self.count])
        self.count += 1
        return copy


def start(copies):
    for copy in copies:
        copy.start()


def wait(copies):
    for copy in copies:
        copy.wait()


def struct(*shape, dtype=BF16):
    return jax.ShapeDtypeStruct(shape, dtype)


def call(kernel, scalars, out_shape, scratch, sems, name, arrays, fast=(), aliases=None, flops=0, traffic=0):
    return pl.pallas_call(
        kernel,
        name=name,
        in_specs=[SMEM] * len(scalars) + [ANY] * len(arrays) + [FAST] * len(fast),
        out_specs=[FAST if is_fast(item) else ANY for item in out_shape],
        out_shape=out_shape,
        scratch_shapes=[
            pltpu.VMEM(item.shape, item.dtype) if isinstance(item, jax.ShapeDtypeStruct) else item
            for item in scratch
        ]
        + [pltpu.SemaphoreType.DMA((sems,))],
        input_output_aliases=aliases or {},
        compiler_params=pltpu.CompilerParams(vmem_limit_bytes=ROOM_BYTES),
        cost_estimate=pl.CostEstimate(flops=flops, bytes_accessed=traffic, transcendentals=0),
    )(*scalars, *arrays, *[pltpu.with_memory_space_constraint(item, pltpu.VMEM) for item in fast])


def is_fast(item):
    return not isinstance(item, jax.ShapeDtypeStruct) and item.memory_space == pltpu.VMEM


def vmem(*shape, dtype=BF16):
    return pltpu.VMEM(shape, dtype)


def hbm(*shape, dtype=BF16):
    return pltpu.HBM(shape, dtype)


def slow(array):
    return pltpu.with_memory_space_constraint(array, pltpu.HBM)


def forward_kernel(slot, *refs):
    if slot == 0:
        section, place, slot_plot, table_len, gains, keep, acts, *given = refs[:12]
        (pack_o, qkv_o, p_o, h1_v, query_v, g1_o, g2_o, h2_o, send_v, memory_v, info, gains_v, acts_v, wqkv_v, wout_v, win_v, wdown_v, wcross_v) = refs[12:30]
        (pack_v, qkv_v, p_v, keep_v, plot_s, tokens_s, g1_v, g2_v, h2_v, sems) = refs[30:]
    else:
        cot, info, gains_v, acts_v, wqkv_v, wout_v, win_v, wdown_v, wcross_v = refs[:9]
        (pack_o, qkv_o, p_o, h1_v, query_v, g1_v, g2_v, h2_v, send_v, memory_v, cot_v) = refs[9:20]
        (pack_v, qkv_v, p_v, sems) = refs[20:]
    copies = Copies(sems)
    tile = 512
    get_qkv, get_in, get_out, get_down, get_cross, get_next = [], [], [], [], [], []
    if slot == 0:
        encoding = section[0] == 0
        get_small = [
            copies(slot_plot, plot_s),
            copies(table_len, tokens_s),
            copies(acts.at[0], acts_v),
            copies(gains, gains_v),
            copies(keep, keep_v),
        ]
        w_qkv, w_out, w_in, w_down, w_cross = given
        get_qkv = [
            copies(w_qkv.at[0, :, pl.ds(i * D, D)], wqkv_v.at[:, pl.ds(i * D, D)]) for i in range(3)
        ]
        get_out = [copies(w_out.at[0], wout_v)]
        for i in range(FF // tile):
            get_in += [
                copies(
                    w_in.at[0, :, pl.ds(base + i * tile, tile)],
                    win_v.at[:, pl.ds(base + i * tile, tile)],
                )
                for base in (0, FF)
            ]
        get_down = [copies(w_down.at[0], wdown_v)]
        get_cross = [copies(w_cross.at[0], wcross_v)]
        start(get_small + get_qkv + get_out + get_in + get_down + get_cross)
        wait(get_small)
        plots = [plot_s[0, i] for i in range(2)]
        numbers = [section[0], place[0], *plots, *[tokens_s[plot] for plot in plots]]
        for row, value in enumerate(numbers):
            info[row : row + 1, :] = jnp.broadcast_to(value, (1, 128)).astype(jnp.int32)
        for i in range(2):
            info[COUNT + i : COUNT + i + 1, :] = jnp.broadcast_to(kept(keep_v, plots[i]), (1, 128))
    else:
        encoding = number(info, SECTION) == 0
        plots = [None, number(info, PLOT + 1)]
        get_next = [copies(cot, cot_v)]
        start(get_next)
    masks = lane_masks()
    rows_in = acts_v[plots[slot]].astype(F32)
    normal = rms(rows_in, gains_v[0]).astype(BF16)
    pack_v[:, 0:D] = normal
    for i in range(3):
        wait(get_qkv[i : i + 1])
        qkv_v[:, i * D : (i + 1) * D] = mm(normal, wqkv_v[:, i * D : (i + 1) * D]).astype(BF16)
    puts = [copies(qkv_v, qkv_o)]
    puts[-1].start()
    put_slow = []
    if slot == 0:
        put_slow = [copies(g1_v, g1_o), copies(g2_v, g2_o), copies(h2_v, h2_o)]
    query_index = lax.broadcasted_iota(jnp.int32, (2 * SEQ, SEQ), 1)
    key_index = key_index_rows()
    count = info[COUNT + slot : COUNT + slot + 1, 0:1]
    limit = jnp.where(encoding, jnp.broadcast_to(count - 1, (2 * SEQ, SEQ)), query_index)
    allowed = key_index <= limit
    for pair in range(PAIRS):
        lanes = slice(pair * 128, (pair + 1) * 128)
        weights, mixed = attend(
            qkv_v[:, lanes],
            qkv_v[:, D + pair * 128 : D + (pair + 1) * 128],
            qkv_v[:, 2 * D + pair * 128 : 2 * D + (pair + 1) * 128],
            allowed,
            masks,
        )
        p_v[pair] = weights
        pack_v[:, D + pair * 128 : D + (pair + 1) * 128] = mixed
    puts.append(copies(p_v, p_o))
    puts[-1].start()
    wait(get_out)
    first = rows_in + mm(pack_v[:, D : 2 * D], wout_v[...])
    h1_v[...] = first
    normal = rms(first, gains_v[1]).astype(BF16)
    pack_v[:, 2 * D : 3 * D] = normal
    put_units = copies(pack_v.at[:, pl.ds(3 * D, FF)], pack_o.at[:, pl.ds(3 * D, FF)])
    puts.append(copies(pack_v.at[:, pl.ds(0, 3 * D)], pack_o.at[:, pl.ds(0, 3 * D)]))
    puts[-1].start()

    @pl.when(encoding)
    def _():
        inputs = pack_v[:, 2 * D : 3 * D]
        for i in range(FF // tile):
            wait(get_in[2 * i : 2 * i + 2])
            columns = slice(i * tile, (i + 1) * tile)
            gate = mm(inputs, win_v[:, columns])
            up = mm(inputs, win_v[:, FF + i * tile : FF + (i + 1) * tile])
            unit, to_gate, to_up = gate_parts(gate, up)
            pack_v[:, 3 * D + i * tile : 3 * D + (i + 1) * tile] = unit.astype(BF16)
            g1_v[:, columns] = to_gate.astype(BF16)
            g2_v[:, columns] = to_up.astype(BF16)
        put_units.start()
        start(put_slow[:2])
        wait(get_down)
        second = h1_v[...] + mm(pack_v[:, 3 * D :], wdown_v[...])
        h2_v[...] = second
        start(put_slow[2:])
        memory = rms(second, gains_v[2])
        memory = jnp.where(rows_below(info, COUNT + slot), memory, 0.0).astype(BF16)
        memory_v[...] = memory
        wait(get_cross)
        send_v[...] = mm(memory, wcross_v[...]).astype(BF16)
        put_units.wait()
        wait(put_slow)

    @pl.when(jnp.logical_not(encoding))
    def _():
        wait(get_cross)
        query_v[...] = mm(pack_v[:, 2 * D : 3 * D], wcross_v[:, 0:D]).astype(BF16)
        wait(get_in + get_down)

    wait(puts + get_next)


def forward(slot, scalars, arrays, fast):
    kind = (hbm, vmem)[slot]
    outs = [
        hbm(SEQ, 3 * D + FF),
        hbm(SEQ, 3 * D),
        hbm(PAIRS, 2 * SEQ, SEQ),
        vmem(SEQ, D, dtype=F32),
        vmem(SEQ, D),
        kind(SEQ, FF),
        kind(SEQ, FF),
        kind(SEQ, D, dtype=F32),
        vmem(SEQ, 2 * D),
        vmem(SEQ, D),
    ]
    scratch = [struct(SEQ, 3 * D + FF), struct(SEQ, 3 * D), struct(PAIRS, 2 * SEQ, SEQ)]
    if slot == 0:
        outs += [vmem(8, 128, dtype=jnp.int32), vmem(3, 1, D, dtype=F32), vmem(2, SEQ, D)]
        outs += [vmem(*weight.shape[1:]) for weight in arrays[5:]]
        scratch += [struct(2, SEQ, dtype=jnp.int32)]
        scratch += [pltpu.SMEM((1, 2), jnp.int32), pltpu.SMEM((2,), jnp.int32)]
        scratch += [struct(SEQ, FF), struct(SEQ, FF), struct(SEQ, D, dtype=F32)]
    else:
        outs += [vmem(2, SEQ, D)]
    return call(
        functools.partial(forward_kernel, slot), scalars, outs, scratch, 34, "forward",
        [slow(item) for item in arrays], fast,
    )


def turn_all(sources, results):
    for source, result in zip(sources, results):

        def step(i, carry):
            at = pl.ds(pl.multiple_of(i * 256, 256), 256)
            result[at, :] = source[:, at].T
            return carry

        lax.fori_loop(0, source.shape[1] // 256, step, 0)


def turn_kernel(count, *refs):
    turn_all(refs[1 : count + 1], refs[count + 1 : 2 * count + 1])


def turn(after, weights):
    return call(
        functools.partial(turn_kernel, len(weights)), [],
        [vmem(*weight.shape[::-1]) for weight in weights], [], 1, "turn", [after], weights,
    )


def turn_last_kernel(info, cot, wdownt, *refs):
    turn_all(refs[0:2], refs[2:4])
    units = refs[4]

    @pl.when(number(info, SECTION) == 1)
    def _():
        branch = halves(
            *[
                jnp.where(rows_below(info, TOKENS + i), cot[i].astype(F32), 0.0).astype(BF16)
                for i in range(2)
            ]
        )
        units[...] = mm(branch, wdownt[...])


def turn_last(fast):
    return call(
        turn_last_kernel, [],
        [vmem(3 * D, D), vmem(D, D), vmem(2 * SEQ, FF, dtype=F32)], [], 1, "turn_last", [], fast,
    )


def middle_kernel(slot, *refs):
    packs, refs = refs[: 2 * slot], refs[2 * slot :]
    info, units, gains_v, kv_v, h1_v, query_v, cot_v, win_v, wcross_v, wint_v, wcrosst_v = refs[:11]
    memory, refs = refs[11 : 11 + 2 * slot], refs[11 + 2 * slot :]
    pack_o, rhs_o, late_v, dkv_v, e2_o, de2_o, gain_o = refs[:7]
    lefts, refs = refs[7 : 7 + 2 * slot], refs[7 + 2 * slot :]
    pack_v, g1_v, g2_v, rhs_v, p_v, e2_v, de2_v, gain_v, mixed_v = refs[:9]
    held, sems = refs[9:-1], refs[-1]
    if slot == 1:

        @pl.when(number(info, SECTION) == 0)
        def _():
            copies = Copies(sems)
            get = [copies(source, target) for source, target in zip(packs, held)]
            start(get)
            wait(get)
            left_operands(0, number(info, PLACE), held, None, memory, lefts)

    @pl.when(number(info, SECTION) != 0)
    def _():
        copies = Copies(sems)
        tile = 512
        masks = lane_masks()
        count = info[COUNT + slot : COUNT + slot + 1, 0:1]
        allowed = key_index_rows() < jnp.broadcast_to(count, (2 * SEQ, SEQ))
        for pair in range(PAIRS):
            lanes = slice(pair * 128, (pair + 1) * 128)
            weights, mixed = attend(
                query_v[:, lanes],
                kv_v[:, lanes],
                kv_v[:, D + pair * 128 : D + (pair + 1) * 128],
                allowed,
                masks,
            )
            p_v[pair] = weights
            pack_v[:, D + pair * 128 : D + (pair + 1) * 128] = mixed
        second = h1_v[...] + mm(pack_v[:, D : 2 * D], wcross_v[:, D : 2 * D])
        e2_v[...] = second
        puts = [copies(e2_v, e2_o)]
        puts[-1].start()
        normal = rms(second, gains_v[2]).astype(BF16)
        pack_v[:, 0:D] = normal
        for i in range(FF // tile):
            columns = slice(i * tile, (i + 1) * tile)
            gate = mm(normal, win_v[:, columns])
            up = mm(normal, win_v[:, FF + i * tile : FF + (i + 1) * tile])
            unit, to_gate, to_up = gate_parts(gate, up)
            pack_v[:, 2 * D + i * tile : 2 * D + (i + 1) * tile] = unit.astype(BF16)
            g1_v[:, columns] = to_gate.astype(BF16)
            g2_v[:, columns] = to_up.astype(BF16)
        puts.append(copies(pack_v, pack_o))
        puts[-1].start()
        upstream = jnp.where(rows_below(info, TOKENS + slot), cot_v[slot].astype(F32), 0.0)
        branch = upstream.astype(BF16)
        rhs_v[:, 0:D] = branch
        for i in range(FF // tile):
            columns = slice(i * tile, (i + 1) * tile)
            grad_unit = units[slot * SEQ : (slot + 1) * SEQ, columns]
            rhs_v[:, D + i * tile : D + (i + 1) * tile] = (
                grad_unit * g1_v[:, columns].astype(F32)
            ).astype(BF16)
            rhs_v[:, D + FF + i * tile : D + FF + (i + 1) * tile] = (
                grad_unit * g2_v[:, columns].astype(F32)
            ).astype(BF16)
        puts.append(copies(rhs_v, rhs_o))
        puts[-1].start()
        grad_normal = mm(rhs_v[:, D : D + 2 * FF], wint_v[...])
        back, grad_gain = rms_back(second, gains_v[2], grad_normal)
        grad_second = upstream + back
        gain_v[...] = jnp.zeros_like(gain_v)
        gain_v[2:3, :] = grad_gain
        de2_v[...] = grad_second
        puts += [copies(de2_v, de2_o), copies(gain_v, gain_o)]
        start(puts[-2:])
        branch = grad_second.astype(BF16)
        late_v[:, D : 2 * D] = branch
        mixed_v[...] = mm(branch, wcrosst_v[D : 2 * D, :]).astype(BF16)
        for pair in range(PAIRS):
            lanes = slice(pair * 128, (pair + 1) * 128)
            high = slice(D + pair * 128, D + (pair + 1) * 128)
            grad_query, grad_keys, grad_values = attend_back(
                query_v[:, lanes], kv_v[:, lanes], kv_v[:, high], p_v[pair], mixed_v[:, lanes], masks
            )
            late_v[:, lanes] = grad_query
            dkv_v[:, lanes] = grad_keys
            dkv_v[:, high] = grad_values
        wait(puts)


def middle(slot, packs, fast):
    return call(
        functools.partial(middle_kernel, slot),
        [],
        [
            hbm(SEQ, 2 * D + FF),
            hbm(SEQ, D + 2 * FF),
            vmem(SEQ, 2 * D),
            vmem(SEQ, 2 * D),
            hbm(SEQ, D, dtype=F32),
            hbm(SEQ, D, dtype=F32),
            hbm(8, D, dtype=F32),
        ]
        + [vmem(3328, 256)] * (2 * slot),
        [
            struct(SEQ, 2 * D + FF),
            struct(SEQ, FF),
            struct(SEQ, FF),
            struct(SEQ, D + 2 * FF),
            struct(PAIRS, 2 * SEQ, SEQ),
            struct(SEQ, D, dtype=F32),
            struct(SEQ, D, dtype=F32),
            struct(8, D, dtype=F32),
            struct(SEQ, D),
        ]
        + [struct(*pack.shape) for pack in packs],
        8,
        "middle",
        [slow(pack) for pack in packs],
        fast,
    )


def outer_rows(slot, info, gains_v, dkv_v, h2_v, g1_v, g2_v, wdownt_v, wcrosst_v, rhs_v):
    rhs_v[:, D + 2 * FF :] = dkv_v[...]
    grad_memory = mm(dkv_v[...], wcrosst_v[...])
    grad_memory = jnp.where(rows_below(info, COUNT + slot), grad_memory, 0.0)
    grad_second, grad_gain = rms_back(h2_v[...], gains_v[2], grad_memory)
    branch = grad_second.astype(BF16)
    rhs_v[:, 0:D] = branch
    tile = 512
    for i in range(FF // tile):
        columns = slice(i * tile, (i + 1) * tile)
        grad_unit = mm(branch, wdownt_v[:, columns])
        for k, scale in ((0, g1_v), (1, g2_v)):
            first = D + k * FF + i * tile
            rhs_v[:, first : first + tile] = (grad_unit * scale[:, columns].astype(F32)).astype(BF16)
    return grad_second, grad_gain


def inner_rows(slot, info, gains_v, acts_v, h1_v, dn_v, up_v, qkv_v, p_v, woutt_v, wqkvt_v, rhs_v, grad_v):
    rows = slice(0, SEQ)
    plot = number(info, PLOT + slot)
    back, first_gain = rms_back(h1_v[...], gains_v[1], dn_v[...])
    grad_first = up_v[...] + back
    branch = grad_first.astype(BF16)
    rhs_v[rows, 0:D] = branch
    masks = lane_masks()
    grad_mixed = mm(branch, woutt_v[...]).astype(BF16)
    for pair in range(PAIRS):
        spans = [slice(k * D + pair * 128, k * D + (pair + 1) * 128) for k in range(3)]
        parts = attend_back(
            qkv_v[:, spans[0]],
            qkv_v[:, spans[1]],
            qkv_v[:, spans[2]],
            p_v[pair],
            grad_mixed[:, pair * 128 : (pair + 1) * 128],
            masks,
        )
        for k in range(3):
            rhs_v[rows, D + k * D + pair * 128 : D + k * D + (pair + 1) * 128] = parts[k]
    grad_normal = mm(rhs_v[rows, D : 4 * D], wqkvt_v[...])
    back, zeroth_gain = rms_back(acts_v[plot].astype(F32), gains_v[0], grad_normal)
    grad_v[0, plot] = grad_first + back
    return zeroth_gain, first_gain


def early_kernel(*refs):
    packs, (qkv, p, rhs2, de2, gain2, h2, g1, g2) = refs[0:4], refs[4:12]
    info, gains_v, acts_v, dkv_v, h1_v, late_v = refs[12:18]
    wqkvt_v, woutt_v, wint_v, wdownt_v, wcrosst_v, ready_v = refs[18:24]
    (kept_v, given_v, rhs3_v, rhs_v, gain_v, grad_v) = refs[24:30]
    held = refs[30:34]
    qkv_v, p_v, up_v, dn_v, gain2_v, h2_v, units_v, sems = refs[34:]
    g1_v, g2_v = units_v.at[0], units_v.at[1]
    encoding = number(info, SECTION) == 0
    copies = Copies(sems)
    get_rows = [copies(qkv, qkv_v), copies(p, p_v)]
    get_packs = [copies(source, target) for source, target in zip(packs, held)]
    get_rhs = copies(rhs2, rhs3_v.at[:, pl.ds(0, D + 2 * FF)])
    get_rest = [copies(de2, up_v), copies(gain2, gain2_v)]
    get_enc = [copies(h2, h2_v), copies(g1, g1_v), copies(g2, g2_v)]
    start(get_rows)

    @pl.when(encoding)
    def _():
        start(get_enc)
        wait(get_enc)
        grad_second, grad_gain = outer_rows(
            0, info, gains_v, dkv_v, h2_v, g1_v, g2_v, wdownt_v, wcrosst_v, rhs3_v
        )
        up_v[...] = grad_second
        gain2_v[2:3, :] = grad_gain
        given_v[...] = ready_v[...]
        dn_v[...] = mm(rhs3_v[:, D : D + 2 * FF], wint_v[...])

    @pl.when(jnp.logical_not(encoding))
    def _():
        start(get_packs + get_rest + [get_rhs])
        wait(get_packs)
        left_operands(1, number(info, PLACE), held[:2], held[2:], None, (kept_v, given_v))
        rhs3_v[:, D + 2 * FF :] = late_v[...]
        dn_v[...] = mm(late_v[:, 0:D], wcrosst_v[0:D, :])
        wait(get_rest)
        get_rhs.wait()

    wait(get_rows)
    zeroth_gain, first_gain = inner_rows(
        0, info, gains_v, acts_v, h1_v, dn_v, up_v, qkv_v, p_v, woutt_v, wqkvt_v, rhs_v, grad_v
    )
    gain_v[...] = jnp.concatenate(
        [zeroth_gain, first_gain, gain2_v[2:3, :], jnp.zeros((5, D), F32)], axis=0
    )


def early(arrays, fast):
    return call(
        early_kernel,
        [],
        [
            vmem(3328, 256),
            vmem(3328, 256),
            vmem(SEQ, 3 * D + 2 * FF),
            vmem(SEQ, 4 * D),
            vmem(8, D, dtype=F32),
            vmem(1, 2, SEQ, D, dtype=F32),
        ],
        [struct(*pack.shape) for pack in arrays[:4]]
        + [
            struct(SEQ, 3 * D),
            struct(PAIRS, 2 * SEQ, SEQ),
            struct(SEQ, D, dtype=F32),
            struct(SEQ, D, dtype=F32),
            struct(8, D, dtype=F32),
            struct(SEQ, D, dtype=F32),
            struct(2, SEQ, FF),
        ],
        14,
        "early",
        [slow(item) for item in arrays],
        fast,
    )


def outer_kernel(rhs2, after, info, gains_v, dkv_v, h2_v, g1_v, g2_v, late_v, wdownt_v, wcrosst_v, rhs_v, up_v, gain_v, sems):
    encoding = number(info, SECTION) == 0

    @pl.when(encoding)
    def _():
        grad_second, grad_gain = outer_rows(
            1, info, gains_v, dkv_v, h2_v, g1_v, g2_v, wdownt_v, wcrosst_v, rhs_v
        )
        up_v[...] = grad_second
        gain_v[2:3, :] = grad_gain

    @pl.when(jnp.logical_not(encoding))
    def _():
        get = Copies(sems)(rhs2, rhs_v.at[:, pl.ds(0, D + 2 * FF)])
        get.start()
        rhs_v[:, D + 2 * FF :] = late_v[...]
        get.wait()


def outer(rhs2, after, fast):
    return call(
        outer_kernel,
        [],
        [vmem(SEQ, 3 * D + 2 * FF), vmem(SEQ, D, dtype=F32), vmem(8, D, dtype=F32)],
        [],
        1,
        "outer",
        [slow(rhs2), after],
        fast,
    )


def inner_kernel(*refs):
    qkv, p, de2, gain2 = refs[:4]
    info, gains_v, acts_v, h1_v, rhs3_v, dh2_v, gain3_v, before_v = refs[4:12]
    wqkvt_v, woutt_v, wint_v, wcrosst_v = refs[12:16]
    (rhs_v, grad_v, qkv_v, p_v, up_v, dn_v, gain2_v, sems) = refs[17:]
    encoding = number(info, SECTION) == 0
    copies = Copies(sems)
    get_rows = [copies(qkv, qkv_v), copies(p, p_v)]
    get_dec = [
        copies(de2, up_v),
        copies(gain2, gain2_v),
    ]
    start(get_rows)

    @pl.when(encoding)
    def _():
        dn_v[...] = mm(rhs3_v[:, D : D + 2 * FF], wint_v[...])
        up_v[...] = dh2_v[...]
        gain2_v[...] = gain3_v[...]

    @pl.when(jnp.logical_not(encoding))
    def _():
        start(get_dec)
        dn_v[...] = mm(rhs3_v[:, D + 2 * FF : 2 * D + 2 * FF], wcrosst_v[0:D, :])
        wait(get_dec)

    wait(get_rows)
    zeroth_gain, first_gain = inner_rows(
        1, info, gains_v, acts_v, h1_v, dn_v, up_v, qkv_v, p_v, woutt_v, wqkvt_v, rhs_v, grad_v
    )
    total = before_v[...] + jnp.concatenate(
        [zeroth_gain, first_gain, gain2_v[2:3, :], jnp.zeros((5, D), F32)], axis=0
    )
    upper = total.astype(BF16)
    lower = (total - upper.astype(F32)).astype(BF16)
    rhs_v[SEQ:, 0:D] = halves(upper, lower)
    rhs_v[SEQ:, D : 4 * D] = jnp.zeros((16, 3 * D), BF16)


def inner(arrays, fast):
    return call(
        inner_kernel,
        [],
        [vmem(SEQ + 16, 4 * D), vmem(1, 2, SEQ, D, dtype=F32)],
        [
            struct(SEQ, 3 * D),
            struct(PAIRS, 2 * SEQ, SEQ),
            struct(SEQ, D, dtype=F32),
            struct(SEQ, D, dtype=F32),
            struct(8, D, dtype=F32),
        ],
        8,
        "inner",
        [slow(item) for item in arrays],
        fast,
        aliases={len(arrays) + 12: 1},
    )


def output_kernel(*refs):
    pack2, e2 = refs[0:2], refs[2:4]
    info, memory, wdownt_v, out_o, out_v, z_v, e2_v, sems = refs[4], *[refs[5:7]], *refs[7:]
    encoding = number(info, SECTION) == 0
    copies = Copies(sems)
    get = []
    for i in range(2):
        at = pl.ds(i * SEQ, SEQ)
        get += [copies(pack2[i].at[:, pl.ds(2 * D, FF)], z_v.at[at]), copies(e2[i], e2_v.at[at])]

    @pl.when(encoding)
    def _():
        for i in range(2):
            out_v[0, i] = memory[i][...]

    @pl.when(jnp.logical_not(encoding))
    def _():
        start(get)
        wait(get)
        third = e2_v[...] + mm_t(z_v[...], wdownt_v[...])
        for i in range(2):
            part = third[i * SEQ : (i + 1) * SEQ]
            out_v[0, i] = jnp.where(rows_below(info, TOKENS + i), part, 0.0).astype(BF16)

    put = copies(out_v, out_o)
    put.start()
    put.wait()


def output(arrays, after, fast):
    def kernel(*refs):
        output_kernel(*refs[len(after) :])

    return call(
        kernel,
        [],
        [struct(1, 2, SEQ, D)],
        [struct(1, 2, SEQ, D), struct(2 * SEQ, FF), struct(2 * SEQ, D, dtype=F32)],
        5,
        "output",
        after + [slow(item) for item in arrays],
        fast,
    )[0]


def place_parts(place):
    return (
        lax.shift_right_logical(place, 5),
        jnp.bitwise_and(lax.shift_right_logical(place, 3), 3),
        jnp.bitwise_and(lax.shift_right_logical(place, 1), 3),
        jnp.bitwise_and(place, 1),
    )


def matching(target, columns):
    rows = target.shape[0]
    lane = lax.broadcasted_iota(jnp.int32, (rows, 128), 1)
    blocks = [jnp.where(lane + i * 128 == target, 1.0, 0.0) for i in range(columns // 128)]
    return jnp.concatenate(blocks, axis=1).astype(BF16)


def selector(place, other=0):
    y, x, z, core = place_parts(place)
    core = jnp.bitwise_xor(core, other)
    index = lax.broadcasted_iota(jnp.int32, (384, 128), 0)

    def at_least(value, *bounds):
        return sum(jnp.where(value >= bound, 1, 0) for bound in bounds)

    first = at_least(index, 96, 192, 288)
    rest = index - first * 96
    second = at_least(rest, 24, 48, 72)
    rest = rest - second * 24
    third = at_least(rest, 12)
    rest = rest - third * 12
    to_z, to_x = first, second
    return matching(
        jnp.bitwise_and(y + third, 1) * 384
        + jnp.bitwise_and(x + to_x, 3) * 96
        + jnp.bitwise_and(z + to_z, 3) * 24
        + core * 12
        + rest,
        D,
    )


def stacked(sources, first, width):
    return jnp.concatenate([source[0:SEQ, first : first + width] for source in sources], axis=0)


def along_down(place, other):
    y, x, z, core = place_parts(place)
    core = jnp.bitwise_xor(core, other)
    index = lax.broadcasted_iota(jnp.int32, (256, 128), 0)
    return matching(
        jnp.bitwise_and(y + jnp.bitwise_and(lax.shift_right_logical(index, 5), 1), 1) * 256
        + jnp.bitwise_and(z + lax.shift_right_logical(index, 6), 3) * 64
        + core * 32
        + jnp.bitwise_and(index, 31),
        512,
    )


def prepare_down(place, sources, first, result, order):
    y, x, z, core = place_parts(place)
    for chunk in range(4):
        block = first + jnp.bitwise_and(x + chunk, 3) * 256
        columns = [pl.ds(pl.multiple_of(block + half, 256), 256) for half in (0, 1024)]
        picked = jnp.concatenate(
            [jnp.concatenate([source[:, at] for source in sources], axis=0) for at in columns],
            axis=1,
        )
        at = 1920 + 256 * chunk
        result[at : at + 256, :] = mm_t(order, picked).astype(BF16)


def x_first(rows):
    blocks = [rows[(z * 4 + x) * 24 : (z * 4 + x + 1) * 24] for x in range(4) for z in range(4)]
    return jnp.concatenate(blocks, axis=0)


def left_operands(which, place, pack1, pack2, memory, results):
    last = pack2 if which else pack1
    for other, result in enumerate(results):
        along_z = selector(place, other)
        steps = (
            (0, True, pack1, 0),
            (384, True, pack1, D),
            (768, False, last, 0 if which else 2 * D),
            (1152, False, pack1 if which else memory, 2 * D if which else 0),
            (1536, False, last if which else memory, D if which else 0),
        )
        for row, to_x, sources, first in steps:
            rows = mm_t(along_z, stacked(sources, first, D))
            rows = x_first(rows) if to_x else rows
            result[row : row + 384, :] = rows.astype(BF16)
        prepare_down(place, last, 2 * D if which else 3 * D, result, along_down(place, other))


class Buffers:
    def __init__(self, refs, size):
        self.own, self.ahead, self.behind, self.one, self.three = refs
        self.size = size

    def spot(self, chunk, block):
        quarter = self.size // 4
        half = self.size // 2
        row = block * quarter
        if chunk == 0:
            return self.own, row
        low = block < 2
        if chunk == 1:
            return (self.one, row) if low else (self.ahead, row)
        if chunk == 2:
            return (self.ahead, row) if low else (self.behind, row - half)
        return (self.behind, half + row) if low else (self.three, row - half)


SENT = ((1, 2), (1, 3), (2, 0), (2, 1), (2, 2), (2, 3), (3, 0), (3, 1))
KEPT = ((0, 0), (0, 1), (0, 2), (0, 3), (1, 0), (1, 1), (3, 2), (3, 3))


def buffer_shapes(sent, size):
    return [vmem(size, 128)] * 2 if sent else [vmem(size, 128)] + [vmem(size // 2, 128)] * 2


def buffers_of(sent, refs, size):
    return Buffers((None, *refs, None, None) if sent else (refs[0], None, None, *refs[1:]), size)


def rows_of(sent, first, unit, pick):
    if sent:
        return pick(first + 3 * unit // 2, 2 * unit)
    return jnp.concatenate([pick(first, 3 * unit // 2), pick(first + 7 * unit // 2, unit // 2)], axis=0)


def store_narrow(sent, buffers, grad, offset):
    for i, (chunk, block) in enumerate(SENT if sent else KEPT):
        rows = grad[24 * i : 24 * (i + 1)]
        piece = jnp.concatenate([rows[:, 0:128], rows[:, 128:256]], axis=0).astype(BF16)
        target, row = buffers.spot(chunk, block)
        target[row + offset : row + offset + 48, :] = piece


SIZE_X, SIZE_Z = 4 * 1008, 4 * 1056


def both_sides(lefts, first, count):
    return jnp.concatenate([left[first : first + count, :] for left in lefts], axis=1)


def right_of(sources, first, width=256):
    return stacked(sources, first, width)


def left_of(sent, lefts, first):
    return rows_of(sent, first, 96, lambda row, count: both_sides(lefts, row, count))


def grads_wide_kernel(sent, lefts, wide, along_x, along_z):
    left = left_of(sent, lefts, 768)
    for i in range(16):
        store_narrow(sent, along_z, mm(left, right_of(wide, D + 256 * i)), 48 * i)
    for i in range(6):
        left = left_of(sent, lefts, 1152 if i < 3 else 1536)
        grad = mm(left, right_of(wide, D + 2 * FF + 256 * i))
        store_narrow(sent, along_z, grad, 768 + 48 * i)
    branch = right_of(wide, 0, D)
    left = rows_of(sent, 1920, 256, lambda row, count: both_sides(lefts, row, count))
    for half in range(2):
        grad = mm(left[256 * half : 256 * (half + 1)], branch)
        for k, (chunk, block) in enumerate((SENT if sent else KEPT)[4 * half : 4 * half + 4]):
            target, row = along_x.spot(chunk, block)
            for i in range(6):
                spot = row + 64 * i
                target[spot : spot + 64, :] = grad[
                    64 * k : 64 * (k + 1), 128 * i : 128 * (i + 1)
                ].astype(BF16)


def grads_thin_kernel(sent, place, lefts, thin, along_x):
    total_of = selector(place)
    total = sum(
        item[row : row + 8, 0:D].astype(F32) for item in (thin[1], thin[3]) for row in (SEQ, SEQ + 8)
    )
    upper = total.astype(BF16)
    lower = (total - upper.astype(F32)).astype(BF16)
    ordered = mm_t(upper, total_of) + mm_t(lower, total_of)
    tall = jnp.concatenate([ordered, jnp.zeros((120, 384), F32)], axis=0).T
    tall = x_first(jnp.concatenate([tall, jnp.zeros((384, 128), F32)], axis=1))
    tall = rows_of(sent, 0, 96, lambda row, count: tall[row : row + count])
    store_narrow(sent, along_x, tall, 960)
    left = left_of(sent, lefts, 0)
    for i in range(9):
        store_narrow(sent, along_x, mm(left, right_of(thin, D + 256 * i)), 384 + 48 * i)
    left = left_of(sent, lefts, 384)
    for i in range(3):
        store_narrow(sent, along_x, mm(left, right_of(thin, 256 * i)), 816 + 48 * i)


def grads(sent, thin, info, lefts, right, before):
    shapes_x = buffer_shapes(sent, SIZE_X)
    shapes = shapes_x if thin else shapes_x + buffer_shapes(sent, SIZE_Z)

    def kernel(info, *refs):
        encoding = number(info, SECTION) == 0
        results = refs[-1 - len(shapes) : -1]
        along_x = buffers_of(sent, results[: len(shapes_x)], SIZE_X)

        def run(lefts):
            if thin:
                grads_thin_kernel(sent, number(info, PLACE), lefts, refs[3:7], along_x)
            else:
                along_z = buffers_of(sent, results[len(shapes_x) :], SIZE_Z)
                grads_wide_kernel(sent, lefts, refs[3:7], along_x, along_z)

        @pl.when(encoding)
        def _():
            run((refs[0], refs[2]))

        @pl.when(jnp.logical_not(encoding))
        def _():
            run(refs[1:3])

    return call(
        kernel, [], shapes, [], 1, "grads", [], [info, *lefts, *right, *before],
        aliases={8 + i: i for i in range(len(before))},
    )


RUNS_X = ((0, 6, 32), (384, 26, 12))
RUNS_Z = ((0, 44, 12),)
LAST_ROWS = 1152


def rows_for_y(runs):
    needed = sum(tiles * rows for _, tiles, rows in runs)
    return max(-(-needed // 16) * 16, 544 if runs is RUNS_X else 0)


def combine_kernel(runs, total, *refs):
    got, (last, sent, line_v) = refs[:3], refs[3:]
    size = got[0].shape[0]
    last[0:size, :] = total[0:size, :].astype(F32) + sum(item[...].astype(F32) for item in got)
    last[size:, :] = jnp.zeros((last.shape[0] - size, 128), F32)
    line_v[...] = jnp.zeros_like(line_v)
    to = 0
    for first, tiles, rows in runs:
        if rows == 12:
            for at in range(12):
                line_v[to : to + tiles, :] = last[pl.ds(first + 12 + at, tiles, stride=24), :]
                to += tiles
        else:
            for tile in range(tiles):
                line_v[to : to + rows, :] = last[first + (2 * tile + 1) * rows : first + (2 * tile + 2) * rows, :]
                to += rows
    sent[...] = line_v[0 : sent.shape[0], :].astype(BF16)


def combine(runs, total, got, after):
    rows = rows_for_y(runs)

    def kernel(*refs):
        combine_kernel(runs, *refs[len(after) :])

    return pl.pallas_call(
        kernel,
        name="combine",
        in_specs=[ANY] * len(after) + [FAST] * 4,
        out_specs=[FAST] * 2,
        out_shape=[vmem(LAST_ROWS, 128, dtype=F32), vmem(rows, 128)],
        scratch_shapes=[pltpu.VMEM((rows + 32, 128), F32)],
        compiler_params=pltpu.CompilerParams(vmem_limit_bytes=ROOM_BYTES),
    )(*after, *[pltpu.with_memory_space_constraint(item, pltpu.VMEM) for item in (total, *got)])


def lay(own, got, first, got_first, tiles, parts):
    for at in range(12):
        line = own[pl.ds(first + at, tiles, stride=24), :]
        line = line + got[got_first + at * tiles : got_first + (at + 1) * tiles, :]
        tile = 0
        for result, count in parts:
            for i in range(count):
                result[at, :, 128 * i : 128 * (i + 1)] = line[tile : tile + 1, :]
                tile += 1


def take(got, sent):
    rows = sent.shape[0]
    got[0:rows, :] = sent[...].astype(F32)
    got[rows:, :] = jnp.zeros((got.shape[0] - rows, 128), F32)


def finish_wide_kernel(own, sent, in_o, cross_o, got):
    take(got, sent)
    lay(own, got, 0, 0, 44, ((in_o, 32), (cross_o, 12)))


def finish_rest_kernel(own, sent, qkv_o, out_o, down_o, gains_o, got, tall_v):
    take(got, sent)
    for tile in range(6):
        columns = slice(128 * tile, 128 * (tile + 1))
        down_o[:, columns] = own[64 * tile : 64 * tile + 32, :] + got[32 * tile : 32 * tile + 32, :]
    lay(own, got, 384, 192, 26, ((qkv_o, 18), (out_o, 6)))
    tall_v[...] = jnp.zeros_like(tall_v)
    tall_v[0:12, :] = own[960:972, :] + got[pl.ds(192 + 24, 12, stride=26), :]
    tall = tall_v[...].T
    for i in range(3):
        gains_o[i] = tall[i : i + 1, 0:12]


def finish(kernel, own, sent, shapes, more):
    return pl.pallas_call(
        kernel,
        name="finish",
        in_specs=[FAST] * 2,
        out_specs=[FAST] * len(shapes),
        out_shape=[struct(*shape, dtype=F32) for shape in shapes],
        scratch_shapes=[pltpu.VMEM(shape, F32) for shape in ((sent.shape[0] + 96, 128), *more)],
        compiler_params=pltpu.CompilerParams(vmem_limit_bytes=ROOM_BYTES),
    )(*[pltpu.with_memory_space_constraint(item, pltpu.VMEM) for item in (own, sent)])


def flat(y, x, z, core):
    return ((y * 4 + x) * 4 + z) * 2 + core


def shifted(array, y=0, x=0, z=0, core=0):
    pairs = []
    for a in range(2):
        for b in range(4):
            for c in range(4):
                for d in range(2):
                    source = flat(a, b, c, d)
                    target = flat((a + y) % 2, (b + x) % 4, (c + z) % 4, (d + core) % 2)
                    pairs.append((source, target))
    return lax.ppermute(array, "dp", pairs)


def add(*terms):
    total = terms[0].astype(F32)
    for term in terms[1:]:
        total = total + term.astype(F32)
    return total


def first_round(sent, axis):
    ahead, behind = sent
    return shifted(ahead, **{axis: 1}), shifted(behind, **{axis: 3})


def second_round(kept, firsts, axis):
    own, one, three = kept
    got_ahead, got_behind = firsts
    half = one.shape[0]
    last_ahead = shifted(add(one, got_ahead[:half]).astype(BF16), **{axis: 1})
    last_behind = shifted(add(three, got_behind[:half]).astype(BF16), **{axis: 3})
    low = add(own[:half], last_ahead, got_behind[half:])
    high = add(own[half:], got_ahead[half:], last_behind)
    return jnp.concatenate([low, high], axis=0).astype(BF16)


def along_one_round(total, axis):
    size = total.shape[0] // 4
    return [
        shifted(total[step * size : (step + 1) * size], **{axis: step}) for step in (2, 1, 3)
    ]


def local(
    acts,
    gains,
    qkv_weight,
    out_weight,
    mlp_in,
    mlp_out,
    cross_weight,
    patch_mask,
    table_len,
    slot_plot,
    cotangent,
):
    section = lax.axis_index("section").astype(jnp.int32).reshape(1)
    place = lax.axis_index("dp").astype(jnp.int32).reshape(1)
    gains = gains.transpose(1, 0, 2)
    weights = (qkv_weight, out_weight, mlp_in, mlp_out, cross_weight)
    made = [
        forward(0, [section, place], [slot_plot, table_len, gains, patch_mask, acts, *weights], [])
    ]
    info, gains, acts, *weights = made[0][10:]
    received = [lax.ppermute(made[0][8], "section", [(0, 1)])]
    made.append(forward(1, [], [cotangent], [info, gains, acts, *weights]))
    received.append(lax.ppermute(made[1][8], "section", [(0, 1)]))
    cot = made[1][10]
    turned = turn(slow(made[1][1]), weights[2:])
    *last, units = turn_last([info, cot, turned[1], *weights[:2]])
    turned = [*last, *turned]
    middles = []
    back = []
    memory = [item[9] for item in made]
    packs = [item[0] for item in made]
    for slot in range(2):
        h1, query = made[slot][3:5]
        middles.append(
            middle(
                slot,
                packs * slot,
                [info, units, gains, received[slot], h1, query, cot, weights[2], weights[4],
                 turned[2], turned[4], *memory * slot],
            )
        )
        back.append(lax.ppermute(middles[slot][3], "section", [(1, 0)]))
    lefts = [middles[1][7]]
    pack1, qkv, p, h1, query, g1, g2, h2 = made[0][:8]
    pack2, rhs2, late, _, e2, de2, gain2 = middles[0]
    kept_left, given_left, wide0, thin0, gain, grad_chain = early(
        [*packs, pack2, middles[1][0], qkv, p, rhs2, de2, gain2, h2, g1, g2],
        [info, gains, acts, back[0], h1, late, *turned, middles[1][8]],
    )
    lefts += [kept_left, shifted(given_left, core=1)]
    pack1, qkv, p, h1, query, g1, g2, h2 = made[1][:8]
    pack2, rhs2, late, _, e2, de2, gain2 = middles[1][:7]
    wide1, dh2, gain3 = outer(
        rhs2, gain, [info, gains, back[1], h2, g1, g2, late, turned[3], turned[4]]
    )
    wide = [wide0, wide1, shifted(wide0, core=1), shifted(wide1, core=1)]
    thin1, grad_chain = inner(
        [qkv, p, de2, gain2],
        [info, gains, acts, h1, wide1, dh2, gain3, gain, *turned[:3], turned[4], grad_chain],
    )
    thin = [thin0, thin1, shifted(thin0, core=1), shifted(thin1, core=1)]
    sent = grads(True, False, info, lefts, wide, [])
    sent_x, sent_z = grads(True, True, info, lefts, thin, sent[:2]), sent[2:]
    firsts_x, firsts_z = first_round(sent_x, "x"), first_round(sent_z, "z")
    kept = grads(False, False, info, lefts, wide, [])
    part_x, part_z = grads(False, True, info, lefts, thin, kept[:3]), kept[3:]
    out_rows = output(
        [middles[0][0], middles[1][0], middles[0][4], middles[1][4]],
        [part_x[0]],
        [info, *memory, turned[3]],
    )
    firsts_x, out_rows = lax.optimization_barrier((firsts_x, out_rows))
    total_x = second_round(part_x, firsts_x, "x")
    total_z = second_round(part_z, firsts_z, "z")
    last_x, sent_x = combine(RUNS_X, total_x, along_one_round(total_x, "z"), [])
    last_z, sent_z = combine(RUNS_Z, total_z, along_one_round(total_z, "x"), [last_x])
    grad_qkv, grad_out, grad_mlp_out, grad_gains = finish(
        finish_rest_kernel,
        last_x,
        shifted(sent_x, y=1),
        [(12, 1, 3 * D), (12, 1, D), (32, D), (3, 1, 12)],
        [(128, 128)],
    )
    grad_mlp_in, grad_cross = finish(
        finish_wide_kernel, last_z, shifted(sent_z, y=1), [(12, 1, 2 * FF), (12, 1, 2 * D)], []
    )
    return (
        out_rows,
        grad_chain,
        grad_gains.transpose(1, 0, 2),
        grad_qkv.transpose(1, 0, 2),
        grad_out.transpose(1, 0, 2),
        grad_mlp_in.transpose(1, 0, 2),
        grad_mlp_out[None],
        grad_cross.transpose(1, 0, 2),
    )


def solution(mesh):
    return jax.shard_map(
        local,
        mesh=mesh,
        in_specs=(
            P("section", "dp", None, None),
            P("section", None, None),
            P("section", None, None),
            P("section", None, None),
            P("section", None, None),
            P("section", None, None),
            P("section", None, None),
            P("dp", None),
            P("dp"),
            P("dp", None),
            P("dp", None, None),
        ),
        out_specs=(
            P("section", "dp", None, None),
            P("section", "dp", None, None),
            P("section", None, "dp"),
            P("section", "dp", None),
            P("section", "dp", None),
            P("section", "dp", None),
            P("section", "dp", None),
            P("section", "dp", None),
        ),
        check_vma=False,
    )
```

```python
import functools

import jax
import jax.numpy as jnp
from jax import lax
from jax.experimental import pallas as pl
from jax.experimental.pallas import tpu as pltpu
from jax.sharding import PartitionSpec as P

D = 768
HDIM = 64
FF = 2048
SEQ = 128
PAIRS = 6
EPS = 1e-06
NEGATIVE = -1e30
ROOM_BYTES = 11 * 2**20
SCALE = HDIM ** (-0.5)
BF16 = jnp.bfloat16
F32 = jnp.float32
ANY = pl.BlockSpec(memory_space=pl.ANY)
FAST = pl.BlockSpec(memory_space=pltpu.VMEM)
SMEM = pl.BlockSpec(memory_space=pltpu.SMEM)


def mm(left, right):
    return jnp.dot(left, right, preferred_element_type=F32)


def mm_t(left, right):
    return lax.dot_general(left, right, (((1,), (1,)), ((), ())), preferred_element_type=F32)


def mm_w(left, right):
    return lax.dot_general(left, right, (((0,), (0,)), ((), ())), preferred_element_type=F32)


def halves(first, second):
    return jnp.concatenate([first, second], axis=0)


def rms(hidden, gain):
    inverse = lax.rsqrt(jnp.mean(hidden * hidden, axis=-1, keepdims=True) + EPS)
    return hidden * inverse * gain


def rms_back(hidden, gain, upstream):
    inverse = lax.rsqrt(jnp.mean(hidden * hidden, axis=-1, keepdims=True) + EPS)
    unit = hidden * inverse
    scaled = upstream * gain
    grad_gain = jnp.sum(upstream * unit, axis=0, keepdims=True)
    middle = jnp.mean(scaled * unit, axis=-1, keepdims=True)
    return inverse * (scaled - unit * middle), grad_gain


def gate_parts(gate, up):
    inner = 0.7978845608 * (gate + 0.044715 * gate * gate * gate)
    bend = jnp.tanh(inner)
    half = 0.5 * (1.0 + bend)
    value = gate * half
    slope = half + 0.5 * gate * (1.0 - bend * bend) * 0.7978845608 * (
        1.0 + 3.0 * 0.044715 * gate * gate
    )
    return value * up, slope * up, value


def lane_masks():
    lane = lax.broadcasted_iota(jnp.int32, (SEQ, 2 * HDIM), 1)
    low = jnp.where(lane < HDIM, 1.0, 0.0).astype(F32)
    return low.astype(BF16), (1.0 - low).astype(BF16), low


def stack_heads(pair, masks):
    return jnp.concatenate([pair * masks[0], pair * masks[1]], axis=0)


def attend(query, keys, values, allowed, masks):
    scores = mm_t(stack_heads(keys, masks), query) * SCALE
    scores = jnp.where(allowed, scores, NEGATIVE)
    parts = []
    for head in range(2):
        part = scores[head * SEQ : (head + 1) * SEQ]
        power = jnp.exp(part - jnp.max(part, axis=0, keepdims=True))
        parts.append(power * (1.0 / jnp.sum(power, axis=0, keepdims=True)))
    weights = jnp.concatenate(parts, axis=0).astype(BF16)
    return weights, mm_w(weights, stack_heads(values, masks)).astype(BF16)


def attend_back(query, keys, values, weights, upstream, masks):
    key_stack = stack_heads(keys, masks)
    grad_weights = mm_t(stack_heads(values, masks), upstream)
    wide = weights.astype(F32)
    product = wide * grad_weights
    parts = []
    for head in range(2):
        rows = slice(head * SEQ, (head + 1) * SEQ)
        total = jnp.sum(product[rows], axis=0, keepdims=True)
        parts.append(product[rows] - wide[rows] * total)
    grad_scores = jnp.concatenate(parts, axis=0).astype(BF16)
    grad_query = mm_w(grad_scores, key_stack) * SCALE
    key_both = mm(grad_scores, query) * SCALE
    value_both = mm(weights, upstream)
    low = masks[2]
    high = 1.0 - low
    grad_keys = key_both[:SEQ] * low + key_both[SEQ:] * high
    grad_values = value_both[:SEQ] * low + value_both[SEQ:] * high
    return grad_query.astype(BF16), grad_keys.astype(BF16), grad_values.astype(BF16)


def key_index_rows():
    return jnp.bitwise_and(lax.broadcasted_iota(jnp.int32, (2 * SEQ, SEQ), 0), SEQ - 1)


def kept(keep_ref, plot):
    row = keep_ref[pl.ds(plot, 1), :].astype(F32)
    return jnp.sum(row, axis=1, keepdims=True).astype(jnp.int32)


SECTION, PLACE, PLOT, TOKENS, COUNT = 0, 1, 2, 4, 6


def number(info, row):
    return jnp.max(info[row : row + 1, :].astype(F32)).astype(jnp.int32)


def rows_below(info, row):
    index = lax.broadcasted_iota(jnp.int32, (SEQ, D), 0)
    return index < jnp.broadcast_to(info[row : row + 1, 0:1], (SEQ, D))


class Copies:
    def __init__(self, sems):
        self.sems = sems
        self.count = 0

    def __call__(self, source, target):
        copy = pltpu.make_async_copy(source, target, self.sems.at[self.count])
        self.count += 1
        return copy


def start(copies):
    for copy in copies:
        copy.start()


def wait(copies):
    for copy in copies:
        copy.wait()


def struct(*shape, dtype=BF16):
    return jax.ShapeDtypeStruct(shape, dtype)


def call(kernel, scalars, out_shape, scratch, sems, name, arrays, fast=(), aliases=None, flops=0, traffic=0):
    return pl.pallas_call(
        kernel,
        name=name,
        in_specs=[SMEM] * len(scalars) + [ANY] * len(arrays) + [FAST] * len(fast),
        out_specs=[FAST if is_fast(item) else ANY for item in out_shape],
        out_shape=out_shape,
        scratch_shapes=[
            pltpu.VMEM(item.shape, item.dtype) if isinstance(item, jax.ShapeDtypeStruct) else item
            for item in scratch
        ]
        + [pltpu.SemaphoreType.DMA((sems,))],
        input_output_aliases=aliases or {},
        compiler_params=pltpu.CompilerParams(vmem_limit_bytes=ROOM_BYTES),
        cost_estimate=pl.CostEstimate(flops=flops, bytes_accessed=traffic, transcendentals=0),
    )(*scalars, *arrays, *[pltpu.with_memory_space_constraint(item, pltpu.VMEM) for item in fast])


def is_fast(item):
    return not isinstance(item, jax.ShapeDtypeStruct) and item.memory_space == pltpu.VMEM


def vmem(*shape, dtype=BF16):
    return pltpu.VMEM(shape, dtype)


def hbm(*shape, dtype=BF16):
    return pltpu.HBM(shape, dtype)


def slow(array):
    return pltpu.with_memory_space_constraint(array, pltpu.HBM)


def forward_kernel(slot, *refs):
    if slot == 0:
        section, place, slot_plot, table_len, gains, keep, acts, *given = refs[:12]
        (pack_o, qkv_o, p_o, h1_v, query_v, g1_v, g2_v, h2_v, send_v, memory_v, info, gains_v, acts_v, wqkv_v, wout_v, win_v, wdown_v, wcross_v) = refs[12:30]
        (pack_v, qkv_v, p_v, keep_v, plot_s, tokens_s, sems) = refs[30:]
    else:
        cot, info, gains_v, acts_v, wqkv_v, wout_v, win_v, wdown_v, wcross_v = refs[:9]
        (pack_o, qkv_o, p_o, h1_v, query_v, g1_v, g2_v, h2_v, send_v, memory_v, cot_v) = refs[9:20]
        (pack_v, qkv_v, p_v, sems) = refs[20:]
    copies = Copies(sems)
    tile = 512
    get_qkv, get_in, get_out, get_down, get_cross, get_next = [], [], [], [], [], []
    if slot == 0:
        encoding = section[0] == 0
        get_small = [
            copies(slot_plot, plot_s),
            copies(table_len, tokens_s),
            copies(acts.at[0], acts_v),
            copies(gains, gains_v),
            copies(keep, keep_v),
        ]
        w_qkv, w_out, w_in, w_down, w_cross = given
        get_qkv = [
            copies(w_qkv.at[0, :, pl.ds(i * D, D)], wqkv_v.at[:, pl.ds(i * D, D)]) for i in range(3)
        ]
        get_out = [copies(w_out.at[0], wout_v)]
        for i in range(FF // tile):
            get_in += [
                copies(
                    w_in.at[0, :, pl.ds(base + i * tile, tile)],
                    win_v.at[:, pl.ds(base + i * tile, tile)],
                )
                for base in (0, FF)
            ]
        get_down = [copies(w_down.at[0], wdown_v)]
        get_cross = [copies(w_cross.at[0], wcross_v)]
        start(get_small + get_qkv + get_out + get_in + get_down + get_cross)
        wait(get_small)
        plots = [plot_s[0, i] for i in range(2)]
        numbers = [section[0], place[0], *plots, *[tokens_s[plot] for plot in plots]]
        for row, value in enumerate(numbers):
            info[row : row + 1, :] = jnp.broadcast_to(value, (1, 128)).astype(jnp.int32)
        for i in range(2):
            info[COUNT + i : COUNT + i + 1, :] = jnp.broadcast_to(kept(keep_v, plots[i]), (1, 128))
    else:
        encoding = number(info, SECTION) == 0
        plots = [None, number(info, PLOT + 1)]
        get_next = [copies(cot, cot_v)]
        start(get_next)
    masks = lane_masks()
    rows_in = acts_v[plots[slot]].astype(F32)
    normal = rms(rows_in, gains_v[0]).astype(BF16)
    pack_v[:, 0:D] = normal
    for i in range(3):
        wait(get_qkv[i : i + 1])
        qkv_v[:, i * D : (i + 1) * D] = mm(normal, wqkv_v[:, i * D : (i + 1) * D]).astype(BF16)
    puts = [copies(qkv_v, qkv_o)]
    puts[-1].start()
    query_index = lax.broadcasted_iota(jnp.int32, (2 * SEQ, SEQ), 1)
    key_index = key_index_rows()
    count = info[COUNT + slot : COUNT + slot + 1, 0:1]
    limit = jnp.where(encoding, jnp.broadcast_to(count - 1, (2 * SEQ, SEQ)), query_index)
    allowed = key_index <= limit
    for pair in range(PAIRS):
        lanes = slice(pair * 128, (pair + 1) * 128)
        weights, mixed = attend(
            qkv_v[:, lanes],
            qkv_v[:, D + pair * 128 : D + (pair + 1) * 128],
            qkv_v[:, 2 * D + pair * 128 : 2 * D + (pair + 1) * 128],
            allowed,
            masks,
        )
        p_v[pair] = weights
        pack_v[:, D + pair * 128 : D + (pair + 1) * 128] = mixed
    puts.append(copies(p_v, p_o))
    puts[-1].start()
    wait(get_out)
    first = rows_in + mm(pack_v[:, D : 2 * D], wout_v[...])
    h1_v[...] = first
    normal = rms(first, gains_v[1]).astype(BF16)
    pack_v[:, 2 * D : 3 * D] = normal
    put_units = copies(pack_v.at[:, pl.ds(3 * D, FF)], pack_o.at[:, pl.ds(3 * D, FF)])
    puts.append(copies(pack_v.at[:, pl.ds(0, 3 * D)], pack_o.at[:, pl.ds(0, 3 * D)]))
    puts[-1].start()

    @pl.when(encoding)
    def _():
        inputs = pack_v[:, 2 * D : 3 * D]
        for i in range(FF // tile):
            wait(get_in[2 * i : 2 * i + 2])
            columns = slice(i * tile, (i + 1) * tile)
            gate = mm(inputs, win_v[:, columns])
            up = mm(inputs, win_v[:, FF + i * tile : FF + (i + 1) * tile])
            unit, to_gate, to_up = gate_parts(gate, up)
            pack_v[:, 3 * D + i * tile : 3 * D + (i + 1) * tile] = unit.astype(BF16)
            g1_v[:, columns] = to_gate.astype(BF16)
            g2_v[:, columns] = to_up.astype(BF16)
        put_units.start()
        wait(get_down)
        second = h1_v[...] + mm(pack_v[:, 3 * D :], wdown_v[...])
        h2_v[...] = second
        memory = rms(second, gains_v[2])
        memory = jnp.where(rows_below(info, COUNT + slot), memory, 0.0).astype(BF16)
        memory_v[...] = memory
        wait(get_cross)
        send_v[...] = mm(memory, wcross_v[...]).astype(BF16)
        put_units.wait()

    @pl.when(jnp.logical_not(encoding))
    def _():
        wait(get_cross)
        query_v[...] = mm(pack_v[:, 2 * D : 3 * D], wcross_v[:, 0:D]).astype(BF16)
        wait(get_in + get_down)

    wait(puts + get_next)


def forward(slot, scalars, arrays, fast):
    outs = [
        hbm(SEQ, 3 * D + FF),
        hbm(SEQ, 3 * D),
        hbm(PAIRS, 2 * SEQ, SEQ),
        vmem(SEQ, D, dtype=F32),
        vmem(SEQ, D),
        vmem(SEQ, FF),
        vmem(SEQ, FF),
        vmem(SEQ, D, dtype=F32),
        vmem(SEQ, 2 * D),
        vmem(SEQ, D),
    ]
    scratch = [struct(SEQ, 3 * D + FF), struct(SEQ, 3 * D), struct(PAIRS, 2 * SEQ, SEQ)]
    if slot == 0:
        outs += [vmem(8, 128, dtype=jnp.int32), vmem(3, 1, D, dtype=F32), vmem(2, SEQ, D)]
        outs += [vmem(*weight.shape[1:]) for weight in arrays[5:]]
        scratch += [struct(2, SEQ, dtype=jnp.int32)]
        scratch += [pltpu.SMEM((1, 2), jnp.int32), pltpu.SMEM((2,), jnp.int32)]
    else:
        outs += [vmem(2, SEQ, D)]
    return call(
        functools.partial(forward_kernel, slot), scalars, outs, scratch, 34, "forward",
        [slow(item) for item in arrays], fast,
    )


def turn_all(sources, results):
    for source, result in zip(sources, results):

        def step(i, carry):
            at = pl.ds(pl.multiple_of(i * 256, 256), 256)
            result[at, :] = source[:, at].T
            return carry

        lax.fori_loop(0, source.shape[1] // 256, step, 0)


def turn_kernel(count, *refs):
    turn_all(refs[1 : count + 1], refs[count + 1 : 2 * count + 1])


def turn(after, weights):
    return call(
        functools.partial(turn_kernel, len(weights)), [],
        [vmem(*weight.shape[::-1]) for weight in weights], [], 1, "turn", [after], weights,
    )


def turn_last_kernel(info, cot, wdownt, *refs):
    turn_all(refs[0:2], refs[2:4])
    units = refs[4]

    @pl.when(number(info, SECTION) == 1)
    def _():
        branch = halves(
            *[
                jnp.where(rows_below(info, TOKENS + i), cot[i].astype(F32), 0.0).astype(BF16)
                for i in range(2)
            ]
        )
        units[...] = mm(branch, wdownt[...])


def turn_last(fast):
    return call(
        turn_last_kernel, [],
        [vmem(3 * D, D), vmem(D, D), vmem(2 * SEQ, FF, dtype=F32)], [], 1, "turn_last", [], fast,
    )


def middle_kernel(slot, *refs):
    packs, refs = refs[: 2 * slot], refs[2 * slot :]
    info, units, gains_v, kv_v, h1_v, query_v, cot_v, win_v, wcross_v, wint_v, wcrosst_v = refs[:11]
    memory, refs = refs[11 : 11 + 2 * slot], refs[11 + 2 * slot :]
    pack_o, rhs_o, late_v, dkv_v, e2_o, de2_o, gain_o = refs[:7]
    lefts, refs = refs[7 : 7 + 2 * slot], refs[7 + 2 * slot :]
    pack_v, g1_v, g2_v, rhs_v, p_v, e2_v, de2_v, gain_v, mixed_v = refs[:9]
    held, sems = refs[9:-1], refs[-1]
    if slot == 1:

        @pl.when(number(info, SECTION) == 0)
        def _():
            copies = Copies(sems)
            get = [copies(source, target) for source, target in zip(packs, held)]
            start(get)
            wait(get)
            left_operands(0, number(info, PLACE), held, None, memory, lefts)

    @pl.when(number(info, SECTION) != 0)
    def _():
        copies = Copies(sems)
        tile = 512
        masks = lane_masks()
        count = info[COUNT + slot : COUNT + slot + 1, 0:1]
        allowed = key_index_rows() < jnp.broadcast_to(count, (2 * SEQ, SEQ))
        for pair in range(PAIRS):
            lanes = slice(pair * 128, (pair + 1) * 128)
            weights, mixed = attend(
                query_v[:, lanes],
                kv_v[:, lanes],
                kv_v[:, D + pair * 128 : D + (pair + 1) * 128],
                allowed,
                masks,
            )
            p_v[pair] = weights
            pack_v[:, D + pair * 128 : D + (pair + 1) * 128] = mixed
        second = h1_v[...] + mm(pack_v[:, D : 2 * D], wcross_v[:, D : 2 * D])
        e2_v[...] = second
        puts = [copies(e2_v, e2_o)]
        puts[-1].start()
        normal = rms(second, gains_v[2]).astype(BF16)
        pack_v[:, 0:D] = normal
        for i in range(FF // tile):
            columns = slice(i * tile, (i + 1) * tile)
            gate = mm(normal, win_v[:, columns])
            up = mm(normal, win_v[:, FF + i * tile : FF + (i + 1) * tile])
            unit, to_gate, to_up = gate_parts(gate, up)
            pack_v[:, 2 * D + i * tile : 2 * D + (i + 1) * tile] = unit.astype(BF16)
            g1_v[:, columns] = to_gate.astype(BF16)
            g2_v[:, columns] = to_up.astype(BF16)
        puts.append(copies(pack_v, pack_o))
        puts[-1].start()
        upstream = jnp.where(rows_below(info, TOKENS + slot), cot_v[slot].astype(F32), 0.0)
        branch = upstream.astype(BF16)
        rhs_v[:, 0:D] = branch
        for i in range(FF // tile):
            columns = slice(i * tile, (i + 1) * tile)
            grad_unit = units[slot * SEQ : (slot + 1) * SEQ, columns]
            rhs_v[:, D + i * tile : D + (i + 1) * tile] = (
                grad_unit * g1_v[:, columns].astype(F32)
            ).astype(BF16)
            rhs_v[:, D + FF + i * tile : D + FF + (i + 1) * tile] = (
                grad_unit * g2_v[:, columns].astype(F32)
            ).astype(BF16)
        puts.append(copies(rhs_v, rhs_o))
        puts[-1].start()
        grad_normal = mm(rhs_v[:, D : D + 2 * FF], wint_v[...])
        back, grad_gain = rms_back(second, gains_v[2], grad_normal)
        grad_second = upstream + back
        gain_v[...] = jnp.zeros_like(gain_v)
        gain_v[2:3, :] = grad_gain
        de2_v[...] = grad_second
        puts += [copies(de2_v, de2_o), copies(gain_v, gain_o)]
        start(puts[-2:])
        branch = grad_second.astype(BF16)
        late_v[:, D : 2 * D] = branch
        mixed_v[...] = mm(branch, wcrosst_v[D : 2 * D, :]).astype(BF16)
        for pair in range(PAIRS):
            lanes = slice(pair * 128, (pair + 1) * 128)
            high = slice(D + pair * 128, D + (pair + 1) * 128)
            grad_query, grad_keys, grad_values = attend_back(
                query_v[:, lanes], kv_v[:, lanes], kv_v[:, high], p_v[pair], mixed_v[:, lanes], masks
            )
            late_v[:, lanes] = grad_query
            dkv_v[:, lanes] = grad_keys
            dkv_v[:, high] = grad_values
        wait(puts)


def middle(slot, packs, fast):
    return call(
        functools.partial(middle_kernel, slot),
        [],
        [
            hbm(SEQ, 2 * D + FF),
            hbm(SEQ, D + 2 * FF),
            vmem(SEQ, 2 * D),
            vmem(SEQ, 2 * D),
            hbm(SEQ, D, dtype=F32),
            hbm(SEQ, D, dtype=F32),
            hbm(8, D, dtype=F32),
        ]
        + [vmem(3328, 256)] * (2 * slot),
        [
            struct(SEQ, 2 * D + FF),
            struct(SEQ, FF),
            struct(SEQ, FF),
            struct(SEQ, D + 2 * FF),
            struct(PAIRS, 2 * SEQ, SEQ),
            struct(SEQ, D, dtype=F32),
            struct(SEQ, D, dtype=F32),
            struct(8, D, dtype=F32),
            struct(SEQ, D),
        ]
        + [struct(*pack.shape) for pack in packs],
        8,
        "middle",
        [slow(pack) for pack in packs],
        fast,
    )


def outer_rows(slot, info, gains_v, dkv_v, h2_v, g1_v, g2_v, wdownt_v, wcrosst_v, rhs_v):
    rhs_v[:, D + 2 * FF :] = dkv_v[...]
    grad_memory = mm(dkv_v[...], wcrosst_v[...])
    grad_memory = jnp.where(rows_below(info, COUNT + slot), grad_memory, 0.0)
    grad_second, grad_gain = rms_back(h2_v[...], gains_v[2], grad_memory)
    branch = grad_second.astype(BF16)
    rhs_v[:, 0:D] = branch
    tile = 512
    for i in range(FF // tile):
        columns = slice(i * tile, (i + 1) * tile)
        grad_unit = mm(branch, wdownt_v[:, columns])
        for k, scale in ((0, g1_v), (1, g2_v)):
            first = D + k * FF + i * tile
            rhs_v[:, first : first + tile] = (grad_unit * scale[:, columns].astype(F32)).astype(BF16)
    return grad_second, grad_gain


def inner_rows(slot, info, gains_v, acts_v, h1_v, dn_v, up_v, qkv_v, p_v, woutt_v, wqkvt_v, rhs_v, grad_v):
    rows = slice(0, SEQ)
    plot = number(info, PLOT + slot)
    back, first_gain = rms_back(h1_v[...], gains_v[1], dn_v[...])
    grad_first = up_v[...] + back
    branch = grad_first.astype(BF16)
    rhs_v[rows, 0:D] = branch
    masks = lane_masks()
    grad_mixed = mm(branch, woutt_v[...]).astype(BF16)
    for pair in range(PAIRS):
        spans = [slice(k * D + pair * 128, k * D + (pair + 1) * 128) for k in range(3)]
        parts = attend_back(
            qkv_v[:, spans[0]],
            qkv_v[:, spans[1]],
            qkv_v[:, spans[2]],
            p_v[pair],
            grad_mixed[:, pair * 128 : (pair + 1) * 128],
            masks,
        )
        for k in range(3):
            rhs_v[rows, D + k * D + pair * 128 : D + k * D + (pair + 1) * 128] = parts[k]
    grad_normal = mm(rhs_v[rows, D : 4 * D], wqkvt_v[...])
    back, zeroth_gain = rms_back(acts_v[plot].astype(F32), gains_v[0], grad_normal)
    grad_v[0, plot] = grad_first + back
    return zeroth_gain, first_gain


def early_kernel(*refs):
    packs, (qkv, p, rhs2, de2, gain2) = refs[0:4], refs[4:9]
    info, gains_v, acts_v, dkv_v, h1_v, late_v, h2_v, g1_v, g2_v = refs[9:18]
    wqkvt_v, woutt_v, wint_v, wdownt_v, wcrosst_v, ready_v = refs[18:24]
    (kept_v, given_v, rhs3_v, rhs_v, gain_v, grad_v) = refs[24:30]
    held = refs[30:34]
    qkv_v, p_v, up_v, dn_v, gain2_v, sems = refs[34:]
    encoding = number(info, SECTION) == 0
    copies = Copies(sems)
    get_rows = [copies(qkv, qkv_v), copies(p, p_v)]
    get_packs = [copies(source, target) for source, target in zip(packs, held)]
    get_rhs = copies(rhs2, rhs3_v.at[:, pl.ds(0, D + 2 * FF)])
    get_rest = [copies(de2, up_v), copies(gain2, gain2_v)]
    start(get_rows)

    @pl.when(encoding)
    def _():
        grad_second, grad_gain = outer_rows(
            0, info, gains_v, dkv_v, h2_v, g1_v, g2_v, wdownt_v, wcrosst_v, rhs3_v
        )
        up_v[...] = grad_second
        gain2_v[2:3, :] = grad_gain
        given_v[...] = ready_v[...]
        dn_v[...] = mm(rhs3_v[:, D : D + 2 * FF], wint_v[...])

    @pl.when(jnp.logical_not(encoding))
    def _():
        start(get_packs + get_rest + [get_rhs])
        wait(get_packs)
        left_operands(1, number(info, PLACE), held[:2], held[2:], None, (kept_v, given_v))
        rhs3_v[:, D + 2 * FF :] = late_v[...]
        dn_v[...] = mm(late_v[:, 0:D], wcrosst_v[0:D, :])
        wait(get_rest)
        get_rhs.wait()

    wait(get_rows)
    zeroth_gain, first_gain = inner_rows(
        0, info, gains_v, acts_v, h1_v, dn_v, up_v, qkv_v, p_v, woutt_v, wqkvt_v, rhs_v, grad_v
    )
    gain_v[...] = jnp.concatenate(
        [zeroth_gain, first_gain, gain2_v[2:3, :], jnp.zeros((5, D), F32)], axis=0
    )


def early(arrays, fast):
    return call(
        early_kernel,
        [],
        [
            vmem(3328, 256),
            vmem(3328, 256),
            vmem(SEQ, 3 * D + 2 * FF),
            vmem(SEQ, 4 * D),
            vmem(8, D, dtype=F32),
            vmem(1, 2, SEQ, D, dtype=F32),
        ],
        [struct(*pack.shape) for pack in arrays[:4]]
        + [
            struct(SEQ, 3 * D),
            struct(PAIRS, 2 * SEQ, SEQ),
            struct(SEQ, D, dtype=F32),
            struct(SEQ, D, dtype=F32),
            struct(8, D, dtype=F32),
        ],
        14,
        "early",
        [slow(item) for item in arrays],
        fast,
    )


def outer_kernel(rhs2, after, info, gains_v, dkv_v, h2_v, g1_v, g2_v, late_v, wdownt_v, wcrosst_v, rhs_v, up_v, gain_v, sems):
    encoding = number(info, SECTION) == 0

    @pl.when(encoding)
    def _():
        grad_second, grad_gain = outer_rows(
            1, info, gains_v, dkv_v, h2_v, g1_v, g2_v, wdownt_v, wcrosst_v, rhs_v
        )
        up_v[...] = grad_second
        gain_v[2:3, :] = grad_gain

    @pl.when(jnp.logical_not(encoding))
    def _():
        get = Copies(sems)(rhs2, rhs_v.at[:, pl.ds(0, D + 2 * FF)])
        get.start()
        rhs_v[:, D + 2 * FF :] = late_v[...]
        get.wait()


def outer(rhs2, after, fast):
    return call(
        outer_kernel,
        [],
        [vmem(SEQ, 3 * D + 2 * FF), vmem(SEQ, D, dtype=F32), vmem(8, D, dtype=F32)],
        [],
        1,
        "outer",
        [slow(rhs2), after],
        fast,
    )


def inner_kernel(*refs):
    qkv, p, de2, gain2 = refs[:4]
    info, gains_v, acts_v, h1_v, rhs3_v, dh2_v, gain3_v, before_v = refs[4:12]
    wqkvt_v, woutt_v, wint_v, wcrosst_v = refs[12:16]
    (rhs_v, grad_v, qkv_v, p_v, up_v, dn_v, gain2_v, sems) = refs[17:]
    encoding = number(info, SECTION) == 0
    copies = Copies(sems)
    get_rows = [copies(qkv, qkv_v), copies(p, p_v)]
    get_dec = [
        copies(de2, up_v),
        copies(gain2, gain2_v),
    ]
    start(get_rows)

    @pl.when(encoding)
    def _():
        dn_v[...] = mm(rhs3_v[:, D : D + 2 * FF], wint_v[...])
        up_v[...] = dh2_v[...]
        gain2_v[...] = gain3_v[...]

    @pl.when(jnp.logical_not(encoding))
    def _():
        start(get_dec)
        dn_v[...] = mm(rhs3_v[:, D + 2 * FF : 2 * D + 2 * FF], wcrosst_v[0:D, :])
        wait(get_dec)

    wait(get_rows)
    zeroth_gain, first_gain = inner_rows(
        1, info, gains_v, acts_v, h1_v, dn_v, up_v, qkv_v, p_v, woutt_v, wqkvt_v, rhs_v, grad_v
    )
    total = before_v[...] + jnp.concatenate(
        [zeroth_gain, first_gain, gain2_v[2:3, :], jnp.zeros((5, D), F32)], axis=0
    )
    upper = total.astype(BF16)
    lower = (total - upper.astype(F32)).astype(BF16)
    rhs_v[SEQ:, 0:D] = halves(upper, lower)
    rhs_v[SEQ:, D : 4 * D] = jnp.zeros((16, 3 * D), BF16)


def inner(arrays, fast):
    return call(
        inner_kernel,
        [],
        [vmem(SEQ + 16, 4 * D), vmem(1, 2, SEQ, D, dtype=F32)],
        [
            struct(SEQ, 3 * D),
            struct(PAIRS, 2 * SEQ, SEQ),
            struct(SEQ, D, dtype=F32),
            struct(SEQ, D, dtype=F32),
            struct(8, D, dtype=F32),
        ],
        8,
        "inner",
        [slow(item) for item in arrays],
        fast,
        aliases={len(arrays) + 12: 1},
    )


def output_kernel(*refs):
    pack2, e2 = refs[0:2], refs[2:4]
    info, memory, wdownt_v, out_o, out_v, z_v, e2_v, sems = refs[4], *[refs[5:7]], *refs[7:]
    encoding = number(info, SECTION) == 0
    copies = Copies(sems)
    get = []
    for i in range(2):
        at = pl.ds(i * SEQ, SEQ)
        get += [copies(pack2[i].at[:, pl.ds(2 * D, FF)], z_v.at[at]), copies(e2[i], e2_v.at[at])]

    @pl.when(encoding)
    def _():
        for i in range(2):
            out_v[0, i] = memory[i][...]

    @pl.when(jnp.logical_not(encoding))
    def _():
        start(get)
        wait(get)
        third = e2_v[...] + mm_t(z_v[...], wdownt_v[...])
        for i in range(2):
            part = third[i * SEQ : (i + 1) * SEQ]
            out_v[0, i] = jnp.where(rows_below(info, TOKENS + i), part, 0.0).astype(BF16)

    put = copies(out_v, out_o)
    put.start()
    put.wait()


def output(arrays, after, fast):
    def kernel(*refs):
        output_kernel(*refs[len(after) :])

    return call(
        kernel,
        [],
        [struct(1, 2, SEQ, D)],
        [struct(1, 2, SEQ, D), struct(2 * SEQ, FF), struct(2 * SEQ, D, dtype=F32)],
        5,
        "output",
        after + [slow(item) for item in arrays],
        fast,
    )[0]


def place_parts(place):
    return (
        lax.shift_right_logical(place, 5),
        jnp.bitwise_and(lax.shift_right_logical(place, 3), 3),
        jnp.bitwise_and(lax.shift_right_logical(place, 1), 3),
        jnp.bitwise_and(place, 1),
    )


def matching(target, columns):
    rows = target.shape[0]
    lane = lax.broadcasted_iota(jnp.int32, (rows, 128), 1)
    blocks = [jnp.where(lane + i * 128 == target, 1.0, 0.0) for i in range(columns // 128)]
    return jnp.concatenate(blocks, axis=1).astype(BF16)


def selector(place, other=0):
    y, x, z, core = place_parts(place)
    core = jnp.bitwise_xor(core, other)
    index = lax.broadcasted_iota(jnp.int32, (384, 128), 0)

    def at_least(value, *bounds):
        return sum(jnp.where(value >= bound, 1, 0) for bound in bounds)

    first = at_least(index, 96, 192, 288)
    rest = index - first * 96
    second = at_least(rest, 24, 48, 72)
    rest = rest - second * 24
    third = at_least(rest, 12)
    rest = rest - third * 12
    to_z, to_x = first, second
    return matching(
        jnp.bitwise_and(y + third, 1) * 384
        + jnp.bitwise_and(x + to_x, 3) * 96
        + jnp.bitwise_and(z + to_z, 3) * 24
        + core * 12
        + rest,
        D,
    )


def stacked(sources, first, width):
    return jnp.concatenate([source[0:SEQ, first : first + width] for source in sources], axis=0)


def along_down(place, other):
    y, x, z, core = place_parts(place)
    core = jnp.bitwise_xor(core, other)
    index = lax.broadcasted_iota(jnp.int32, (256, 128), 0)
    return matching(
        jnp.bitwise_and(y + jnp.bitwise_and(lax.shift_right_logical(index, 5), 1), 1) * 256
        + jnp.bitwise_and(z + lax.shift_right_logical(index, 6), 3) * 64
        + core * 32
        + jnp.bitwise_and(index, 31),
        512,
    )


def prepare_down(place, sources, first, result, order):
    y, x, z, core = place_parts(place)
    for chunk in range(4):
        block = first + jnp.bitwise_and(x + chunk, 3) * 256
        columns = [pl.ds(pl.multiple_of(block + half, 256), 256) for half in (0, 1024)]
        picked = jnp.concatenate(
            [jnp.concatenate([source[:, at] for source in sources], axis=0) for at in columns],
            axis=1,
        )
        at = 1920 + 256 * chunk
        result[at : at + 256, :] = mm_t(order, picked).astype(BF16)


def x_first(rows):
    blocks = [rows[(z * 4 + x) * 24 : (z * 4 + x + 1) * 24] for x in range(4) for z in range(4)]
    return jnp.concatenate(blocks, axis=0)


def left_operands(which, place, pack1, pack2, memory, results):
    last = pack2 if which else pack1
    for other, result in enumerate(results):
        along_z = selector(place, other)
        steps = (
            (0, True, pack1, 0),
            (384, True, pack1, D),
            (768, False, last, 0 if which else 2 * D),
            (1152, False, pack1 if which else memory, 2 * D if which else 0),
            (1536, False, last if which else memory, D if which else 0),
        )
        for row, to_x, sources, first in steps:
            rows = mm_t(along_z, stacked(sources, first, D))
            rows = x_first(rows) if to_x else rows
            result[row : row + 384, :] = rows.astype(BF16)
        prepare_down(place, last, 2 * D if which else 3 * D, result, along_down(place, other))


class Buffers:
    def __init__(self, refs, size):
        self.own, self.ahead, self.behind, self.one, self.three = refs
        self.size = size

    def spot(self, chunk, block):
        quarter = self.size // 4
        half = self.size // 2
        row = block * quarter
        if chunk == 0:
            return self.own, row
        low = block < 2
        if chunk == 1:
            return (self.one, row) if low else (self.ahead, row)
        if chunk == 2:
            return (self.ahead, row) if low else (self.behind, row - half)
        return (self.behind, half + row) if low else (self.three, row - half)


SENT = ((1, 2), (1, 3), (2, 0), (2, 1), (2, 2), (2, 3), (3, 0), (3, 1))
KEPT = ((0, 0), (0, 1), (0, 2), (0, 3), (1, 0), (1, 1), (3, 2), (3, 3))


def buffer_shapes(sent, size):
    return [vmem(size, 128)] * 2 if sent else [vmem(size, 128)] + [vmem(size // 2, 128)] * 2


def buffers_of(sent, refs, size):
    return Buffers((None, *refs, None, None) if sent else (refs[0], None, None, *refs[1:]), size)


def rows_of(sent, first, unit, pick):
    if sent:
        return pick(first + 3 * unit // 2, 2 * unit)
    return jnp.concatenate([pick(first, 3 * unit // 2), pick(first + 7 * unit // 2, unit // 2)], axis=0)


def store_narrow(sent, buffers, grad, offset):
    for i, (chunk, block) in enumerate(SENT if sent else KEPT):
        rows = grad[24 * i : 24 * (i + 1)]
        piece = jnp.concatenate([rows[:, 0:128], rows[:, 128:256]], axis=0).astype(BF16)
        target, row = buffers.spot(chunk, block)
        target[row + offset : row + offset + 48, :] = piece


SIZE_X, SIZE_Z = 4 * 1008, 4 * 1056


def both_sides(lefts, first, count):
    return jnp.concatenate([left[first : first + count, :] for left in lefts], axis=1)


def right_of(sources, first, width=256):
    return stacked(sources, first, width)


def left_of(sent, lefts, first):
    return rows_of(sent, first, 96, lambda row, count: both_sides(lefts, row, count))


def grads_wide_kernel(sent, lefts, wide, along_x, along_z):
    left = left_of(sent, lefts, 768)
    for i in range(16):
        store_narrow(sent, along_z, mm(left, right_of(wide, D + 256 * i)), 48 * i)
    for i in range(6):
        left = left_of(sent, lefts, 1152 if i < 3 else 1536)
        grad = mm(left, right_of(wide, D + 2 * FF + 256 * i))
        store_narrow(sent, along_z, grad, 768 + 48 * i)
    branch = right_of(wide, 0, D)
    left = rows_of(sent, 1920, 256, lambda row, count: both_sides(lefts, row, count))
    for half in range(2):
        grad = mm(left[256 * half : 256 * (half + 1)], branch)
        for k, (chunk, block) in enumerate((SENT if sent else KEPT)[4 * half : 4 * half + 4]):
            target, row = along_x.spot(chunk, block)
            for i in range(6):
                spot = row + 64 * i
                target[spot : spot + 64, :] = grad[
                    64 * k : 64 * (k + 1), 128 * i : 128 * (i + 1)
                ].astype(BF16)


def grads_thin_kernel(sent, place, lefts, thin, along_x):
    total_of = selector(place)
    total = sum(
        item[row : row + 8, 0:D].astype(F32) for item in (thin[1], thin[3]) for row in (SEQ, SEQ + 8)
    )
    upper = total.astype(BF16)
    lower = (total - upper.astype(F32)).astype(BF16)
    ordered = mm_t(upper, total_of) + mm_t(lower, total_of)
    tall = jnp.concatenate([ordered, jnp.zeros((120, 384), F32)], axis=0).T
    tall = x_first(jnp.concatenate([tall, jnp.zeros((384, 128), F32)], axis=1))
    tall = rows_of(sent, 0, 96, lambda row, count: tall[row : row + count])
    store_narrow(sent, along_x, tall, 960)
    left = left_of(sent, lefts, 0)
    for i in range(9):
        store_narrow(sent, along_x, mm(left, right_of(thin, D + 256 * i)), 384 + 48 * i)
    left = left_of(sent, lefts, 384)
    for i in range(3):
        store_narrow(sent, along_x, mm(left, right_of(thin, 256 * i)), 816 + 48 * i)


def grads(sent, thin, info, lefts, right, before):
    shapes_x = buffer_shapes(sent, SIZE_X)
    shapes = shapes_x if thin else shapes_x + buffer_shapes(sent, SIZE_Z)

    def kernel(info, *refs):
        encoding = number(info, SECTION) == 0
        results = refs[-1 - len(shapes) : -1]
        along_x = buffers_of(sent, results[: len(shapes_x)], SIZE_X)

        def run(lefts):
            if thin:
                grads_thin_kernel(sent, number(info, PLACE), lefts, refs[3:7], along_x)
            else:
                along_z = buffers_of(sent, results[len(shapes_x) :], SIZE_Z)
                grads_wide_kernel(sent, lefts, refs[3:7], along_x, along_z)

        @pl.when(encoding)
        def _():
            run((refs[0], refs[2]))

        @pl.when(jnp.logical_not(encoding))
        def _():
            run(refs[1:3])

    return call(
        kernel, [], shapes, [], 1, "grads", [], [info, *lefts, *right, *before],
        aliases={8 + i: i for i in range(len(before))},
    )


RUNS_X = ((0, 6, 32), (384, 26, 12))
RUNS_Z = ((0, 44, 12),)
LAST_ROWS = 1152


def rows_for_y(runs):
    needed = sum(tiles * rows for _, tiles, rows in runs)
    return max(-(-needed // 16) * 16, 544 if runs is RUNS_X else 0)


def combine_kernel(runs, total, *refs):
    got, (last, sent, line_v) = refs[:3], refs[3:]
    size = got[0].shape[0]
    last[0:size, :] = total[0:size, :].astype(F32) + sum(item[...].astype(F32) for item in got)
    last[size:, :] = jnp.zeros((last.shape[0] - size, 128), F32)
    line_v[...] = jnp.zeros_like(line_v)
    to = 0
    for first, tiles, rows in runs:
        if rows == 12:
            for at in range(12):
                line_v[to : to + tiles, :] = last[pl.ds(first + 12 + at, tiles, stride=24), :]
                to += tiles
        else:
            for tile in range(tiles):
                line_v[to : to + rows, :] = last[first + (2 * tile + 1) * rows : first + (2 * tile + 2) * rows, :]
                to += rows
    sent[...] = line_v[0 : sent.shape[0], :].astype(BF16)


def combine(runs, total, got, after):
    rows = rows_for_y(runs)

    def kernel(*refs):
        combine_kernel(runs, *refs[len(after) :])

    return pl.pallas_call(
        kernel,
        name="combine",
        in_specs=[ANY] * len(after) + [FAST] * 4,
        out_specs=[FAST] * 2,
        out_shape=[vmem(LAST_ROWS, 128, dtype=F32), vmem(rows, 128)],
        scratch_shapes=[pltpu.VMEM((rows + 32, 128), F32)],
        compiler_params=pltpu.CompilerParams(vmem_limit_bytes=ROOM_BYTES),
    )(*after, *[pltpu.with_memory_space_constraint(item, pltpu.VMEM) for item in (total, *got)])


def lay(own, got, first, got_first, tiles, parts):
    for at in range(12):
        line = own[pl.ds(first + at, tiles, stride=24), :]
        line = line + got[got_first + at * tiles : got_first + (at + 1) * tiles, :]
        tile = 0
        for result, count in parts:
            for i in range(count):
                result[at, :, 128 * i : 128 * (i + 1)] = line[tile : tile + 1, :]
                tile += 1


def take(got, sent):
    rows = sent.shape[0]
    got[0:rows, :] = sent[...].astype(F32)
    got[rows:, :] = jnp.zeros((got.shape[0] - rows, 128), F32)


def finish_wide_kernel(own, sent, in_o, cross_o, got):
    take(got, sent)
    lay(own, got, 0, 0, 44, ((in_o, 32), (cross_o, 12)))


def finish_rest_kernel(own, sent, qkv_o, out_o, down_o, gains_o, got, tall_v):
    take(got, sent)
    for tile in range(6):
        columns = slice(128 * tile, 128 * (tile + 1))
        down_o[:, columns] = own[64 * tile : 64 * tile + 32, :] + got[32 * tile : 32 * tile + 32, :]
    lay(own, got, 384, 192, 26, ((qkv_o, 18), (out_o, 6)))
    tall_v[...] = jnp.zeros_like(tall_v)
    tall_v[0:12, :] = own[960:972, :] + got[pl.ds(192 + 24, 12, stride=26), :]
    tall = tall_v[...].T
    for i in range(3):
        gains_o[i] = tall[i : i + 1, 0:12]


def finish(kernel, own, sent, shapes, more):
    return pl.pallas_call(
        kernel,
        name="finish",
        in_specs=[FAST] * 2,
        out_specs=[FAST] * len(shapes),
        out_shape=[struct(*shape, dtype=F32) for shape in shapes],
        scratch_shapes=[pltpu.VMEM(shape, F32) for shape in ((sent.shape[0] + 96, 128), *more)],
        compiler_params=pltpu.CompilerParams(vmem_limit_bytes=ROOM_BYTES),
    )(*[pltpu.with_memory_space_constraint(item, pltpu.VMEM) for item in (own, sent)])


def flat(y, x, z, core):
    return ((y * 4 + x) * 4 + z) * 2 + core


def shifted(array, y=0, x=0, z=0, core=0):
    pairs = []
    for a in range(2):
        for b in range(4):
            for c in range(4):
                for d in range(2):
                    source = flat(a, b, c, d)
                    target = flat((a + y) % 2, (b + x) % 4, (c + z) % 4, (d + core) % 2)
                    pairs.append((source, target))
    return lax.ppermute(array, "dp", pairs)


def add(*terms):
    total = terms[0].astype(F32)
    for term in terms[1:]:
        total = total + term.astype(F32)
    return total


def first_round(sent, axis):
    ahead, behind = sent
    return shifted(ahead, **{axis: 1}), shifted(behind, **{axis: 3})


def second_round(kept, firsts, axis):
    own, one, three = kept
    got_ahead, got_behind = firsts
    half = one.shape[0]
    last_ahead = shifted(add(one, got_ahead[:half]).astype(BF16), **{axis: 1})
    last_behind = shifted(add(three, got_behind[:half]).astype(BF16), **{axis: 3})
    low = add(own[:half], last_ahead, got_behind[half:])
    high = add(own[half:], got_ahead[half:], last_behind)
    return jnp.concatenate([low, high], axis=0).astype(BF16)


def along_one_round(total, axis):
    size = total.shape[0] // 4
    return [
        shifted(total[step * size : (step + 1) * size], **{axis: step}) for step in (2, 1, 3)
    ]


def local(
    acts,
    gains,
    qkv_weight,
    out_weight,
    mlp_in,
    mlp_out,
    cross_weight,
    patch_mask,
    table_len,
    slot_plot,
    cotangent,
):
    section = lax.axis_index("section").astype(jnp.int32).reshape(1)
    place = lax.axis_index("dp").astype(jnp.int32).reshape(1)
    gains = gains.transpose(1, 0, 2)
    weights = (qkv_weight, out_weight, mlp_in, mlp_out, cross_weight)
    made = [
        forward(0, [section, place], [slot_plot, table_len, gains, patch_mask, acts, *weights], [])
    ]
    info, gains, acts, *weights = made[0][10:]
    received = [lax.ppermute(made[0][8], "section", [(0, 1)])]
    made.append(forward(1, [], [cotangent], [info, gains, acts, *weights]))
    received.append(lax.ppermute(made[1][8], "section", [(0, 1)]))
    cot = made[1][10]
    turned = turn(slow(made[1][1]), weights[2:])
    *last, units = turn_last([info, cot, turned[1], *weights[:2]])
    turned = [*last, *turned]
    middles = []
    back = []
    memory = [item[9] for item in made]
    packs = [item[0] for item in made]
    for slot in range(2):
        h1, query = made[slot][3:5]
        middles.append(
            middle(
                slot,
                packs * slot,
                [info, units, gains, received[slot], h1, query, cot, weights[2], weights[4],
                 turned[2], turned[4], *memory * slot],
            )
        )
        back.append(lax.ppermute(middles[slot][3], "section", [(1, 0)]))
    lefts = [middles[1][7]]
    pack1, qkv, p, h1, query, g1, g2, h2 = made[0][:8]
    pack2, rhs2, late, _, e2, de2, gain2 = middles[0]
    kept_left, given_left, wide0, thin0, gain, grad_chain = early(
        [*packs, pack2, middles[1][0], qkv, p, rhs2, de2, gain2],
        [info, gains, acts, back[0], h1, late, h2, g1, g2, *turned, middles[1][8]],
    )
    lefts += [kept_left, shifted(given_left, core=1)]
    pack1, qkv, p, h1, query, g1, g2, h2 = made[1][:8]
    pack2, rhs2, late, _, e2, de2, gain2 = middles[1][:7]
    wide1, dh2, gain3 = outer(
        rhs2, gain, [info, gains, back[1], h2, g1, g2, late, turned[3], turned[4]]
    )
    wide = [wide0, wide1, shifted(wide0, core=1), shifted(wide1, core=1)]
    thin1, grad_chain = inner(
        [qkv, p, de2, gain2],
        [info, gains, acts, h1, wide1, dh2, gain3, gain, *turned[:3], turned[4], grad_chain],
    )
    thin = [thin0, thin1, shifted(thin0, core=1), shifted(thin1, core=1)]
    sent = grads(True, False, info, lefts, wide, [])
    sent_x, sent_z = grads(True, True, info, lefts, thin, sent[:2]), sent[2:]
    firsts_x, firsts_z = first_round(sent_x, "x"), first_round(sent_z, "z")
    kept = grads(False, False, info, lefts, wide, [])
    part_x, part_z = grads(False, True, info, lefts, thin, kept[:3]), kept[3:]
    out_rows = output(
        [middles[0][0], middles[1][0], middles[0][4], middles[1][4]],
        [part_x[0]],
        [info, *memory, turned[3]],
    )
    firsts_x, out_rows = lax.optimization_barrier((firsts_x, out_rows))
    total_x = second_round(part_x, firsts_x, "x")
    total_z = second_round(part_z, firsts_z, "z")
    last_x, sent_x = combine(RUNS_X, total_x, along_one_round(total_x, "z"), [])
    last_z, sent_z = combine(RUNS_Z, total_z, along_one_round(total_z, "x"), [last_x])
    grad_qkv, grad_out, grad_mlp_out, grad_gains = finish(
        finish_rest_kernel,
        last_x,
        shifted(sent_x, y=1),
        [(12, 1, 3 * D), (12, 1, D), (32, D), (3, 1, 12)],
        [(128, 128)],
    )
    grad_mlp_in, grad_cross = finish(
        finish_wide_kernel, last_z, shifted(sent_z, y=1), [(12, 1, 2 * FF), (12, 1, 2 * D)], []
    )
    return (
        out_rows,
        grad_chain,
        grad_gains.transpose(1, 0, 2),
        grad_qkv.transpose(1, 0, 2),
        grad_out.transpose(1, 0, 2),
        grad_mlp_in.transpose(1, 0, 2),
        grad_mlp_out[None],
        grad_cross.transpose(1, 0, 2),
    )


def solution(mesh):
    return jax.shard_map(
        local,
        mesh=mesh,
        in_specs=(
            P("section", "dp", None, None),
            P("section", None, None),
            P("section", None, None),
            P("section", None, None),
            P("section", None, None),
            P("section", None, None),
            P("section", None, None),
            P("dp", None),
            P("dp"),
            P("dp", None),
            P("dp", None, None),
        ),
        out_specs=(
            P("section", "dp", None, None),
            P("section", "dp", None, None),
            P("section", None, "dp"),
            P("section", "dp", None),
            P("section", "dp", None),
            P("section", "dp", None),
            P("section", "dp", None),
            P("section", "dp", None),
        ),
        check_vma=False,
    )
```
